32 devices in a mesh: tm: 8 (over y, x, core), space: 4 (over z).
Axes of the slice: x: 2, y: 2, z: 4, core: 2. Of those that a mesh axis runs over, the one named last changes fastest.
Arguments:
- video_tokens: bfloat16 [8, 16, 64, 1152], P('tm', 'space'), may hold values from -6 to 6
- qkv_weight: bfloat16 [1152, 3456], P('space'), may hold values from -0.1875 to 0.1875
- out_weight: bfloat16 [1152, 1152], P('space'), may hold values from -0.1875 to 0.1875
- conv_weight: float32 [3, 3, 1152], replicated, may hold values from -2 to 2
- norm_gain: float32 [1152], replicated, may hold values from 0.1 to 1.9
Outputs:
- attended: bfloat16 [8, 16, 64, 1152], P('tm', 'space')
The draws below stay inside these ranges and needn't reach their ends.
All inputs are finite; a program needn't handle non-finite values.
Results may differ from the reference program's by a relative error of at most 0.015.
Values may be sent and summed in bfloat16 or wider, within the bound.
No kernel may reach another device: no remote copies, remote signals or barrier semaphores. Data moves between devices by JAX's collectives and lax.ppermute only.
A program may use at most 64 MiB of HBM per device.

```python
import jax
import jax.numpy as jnp
from jax import lax

HEADS = 36
HEAD_DIM = 32
D = 1152
COLS = 64
ROWS = 16
FRAMES = 8


def levels(key, shape, split, least, top_value):
    factor_of = 1.0
    for axis_at, parts in split:
        steps = jax.random.uniform(jax.random.fold_in(jax.random.fold_in(key, 6), axis_at), (parts,), jnp.float32, least / len(split), top_value / len(split))
        factor_of = factor_of * jnp.repeat(jnp.exp(steps), shape[axis_at] // parts).reshape((-1,) + (1,) * (len(shape) - 1 - axis_at))
    return factor_of


def noise(rng, extent, spread, reach, cuts=(), dtype=jnp.bfloat16):
    values = spread * jax.random.normal(rng, extent, jnp.float32)
    if cuts:
        values = values * levels(rng, extent, cuts, -0.22, 0.18)
    return jnp.clip(values, -reach, reach).astype(dtype)


def setup_inputs(seed: int = 0) -> dict:
    streams_of = jax.random.split(jax.random.key(seed), 6)
    return {
        "video_tokens": noise(streams_of[0], (FRAMES, ROWS, COLS, D), 1.0, 6.0, ((0, 8), (1, 4))),
        "qkv_weight": noise(streams_of[1], (D, 3 * D), D ** -0.5, 0.1875, ((0, 4),)),
        "out_weight": noise(streams_of[2], (D, D), D ** -0.5, 0.1875, ((0, 4),)),
        "conv_weight": noise(streams_of[3], (3, 3, D), 9 ** -0.5, 2.0, (), jnp.float32),
        "norm_gain": jnp.clip(1.0 + 0.18 * jax.random.normal(streams_of[4], (D,), jnp.float32), 0.1, 1.9),
    }


def project_frame(frame_tokens, qkv_weight):
    feat_width = frame_tokens.shape[-1]
    flat_tokens = frame_tokens.reshape(-1, feat_width)
    projected = jnp.dot(flat_tokens, qkv_weight, preferred_element_type=jnp.float32)
    query_feat = lax.optimization_barrier(jax.nn.relu(projected[:, :feat_width]).astype(jnp.bfloat16))
    key_feat = lax.optimization_barrier(jax.nn.relu(projected[:, feat_width:2 * feat_width]).astype(jnp.bfloat16))
    values = lax.optimization_barrier(projected[:, 2 * feat_width:].astype(jnp.bfloat16))
    key_heads = key_feat.astype(jnp.float32).reshape(-1, HEADS, HEAD_DIM)
    value_heads = values.astype(jnp.float32).reshape(-1, HEADS, HEAD_DIM)
    frame_state = jnp.einsum('thd,the->hde', key_heads, value_heads, precision=lax.Precision.HIGHEST)
    return (query_feat, values, frame_state)

def finish_frame(query_feat, values, causal_state, out_weight, conv_weight, norm_gain):
    feat_width = query_feat.shape[-1]
    state_low = lax.optimization_barrier(causal_state.astype(jnp.bfloat16))
    query_heads = query_feat.astype(jnp.float32).reshape(-1, HEADS, HEAD_DIM)
    readout = jnp.einsum('thd,hde->the', query_heads, state_low.astype(jnp.float32), precision=lax.Precision.HIGHEST)
    readout = readout.reshape(-1, feat_width)
    mean_square = lax.optimization_barrier(jnp.mean(readout * readout, axis=-1, keepdims=True))
    normed = readout * lax.rsqrt(mean_square + 1e-06) * norm_gain
    value_grid = values.astype(jnp.float32).reshape(ROWS, COLS, feat_width)
    padded = jnp.pad(value_grid, ((1, 1), (1, 1), (0, 0)))
    local_term = jnp.zeros((ROWS, COLS, feat_width), jnp.float32)
    for row_shift in range(3):
        for col_shift in range(3):
            local_term = local_term + conv_weight[row_shift, col_shift] * padded[row_shift:row_shift + ROWS, col_shift:col_shift + COLS]
    mixture = (normed + local_term.reshape(-1, feat_width)).astype(jnp.bfloat16)
    result = jnp.dot(mixture, out_weight, preferred_element_type=jnp.float32).astype(jnp.bfloat16)
    return result.reshape(ROWS, COLS, feat_width)

def reference(video_tokens, qkv_weight, out_weight, conv_weight, norm_gain):
    query_all, value_all, frame_states = lax.map(lambda frame_tokens: project_frame(frame_tokens, qkv_weight), video_tokens)
    causal_states = jnp.cumsum(frame_states, axis=0)

    def finish_one(packed):
        return finish_frame(packed[0], packed[1], packed[2], out_weight, conv_weight, norm_gain)
    return lax.map(finish_one, (query_all, value_all, causal_states))
```

```python
import functools

import jax
import jax.numpy as jnp
from jax import lax
from jax.experimental import pallas as pl
from jax.experimental.pallas import tpu as pltpu
from jax.sharding import PartitionSpec as P

HEADS = 36
HEAD_DIM = 32
LANES = 128
MAIN = 64
REST = 16
STEPS = (1, 2, 3)
VMEM_LIMIT = 24 * 1024 * 1024
WHOLE_VMEM = 63 * 1024 * 1024


def entering(value, axis, combine, identity):
    devices, place = (lax.axis_size(axis), lax.axis_index(axis))
    everything = lax.all_gather(value.astype(jnp.bfloat16), axis)
    start = jnp.broadcast_to(jnp.asarray(identity, value.dtype), value.shape)

    def lap(k, before):
        reached = k < place
        new = combine(before, everything[k].astype(value.dtype))
        return jnp.where(reached, new, before)

    return lax.fori_loop(0, devices, lap, start)


def with_halo(block, sides, width):
    for axis, dim in sides:
        count = lax.axis_size(axis)
        forward = [(i, i + 1) for i in range(count - 1)]
        backward = [(target, source) for source, target in forward]
        low = lax.ppermute(
            lax.slice_in_dim(block, block.shape[dim] - width, None, axis=dim), axis, forward
        )
        high = lax.ppermute(lax.slice_in_dim(block, 0, width, axis=dim), axis, backward)
        block = jnp.concatenate([low, block, high], axis=dim)
    return block


def fold_product(left_side, block_rows):
    return jnp.dot(left_side, block_rows, preferred_element_type=jnp.float32)


def add_states(earlier, later):
    return earlier + later


def causal_states(key_feat, values):
    key_heads = key_feat.reshape(-1, HEADS, HEAD_DIM)
    value_heads = values.reshape(-1, HEADS, HEAD_DIM)
    frame_state = jnp.einsum(
        "thd,the->hde", key_heads, value_heads, preferred_element_type=jnp.float32
    )
    flat_state = frame_state.reshape(-1)
    frame_sum = lax.psum(flat_state.astype(jnp.bfloat16), "space").astype(jnp.float32)
    earlier = entering(frame_sum, "tm", add_states, jnp.zeros_like(frame_sum))
    whole_state = earlier + frame_sum
    return whole_state.reshape(HEADS, HEAD_DIM, HEAD_DIM)


def general_form(video_tokens, qkv_weight, out_weight, conv_weight, norm_gain):
    frame_now = video_tokens[0]
    row_count, col_count, feat_width = frame_now.shape
    tokens = frame_now.reshape(row_count * col_count, feat_width)
    projected = fold_product(tokens, lax.all_gather(qkv_weight, "space", axis=0, tiled=True))
    query_feat = jax.nn.relu(projected[:, :feat_width]).astype(jnp.bfloat16)
    key_feat = jax.nn.relu(projected[:, feat_width : 2 * feat_width]).astype(jnp.bfloat16)
    values = projected[:, 2 * feat_width :].astype(jnp.bfloat16)
    state_all = causal_states(key_feat, values)
    padded_rows = with_halo(values.reshape(row_count, col_count, feat_width), (("space", 0),), 1)
    padded = jnp.pad(padded_rows, ((0, 0), (1, 1), (0, 0))).astype(jnp.float32)
    local_term = jnp.zeros((row_count, col_count, feat_width), jnp.float32)
    for row_shift in range(3):
        for col_shift in range(3):
            local_term = (
                local_term
                + conv_weight[row_shift, col_shift]
                * padded[row_shift : row_shift + row_count, col_shift : col_shift + col_count]
            )
    state_low = state_all.astype(jnp.bfloat16)
    query_heads = query_feat.reshape(-1, HEADS, HEAD_DIM)
    readout = jnp.einsum("thd,hde->the", query_heads, state_low, preferred_element_type=jnp.float32)
    readout = readout.reshape(-1, feat_width)
    mean_square = jnp.mean(readout * readout, axis=-1, keepdims=True)
    normed = readout * lax.rsqrt(mean_square + 1e-06) * norm_gain
    mixture = (normed + local_term.reshape(-1, feat_width)).astype(jnp.bfloat16)
    result = fold_product(mixture, lax.all_gather(out_weight, "space", axis=0, tiled=True))
    return result.astype(jnp.bfloat16).reshape(1, row_count, col_count, feat_width)


def coordinates():
    place = lax.axis_index("tm")
    return lax.rem(place // 4, 2), lax.rem(place // 2, 2), lax.rem(place, 2)


def shifted(value, step):
    count = lax.axis_size("space")
    return lax.ppermute(value, "space", [(i, (i + step) % count) for i in range(count)])


def flipped(value, bit_on_core):
    return lax.ppermute(value, "tm", [(t, t ^ bit_on_core[t % 2]) for t in range(8)])


def after(value, *earlier):
    return lax.optimization_barrier((value,) + earlier)[0]


def chip_places(y, x):
    return (2 * y + x, 2 * y + (1 - x), 2 * (1 - y) + x, 2 * (1 - y) + (1 - x))


def source_plane(step):
    count = lax.axis_size("space")
    return lax.rem(lax.axis_index("space") - step + count, count)


def steps_through(within, size):
    run = sum(jnp.where(within >= size * k, 1, 0) for k in range(1, len(STEPS)))
    return run, within - size * run


def landed_order(at, width, rows):
    y, x, _ = coordinates()
    planes = [source_plane(step) for step in STEPS]
    row = at + lax.broadcasted_iota(jnp.int32, (1, width), 1)

    def pick(choices, index):
        chosen = choices[-1]
        for k in range(len(choices) - 2, -1, -1):
            chosen = jnp.where(index == k, choices[k], chosen)
        return chosen

    def landed(within, size, starts):
        count = len(STEPS) * size
        slot = sum(jnp.where(within >= count * k, 1, 0) for k in range(1, len(starts)))
        run, left = steps_through(within - count * slot, size)
        return pick(planes, run) * rows + pick(starts, slot) + left

    main = landed(row - rows, MAIN, [place * MAIN for place in chip_places(y, x)])
    rest_at = rows + 4 * len(STEPS) * MAIN
    rest = landed(row - rest_at, REST, [4 * MAIN + tile * REST for tile in (y, 1 - y)])
    own = lax.axis_index("space") * rows + row
    return jnp.where(row < rows, own, jnp.where(row < rest_at, main, rest))


def whole_vmem():
    return pl.BlockSpec(memory_space=pltpu.VMEM)


def anywhere():
    return pl.BlockSpec(memory_space=pltpu.HBM)


def kernel_call(
    body, outputs, inputs, in_specs, scratch=(), flops=0, bytes_accessed=0, limit=VMEM_LIMIT
):
    return pl.pallas_call(
        body,
        out_shape=outputs,
        in_specs=in_specs,
        out_specs=jax.tree.map(lambda _: whole_vmem(), outputs),
        scratch_shapes=list(scratch),
        compiler_params=pltpu.CompilerParams(vmem_limit_bytes=limit),
        cost_estimate=pl.CostEstimate(
            flops=flops, bytes_accessed=bytes_accessed, transcendentals=0
        ),
    )(*inputs)


def pieces_kernel(qkv_ref, out_ref, first_ref, second_ref, sems):
    y, x, core = coordinates()
    depth = out_ref.shape[1]
    main = pl.ds(pl.multiple_of((2 * y + x) * MAIN, REST), MAIN)
    rest = pl.ds(pl.multiple_of(4 * MAIN + y * REST, REST), REST)
    first_columns = pl.ds(pl.multiple_of(depth * (1 + core), LANES), depth)
    rest_columns = pl.ds(pl.multiple_of(jnp.where(x == 0, depth * (1 + core), 0), LANES), depth)

    def copy(source, target, k):
        return pltpu.make_async_copy(source, target, sems.at[k])

    first_main = copy(qkv_ref.at[main, first_columns], first_ref.at[pl.ds(0, MAIN), :], 0)
    first_main.start()
    rest_target = first_ref.at[pl.ds(MAIN, REST), :]
    from_out = (core == 1) & (x == 1)

    @pl.when(from_out)
    def _():
        copy(out_ref.at[rest, :], rest_target, 1).start()

    @pl.when(jnp.logical_not(from_out))
    def _():
        copy(qkv_ref.at[rest, rest_columns], rest_target, 1).start()

    places = chip_places(y, x)
    for k, place in enumerate((places[0], places[3])):
        rows = pl.ds(pl.multiple_of(place * MAIN, REST), MAIN)

        @pl.when(core == 0)
        def _():
            copy(qkv_ref.at[rows, pl.ds(0, depth)], second_ref.at[k], 2 + k).start()

        @pl.when(core == 1)
        def _():
            copy(out_ref.at[rows, :], second_ref.at[k], 2 + k).start()

    first_main.wait()
    copy(out_ref.at[rest, :], rest_target, 1).wait()
    for k in range(2):
        copy(out_ref.at[main, :], second_ref.at[k], 2 + k).wait()


def pieces_call(qkv_weight, out_weight):
    depth = out_weight.shape[1]
    outputs = [
        jax.ShapeDtypeStruct((MAIN + REST, depth), jnp.bfloat16),
        jax.ShapeDtypeStruct((2, MAIN, depth), jnp.bfloat16),
    ]
    return kernel_call(
        pieces_kernel,
        outputs,
        (qkv_weight, out_weight),
        [anywhere(), anywhere()],
        [pltpu.SemaphoreType.DMA((4,))],
        bytes_accessed=4 * (3 * MAIN + REST) * depth,
        limit=WHOLE_VMEM,
    )


def reorder_kernel(rows, tokens_ref, moved_ref):
    depth = tokens_ref.shape[1]
    width = 3 * LANES
    row = lax.broadcasted_iota(jnp.int32, (depth, width), 0)
    for at in range(0, depth, width):
        order = landed_order(at, width, rows)
        chosen = jnp.where(row == order, 1.0, 0.0).astype(jnp.bfloat16)
        moved = jnp.dot(tokens_ref[...], chosen, preferred_element_type=jnp.float32)
        moved_ref[:, at : at + width] = moved.astype(jnp.bfloat16)


def reorder_call(tokens, rows):
    depth = tokens.shape[1]
    return kernel_call(
        functools.partial(reorder_kernel, rows),
        jax.ShapeDtypeStruct(tokens.shape, jnp.bfloat16),
        (tokens,),
        [whole_vmem()],
        flops=2 * tokens.size * depth,
        bytes_accessed=2 * tokens.size,
    )


def first_kernel(*refs):
    tokens_ref, other_ref, qkv_ref, near_ref, away_ref, first_ref, far_ref, mine_ref = refs
    slots = (
        ((near_ref, 0), (near_ref, 4), (near_ref, 1)),
        ((near_ref, 2), (first_ref, 0), (near_ref, 3)),
        ((away_ref, 0), (away_ref, 4), (away_ref, 1)),
        ((away_ref, 2), (far_ref, 0), (away_ref, 3)),
    )
    _, x, core = coordinates()
    count, depth = tokens_ref.shape
    floor = jnp.where(core == 0, 0.0, -jnp.inf).astype(jnp.float32)
    width = 3 * LANES

    for at in range(0, depth, width):
        lanes = slice(at, at + width)

        def slot(k, low, high):
            return jnp.concatenate([ref[at, low:high, lanes] for ref, at in slots[k]], axis=0)

        def by_place(low, high):
            own, first, second, far = [slot(k, low, high) for k in range(4)]
            along_x = jnp.where(core == 0, first, second)
            along_y = jnp.where(core == 0, second, first)
            return own, along_x, along_y, far

        keys, values = [qkv_ref[:, depth * k + at : depth * k + at + width] for k in (1, 2)]
        own = jnp.where(core == 0, keys, values)
        rest = by_place(MAIN, MAIN + REST)
        even = jnp.concatenate([rest[0], rest[2]], axis=0)
        odd = jnp.concatenate([rest[1], rest[3]], axis=0)
        mine_ref[2 * count :, lanes] = jnp.where(x == 1, even, odd)
        columns = jnp.concatenate(
            (own,) + by_place(0, MAIN) + (jnp.where(x == 0, even, odd),), axis=0
        )
        for k, ref in enumerate((tokens_ref, other_ref)):
            product = jnp.dot(ref[...], columns, preferred_element_type=jnp.float32)
            product = jnp.maximum(product, floor).astype(jnp.bfloat16)
            mine_ref[k * count : (k + 1) * count, lanes] = product


def first_call(tokens, other, qkv_weight, *landed):
    count, depth = tokens.shape
    inputs = (tokens, other, qkv_weight) + landed
    return kernel_call(
        first_kernel,
        jax.ShapeDtypeStruct((2 * count + 2 * len(STEPS) * REST, depth), jnp.bfloat16),
        inputs,
        [whole_vmem()] * len(inputs),
        flops=4 * tokens.size * depth,
        bytes_accessed=2 * depth * depth,
    )


def diagonal_mask():
    rows = lax.broadcasted_iota(jnp.int32, (LANES, LANES), 0) // HEAD_DIM
    columns = lax.broadcasted_iota(jnp.int32, (LANES, LANES), 1) // HEAD_DIM
    return rows == columns


def state_kernel(mine_ref, other_ref, values_ref, top_ref, bottom_ref, upto_ref, total_ref):
    _, _, core = coordinates()
    mask = diagonal_mask()
    columns = top_ref.shape[1]
    count = values_ref.shape[0]
    later = jnp.where(core == 1, 1.0, 0.0).astype(jnp.float32)
    for group in range(mine_ref.shape[1] // LANES):
        at = slice(group * LANES, (group + 1) * LANES)

        def state(mine, other):
            keys = jnp.where(core == 0, mine, other)
            values = jnp.where(core == 0, other, mine)
            full = lax.dot_general(
                keys, values, (((0,), (0,)), ((), ())), preferred_element_type=jnp.float32
            )
            full = jnp.where(mask, full, 0.0)
            total = full[0:HEAD_DIM]
            for k in range(1, LANES // HEAD_DIM):
                total = total + full[k * HEAD_DIM : (k + 1) * HEAD_DIM]
            return total, values

        low, high = slice(0, count), slice(count, 2 * count)
        here, values = state(mine_ref[low, at], other_ref[high, at])
        there, _ = state(mine_ref[high, at], other_ref[low, at])
        values_ref[:, at] = values
        top_ref[0, :, at] = values[:columns]
        bottom_ref[0, :, at] = values[-columns:]
        upto_ref[group] = here + later * there
        total_ref[group] = (here + there).astype(jnp.bfloat16)


def state_call(mine, other, count, columns):
    depth = mine.shape[1]
    compact = (depth // LANES, HEAD_DIM, LANES)
    edge = jax.ShapeDtypeStruct((1, columns, depth), jnp.bfloat16)
    return kernel_call(
        state_kernel,
        [
            jax.ShapeDtypeStruct((count, depth), jnp.bfloat16),
            edge,
            edge,
            jax.ShapeDtypeStruct(compact, jnp.float32),
            jax.ShapeDtypeStruct(compact, jnp.bfloat16),
        ],
        (mine, other),
        [whole_vmem()] * 2,
        flops=4 * count * depth * LANES,
        bytes_accessed=8 * count * depth,
    )


def local_kernel(values_ref, above_ref, below_ref, conv_ref, local_ref):
    rows, columns, depth = values_ref.shape
    for at in range(0, depth, LANES):
        lanes = slice(at, at + LANES)
        taps = conv_ref[:, :, lanes]
        sheet = jnp.concatenate(
            [above_ref[:, :, lanes], values_ref[:, :, lanes], below_ref[:, :, lanes]], axis=0
        ).astype(jnp.float32)
        edge = jnp.zeros((rows + 2, 1, LANES), jnp.float32)
        before = jnp.concatenate([edge, sheet[:, :-1]], axis=1)
        behind = jnp.concatenate([sheet[:, 1:], edge], axis=1)
        total = jnp.zeros((rows, columns, LANES), jnp.float32)
        for col_shift, moved in enumerate((before, sheet, behind)):
            for row_shift in range(3):
                total = total + taps[row_shift, col_shift] * moved[row_shift : row_shift + rows]
        local_ref[:, :, lanes] = total


def local_call(values, above, below, conv_weight):
    return kernel_call(
        local_kernel,
        jax.ShapeDtypeStruct(values.shape, jnp.float32),
        (values, above, below, conv_weight),
        [whole_vmem()] * 4,
        flops=18 * values.size,
        bytes_accessed=6 * values.size,
    )


def query_kernel(*refs):
    tokens_ref, qkv_ref, out_ref, mine_ref, theirs_ref, ours_ref, other_ref, *results = refs
    query_ref, weight_ref = results
    y, x, core = coordinates()
    depth = tokens_ref.shape[1]
    rows = qkv_ref.shape[0]
    steps = len(STEPS)
    rest_at = ours_ref.shape[0] - 2 * steps * REST
    places = chip_places(y, x)
    width = 3 * LANES

    def block(of_core, k, lanes):
        return jnp.where(core == of_core, mine_ref[k, :, lanes], theirs_ref[k, :, lanes])

    def rest(of_core, lanes):
        return jnp.where(core == of_core, ours_ref[rest_at:, lanes], other_ref[rest_at:, lanes])

    def put(row, value, lanes):
        weight_ref[pl.ds(pl.multiple_of(row, REST), value.shape[0]), lanes] = value

    for at in range(0, depth, width):
        lanes = slice(at, at + width)
        order = [2 * k for k in range(steps)] + [2 * steps + k for k in range(2 * steps)]
        order += [2 * k + 1 for k in range(steps)]
        columns = [qkv_ref[:, lanes]] + [block(0, k, lanes) for k in order] + [rest(0, lanes)]
        queries = jnp.dot(
            tokens_ref[...], jnp.concatenate(columns, axis=0), preferred_element_type=jnp.float32
        )
        query_ref[:, lanes] = jnp.maximum(queries, 0.0).astype(jnp.bfloat16)

        put(lax.axis_index("space") * rows, out_ref[:, lanes], lanes)
        tiles = rest(1, lanes)
        for k, step in enumerate(STEPS):
            base = source_plane(step) * rows
            held = (2 * k, 3 * steps + k, 2 * steps + k, 2 * k + 1)
            for place, index in zip(places, held):
                put(base + place * MAIN, block(1, index, lanes), lanes)
            for run, tile in enumerate((y, 1 - y)):
                start = (run * steps + k) * REST
                put(base + 4 * MAIN + tile * REST, tiles[start : start + REST], lanes)


def query_call(tokens, qkv_weight, out_weight, mine, theirs, ours, other):
    depth = tokens.shape[1]
    inputs = (tokens, qkv_weight, out_weight, mine, theirs, ours, other)
    return kernel_call(
        query_kernel,
        [
            jax.ShapeDtypeStruct(tokens.shape, jnp.bfloat16),
            jax.ShapeDtypeStruct((depth, depth), jnp.bfloat16),
        ],
        inputs,
        [whole_vmem()] * len(inputs),
        flops=2 * tokens.size * depth,
        bytes_accessed=4 * depth * depth,
    )


def finish_kernel(queries_ref, weight_ref, state_ref, local_ref, gain_ref, result_ref, read_ref):
    count, depth = queries_ref.shape
    mask = diagonal_mask()
    square = jnp.zeros((count, LANES), jnp.float32)
    for group in range(depth // LANES):
        lanes = slice(group * LANES, (group + 1) * LANES)
        spread = jnp.concatenate([state_ref[group]] * (LANES // HEAD_DIM), axis=0)
        spread = jnp.where(mask, spread, 0.0).astype(jnp.bfloat16)
        read = jnp.dot(queries_ref[:, lanes], spread, preferred_element_type=jnp.float32)
        read_ref[:, lanes] = read
        square = square + read * read
    scale = lax.rsqrt(jnp.sum(square, axis=1, keepdims=True) / depth + 1e-06)
    mixture = read_ref[...] * scale * gain_ref[...] + local_ref[...]
    mixture = mixture.astype(jnp.bfloat16)
    width = 3 * LANES
    for at in range(0, depth, width):
        lanes = slice(at, at + width)
        product = jnp.dot(mixture, weight_ref[:, lanes], preferred_element_type=jnp.float32)
        result_ref[:, lanes] = product.astype(jnp.bfloat16)


def finish_call(queries, weight, state, local_term, gain):
    inputs = (queries, weight, state, local_term, gain)
    return kernel_call(
        finish_kernel,
        jax.ShapeDtypeStruct(queries.shape, jnp.bfloat16),
        inputs,
        [whole_vmem()] * len(inputs),
        [pltpu.VMEM(queries.shape, jnp.float32)],
        flops=2 * queries.size * queries.shape[1],
        bytes_accessed=2 * weight.size,
    )


def plane_form(video_tokens, qkv_weight, out_weight, conv_weight, norm_gain):
    frame_now = video_tokens[0]
    row_count, col_count, depth = frame_now.shape
    tokens = frame_now.reshape(row_count * col_count, depth)

    first_piece, second_piece = pieces_call(qkv_weight, out_weight)
    first_piece = first_piece[None]
    one = shifted(first_piece, 1)
    three = shifted(first_piece, -1)
    tokens = reorder_call(after(tokens, second_piece), qkv_weight.shape[0])
    other_tokens = flipped(tokens, (1, 1))
    one, three = after((one, three), tokens)

    pair = jnp.concatenate([one, three])
    two = shifted(one, 1)
    pair_first = flipped(pair, (2, 4))
    near = jnp.concatenate(after((pair, pair_first, two), other_tokens))
    away = flipped(near, (4, 2))
    two_first = flipped(two, (2, 4))
    two_far = flipped(two, (6, 6))

    second_ready = after(second_piece, near)
    second_one = shifted(second_ready, 1)
    second_three = shifted(second_ready, -1)
    second_two = shifted(after(second_one, two_first, two_far), 1)

    mine = first_call(after(tokens, second_one, second_three), other_tokens, qkv_weight, near, away, two_first, two_far)
    other = flipped(mine, (1, 1))
    values, top, bottom, upto, total = state_call(mine, other, tokens.shape[0], col_count)

    second_two = after(second_two, total)
    second_own = jnp.stack([second_one[0], second_two[0], second_three[0]])
    second_first = flipped(second_own, (2, 4))
    second_second = flipped(second_own, (4, 2))

    for bit, guard in ((2, 2), (4, 4), (6, 4)):
        pairs = [(t, t ^ bit) for t in range(8) if not t & guard]
        upto = upto + lax.ppermute(total, "tm", pairs).astype(jnp.float32)
    count = lax.axis_size("space")
    state = upto
    for bit in (1, 2):
        share = state.astype(jnp.bfloat16)
        if bit == 2:
            top, bottom = after((top, bottom), share)
        pairs = [(i, i ^ bit) for i in range(count)]
        state = share.astype(jnp.float32) + lax.ppermute(share, "space", pairs).astype(jnp.float32)
    forward = [(i, i + 1) for i in range(count - 1)]
    backward = [(target, source) for source, target in forward]
    above = lax.ppermute(bottom, "space", forward)
    below = lax.ppermute(top, "space", backward)
    grid = values.reshape(row_count, col_count, depth)
    local_term = local_call(grid, above, below, conv_weight).reshape(-1, depth)

    parts = (second_one, second_two, second_three, second_first, second_second)
    held = jnp.concatenate(after(parts, state, above, below))
    swapped = flipped(held, (1, 1))
    queries, weight = query_call(tokens, qkv_weight, out_weight, held, swapped, mine, other)
    result = finish_call(queries, weight, state, local_term, norm_gain[None])
    return result.reshape(1, row_count, col_count, depth)


def solution(mesh):
    def per_device(video_tokens, qkv_weight, out_weight, conv_weight, norm_gain):
        fits = mesh.shape["tm"] == 8 and mesh.shape["space"] == 4
        fits = fits and qkv_weight.shape[0] == 4 * MAIN + 2 * REST
        form = plane_form if fits else general_form
        return form(video_tokens, qkv_weight, out_weight, conv_weight, norm_gain)

    in_specs = (P("tm", "space", None, None), P("space", None), P("space", None), P(), P())
    out_specs = P("tm", "space", None, None)
    return jax.shard_map(
        per_device, mesh=mesh, in_specs=in_specs, out_specs=out_specs, check_vma=False
    )
```

```python
import functools

import jax
import jax.numpy as jnp
from jax import lax
from jax.experimental import pallas as pl
from jax.experimental.pallas import tpu as pltpu
from jax.sharding import PartitionSpec as P

HEADS = 36
HEAD_DIM = 32
LANES = 128
MAIN = 64
REST = 16
STEPS = (1, 2, 3)
VMEM_LIMIT = 24 * 1024 * 1024
WHOLE_VMEM = 63 * 1024 * 1024


def entering(value, axis, combine, identity):
    devices, place = (lax.axis_size(axis), lax.axis_index(axis))
    everything = lax.all_gather(value.astype(jnp.bfloat16), axis)
    start = jnp.broadcast_to(jnp.asarray(identity, value.dtype), value.shape)

    def lap(k, before):
        reached = k < place
        new = combine(before, everything[k].astype(value.dtype))
        return jnp.where(reached, new, before)

    return lax.fori_loop(0, devices, lap, start)


def with_halo(block, sides, width):
    for axis, dim in sides:
        count = lax.axis_size(axis)
        forward = [(i, i + 1) for i in range(count - 1)]
        backward = [(target, source) for source, target in forward]
        low = lax.ppermute(
            lax.slice_in_dim(block, block.shape[dim] - width, None, axis=dim), axis, forward
        )
        high = lax.ppermute(lax.slice_in_dim(block, 0, width, axis=dim), axis, backward)
        block = jnp.concatenate([low, block, high], axis=dim)
    return block


def fold_product(left_side, block_rows):
    return jnp.dot(left_side, block_rows, preferred_element_type=jnp.float32)


def add_states(earlier, later):
    return earlier + later


def causal_states(key_feat, values):
    key_heads = key_feat.reshape(-1, HEADS, HEAD_DIM)
    value_heads = values.reshape(-1, HEADS, HEAD_DIM)
    frame_state = jnp.einsum(
        "thd,the->hde", key_heads, value_heads, preferred_element_type=jnp.float32
    )
    flat_state = frame_state.reshape(-1)
    frame_sum = lax.psum(flat_state.astype(jnp.bfloat16), "space").astype(jnp.float32)
    earlier = entering(frame_sum, "tm", add_states, jnp.zeros_like(frame_sum))
    whole_state = earlier + frame_sum
    return whole_state.reshape(HEADS, HEAD_DIM, HEAD_DIM)


def general_form(video_tokens, qkv_weight, out_weight, conv_weight, norm_gain):
    frame_now = video_tokens[0]
    row_count, col_count, feat_width = frame_now.shape
    tokens = frame_now.reshape(row_count * col_count, feat_width)
    projected = fold_product(tokens, lax.all_gather(qkv_weight, "space", axis=0, tiled=True))
    query_feat = jax.nn.relu(projected[:, :feat_width]).astype(jnp.bfloat16)
    key_feat = jax.nn.relu(projected[:, feat_width : 2 * feat_width]).astype(jnp.bfloat16)
    values = projected[:, 2 * feat_width :].astype(jnp.bfloat16)
    state_all = causal_states(key_feat, values)
    padded_rows = with_halo(values.reshape(row_count, col_count, feat_width), (("space", 0),), 1)
    padded = jnp.pad(padded_rows, ((0, 0), (1, 1), (0, 0))).astype(jnp.float32)
    local_term = jnp.zeros((row_count, col_count, feat_width), jnp.float32)
    for row_shift in range(3):
        for col_shift in range(3):
            local_term = (
                local_term
                + conv_weight[row_shift, col_shift]
                * padded[row_shift : row_shift + row_count, col_shift : col_shift + col_count]
            )
    state_low = state_all.astype(jnp.bfloat16)
    query_heads = query_feat.reshape(-1, HEADS, HEAD_DIM)
    readout = jnp.einsum("thd,hde->the", query_heads, state_low, preferred_element_type=jnp.float32)
    readout = readout.reshape(-1, feat_width)
    mean_square = jnp.mean(readout * readout, axis=-1, keepdims=True)
    normed = readout * lax.rsqrt(mean_square + 1e-06) * norm_gain
    mixture = (normed + local_term.reshape(-1, feat_width)).astype(jnp.bfloat16)
    result = fold_product(mixture, lax.all_gather(out_weight, "space", axis=0, tiled=True))
    return result.astype(jnp.bfloat16).reshape(1, row_count, col_count, feat_width)


def coordinates():
    place = lax.axis_index("tm")
    return lax.rem(place // 4, 2), lax.rem(place // 2, 2), lax.rem(place, 2)


def shifted(value, step):
    count = lax.axis_size("space")
    return lax.ppermute(value, "space", [(i, (i + step) % count) for i in range(count)])


def flipped(value, bit_on_core):
    return lax.ppermute(value, "tm", [(t, t ^ bit_on_core[t % 2]) for t in range(8)])


def after(value, *earlier):
    return lax.optimization_barrier((value,) + earlier)[0]


def chip_places(y, x):
    return (2 * y + x, 2 * y + (1 - x), 2 * (1 - y) + x, 2 * (1 - y) + (1 - x))


def source_plane(step):
    count = lax.axis_size("space")
    return lax.rem(lax.axis_index("space") - step + count, count)


def steps_through(within, size):
    run = sum(jnp.where(within >= size * k, 1, 0) for k in range(1, len(STEPS)))
    return run, within - size * run


def landed_order(at, width, rows):
    y, x, _ = coordinates()
    planes = [source_plane(step) for step in STEPS]
    row = at + lax.broadcasted_iota(jnp.int32, (1, width), 1)

    def pick(choices, index):
        chosen = choices[-1]
        for k in range(len(choices) - 2, -1, -1):
            chosen = jnp.where(index == k, choices[k], chosen)
        return chosen

    def landed(within, size, starts):
        count = len(STEPS) * size
        slot = sum(jnp.where(within >= count * k, 1, 0) for k in range(1, len(starts)))
        run, left = steps_through(within - count * slot, size)
        return pick(planes, run) * rows + pick(starts, slot) + left

    main = landed(row - rows, MAIN, [place * MAIN for place in chip_places(y, x)])
    rest_at = rows + 4 * len(STEPS) * MAIN
    rest = landed(row - rest_at, REST, [4 * MAIN + tile * REST for tile in (y, 1 - y)])
    own = lax.axis_index("space") * rows + row
    return jnp.where(row < rows, own, jnp.where(row < rest_at, main, rest))


def whole_vmem():
    return pl.BlockSpec(memory_space=pltpu.VMEM)


def anywhere():
    return pl.BlockSpec(memory_space=pltpu.HBM)


def kernel_call(
    body, outputs, inputs, in_specs, scratch=(), flops=0, bytes_accessed=0, limit=VMEM_LIMIT
):
    return pl.pallas_call(
        body,
        out_shape=outputs,
        in_specs=in_specs,
        out_specs=jax.tree.map(lambda _: whole_vmem(), outputs),
        scratch_shapes=list(scratch),
        compiler_params=pltpu.CompilerParams(vmem_limit_bytes=limit),
        cost_estimate=pl.CostEstimate(
            flops=flops, bytes_accessed=bytes_accessed, transcendentals=0
        ),
    )(*inputs)


def pieces_kernel(qkv_ref, out_ref, first_ref, second_ref, sems):
    y, x, core = coordinates()
    depth = out_ref.shape[1]
    main = pl.ds(pl.multiple_of((2 * y + x) * MAIN, REST), MAIN)
    rest = pl.ds(pl.multiple_of(4 * MAIN + y * REST, REST), REST)
    first_columns = pl.ds(pl.multiple_of(depth * (1 + core), LANES), depth)
    rest_columns = pl.ds(pl.multiple_of(jnp.where(x == 0, depth * (1 + core), 0), LANES), depth)

    def copy(source, target, k):
        return pltpu.make_async_copy(source, target, sems.at[k])

    first_main = copy(qkv_ref.at[main, first_columns], first_ref.at[pl.ds(0, MAIN), :], 0)
    first_main.start()
    rest_target = first_ref.at[pl.ds(MAIN, REST), :]
    from_out = (core == 1) & (x == 1)

    @pl.when(from_out)
    def _():
        copy(out_ref.at[rest, :], rest_target, 1).start()

    @pl.when(jnp.logical_not(from_out))
    def _():
        copy(qkv_ref.at[rest, rest_columns], rest_target, 1).start()

    places = chip_places(y, x)
    for k, place in enumerate((places[0], places[3])):
        rows = pl.ds(pl.multiple_of(place * MAIN, REST), MAIN)

        @pl.when(core == 0)
        def _():
            copy(qkv_ref.at[rows, pl.ds(0, depth)], second_ref.at[k], 2 + k).start()

        @pl.when(core == 1)
        def _():
            copy(out_ref.at[rows, :], second_ref.at[k], 2 + k).start()

    first_main.wait()
    copy(out_ref.at[rest, :], rest_target, 1).wait()
    for k in range(2):
        copy(out_ref.at[main, :], second_ref.at[k], 2 + k).wait()


def pieces_call(qkv_weight, out_weight):
    depth = out_weight.shape[1]
    outputs = [
        jax.ShapeDtypeStruct((MAIN + REST, depth), jnp.bfloat16),
        jax.ShapeDtypeStruct((2, MAIN, depth), jnp.bfloat16),
    ]
    return kernel_call(
        pieces_kernel,
        outputs,
        (qkv_weight, out_weight),
        [anywhere(), anywhere()],
        [pltpu.SemaphoreType.DMA((4,))],
        bytes_accessed=4 * (3 * MAIN + REST) * depth,
        limit=WHOLE_VMEM,
    )


def reorder_kernel(rows, tokens_ref, moved_ref):
    depth = tokens_ref.shape[1]
    width = 3 * LANES
    row = lax.broadcasted_iota(jnp.int32, (depth, width), 0)
    for at in range(0, depth, width):
        order = landed_order(at, width, rows)
        chosen = jnp.where(row == order, 1.0, 0.0).astype(jnp.bfloat16)
        moved = jnp.dot(tokens_ref[...], chosen, preferred_element_type=jnp.float32)
        moved_ref[:, at : at + width] = moved.astype(jnp.bfloat16)


def reorder_call(tokens, rows):
    depth = tokens.shape[1]
    return kernel_call(
        functools.partial(reorder_kernel, rows),
        jax.ShapeDtypeStruct(tokens.shape, jnp.bfloat16),
        (tokens,),
        [whole_vmem()],
        flops=2 * tokens.size * depth,
        bytes_accessed=2 * tokens.size,
    )


def first_kernel(*refs):
    tokens_ref, other_ref, qkv_ref, near_ref, away_ref, first_ref, far_ref, mine_ref = refs
    slots = (
        ((near_ref, 0), (near_ref, 4), (near_ref, 1)),
        ((near_ref, 2), (first_ref, 0), (near_ref, 3)),
        ((away_ref, 0), (away_ref, 4), (away_ref, 1)),
        ((away_ref, 2), (far_ref, 0), (away_ref, 3)),
    )
    _, x, core = coordinates()
    count, depth = tokens_ref.shape
    floor = jnp.where(core == 0, 0.0, -jnp.inf).astype(jnp.float32)
    width = 3 * LANES

    for at in range(0, depth, width):
        lanes = slice(at, at + width)

        def slot(k, low, high):
            return jnp.concatenate([ref[at, low:high, lanes] for ref, at in slots[k]], axis=0)

        def by_place(low, high):
            own, first, second, far = [slot(k, low, high) for k in range(4)]
            along_x = jnp.where(core == 0, first, second)
            along_y = jnp.where(core == 0, second, first)
            return own, along_x, along_y, far

        keys, values = [qkv_ref[:, depth * k + at : depth * k + at + width] for k in (1, 2)]
        own = jnp.where(core == 0, keys, values)
        rest = by_place(MAIN, MAIN + REST)
        even = jnp.concatenate([rest[0], rest[2]], axis=0)
        odd = jnp.concatenate([rest[1], rest[3]], axis=0)
        mine_ref[2 * count :, lanes] = jnp.where(x == 1, even, odd)
        columns = jnp.concatenate(
            (own,) + by_place(0, MAIN) + (jnp.where(x == 0, even, odd),), axis=0
        )
        for k, ref in enumerate((tokens_ref, other_ref)):
            product = jnp.dot(ref[...], columns, preferred_element_type=jnp.float32)
            product = jnp.maximum(product, floor).astype(jnp.bfloat16)
            mine_ref[k * count : (k + 1) * count, lanes] = product


def first_call(tokens, other, qkv_weight, *landed):
    count, depth = tokens.shape
    inputs = (tokens, other, qkv_weight) + landed
    return kernel_call(
        first_kernel,
        jax.ShapeDtypeStruct((2 * count + 2 * len(STEPS) * REST, depth), jnp.bfloat16),
        inputs,
        [whole_vmem()] * len(inputs),
        flops=4 * tokens.size * depth,
        bytes_accessed=2 * depth * depth,
    )


def diagonal_mask():
    rows = lax.broadcasted_iota(jnp.int32, (LANES, LANES), 0) // HEAD_DIM
    columns = lax.broadcasted_iota(jnp.int32, (LANES, LANES), 1) // HEAD_DIM
    return rows == columns


def state_kernel(mine_ref, other_ref, values_ref, top_ref, bottom_ref, upto_ref, total_ref):
    _, _, core = coordinates()
    mask = diagonal_mask()
    columns = top_ref.shape[1]
    count = values_ref.shape[0]
    later = jnp.where(core == 1, 1.0, 0.0).astype(jnp.float32)
    for group in range(mine_ref.shape[1] // LANES):
        at = slice(group * LANES, (group + 1) * LANES)

        def state(mine, other):
            keys = jnp.where(core == 0, mine, other)
            values = jnp.where(core == 0, other, mine)
            full = lax.dot_general(
                keys, values, (((0,), (0,)), ((), ())), preferred_element_type=jnp.float32
            )
            full = jnp.where(mask, full, 0.0)
            total = full[0:HEAD_DIM]
            for k in range(1, LANES // HEAD_DIM):
                total = total + full[k * HEAD_DIM : (k + 1) * HEAD_DIM]
            return total, values

        low, high = slice(0, count), slice(count, 2 * count)
        here, values = state(mine_ref[low, at], other_ref[high, at])
        there, _ = state(mine_ref[high, at], other_ref[low, at])
        values_ref[:, at] = values
        top_ref[0, :, at] = values[:columns]
        bottom_ref[0, :, at] = values[-columns:]
        upto_ref[group] = here + later * there
        total_ref[group] = (here + there).astype(jnp.bfloat16)


def state_call(mine, other, count, columns):
    depth = mine.shape[1]
    compact = (depth // LANES, HEAD_DIM, LANES)
    edge = jax.ShapeDtypeStruct((1, columns, depth), jnp.bfloat16)
    return kernel_call(
        state_kernel,
        [
            jax.ShapeDtypeStruct((count, depth), jnp.bfloat16),
            edge,
            edge,
            jax.ShapeDtypeStruct(compact, jnp.float32),
            jax.ShapeDtypeStruct(compact, jnp.bfloat16),
        ],
        (mine, other),
        [whole_vmem()] * 2,
        flops=4 * count * depth * LANES,
        bytes_accessed=8 * count * depth,
    )


def local_kernel(values_ref, above_ref, below_ref, conv_ref, local_ref):
    rows, columns, depth = values_ref.shape
    for at in range(0, depth, LANES):
        lanes = slice(at, at + LANES)
        taps = conv_ref[:, :, lanes]
        sheet = jnp.concatenate(
            [above_ref[:, :, lanes], values_ref[:, :, lanes], below_ref[:, :, lanes]], axis=0
        ).astype(jnp.float32)
        edge = jnp.zeros((rows + 2, 1, LANES), jnp.float32)
        before = jnp.concatenate([edge, sheet[:, :-1]], axis=1)
        behind = jnp.concatenate([sheet[:, 1:], edge], axis=1)
        total = jnp.zeros((rows, columns, LANES), jnp.float32)
        for col_shift, moved in enumerate((before, sheet, behind)):
            for row_shift in range(3):
                total = total + taps[row_shift, col_shift] * moved[row_shift : row_shift + rows]
        local_ref[:, :, lanes] = total


def local_call(values, above, below, conv_weight):
    return kernel_call(
        local_kernel,
        jax.ShapeDtypeStruct(values.shape, jnp.float32),
        (values, above, below, conv_weight),
        [whole_vmem()] * 4,
        flops=18 * values.size,
        bytes_accessed=6 * values.size,
    )


def query_kernel(*refs):
    tokens_ref, qkv_ref, out_ref, mine_ref, theirs_ref, ours_ref, other_ref, *results = refs
    query_ref, weight_ref = results
    y, x, core = coordinates()
    depth = tokens_ref.shape[1]
    rows = qkv_ref.shape[0]
    steps = len(STEPS)
    rest_at = ours_ref.shape[0] - 2 * steps * REST
    places = chip_places(y, x)
    width = 3 * LANES

    def block(of_core, k, lanes):
        return jnp.where(core == of_core, mine_ref[k, :, lanes], theirs_ref[k, :, lanes])

    def rest(of_core, lanes):
        return jnp.where(core == of_core, ours_ref[rest_at:, lanes], other_ref[rest_at:, lanes])

    def put(row, value, lanes):
        weight_ref[pl.ds(pl.multiple_of(row, REST), value.shape[0]), lanes] = value

    for at in range(0, depth, width):
        lanes = slice(at, at + width)
        order = [2 * k for k in range(steps)] + [2 * steps + k for k in range(2 * steps)]
        order += [2 * k + 1 for k in range(steps)]
        columns = [qkv_ref[:, lanes]] + [block(0, k, lanes) for k in order] + [rest(0, lanes)]
        queries = jnp.dot(
            tokens_ref[...], jnp.concatenate(columns, axis=0), preferred_element_type=jnp.float32
        )
        query_ref[:, lanes] = jnp.maximum(queries, 0.0).astype(jnp.bfloat16)

        put(lax.axis_index("space") * rows, out_ref[:, lanes], lanes)
        tiles = rest(1, lanes)
        for k, step in enumerate(STEPS):
            base = source_plane(step) * rows
            held = (2 * k, 3 * steps + k, 2 * steps + k, 2 * k + 1)
            for place, index in zip(places, held):
                put(base + place * MAIN, block(1, index, lanes), lanes)
            for run, tile in enumerate((y, 1 - y)):
                start = (run * steps + k) * REST
                put(base + 4 * MAIN + tile * REST, tiles[start : start + REST], lanes)


def query_call(tokens, qkv_weight, out_weight, mine, theirs, ours, other):
    depth = tokens.shape[1]
    inputs = (tokens, qkv_weight, out_weight, mine, theirs, ours, other)
    return kernel_call(
        query_kernel,
        [
            jax.ShapeDtypeStruct(tokens.shape, jnp.bfloat16),
            jax.ShapeDtypeStruct((depth, depth), jnp.bfloat16),
        ],
        inputs,
        [whole_vmem()] * len(inputs),
        flops=2 * tokens.size * depth,
        bytes_accessed=4 * depth * depth,
    )


def finish_kernel(queries_ref, weight_ref, state_ref, local_ref, gain_ref, result_ref, read_ref):
    count, depth = queries_ref.shape
    mask = diagonal_mask()
    square = jnp.zeros((count, LANES), jnp.float32)
    for group in range(depth // LANES):
        lanes = slice(group * LANES, (group + 1) * LANES)
        spread = jnp.concatenate([state_ref[group]] * (LANES // HEAD_DIM), axis=0)
        spread = jnp.where(mask, spread, 0.0).astype(jnp.bfloat16)
        read = jnp.dot(queries_ref[:, lanes], spread, preferred_element_type=jnp.float32)
        read_ref[:, lanes] = read
        square = square + read * read
    scale = lax.rsqrt(jnp.sum(square, axis=1, keepdims=True) / depth + 1e-06)
    mixture = read_ref[...] * scale * gain_ref[...] + local_ref[...]
    mixture = mixture.astype(jnp.bfloat16)
    width = 3 * LANES
    for at in range(0, depth, width):
        lanes = slice(at, at + width)
        product = jnp.dot(mixture, weight_ref[:, lanes], preferred_element_type=jnp.float32)
        result_ref[:, lanes] = product.astype(jnp.bfloat16)


def finish_call(queries, weight, state, local_term, gain):
    inputs = (queries, weight, state, local_term, gain)
    return kernel_call(
        finish_kernel,
        jax.ShapeDtypeStruct(queries.shape, jnp.bfloat16),
        inputs,
        [whole_vmem()] * len(inputs),
        [pltpu.VMEM(queries.shape, jnp.float32)],
        flops=2 * queries.size * queries.shape[1],
        bytes_accessed=2 * weight.size,
    )


def plane_form(video_tokens, qkv_weight, out_weight, conv_weight, norm_gain):
    frame_now = video_tokens[0]
    row_count, col_count, depth = frame_now.shape
    tokens = frame_now.reshape(row_count * col_count, depth)

    first_piece, second_piece = pieces_call(qkv_weight, out_weight)
    first_piece = first_piece[None]
    one = shifted(first_piece, 1)
    three = shifted(first_piece, -1)
    tokens = reorder_call(after(tokens, second_piece), qkv_weight.shape[0])
    other_tokens = flipped(tokens, (1, 1))
    one, three = after((one, three), tokens)

    pair = jnp.concatenate([one, three])
    two = shifted(one, 1)
    pair_first = flipped(pair, (2, 4))
    near = jnp.concatenate(after((pair, pair_first, two), other_tokens))
    away = flipped(near, (4, 2))
    two_first = flipped(two, (2, 4))
    two_far = flipped(two, (6, 6))

    second_ready = after(second_piece, near)
    second_one = shifted(second_ready, 1)
    second_three = shifted(second_ready, -1)
    second_two = shifted(after(second_one, two_first, two_far), 1)

    mine = first_call(after(tokens, second_one, second_three), other_tokens, qkv_weight, near, away, two_first, two_far)
    other = flipped(after(mine, second_two), (1, 1))
    values, top, bottom, upto, total = state_call(mine, other, tokens.shape[0], col_count)

    second_own = jnp.stack([second_one[0], second_two[0], second_three[0]])
    second_first = flipped(second_own, (2, 4))
    second_second = flipped(second_own, (4, 2))

    for bit, guard in ((2, 2), (4, 4), (6, 4)):
        pairs = [(t, t ^ bit) for t in range(8) if not t & guard]
        upto = upto + lax.ppermute(total, "tm", pairs).astype(jnp.float32)
    count = lax.axis_size("space")
    top, bottom = after((top, bottom), upto)
    forward = [(i, i + 1) for i in range(count - 1)]
    backward = [(target, source) for source, target in forward]
    above = lax.ppermute(bottom, "space", forward)
    below = lax.ppermute(top, "space", backward)
    state = after(upto, second_first, second_second)
    for bit in (1, 2):
        share = state.astype(jnp.bfloat16)
        if bit == 2:
            share = after(share, above, below)
        pairs = [(i, i ^ bit) for i in range(count)]
        state = share.astype(jnp.float32) + lax.ppermute(share, "space", pairs).astype(jnp.float32)
    grid = values.reshape(row_count, col_count, depth)
    local_term = local_call(grid, above, below, conv_weight).reshape(-1, depth)

    parts = (second_one, second_two, second_three, second_first, second_second)
    held = jnp.concatenate(after(parts, share))
    swapped = flipped(held, (1, 1))
    queries, weight = query_call(tokens, qkv_weight, out_weight, held, swapped, mine, other)
    result = finish_call(queries, weight, state, local_term, norm_gain[None])
    return result.reshape(1, row_count, col_count, depth)


def solution(mesh):
    def per_device(video_tokens, qkv_weight, out_weight, conv_weight, norm_gain):
        fits = mesh.shape["tm"] == 8 and mesh.shape["space"] == 4
        fits = fits and qkv_weight.shape[0] == 4 * MAIN + 2 * REST
        form = plane_form if fits else general_form
        return form(video_tokens, qkv_weight, out_weight, conv_weight, norm_gain)

    in_specs = (P("tm", "space", None, None), P("space", None), P("space", None), P(), P())
    out_specs = P("tm", "space", None, None)
    return jax.shard_map(
        per_device, mesh=mesh, in_specs=in_specs, out_specs=out_specs, check_vma=False
    )
```

```python
import functools

import jax
import jax.numpy as jnp
from jax import lax
from jax.experimental import pallas as pl
from jax.experimental.pallas import tpu as pltpu
from jax.sharding import PartitionSpec as P

HEADS = 36
HEAD_DIM = 32
LANES = 128
MAIN = 64
REST = 16
STEPS = (1, 2, 3)
VMEM_LIMIT = 24 * 1024 * 1024
WHOLE_VMEM = 63 * 1024 * 1024


def entering(value, axis, combine, identity):
    devices, place = (lax.axis_size(axis), lax.axis_index(axis))
    everything = lax.all_gather(value.astype(jnp.bfloat16), axis)
    start = jnp.broadcast_to(jnp.asarray(identity, value.dtype), value.shape)

    def lap(k, before):
        reached = k < place
        new = combine(before, everything[k].astype(value.dtype))
        return jnp.where(reached, new, before)

    return lax.fori_loop(0, devices, lap, start)


def with_halo(block, sides, width):
    for axis, dim in sides:
        count = lax.axis_size(axis)
        forward = [(i, i + 1) for i in range(count - 1)]
        backward = [(target, source) for source, target in forward]
        low = lax.ppermute(
            lax.slice_in_dim(block, block.shape[dim] - width, None, axis=dim), axis, forward
        )
        high = lax.ppermute(lax.slice_in_dim(block, 0, width, axis=dim), axis, backward)
        block = jnp.concatenate([low, block, high], axis=dim)
    return block


def fold_product(left_side, block_rows):
    return jnp.dot(left_side, block_rows, preferred_element_type=jnp.float32)


def add_states(earlier, later):
    return earlier + later


def causal_states(key_feat, values):
    key_heads = key_feat.reshape(-1, HEADS, HEAD_DIM)
    value_heads = values.reshape(-1, HEADS, HEAD_DIM)
    frame_state = jnp.einsum(
        "thd,the->hde", key_heads, value_heads, preferred_element_type=jnp.float32
    )
    flat_state = frame_state.reshape(-1)
    frame_sum = lax.psum(flat_state.astype(jnp.bfloat16), "space").astype(jnp.float32)
    earlier = entering(frame_sum, "tm", add_states, jnp.zeros_like(frame_sum))
    whole_state = earlier + frame_sum
    return whole_state.reshape(HEADS, HEAD_DIM, HEAD_DIM)


def general_form(video_tokens, qkv_weight, out_weight, conv_weight, norm_gain):
    frame_now = video_tokens[0]
    row_count, col_count, feat_width = frame_now.shape
    tokens = frame_now.reshape(row_count * col_count, feat_width)
    projected = fold_product(tokens, lax.all_gather(qkv_weight, "space", axis=0, tiled=True))
    query_feat = jax.nn.relu(projected[:, :feat_width]).astype(jnp.bfloat16)
    key_feat = jax.nn.relu(projected[:, feat_width : 2 * feat_width]).astype(jnp.bfloat16)
    values = projected[:, 2 * feat_width :].astype(jnp.bfloat16)
    state_all = causal_states(key_feat, values)
    padded_rows = with_halo(values.reshape(row_count, col_count, feat_width), (("space", 0),), 1)
    padded = jnp.pad(padded_rows, ((0, 0), (1, 1), (0, 0))).astype(jnp.float32)
    local_term = jnp.zeros((row_count, col_count, feat_width), jnp.float32)
    for row_shift in range(3):
        for col_shift in range(3):
            local_term = (
                local_term
                + conv_weight[row_shift, col_shift]
                * padded[row_shift : row_shift + row_count, col_shift : col_shift + col_count]
            )
    state_low = state_all.astype(jnp.bfloat16)
    query_heads = query_feat.reshape(-1, HEADS, HEAD_DIM)
    readout = jnp.einsum("thd,hde->the", query_heads, state_low, preferred_element_type=jnp.float32)
    readout = readout.reshape(-1, feat_width)
    mean_square = jnp.mean(readout * readout, axis=-1, keepdims=True)
    normed = readout * lax.rsqrt(mean_square + 1e-06) * norm_gain
    mixture = (normed + local_term.reshape(-1, feat_width)).astype(jnp.bfloat16)
    result = fold_product(mixture, lax.all_gather(out_weight, "space", axis=0, tiled=True))
    return result.astype(jnp.bfloat16).reshape(1, row_count, col_count, feat_width)


def coordinates():
    place = lax.axis_index("tm")
    return lax.rem(place // 4, 2), lax.rem(place // 2, 2), lax.rem(place, 2)


def shifted(value, step):
    count = lax.axis_size("space")
    return lax.ppermute(value, "space", [(i, (i + step) % count) for i in range(count)])


def flipped(value, bit_on_core):
    return lax.ppermute(value, "tm", [(t, t ^ bit_on_core[t % 2]) for t in range(8)])


def after(value, *earlier):
    return lax.optimization_barrier((value,) + earlier)[0]


def chip_places(y, x):
    return (2 * y + x, 2 * y + (1 - x), 2 * (1 - y) + x, 2 * (1 - y) + (1 - x))


def source_plane(step):
    count = lax.axis_size("space")
    return lax.rem(lax.axis_index("space") - step + count, count)


def steps_through(within, size):
    run = sum(jnp.where(within >= size * k, 1, 0) for k in range(1, len(STEPS)))
    return run, within - size * run


def landed_order(at, width, rows):
    y, x, _ = coordinates()
    planes = [source_plane(step) for step in STEPS]
    row = at + lax.broadcasted_iota(jnp.int32, (1, width), 1)

    def pick(choices, index):
        chosen = choices[-1]
        for k in range(len(choices) - 2, -1, -1):
            chosen = jnp.where(index == k, choices[k], chosen)
        return chosen

    def landed(within, size, starts):
        count = len(STEPS) * size
        slot = sum(jnp.where(within >= count * k, 1, 0) for k in range(1, len(starts)))
        run, left = steps_through(within - count * slot, size)
        return pick(planes, run) * rows + pick(starts, slot) + left

    main = landed(row - rows, MAIN, [place * MAIN for place in chip_places(y, x)])
    rest_at = rows + 4 * len(STEPS) * MAIN
    rest = landed(row - rest_at, REST, [4 * MAIN + tile * REST for tile in (y, 1 - y)])
    own = lax.axis_index("space") * rows + row
    return jnp.where(row < rows, own, jnp.where(row < rest_at, main, rest))


def whole_vmem():
    return pl.BlockSpec(memory_space=pltpu.VMEM)


def anywhere():
    return pl.BlockSpec(memory_space=pltpu.HBM)


def kernel_call(
    body, outputs, inputs, in_specs, scratch=(), flops=0, bytes_accessed=0, limit=VMEM_LIMIT
):
    return pl.pallas_call(
        body,
        out_shape=outputs,
        in_specs=in_specs,
        out_specs=jax.tree.map(lambda _: whole_vmem(), outputs),
        scratch_shapes=list(scratch),
        compiler_params=pltpu.CompilerParams(vmem_limit_bytes=limit),
        cost_estimate=pl.CostEstimate(
            flops=flops, bytes_accessed=bytes_accessed, transcendentals=0
        ),
    )(*inputs)


def pieces_kernel(qkv_ref, out_ref, first_ref, second_ref, sems):
    y, x, core = coordinates()
    depth = out_ref.shape[1]
    main = pl.ds(pl.multiple_of((2 * y + x) * MAIN, REST), MAIN)
    rest = pl.ds(pl.multiple_of(4 * MAIN + y * REST, REST), REST)
    first_columns = pl.ds(pl.multiple_of(depth * (1 + core), LANES), depth)
    rest_columns = pl.ds(pl.multiple_of(jnp.where(x == 0, depth * (1 + core), 0), LANES), depth)

    def copy(source, target, k):
        return pltpu.make_async_copy(source, target, sems.at[k])

    first_main = copy(qkv_ref.at[main, first_columns], first_ref.at[pl.ds(0, MAIN), :], 0)
    first_main.start()
    rest_target = first_ref.at[pl.ds(MAIN, REST), :]
    from_out = (core == 1) & (x == 1)

    @pl.when(from_out)
    def _():
        copy(out_ref.at[rest, :], rest_target, 1).start()

    @pl.when(jnp.logical_not(from_out))
    def _():
        copy(qkv_ref.at[rest, rest_columns], rest_target, 1).start()

    places = chip_places(y, x)
    for k, place in enumerate((places[0], places[3])):
        rows = pl.ds(pl.multiple_of(place * MAIN, REST), MAIN)

        @pl.when(core == 0)
        def _():
            copy(qkv_ref.at[rows, pl.ds(0, depth)], second_ref.at[k], 2 + k).start()

        @pl.when(core == 1)
        def _():
            copy(out_ref.at[rows, :], second_ref.at[k], 2 + k).start()

    first_main.wait()
    copy(out_ref.at[rest, :], rest_target, 1).wait()
    for k in range(2):
        copy(out_ref.at[main, :], second_ref.at[k], 2 + k).wait()


def pieces_call(qkv_weight, out_weight):
    depth = out_weight.shape[1]
    outputs = [
        jax.ShapeDtypeStruct((MAIN + REST, depth), jnp.bfloat16),
        jax.ShapeDtypeStruct((2, MAIN, depth), jnp.bfloat16),
    ]
    return kernel_call(
        pieces_kernel,
        outputs,
        (qkv_weight, out_weight),
        [anywhere(), anywhere()],
        [pltpu.SemaphoreType.DMA((4,))],
        bytes_accessed=4 * (3 * MAIN + REST) * depth,
        limit=WHOLE_VMEM,
    )


def reorder_kernel(rows, tokens_ref, moved_ref):
    depth = tokens_ref.shape[1]
    width = 3 * LANES
    row = lax.broadcasted_iota(jnp.int32, (depth, width), 0)
    for at in range(0, depth, width):
        order = landed_order(at, width, rows)
        chosen = jnp.where(row == order, 1.0, 0.0).astype(jnp.bfloat16)
        moved = jnp.dot(tokens_ref[...], chosen, preferred_element_type=jnp.float32)
        moved_ref[:, at : at + width] = moved.astype(jnp.bfloat16)


def reorder_call(tokens, rows):
    depth = tokens.shape[1]
    return kernel_call(
        functools.partial(reorder_kernel, rows),
        jax.ShapeDtypeStruct(tokens.shape, jnp.bfloat16),
        (tokens,),
        [whole_vmem()],
        flops=2 * tokens.size * depth,
        bytes_accessed=2 * tokens.size,
    )


def first_kernel(*refs):
    tokens_ref, other_ref, qkv_ref, near_ref, away_ref, first_ref, far_ref, mine_ref = refs
    slots = (
        ((near_ref, 0), (first_ref, 0), (near_ref, 1)),
        ((near_ref, 2), (first_ref, 1), (near_ref, 3)),
        ((away_ref, 0), (far_ref, 0), (away_ref, 1)),
        ((away_ref, 2), (far_ref, 1), (away_ref, 3)),
    )
    _, x, core = coordinates()
    count, depth = tokens_ref.shape
    floor = jnp.where(core == 0, 0.0, -jnp.inf).astype(jnp.float32)
    width = 3 * LANES

    for at in range(0, depth, width):
        lanes = slice(at, at + width)

        def slot(k, low, high):
            return jnp.concatenate([ref[at, low:high, lanes] for ref, at in slots[k]], axis=0)

        def by_place(low, high):
            own, first, second, far = [slot(k, low, high) for k in range(4)]
            along_x = jnp.where(core == 0, first, second)
            along_y = jnp.where(core == 0, second, first)
            return own, along_x, along_y, far

        keys, values = [qkv_ref[:, depth * k + at : depth * k + at + width] for k in (1, 2)]
        own = jnp.where(core == 0, keys, values)
        rest = by_place(MAIN, MAIN + REST)
        even = jnp.concatenate([rest[0], rest[2]], axis=0)
        odd = jnp.concatenate([rest[1], rest[3]], axis=0)
        mine_ref[2 * count :, lanes] = jnp.where(x == 1, even, odd)
        columns = jnp.concatenate(
            (own,) + by_place(0, MAIN) + (jnp.where(x == 0, even, odd),), axis=0
        )
        for k, ref in enumerate((tokens_ref, other_ref)):
            product = jnp.dot(ref[...], columns, preferred_element_type=jnp.float32)
            product = jnp.maximum(product, floor).astype(jnp.bfloat16)
            mine_ref[k * count : (k + 1) * count, lanes] = product


def first_call(tokens, other, qkv_weight, *landed):
    count, depth = tokens.shape
    inputs = (tokens, other, qkv_weight) + landed
    return kernel_call(
        first_kernel,
        jax.ShapeDtypeStruct((2 * count + 2 * len(STEPS) * REST, depth), jnp.bfloat16),
        inputs,
        [whole_vmem()] * len(inputs),
        flops=4 * tokens.size * depth,
        bytes_accessed=2 * depth * depth,
    )


def diagonal_mask():
    rows = lax.broadcasted_iota(jnp.int32, (LANES, LANES), 0) // HEAD_DIM
    columns = lax.broadcasted_iota(jnp.int32, (LANES, LANES), 1) // HEAD_DIM
    return rows == columns


def state_kernel(mine_ref, other_ref, values_ref, top_ref, bottom_ref, upto_ref, total_ref):
    _, _, core = coordinates()
    mask = diagonal_mask()
    columns = top_ref.shape[1]
    count = values_ref.shape[0]
    later = jnp.where(core == 1, 1.0, 0.0).astype(jnp.float32)
    for group in range(mine_ref.shape[1] // LANES):
        at = slice(group * LANES, (group + 1) * LANES)

        def state(mine, other):
            keys = jnp.where(core == 0, mine, other)
            values = jnp.where(core == 0, other, mine)
            full = lax.dot_general(
                keys, values, (((0,), (0,)), ((), ())), preferred_element_type=jnp.float32
            )
            full = jnp.where(mask, full, 0.0)
            total = full[0:HEAD_DIM]
            for k in range(1, LANES // HEAD_DIM):
                total = total + full[k * HEAD_DIM : (k + 1) * HEAD_DIM]
            return total, values

        low, high = slice(0, count), slice(count, 2 * count)
        here, values = state(mine_ref[low, at], other_ref[high, at])
        there, _ = state(mine_ref[high, at], other_ref[low, at])
        values_ref[:, at] = values
        top_ref[0, :, at] = values[:columns]
        bottom_ref[0, :, at] = values[-columns:]
        upto_ref[group] = here + later * there
        total_ref[group] = (here + there).astype(jnp.bfloat16)


def state_call(mine, other, count, columns):
    depth = mine.shape[1]
    compact = (depth // LANES, HEAD_DIM, LANES)
    edge = jax.ShapeDtypeStruct((1, columns, depth), jnp.bfloat16)
    return kernel_call(
        state_kernel,
        [
            jax.ShapeDtypeStruct((count, depth), jnp.bfloat16),
            edge,
            edge,
            jax.ShapeDtypeStruct(compact, jnp.float32),
            jax.ShapeDtypeStruct(compact, jnp.bfloat16),
        ],
        (mine, other),
        [whole_vmem()] * 2,
        flops=4 * count * depth * LANES,
        bytes_accessed=8 * count * depth,
    )


def local_kernel(values_ref, above_ref, below_ref, conv_ref, local_ref):
    rows, columns, depth = values_ref.shape
    for at in range(0, depth, LANES):
        lanes = slice(at, at + LANES)
        taps = conv_ref[:, :, lanes]
        sheet = jnp.concatenate(
            [above_ref[:, :, lanes], values_ref[:, :, lanes], below_ref[:, :, lanes]], axis=0
        ).astype(jnp.float32)
        edge = jnp.zeros((rows + 2, 1, LANES), jnp.float32)
        before = jnp.concatenate([edge, sheet[:, :-1]], axis=1)
        behind = jnp.concatenate([sheet[:, 1:], edge], axis=1)
        total = jnp.zeros((rows, columns, LANES), jnp.float32)
        for col_shift, moved in enumerate((before, sheet, behind)):
            for row_shift in range(3):
                total = total + taps[row_shift, col_shift] * moved[row_shift : row_shift + rows]
        local_ref[:, :, lanes] = total


def local_call(values, above, below, conv_weight):
    return kernel_call(
        local_kernel,
        jax.ShapeDtypeStruct(values.shape, jnp.float32),
        (values, above, below, conv_weight),
        [whole_vmem()] * 4,
        flops=18 * values.size,
        bytes_accessed=6 * values.size,
    )


def query_kernel(*refs):
    tokens_ref, qkv_ref, out_ref, *packs, ours_ref, other_ref, query_ref, weight_ref = refs
    y, x, core = coordinates()
    depth = tokens_ref.shape[1]
    rows = qkv_ref.shape[0]
    steps = len(STEPS)
    rest_at = ours_ref.shape[0] - 2 * steps * REST
    places = chip_places(y, x)
    width = 3 * LANES

    def block(of_core, index, lanes):
        pack, k = index
        mine_ref, theirs_ref = packs[2 * pack], packs[2 * pack + 1]
        return jnp.where(core == of_core, mine_ref[k, :, lanes], theirs_ref[k, :, lanes])


    def rest(of_core, lanes):
        return jnp.where(core == of_core, ours_ref[rest_at:, lanes], other_ref[rest_at:, lanes])

    def put(row, value, lanes):
        weight_ref[pl.ds(pl.multiple_of(row, REST), value.shape[0]), lanes] = value

    for at in range(0, depth, width):
        lanes = slice(at, at + width)
        order = [(0, 2 * k) for k in range(steps)] + [(1, k) for k in range(2 * steps)]
        order += [(0, 2 * k + 1) for k in range(steps)]
        columns = [qkv_ref[:, lanes]] + [block(0, k, lanes) for k in order] + [rest(0, lanes)]
        queries = jnp.dot(
            tokens_ref[...], jnp.concatenate(columns, axis=0), preferred_element_type=jnp.float32
        )
        query_ref[:, lanes] = jnp.maximum(queries, 0.0).astype(jnp.bfloat16)

        put(lax.axis_index("space") * rows, out_ref[:, lanes], lanes)
        tiles = rest(1, lanes)
        for k, step in enumerate(STEPS):
            base = source_plane(step) * rows
            held = ((0, 2 * k), (1, steps + k), (1, k), (0, 2 * k + 1))
            for place, index in zip(places, held):
                put(base + place * MAIN, block(1, index, lanes), lanes)
            for run, tile in enumerate((y, 1 - y)):
                start = (run * steps + k) * REST
                put(base + 4 * MAIN + tile * REST, tiles[start : start + REST], lanes)


def query_call(tokens, qkv_weight, out_weight, *landed):
    depth = tokens.shape[1]
    inputs = (tokens, qkv_weight, out_weight) + landed
    return kernel_call(
        query_kernel,
        [
            jax.ShapeDtypeStruct(tokens.shape, jnp.bfloat16),
            jax.ShapeDtypeStruct((depth, depth), jnp.bfloat16),
        ],
        inputs,
        [whole_vmem()] * len(inputs),
        flops=2 * tokens.size * depth,
        bytes_accessed=4 * depth * depth,
    )


def finish_kernel(queries_ref, weight_ref, state_ref, local_ref, gain_ref, result_ref, read_ref):
    count, depth = queries_ref.shape
    mask = diagonal_mask()
    square = jnp.zeros((count, LANES), jnp.float32)
    for group in range(depth // LANES):
        lanes = slice(group * LANES, (group + 1) * LANES)
        spread = jnp.concatenate([state_ref[group]] * (LANES // HEAD_DIM), axis=0)
        spread = jnp.where(mask, spread, 0.0).astype(jnp.bfloat16)
        read = jnp.dot(queries_ref[:, lanes], spread, preferred_element_type=jnp.float32)
        read_ref[:, lanes] = read
        square = square + read * read
    scale = lax.rsqrt(jnp.sum(square, axis=1, keepdims=True) / depth + 1e-06)
    mixture = read_ref[...] * scale * gain_ref[...] + local_ref[...]
    mixture = mixture.astype(jnp.bfloat16)
    width = 3 * LANES
    for at in range(0, depth, width):
        lanes = slice(at, at + width)
        product = jnp.dot(mixture, weight_ref[:, lanes], preferred_element_type=jnp.float32)
        result_ref[:, lanes] = product.astype(jnp.bfloat16)


def finish_call(queries, weight, state, local_term, gain):
    inputs = (queries, weight, state, local_term, gain)
    return kernel_call(
        finish_kernel,
        jax.ShapeDtypeStruct(queries.shape, jnp.bfloat16),
        inputs,
        [whole_vmem()] * len(inputs),
        [pltpu.VMEM(queries.shape, jnp.float32)],
        flops=2 * queries.size * queries.shape[1],
        bytes_accessed=2 * weight.size,
    )


def plane_form(video_tokens, qkv_weight, out_weight, conv_weight, norm_gain):
    frame_now = video_tokens[0]
    row_count, col_count, depth = frame_now.shape
    tokens = frame_now.reshape(row_count * col_count, depth)

    first_piece, second_piece = pieces_call(qkv_weight, out_weight)
    first_piece = first_piece[None]
    one = shifted(first_piece, 1)
    three = shifted(first_piece, -1)
    tokens = reorder_call(after(tokens, second_piece), qkv_weight.shape[0])
    other_tokens = flipped(tokens, (1, 1))
    one, three = after((one, three), tokens)

    pair = jnp.concatenate([one, three])
    two = shifted(one, 1)
    pair_first = flipped(pair, (2, 4))
    near = jnp.concatenate(after((pair, pair_first), other_tokens))
    away = flipped(near, (4, 2))
    two_near = jnp.concatenate([two, flipped(two, (2, 4))])
    two_away = flipped(two_near, (4, 2))

    second_ready = after(second_piece, one, three)
    second_one = shifted(second_ready, 1)
    second_three = shifted(second_ready, -1)
    second_two = shifted(after(second_one, two_near), 1)

    mine = first_call(after(tokens, second_one, second_three), other_tokens, qkv_weight, near, away, two_near, two_away)
    other = flipped(after(mine, second_two), (1, 1))
    straight = jnp.concatenate([second_one, second_two, second_three])
    swapped_straight = flipped(straight, (1, 1))
    values, top, bottom, upto, total = state_call(mine, other, tokens.shape[0], col_count)
    total = after(total, swapped_straight)

    second_own = jnp.stack([second_one[0], second_two[0], second_three[0]])
    second_first = flipped(second_own, (2, 4))
    second_second = flipped(second_own, (4, 2))

    for bit, guard in ((2, 2), (4, 4), (6, 4)):
        pairs = [(t, t ^ bit) for t in range(8) if not t & guard]
        upto = upto + lax.ppermute(total, "tm", pairs).astype(jnp.float32)
    count = lax.axis_size("space")
    forward = [(i, i + 1) for i in range(count - 1)]
    backward = [(target, source) for source, target in forward]
    state = after(upto, second_first, second_second)
    for bit in (1, 2):
        share = state.astype(jnp.bfloat16)
        if bit == 2:
            top, bottom = after((top, bottom), share)
        pairs = [(i, i ^ bit) for i in range(count)]
        state = share.astype(jnp.float32) + lax.ppermute(share, "space", pairs).astype(jnp.float32)
    above = lax.ppermute(bottom, "space", forward)
    below = lax.ppermute(top, "space", backward)
    grid = values.reshape(row_count, col_count, depth)
    local_term = local_call(grid, above, below, conv_weight).reshape(-1, depth)

    turned = jnp.concatenate([second_first, second_second])
    swapped_turned = flipped(after(turned, share), (1, 1))
    queries, weight = query_call(
        tokens,
        qkv_weight,
        out_weight,
        straight,
        swapped_straight,
        turned,
        swapped_turned,
        mine,
        other,
    )
    result = finish_call(queries, weight, state, local_term, norm_gain[None])
    return result.reshape(1, row_count, col_count, depth)


def solution(mesh):
    def per_device(video_tokens, qkv_weight, out_weight, conv_weight, norm_gain):
        fits = mesh.shape["tm"] == 8 and mesh.shape["space"] == 4
        fits = fits and qkv_weight.shape[0] == 4 * MAIN + 2 * REST
        form = plane_form if fits else general_form
        return form(video_tokens, qkv_weight, out_weight, conv_weight, norm_gain)

    in_specs = (P("tm", "space", None, None), P("space", None), P("space", None), P(), P())
    out_specs = P("tm", "space", None, None)
    return jax.shard_map(
        per_device, mesh=mesh, in_specs=in_specs, out_specs=out_specs, check_vma=False
    )
```

```python
import functools

import jax
import jax.numpy as jnp
from jax import lax
from jax.experimental import pallas as pl
from jax.experimental.pallas import tpu as pltpu
from jax.sharding import PartitionSpec as P

HEADS = 36
HEAD_DIM = 32
LANES = 128
MAIN = 64
REST = 16
STEPS = (1, 2, 3)
VMEM_LIMIT = 24 * 1024 * 1024
WHOLE_VMEM = 63 * 1024 * 1024


def entering(value, axis, combine, identity):
    devices, place = (lax.axis_size(axis), lax.axis_index(axis))
    everything = lax.all_gather(value.astype(jnp.bfloat16), axis)
    start = jnp.broadcast_to(jnp.asarray(identity, value.dtype), value.shape)

    def lap(k, before):
        reached = k < place
        new = combine(before, everything[k].astype(value.dtype))
        return jnp.where(reached, new, before)

    return lax.fori_loop(0, devices, lap, start)


def with_halo(block, sides, width):
    for axis, dim in sides:
        count = lax.axis_size(axis)
        forward = [(i, i + 1) for i in range(count - 1)]
        backward = [(target, source) for source, target in forward]
        low = lax.ppermute(
            lax.slice_in_dim(block, block.shape[dim] - width, None, axis=dim), axis, forward
        )
        high = lax.ppermute(lax.slice_in_dim(block, 0, width, axis=dim), axis, backward)
        block = jnp.concatenate([low, block, high], axis=dim)
    return block


def fold_product(left_side, block_rows):
    return jnp.dot(left_side, block_rows, preferred_element_type=jnp.float32)


def add_states(earlier, later):
    return earlier + later


def causal_states(key_feat, values):
    key_heads = key_feat.reshape(-1, HEADS, HEAD_DIM)
    value_heads = values.reshape(-1, HEADS, HEAD_DIM)
    frame_state = jnp.einsum(
        "thd,the->hde", key_heads, value_heads, preferred_element_type=jnp.float32
    )
    flat_state = frame_state.reshape(-1)
    frame_sum = lax.psum(flat_state.astype(jnp.bfloat16), "space").astype(jnp.float32)
    earlier = entering(frame_sum, "tm", add_states, jnp.zeros_like(frame_sum))
    whole_state = earlier + frame_sum
    return whole_state.reshape(HEADS, HEAD_DIM, HEAD_DIM)


def general_form(video_tokens, qkv_weight, out_weight, conv_weight, norm_gain):
    frame_now = video_tokens[0]
    row_count, col_count, feat_width = frame_now.shape
    tokens = frame_now.reshape(row_count * col_count, feat_width)
    projected = fold_product(tokens, lax.all_gather(qkv_weight, "space", axis=0, tiled=True))
    query_feat = jax.nn.relu(projected[:, :feat_width]).astype(jnp.bfloat16)
    key_feat = jax.nn.relu(projected[:, feat_width : 2 * feat_width]).astype(jnp.bfloat16)
    values = projected[:, 2 * feat_width :].astype(jnp.bfloat16)
    state_all = causal_states(key_feat, values)
    padded_rows = with_halo(values.reshape(row_count, col_count, feat_width), (("space", 0),), 1)
    padded = jnp.pad(padded_rows, ((0, 0), (1, 1), (0, 0))).astype(jnp.float32)
    local_term = jnp.zeros((row_count, col_count, feat_width), jnp.float32)
    for row_shift in range(3):
        for col_shift in range(3):
            local_term = (
                local_term
                + conv_weight[row_shift, col_shift]
                * padded[row_shift : row_shift + row_count, col_shift : col_shift + col_count]
            )
    state_low = state_all.astype(jnp.bfloat16)
    query_heads = query_feat.reshape(-1, HEADS, HEAD_DIM)
    readout = jnp.einsum("thd,hde->the", query_heads, state_low, preferred_element_type=jnp.float32)
    readout = readout.reshape(-1, feat_width)
    mean_square = jnp.mean(readout * readout, axis=-1, keepdims=True)
    normed = readout * lax.rsqrt(mean_square + 1e-06) * norm_gain
    mixture = (normed + local_term.reshape(-1, feat_width)).astype(jnp.bfloat16)
    result = fold_product(mixture, lax.all_gather(out_weight, "space", axis=0, tiled=True))
    return result.astype(jnp.bfloat16).reshape(1, row_count, col_count, feat_width)


def coordinates():
    place = lax.axis_index("tm")
    return lax.rem(place // 4, 2), lax.rem(place // 2, 2), lax.rem(place, 2)


def shifted(value, step):
    count = lax.axis_size("space")
    return lax.ppermute(value, "space", [(i, (i + step) % count) for i in range(count)])


def flipped(value, bit_on_core):
    return lax.ppermute(value, "tm", [(t, t ^ bit_on_core[t % 2]) for t in range(8)])


def after(value, *earlier):
    return lax.optimization_barrier((value,) + earlier)[0]


def chip_places(y, x):
    return (2 * y + x, 2 * y + (1 - x), 2 * (1 - y) + x, 2 * (1 - y) + (1 - x))


def source_plane(step):
    count = lax.axis_size("space")
    return lax.rem(lax.axis_index("space") - step + count, count)


def steps_through(within, size):
    run = sum(jnp.where(within >= size * k, 1, 0) for k in range(1, len(STEPS)))
    return run, within - size * run


def landed_order(at, width, rows):
    y, x, _ = coordinates()
    planes = [source_plane(step) for step in STEPS]
    row = at + lax.broadcasted_iota(jnp.int32, (1, width), 1)

    def pick(choices, index):
        chosen = choices[-1]
        for k in range(len(choices) - 2, -1, -1):
            chosen = jnp.where(index == k, choices[k], chosen)
        return chosen

    def landed(within, size, starts):
        count = len(STEPS) * size
        slot = sum(jnp.where(within >= count * k, 1, 0) for k in range(1, len(starts)))
        run, left = steps_through(within - count * slot, size)
        return pick(planes, run) * rows + pick(starts, slot) + left

    main = landed(row - rows, MAIN, [place * MAIN for place in chip_places(y, x)])
    rest_at = rows + 4 * len(STEPS) * MAIN
    rest = landed(row - rest_at, REST, [4 * MAIN + tile * REST for tile in (y, 1 - y)])
    own = lax.axis_index("space") * rows + row
    return jnp.where(row < rows, own, jnp.where(row < rest_at, main, rest))


def whole_vmem():
    return pl.BlockSpec(memory_space=pltpu.VMEM)


def anywhere():
    return pl.BlockSpec(memory_space=pltpu.HBM)


def kernel_call(
    body, outputs, inputs, in_specs, scratch=(), flops=0, bytes_accessed=0, limit=VMEM_LIMIT
):
    return pl.pallas_call(
        body,
        out_shape=outputs,
        in_specs=in_specs,
        out_specs=jax.tree.map(lambda _: whole_vmem(), outputs),
        scratch_shapes=list(scratch),
        compiler_params=pltpu.CompilerParams(vmem_limit_bytes=limit),
        cost_estimate=pl.CostEstimate(
            flops=flops, bytes_accessed=bytes_accessed, transcendentals=0
        ),
    )(*inputs)


def pieces_kernel(qkv_ref, out_ref, first_ref, second_ref, sems):
    y, x, core = coordinates()
    depth = out_ref.shape[1]
    main = pl.ds(pl.multiple_of((2 * y + x) * MAIN, REST), MAIN)
    rest = pl.ds(pl.multiple_of(4 * MAIN + y * REST, REST), REST)
    first_columns = pl.ds(pl.multiple_of(depth * (1 + core), LANES), depth)
    rest_columns = pl.ds(pl.multiple_of(jnp.where(x == 0, depth * (1 + core), 0), LANES), depth)

    def copy(source, target, k):
        return pltpu.make_async_copy(source, target, sems.at[k])

    first_main = copy(qkv_ref.at[main, first_columns], first_ref.at[pl.ds(0, MAIN), :], 0)
    first_main.start()
    rest_target = first_ref.at[pl.ds(MAIN, REST), :]
    from_out = (core == 1) & (x == 1)

    @pl.when(from_out)
    def _():
        copy(out_ref.at[rest, :], rest_target, 1).start()

    @pl.when(jnp.logical_not(from_out))
    def _():
        copy(qkv_ref.at[rest, rest_columns], rest_target, 1).start()

    places = chip_places(y, x)
    for k, place in enumerate((places[0], places[3])):
        rows = pl.ds(pl.multiple_of(place * MAIN, REST), MAIN)

        @pl.when(core == 0)
        def _():
            copy(qkv_ref.at[rows, pl.ds(0, depth)], second_ref.at[k], 2 + k).start()

        @pl.when(core == 1)
        def _():
            copy(out_ref.at[rows, :], second_ref.at[k], 2 + k).start()

    first_main.wait()
    copy(out_ref.at[rest, :], rest_target, 1).wait()
    for k in range(2):
        copy(out_ref.at[main, :], second_ref.at[k], 2 + k).wait()


def pieces_call(qkv_weight, out_weight):
    depth = out_weight.shape[1]
    outputs = [
        jax.ShapeDtypeStruct((MAIN + REST, depth), jnp.bfloat16),
        jax.ShapeDtypeStruct((2, MAIN, depth), jnp.bfloat16),
    ]
    return kernel_call(
        pieces_kernel,
        outputs,
        (qkv_weight, out_weight),
        [anywhere(), anywhere()],
        [pltpu.SemaphoreType.DMA((4,))],
        bytes_accessed=4 * (3 * MAIN + REST) * depth,
        limit=WHOLE_VMEM,
    )


def reorder_kernel(rows, tokens_ref, moved_ref):
    depth = tokens_ref.shape[1]
    width = 3 * LANES
    row = lax.broadcasted_iota(jnp.int32, (depth, width), 0)
    for at in range(0, depth, width):
        order = landed_order(at, width, rows)
        chosen = jnp.where(row == order, 1.0, 0.0).astype(jnp.bfloat16)
        moved = jnp.dot(tokens_ref[...], chosen, preferred_element_type=jnp.float32)
        moved_ref[:, at : at + width] = moved.astype(jnp.bfloat16)


def reorder_call(tokens, rows):
    depth = tokens.shape[1]
    return kernel_call(
        functools.partial(reorder_kernel, rows),
        jax.ShapeDtypeStruct(tokens.shape, jnp.bfloat16),
        (tokens,),
        [whole_vmem()],
        flops=2 * tokens.size * depth,
        bytes_accessed=2 * tokens.size,
    )


def first_kernel(*refs):
    tokens_ref, other_ref, qkv_ref, near_ref, away_ref, first_ref, far_ref, mine_ref = refs
    slots = (
        ((near_ref, 0), (first_ref, 0), (near_ref, 1)),
        ((near_ref, 2), (first_ref, 1), (near_ref, 3)),
        ((away_ref, 0), (far_ref, 0), (away_ref, 1)),
        ((away_ref, 2), (far_ref, 1), (away_ref, 3)),
    )
    _, x, core = coordinates()
    count, depth = tokens_ref.shape
    floor = jnp.where(core == 0, 0.0, -jnp.inf).astype(jnp.float32)
    width = 3 * LANES

    for at in range(0, depth, width):
        lanes = slice(at, at + width)

        def slot(k, low, high):
            return jnp.concatenate([ref[at, low:high, lanes] for ref, at in slots[k]], axis=0)

        def by_place(low, high):
            own, first, second, far = [slot(k, low, high) for k in range(4)]
            along_x = jnp.where(core == 0, first, second)
            along_y = jnp.where(core == 0, second, first)
            return own, along_x, along_y, far

        keys, values = [qkv_ref[:, depth * k + at : depth * k + at + width] for k in (1, 2)]
        own = jnp.where(core == 0, keys, values)
        rest = by_place(MAIN, MAIN + REST)
        even = jnp.concatenate([rest[0], rest[2]], axis=0)
        odd = jnp.concatenate([rest[1], rest[3]], axis=0)
        mine_ref[2 * count :, lanes] = jnp.where(x == 1, even, odd)
        columns = jnp.concatenate(
            (own,) + by_place(0, MAIN) + (jnp.where(x == 0, even, odd),), axis=0
        )
        for k, ref in enumerate((tokens_ref, other_ref)):
            product = jnp.dot(ref[...], columns, preferred_element_type=jnp.float32)
            product = jnp.maximum(product, floor).astype(jnp.bfloat16)
            mine_ref[k * count : (k + 1) * count, lanes] = product


def first_call(tokens, other, qkv_weight, *landed):
    count, depth = tokens.shape
    inputs = (tokens, other, qkv_weight) + landed
    return kernel_call(
        first_kernel,
        jax.ShapeDtypeStruct((2 * count + 2 * len(STEPS) * REST, depth), jnp.bfloat16),
        inputs,
        [whole_vmem()] * len(inputs),
        flops=4 * tokens.size * depth,
        bytes_accessed=2 * depth * depth,
    )


def diagonal_mask():
    rows = lax.broadcasted_iota(jnp.int32, (LANES, LANES), 0) // HEAD_DIM
    columns = lax.broadcasted_iota(jnp.int32, (LANES, LANES), 1) // HEAD_DIM
    return rows == columns


def state_kernel(mine_ref, other_ref, values_ref, top_ref, bottom_ref, upto_ref, total_ref):
    _, _, core = coordinates()
    mask = diagonal_mask()
    columns = top_ref.shape[1]
    count = values_ref.shape[0]
    later = jnp.where(core == 1, 1.0, 0.0).astype(jnp.float32)
    for group in range(mine_ref.shape[1] // LANES):
        at = slice(group * LANES, (group + 1) * LANES)

        def state(mine, other):
            keys = jnp.where(core == 0, mine, other)
            values = jnp.where(core == 0, other, mine)
            full = lax.dot_general(
                keys, values, (((0,), (0,)), ((), ())), preferred_element_type=jnp.float32
            )
            full = jnp.where(mask, full, 0.0)
            total = full[0:HEAD_DIM]
            for k in range(1, LANES // HEAD_DIM):
                total = total + full[k * HEAD_DIM : (k + 1) * HEAD_DIM]
            return total, values

        low, high = slice(0, count), slice(count, 2 * count)
        here, values = state(mine_ref[low, at], other_ref[high, at])
        there, _ = state(mine_ref[high, at], other_ref[low, at])
        values_ref[:, at] = values
        top_ref[0, :, at] = values[:columns]
        bottom_ref[0, :, at] = values[-columns:]
        upto_ref[group] = here + later * there
        total_ref[group] = (here + there).astype(jnp.bfloat16)


def state_call(mine, other, count, columns):
    depth = mine.shape[1]
    compact = (depth // LANES, HEAD_DIM, LANES)
    edge = jax.ShapeDtypeStruct((1, columns, depth), jnp.bfloat16)
    return kernel_call(
        state_kernel,
        [
            jax.ShapeDtypeStruct((count, depth), jnp.bfloat16),
            edge,
            edge,
            jax.ShapeDtypeStruct(compact, jnp.float32),
            jax.ShapeDtypeStruct(compact, jnp.bfloat16),
        ],
        (mine, other),
        [whole_vmem()] * 2,
        flops=4 * count * depth * LANES,
        bytes_accessed=8 * count * depth,
    )


def local_kernel(values_ref, above_ref, below_ref, conv_ref, local_ref):
    rows, columns, depth = values_ref.shape
    for at in range(0, depth, LANES):
        lanes = slice(at, at + LANES)
        taps = conv_ref[:, :, lanes]
        sheet = jnp.concatenate(
            [above_ref[:, :, lanes], values_ref[:, :, lanes], below_ref[:, :, lanes]], axis=0
        ).astype(jnp.float32)
        edge = jnp.zeros((rows + 2, 1, LANES), jnp.float32)
        before = jnp.concatenate([edge, sheet[:, :-1]], axis=1)
        behind = jnp.concatenate([sheet[:, 1:], edge], axis=1)
        total = jnp.zeros((rows, columns, LANES), jnp.float32)
        for col_shift, moved in enumerate((before, sheet, behind)):
            for row_shift in range(3):
                total = total + taps[row_shift, col_shift] * moved[row_shift : row_shift + rows]
        local_ref[:, :, lanes] = total


def local_call(values, above, below, conv_weight):
    return kernel_call(
        local_kernel,
        jax.ShapeDtypeStruct(values.shape, jnp.float32),
        (values, above, below, conv_weight),
        [whole_vmem()] * 4,
        flops=18 * values.size,
        bytes_accessed=6 * values.size,
    )


def query_kernel(*refs):
    tokens_ref, qkv_ref, out_ref, *packs, ours_ref, other_ref, query_ref, weight_ref = refs
    y, x, core = coordinates()
    depth = tokens_ref.shape[1]
    rows = qkv_ref.shape[0]
    steps = len(STEPS)
    rest_at = ours_ref.shape[0] - 2 * steps * REST
    places = chip_places(y, x)
    width = 3 * LANES

    def block(of_core, index, lanes):
        pack, k = index
        mine_ref, theirs_ref = packs[2 * pack], packs[2 * pack + 1]
        return jnp.where(core == of_core, mine_ref[k, :, lanes], theirs_ref[k, :, lanes])


    def rest(of_core, lanes):
        return jnp.where(core == of_core, ours_ref[rest_at:, lanes], other_ref[rest_at:, lanes])

    def put(row, value, lanes):
        weight_ref[pl.ds(pl.multiple_of(row, REST), value.shape[0]), lanes] = value

    for at in range(0, depth, width):
        lanes = slice(at, at + width)
        order = [(0, 2 * k) for k in range(steps)] + [(1, k) for k in range(2 * steps)]
        order += [(0, 2 * k + 1) for k in range(steps)]
        columns = [qkv_ref[:, lanes]] + [block(0, k, lanes) for k in order] + [rest(0, lanes)]
        queries = jnp.dot(
            tokens_ref[...], jnp.concatenate(columns, axis=0), preferred_element_type=jnp.float32
        )
        query_ref[:, lanes] = jnp.maximum(queries, 0.0).astype(jnp.bfloat16)

        put(lax.axis_index("space") * rows, out_ref[:, lanes], lanes)
        tiles = rest(1, lanes)
        for k, step in enumerate(STEPS):
            base = source_plane(step) * rows
            held = ((0, 2 * k), (1, steps + k), (1, k), (0, 2 * k + 1))
            for place, index in zip(places, held):
                put(base + place * MAIN, block(1, index, lanes), lanes)
            for run, tile in enumerate((y, 1 - y)):
                start = (run * steps + k) * REST
                put(base + 4 * MAIN + tile * REST, tiles[start : start + REST], lanes)


def query_call(tokens, qkv_weight, out_weight, *landed):
    depth = tokens.shape[1]
    inputs = (tokens, qkv_weight, out_weight) + landed
    return kernel_call(
        query_kernel,
        [
            jax.ShapeDtypeStruct(tokens.shape, jnp.bfloat16),
            jax.ShapeDtypeStruct((depth, depth), jnp.bfloat16),
        ],
        inputs,
        [whole_vmem()] * len(inputs),
        flops=2 * tokens.size * depth,
        bytes_accessed=4 * depth * depth,
    )


def finish_kernel(queries_ref, weight_ref, state_ref, local_ref, gain_ref, result_ref, read_ref):
    count, depth = queries_ref.shape
    mask = diagonal_mask()
    square = jnp.zeros((count, LANES), jnp.float32)
    for group in range(depth // LANES):
        lanes = slice(group * LANES, (group + 1) * LANES)
        spread = jnp.concatenate([state_ref[group]] * (LANES // HEAD_DIM), axis=0)
        spread = jnp.where(mask, spread, 0.0).astype(jnp.bfloat16)
        read = jnp.dot(queries_ref[:, lanes], spread, preferred_element_type=jnp.float32)
        read_ref[:, lanes] = read
        square = square + read * read
    scale = lax.rsqrt(jnp.sum(square, axis=1, keepdims=True) / depth + 1e-06)
    mixture = read_ref[...] * scale * gain_ref[...] + local_ref[...]
    mixture = mixture.astype(jnp.bfloat16)
    width = 3 * LANES
    for at in range(0, depth, width):
        lanes = slice(at, at + width)
        product = jnp.dot(mixture, weight_ref[:, lanes], preferred_element_type=jnp.float32)
        result_ref[:, lanes] = product.astype(jnp.bfloat16)


def finish_call(queries, weight, state, local_term, gain):
    inputs = (queries, weight, state, local_term, gain)
    return kernel_call(
        finish_kernel,
        jax.ShapeDtypeStruct(queries.shape, jnp.bfloat16),
        inputs,
        [whole_vmem()] * len(inputs),
        [pltpu.VMEM(queries.shape, jnp.float32)],
        flops=2 * queries.size * queries.shape[1],
        bytes_accessed=2 * weight.size,
    )


def plane_form(video_tokens, qkv_weight, out_weight, conv_weight, norm_gain):
    frame_now = video_tokens[0]
    row_count, col_count, depth = frame_now.shape
    tokens = frame_now.reshape(row_count * col_count, depth)

    first_piece, second_piece = pieces_call(qkv_weight, out_weight)
    first_piece = first_piece[None]
    one = shifted(first_piece, 1)
    three = shifted(first_piece, -1)
    tokens = reorder_call(after(tokens, second_piece), qkv_weight.shape[0])
    other_tokens = flipped(tokens, (1, 1))
    one, three = after((one, three), tokens)

    pair = jnp.concatenate([one, three])
    two = shifted(one, 1)
    pair_first = flipped(pair, (2, 4))
    near = jnp.concatenate(after((pair, pair_first), other_tokens))
    away = flipped(near, (4, 2))
    two_near = jnp.concatenate([two, flipped(two, (2, 4))])
    two_away = flipped(two_near, (4, 2))

    second_ready = after(second_piece, one, three)
    second_one = shifted(second_ready, 1)
    second_three = shifted(second_ready, -1)
    second_two = shifted(after(second_one, two_near), 1)

    mine = first_call(after(tokens, second_one, second_three), other_tokens, qkv_weight, near, away, two_near, two_away)
    other = flipped(after(mine, second_two), (1, 1))
    straight = jnp.concatenate([second_one, second_two, second_three])
    swapped_straight = flipped(straight, (1, 1))
    values, top, bottom, upto, total = state_call(mine, other, tokens.shape[0], col_count)
    total = after(total, swapped_straight)

    second_own = jnp.stack([second_one[0], second_two[0], second_three[0]])
    second_first = flipped(second_own, (2, 4))
    second_second = flipped(second_own, (4, 2))

    for bit, guard in ((2, 2), (4, 4), (6, 4)):
        pairs = [(t, t ^ bit) for t in range(8) if not t & guard]
        upto = upto + lax.ppermute(total, "tm", pairs).astype(jnp.float32)
    count = lax.axis_size("space")
    forward = [(i, i + 1) for i in range(count - 1)]
    backward = [(target, source) for source, target in forward]
    above = lax.ppermute(after(bottom, upto), "space", forward)
    share = after(upto, second_first, second_second).astype(jnp.bfloat16)
    arrived = lax.ppermute(share, "space", [(i, i ^ 1) for i in range(count)])
    share = (share.astype(jnp.float32) + arrived.astype(jnp.float32)).astype(jnp.bfloat16)
    share = after(share, above)
    arrived = lax.ppermute(share, "space", [(i, i ^ 2) for i in range(count)])
    below = lax.ppermute(after(top, share), "space", backward)

    turned = jnp.concatenate([second_first, second_second])
    swapped_turned = flipped(after(turned, share), (1, 1))
    queries, weight = query_call(
        tokens,
        qkv_weight,
        out_weight,
        straight,
        swapped_straight,
        turned,
        swapped_turned,
        mine,
        other,
    )
    grid = values.reshape(row_count, col_count, depth)
    local_term = local_call(grid, above, after(below, queries), conv_weight).reshape(-1, depth)
    arrived = after(arrived, local_term)
    state = share.astype(jnp.float32) + arrived.astype(jnp.float32)
    result = finish_call(queries, weight, state, local_term, norm_gain[None])
    return result.reshape(1, row_count, col_count, depth)


def solution(mesh):
    def per_device(video_tokens, qkv_weight, out_weight, conv_weight, norm_gain):
        fits = mesh.shape["tm"] == 8 and mesh.shape["space"] == 4
        fits = fits and qkv_weight.shape[0] == 4 * MAIN + 2 * REST
        form = plane_form if fits else general_form
        return form(video_tokens, qkv_weight, out_weight, conv_weight, norm_gain)

    in_specs = (P("tm", "space", None, None), P("space", None), P("space", None), P(), P())
    out_specs = P("tm", "space", None, None)
    return jax.shard_map(
        per_device, mesh=mesh, in_specs=in_specs, out_specs=out_specs, check_vma=False
    )
```

```python
import functools

import jax
import jax.numpy as jnp
from jax import lax
from jax.experimental import pallas as pl
from jax.experimental.pallas import tpu as pltpu
from jax.sharding import PartitionSpec as P

HEADS = 36
HEAD_DIM = 32
LANES = 128
MAIN = 64
REST = 16
STEPS = (1, 2, 3)
FRAME_ROWS = 4
VMEM_LIMIT = 24 * 1024 * 1024
WHOLE_VMEM = 63 * 1024 * 1024


def entering(value, axis, combine, identity):
    devices, place = (lax.axis_size(axis), lax.axis_index(axis))
    everything = lax.all_gather(value.astype(jnp.bfloat16), axis)
    start = jnp.broadcast_to(jnp.asarray(identity, value.dtype), value.shape)

    def lap(k, before):
        reached = k < place
        new = combine(before, everything[k].astype(value.dtype))
        return jnp.where(reached, new, before)

    return lax.fori_loop(0, devices, lap, start)


def with_halo(block, sides, width):
    for axis, dim in sides:
        count = lax.axis_size(axis)
        forward = [(i, i + 1) for i in range(count - 1)]
        backward = [(target, source) for source, target in forward]
        low = lax.ppermute(
            lax.slice_in_dim(block, block.shape[dim] - width, None, axis=dim), axis, forward
        )
        high = lax.ppermute(lax.slice_in_dim(block, 0, width, axis=dim), axis, backward)
        block = jnp.concatenate([low, block, high], axis=dim)
    return block


def fold_product(left_side, block_rows):
    return jnp.dot(left_side, block_rows, preferred_element_type=jnp.float32)


def add_states(earlier, later):
    return earlier + later


def causal_states(key_feat, values):
    key_heads = key_feat.reshape(-1, HEADS, HEAD_DIM)
    value_heads = values.reshape(-1, HEADS, HEAD_DIM)
    frame_state = jnp.einsum(
        "thd,the->hde", key_heads, value_heads, preferred_element_type=jnp.float32
    )
    flat_state = frame_state.reshape(-1)
    frame_sum = lax.psum(flat_state.astype(jnp.bfloat16), "space").astype(jnp.float32)
    earlier = entering(frame_sum, "tm", add_states, jnp.zeros_like(frame_sum))
    whole_state = earlier + frame_sum
    return whole_state.reshape(HEADS, HEAD_DIM, HEAD_DIM)


def general_form(video_tokens, qkv_weight, out_weight, conv_weight, norm_gain):
    frame_now = video_tokens[0]
    row_count, col_count, feat_width = frame_now.shape
    tokens = frame_now.reshape(row_count * col_count, feat_width)
    projected = fold_product(tokens, lax.all_gather(qkv_weight, "space", axis=0, tiled=True))
    query_feat = jax.nn.relu(projected[:, :feat_width]).astype(jnp.bfloat16)
    key_feat = jax.nn.relu(projected[:, feat_width : 2 * feat_width]).astype(jnp.bfloat16)
    values = projected[:, 2 * feat_width :].astype(jnp.bfloat16)
    state_all = causal_states(key_feat, values)
    padded_rows = with_halo(values.reshape(row_count, col_count, feat_width), (("space", 0),), 1)
    padded = jnp.pad(padded_rows, ((0, 0), (1, 1), (0, 0))).astype(jnp.float32)
    local_term = jnp.zeros((row_count, col_count, feat_width), jnp.float32)
    for row_shift in range(3):
        for col_shift in range(3):
            local_term = (
                local_term
                + conv_weight[row_shift, col_shift]
                * padded[row_shift : row_shift + row_count, col_shift : col_shift + col_count]
            )
    state_low = state_all.astype(jnp.bfloat16)
    query_heads = query_feat.reshape(-1, HEADS, HEAD_DIM)
    readout = jnp.einsum("thd,hde->the", query_heads, state_low, preferred_element_type=jnp.float32)
    readout = readout.reshape(-1, feat_width)
    mean_square = jnp.mean(readout * readout, axis=-1, keepdims=True)
    normed = readout * lax.rsqrt(mean_square + 1e-06) * norm_gain
    mixture = (normed + local_term.reshape(-1, feat_width)).astype(jnp.bfloat16)
    result = fold_product(mixture, lax.all_gather(out_weight, "space", axis=0, tiled=True))
    return result.astype(jnp.bfloat16).reshape(1, row_count, col_count, feat_width)


def coordinates():
    place = lax.axis_index("tm")
    return lax.rem(place // 4, 2), lax.rem(place // 2, 2), lax.rem(place, 2)


def shifted(value, step):
    count = lax.axis_size("space")
    return lax.ppermute(value, "space", [(i, (i + step) % count) for i in range(count)])


def flipped(value, bit_on_core):
    return lax.ppermute(value, "tm", [(t, t ^ bit_on_core[t % 2]) for t in range(8)])


def after(value, *earlier):
    return lax.optimization_barrier((value,) + earlier)[0]


def chip_places(y, x):
    return (2 * y + x, 2 * y + (1 - x), 2 * (1 - y) + x, 2 * (1 - y) + (1 - x))


def source_plane(step):
    count = lax.axis_size("space")
    return lax.rem(lax.axis_index("space") - step + count, count)


def steps_through(within, size):
    run = sum(jnp.where(within >= size * k, 1, 0) for k in range(1, len(STEPS)))
    return run, within - size * run


def landed_order(at, width, rows):
    y, x, _ = coordinates()
    planes = [source_plane(step) for step in STEPS]
    row = at + lax.broadcasted_iota(jnp.int32, (1, width), 1)

    def pick(choices, index):
        chosen = choices[-1]
        for k in range(len(choices) - 2, -1, -1):
            chosen = jnp.where(index == k, choices[k], chosen)
        return chosen

    def landed(within, size, starts):
        count = len(STEPS) * size
        slot = sum(jnp.where(within >= count * k, 1, 0) for k in range(1, len(starts)))
        run, left = steps_through(within - count * slot, size)
        return pick(planes, run) * rows + pick(starts, slot) + left

    main = landed(row - rows, MAIN, [place * MAIN for place in chip_places(y, x)])
    rest_at = rows + 4 * len(STEPS) * MAIN
    rest = landed(row - rest_at, REST, [4 * MAIN + tile * REST for tile in (y, 1 - y)])
    own = lax.axis_index("space") * rows + row
    return jnp.where(row < rows, own, jnp.where(row < rest_at, main, rest))


def whole_vmem():
    return pl.BlockSpec(memory_space=pltpu.VMEM)


def anywhere():
    return pl.BlockSpec(memory_space=pltpu.HBM)


def kernel_call(
    body, outputs, inputs, in_specs, scratch=(), flops=0, bytes_accessed=0, limit=VMEM_LIMIT
):
    return pl.pallas_call(
        body,
        out_shape=outputs,
        in_specs=in_specs,
        out_specs=jax.tree.map(lambda _: whole_vmem(), outputs),
        scratch_shapes=list(scratch),
        compiler_params=pltpu.CompilerParams(vmem_limit_bytes=limit),
        cost_estimate=pl.CostEstimate(
            flops=flops, bytes_accessed=bytes_accessed, transcendentals=0
        ),
    )(*inputs)


def pieces_kernel(qkv_ref, out_ref, first_ref, second_ref, sems):
    y, x, core = coordinates()
    depth = out_ref.shape[1]
    main = pl.ds(pl.multiple_of((2 * y + x) * MAIN, REST), MAIN)
    rest = pl.ds(pl.multiple_of(4 * MAIN + y * REST, REST), REST)
    first_columns = pl.ds(pl.multiple_of(depth * (1 + core), LANES), depth)
    rest_columns = pl.ds(pl.multiple_of(jnp.where(x == 0, depth * (1 + core), 0), LANES), depth)

    def copy(source, target, k):
        return pltpu.make_async_copy(source, target, sems.at[k])

    first_main = copy(qkv_ref.at[main, first_columns], first_ref.at[pl.ds(0, MAIN), :], 0)
    first_main.start()
    rest_target = first_ref.at[pl.ds(MAIN, REST), :]
    from_out = (core == 1) & (x == 1)

    @pl.when(from_out)
    def _():
        copy(out_ref.at[rest, :], rest_target, 1).start()

    @pl.when(jnp.logical_not(from_out))
    def _():
        copy(qkv_ref.at[rest, rest_columns], rest_target, 1).start()

    places = chip_places(y, x)
    for k, place in enumerate((places[0], places[3])):
        rows = pl.ds(pl.multiple_of(place * MAIN, REST), MAIN)

        @pl.when(core == 0)
        def _():
            copy(qkv_ref.at[rows, pl.ds(0, depth)], second_ref.at[k], 2 + k).start()

        @pl.when(core == 1)
        def _():
            copy(out_ref.at[rows, :], second_ref.at[k], 2 + k).start()

    first_main.wait()
    copy(out_ref.at[rest, :], rest_target, 1).wait()
    for k in range(2):
        copy(out_ref.at[main, :], second_ref.at[k], 2 + k).wait()


def pieces_call(qkv_weight, out_weight):
    depth = out_weight.shape[1]
    outputs = [
        jax.ShapeDtypeStruct((MAIN + REST, depth), jnp.bfloat16),
        jax.ShapeDtypeStruct((2, MAIN, depth), jnp.bfloat16),
    ]
    return kernel_call(
        pieces_kernel,
        outputs,
        (qkv_weight, out_weight),
        [anywhere(), anywhere()],
        [pltpu.SemaphoreType.DMA((4,))],
        bytes_accessed=4 * (3 * MAIN + REST) * depth,
        limit=WHOLE_VMEM,
    )


def reorder_kernel(rows, tokens_ref, moved_ref):
    depth = tokens_ref.shape[1]
    width = 3 * LANES
    row = lax.broadcasted_iota(jnp.int32, (depth, width), 0)
    for at in range(0, depth, width):
        order = landed_order(at, width, rows)
        chosen = jnp.where(row == order, 1.0, 0.0).astype(jnp.bfloat16)
        moved = jnp.dot(tokens_ref[...], chosen, preferred_element_type=jnp.float32)
        moved_ref[:, at : at + width] = moved.astype(jnp.bfloat16)


def reorder_call(tokens, rows):
    depth = tokens.shape[1]
    return kernel_call(
        functools.partial(reorder_kernel, rows),
        jax.ShapeDtypeStruct(tokens.shape, jnp.bfloat16),
        (tokens,),
        [whole_vmem()],
        flops=2 * tokens.size * depth,
        bytes_accessed=2 * tokens.size,
    )


def first_kernel(*refs):
    tokens_ref, other_ref, qkv_ref, near_ref, away_ref, first_ref, far_ref, *results = refs
    slots = (
        ((near_ref, 0), (first_ref, 0), (near_ref, 1)),
        ((near_ref, 2), (first_ref, 1), (near_ref, 3)),
        ((away_ref, 0), (far_ref, 0), (away_ref, 1)),
        ((away_ref, 2), (far_ref, 1), (away_ref, 3)),
    )
    _, x, core = coordinates()
    depth = tokens_ref.shape[1]
    floor = jnp.where(core == 0, 0.0, -jnp.inf).astype(jnp.float32)
    width = 3 * LANES

    for at in range(0, depth, width):
        lanes = slice(at, at + width)

        def slot(k, low, high):
            return jnp.concatenate([ref[at, low:high, lanes] for ref, at in slots[k]], axis=0)

        def by_place(low, high):
            own, first, second, far = [slot(k, low, high) for k in range(4)]
            along_x = jnp.where(core == 0, first, second)
            along_y = jnp.where(core == 0, second, first)
            return own, along_x, along_y, far

        keys, values = [qkv_ref[:, depth * k + at : depth * k + at + width] for k in (1, 2)]
        own = jnp.where(core == 0, keys, values)
        rest = by_place(MAIN, MAIN + REST)
        even = jnp.concatenate([rest[0], rest[2]], axis=0)
        odd = jnp.concatenate([rest[1], rest[3]], axis=0)
        for ref in results:
            ref[-even.shape[0] :, lanes] = jnp.where(x == 1, even, odd)
        columns = jnp.concatenate(
            (own,) + by_place(0, MAIN) + (jnp.where(x == 0, even, odd),), axis=0
        )
        for k, ref in enumerate((tokens_ref, other_ref)):
            product = jnp.dot(ref[...], columns, preferred_element_type=jnp.float32)
            product = jnp.maximum(product, floor).astype(jnp.bfloat16)
            count = FRAME_ROWS * product.shape[0] // (FRAME_ROWS + 2)
            for result in results:
                result[k * count : (k + 1) * count, lanes] = product[:count]
            results[k][2 * count : count + product.shape[0], lanes] = product[count:]


def first_call(tokens, other, qkv_weight, *landed):
    count, depth = tokens.shape
    rows = 2 * (FRAME_ROWS + 1) * count // (FRAME_ROWS + 2) + 2 * len(STEPS) * REST
    inputs = (tokens, other, qkv_weight) + landed
    return kernel_call(
        first_kernel,
        [jax.ShapeDtypeStruct((rows, depth), jnp.bfloat16)] * 2,
        inputs,
        [whole_vmem()] * len(inputs),
        flops=4 * tokens.size * depth,
        bytes_accessed=2 * depth * depth,
    )


def diagonal_mask():
    rows = lax.broadcasted_iota(jnp.int32, (LANES, LANES), 0) // HEAD_DIM
    columns = lax.broadcasted_iota(jnp.int32, (LANES, LANES), 1) // HEAD_DIM
    return rows == columns


def state_kernel(mine_ref, other_ref, values_ref, upto_ref, total_ref):
    _, _, core = coordinates()
    mask = diagonal_mask()
    count = values_ref.shape[0]
    later = jnp.where(core == 1, 1.0, 0.0).astype(jnp.float32)
    for group in range(mine_ref.shape[1] // LANES):
        at = slice(group * LANES, (group + 1) * LANES)

        def state(mine, other):
            keys = jnp.where(core == 0, mine, other)
            values = jnp.where(core == 0, other, mine)
            full = lax.dot_general(
                keys, values, (((0,), (0,)), ((), ())), preferred_element_type=jnp.float32
            )
            full = jnp.where(mask, full, 0.0)
            total = full[0:HEAD_DIM]
            for k in range(1, LANES // HEAD_DIM):
                total = total + full[k * HEAD_DIM : (k + 1) * HEAD_DIM]
            return total, values

        low, high = slice(0, count), slice(count, 2 * count)
        here, values = state(mine_ref[low, at], other_ref[high, at])
        there, _ = state(mine_ref[high, at], other_ref[low, at])
        values_ref[:, at] = values
        upto_ref[group] = here + later * there
        total_ref[group] = (here + there).astype(jnp.bfloat16)


def state_call(mine, other, count):
    depth = mine.shape[1]
    compact = (depth // LANES, HEAD_DIM, LANES)
    return kernel_call(
        state_kernel,
        [
            jax.ShapeDtypeStruct((count, depth), jnp.bfloat16),
            jax.ShapeDtypeStruct(compact, jnp.float32),
            jax.ShapeDtypeStruct(compact, jnp.bfloat16),
        ],
        (mine, other),
        [whole_vmem()] * 2,
        flops=4 * count * depth * LANES,
        bytes_accessed=8 * count * depth,
    )


def local_kernel(values_ref, mine_ref, other_ref, conv_ref, local_ref):
    rows, columns, depth = values_ref.shape
    _, _, core = coordinates()
    at_halo = 2 * rows * columns
    for at in range(0, depth, LANES):
        lanes = slice(at, at + LANES)
        taps = conv_ref[:, :, lanes]
        halos = [ref[at_halo : at_halo + 2 * columns, lanes] for ref in (mine_ref, other_ref)]
        halo = jnp.where(core == 1, *halos).reshape(2, columns, LANES)
        sheet = jnp.concatenate([halo[:1], values_ref[:, :, lanes], halo[1:]], axis=0)
        sheet = sheet.astype(jnp.float32)
        edge = jnp.zeros((rows + 2, 1, LANES), jnp.float32)
        before = jnp.concatenate([edge, sheet[:, :-1]], axis=1)
        behind = jnp.concatenate([sheet[:, 1:], edge], axis=1)
        total = jnp.zeros((rows, columns, LANES), jnp.float32)
        for col_shift, moved in enumerate((before, sheet, behind)):
            for row_shift in range(3):
                total = total + taps[row_shift, col_shift] * moved[row_shift : row_shift + rows]
        local_ref[:, :, lanes] = total


def local_call(values, mine, other, conv_weight):
    return kernel_call(
        local_kernel,
        jax.ShapeDtypeStruct(values.shape, jnp.float32),
        (values, mine, other, conv_weight),
        [whole_vmem()] * 4,
        flops=18 * values.size,
        bytes_accessed=6 * values.size,
    )


def query_kernel(*refs):
    tokens_ref, qkv_ref, out_ref, *packs, ours_ref, other_ref, query_ref, weight_ref = refs
    y, x, core = coordinates()
    depth = tokens_ref.shape[1]
    rows = qkv_ref.shape[0]
    steps = len(STEPS)
    rest_at = ours_ref.shape[0] - 2 * steps * REST
    places = chip_places(y, x)
    width = 3 * LANES

    def block(of_core, index, lanes):
        pack, k = index
        mine_ref, theirs_ref = packs[2 * pack], packs[2 * pack + 1]
        return jnp.where(core == of_core, mine_ref[k, :, lanes], theirs_ref[k, :, lanes])


    def rest(of_core, lanes):
        return jnp.where(core == of_core, ours_ref[rest_at:, lanes], other_ref[rest_at:, lanes])

    def put(row, value, lanes):
        weight_ref[pl.ds(pl.multiple_of(row, REST), value.shape[0]), lanes] = value

    for at in range(0, depth, width):
        lanes = slice(at, at + width)
        order = [(0, 2 * k) for k in range(steps)] + [(1, k) for k in range(2 * steps)]
        order += [(0, 2 * k + 1) for k in range(steps)]
        columns = [qkv_ref[:, lanes]] + [block(0, k, lanes) for k in order] + [rest(0, lanes)]
        queries = jnp.dot(
            tokens_ref[: query_ref.shape[0]],
            jnp.concatenate(columns, axis=0),
            preferred_element_type=jnp.float32,
        )
        query_ref[:, lanes] = jnp.maximum(queries, 0.0).astype(jnp.bfloat16)

        put(lax.axis_index("space") * rows, out_ref[:, lanes], lanes)
        tiles = rest(1, lanes)
        for k, step in enumerate(STEPS):
            base = source_plane(step) * rows
            held = ((0, 2 * k), (1, steps + k), (1, k), (0, 2 * k + 1))
            for place, index in zip(places, held):
                put(base + place * MAIN, block(1, index, lanes), lanes)
            for run, tile in enumerate((y, 1 - y)):
                start = (run * steps + k) * REST
                put(base + 4 * MAIN + tile * REST, tiles[start : start + REST], lanes)


def query_call(count, tokens, qkv_weight, out_weight, *landed):
    depth = tokens.shape[1]
    inputs = (tokens, qkv_weight, out_weight) + landed
    return kernel_call(
        query_kernel,
        [
            jax.ShapeDtypeStruct((count, depth), jnp.bfloat16),
            jax.ShapeDtypeStruct((depth, depth), jnp.bfloat16),
        ],
        inputs,
        [whole_vmem()] * len(inputs),
        flops=2 * tokens.size * depth,
        bytes_accessed=4 * depth * depth,
    )


def finish_kernel(queries_ref, weight_ref, state_ref, local_ref, gain_ref, result_ref, read_ref):
    count, depth = queries_ref.shape
    mask = diagonal_mask()
    square = jnp.zeros((count, LANES), jnp.float32)
    for group in range(depth // LANES):
        lanes = slice(group * LANES, (group + 1) * LANES)
        spread = jnp.concatenate([state_ref[group]] * (LANES // HEAD_DIM), axis=0)
        spread = jnp.where(mask, spread, 0.0).astype(jnp.bfloat16)
        read = jnp.dot(queries_ref[:, lanes], spread, preferred_element_type=jnp.float32)
        read_ref[:, lanes] = read
        square = square + read * read
    scale = lax.rsqrt(jnp.sum(square, axis=1, keepdims=True) / depth + 1e-06)
    mixture = read_ref[...] * scale * gain_ref[...] + local_ref[...]
    mixture = mixture.astype(jnp.bfloat16)
    width = 3 * LANES
    for at in range(0, depth, width):
        lanes = slice(at, at + width)
        product = jnp.dot(mixture, weight_ref[:, lanes], preferred_element_type=jnp.float32)
        result_ref[:, lanes] = product.astype(jnp.bfloat16)


def finish_call(queries, weight, state, local_term, gain):
    inputs = (queries, weight, state, local_term, gain)
    return kernel_call(
        finish_kernel,
        jax.ShapeDtypeStruct(queries.shape, jnp.bfloat16),
        inputs,
        [whole_vmem()] * len(inputs),
        [pltpu.VMEM(queries.shape, jnp.float32)],
        flops=2 * queries.size * queries.shape[1],
        bytes_accessed=2 * weight.size,
    )


def plane_form(video_tokens, qkv_weight, out_weight, conv_weight, norm_gain):
    frame_now = video_tokens[0]
    row_count, col_count, depth = frame_now.shape
    tokens = frame_now.reshape(row_count * col_count, depth)

    first_piece, second_piece = pieces_call(qkv_weight, out_weight)
    first_piece = first_piece[None]
    planes = lax.axis_size("space")
    forward = [(i, i + 1) for i in range(planes - 1)]
    backward = [(target, source) for source, target in forward]
    above = lax.ppermute(tokens[-col_count:], "space", forward)
    below = lax.ppermute(tokens[:col_count], "space", backward)
    one = shifted(first_piece, 1)
    three = shifted(first_piece, -1)
    landed = jnp.concatenate([tokens, above, below])
    landed = reorder_call(after(landed, second_piece), qkv_weight.shape[0])
    other_landed = flipped(landed, (1, 1))
    one, three = after((one, three), landed)

    pair = jnp.concatenate([one, three])
    two = shifted(one, 1)
    pair_first = flipped(pair, (2, 4))
    near = jnp.concatenate(after((pair, pair_first), other_landed))
    away = flipped(near, (4, 2))
    two_near = jnp.concatenate([two, flipped(two, (2, 4))])
    two_away = flipped(two_near, (4, 2))

    second_ready = after(second_piece, one, three)
    second_one = shifted(second_ready, 1)
    second_three = shifted(second_ready, -1)
    second_two = shifted(after(second_one, two_near), 1)

    mine, sent = first_call(
        after(landed, second_one, second_three),
        other_landed,
        qkv_weight,
        near,
        away,
        two_near,
        two_away,
    )
    other = flipped(after(sent, second_two), (1, 1))
    straight = jnp.concatenate([second_one, second_two, second_three])
    swapped_straight = flipped(straight, (1, 1))
    values, upto, total = state_call(mine, other, tokens.shape[0])
    total = after(total, swapped_straight)
    grid = values.reshape(row_count, col_count, depth)
    local_term = local_call(grid, mine, other, conv_weight).reshape(-1, depth)

    second_own = jnp.stack([second_one[0], second_two[0], second_three[0]])
    second_first = flipped(second_own, (2, 4))
    second_second = flipped(second_own, (4, 2))

    for bit, guard in ((2, 2), (4, 4), (6, 4)):
        pairs = [(t, t ^ bit) for t in range(8) if not t & guard]
        upto = upto + lax.ppermute(total, "tm", pairs).astype(jnp.float32)
    turned = jnp.concatenate(after((second_first, second_second), upto))
    swapped_turned = flipped(after(turned, upto), (1, 1))
    queries, weight = query_call(
        tokens.shape[0],
        landed,
        qkv_weight,
        out_weight,
        straight,
        swapped_straight,
        turned,
        swapped_turned,
        mine,
        other,
    )
    share = after(upto, turned).astype(jnp.bfloat16)
    arrived = lax.ppermute(share, "space", [(i, i ^ 1) for i in range(planes)])
    share = (share.astype(jnp.float32) + arrived.astype(jnp.float32)).astype(jnp.bfloat16)
    arrived = lax.ppermute(share, "space", [(i, i ^ 2) for i in range(planes)])
    arrived = after(arrived, queries, weight, local_term)
    state = share.astype(jnp.float32) + arrived.astype(jnp.float32)
    result = finish_call(queries, weight, state, local_term, norm_gain[None])
    return result.reshape(1, row_count, col_count, depth)


def solution(mesh):
    def per_device(video_tokens, qkv_weight, out_weight, conv_weight, norm_gain):
        fits = mesh.shape["tm"] == 8 and mesh.shape["space"] == 4
        fits = fits and qkv_weight.shape[0] == 4 * MAIN + 2 * REST
        form = plane_form if fits else general_form
        return form(video_tokens, qkv_weight, out_weight, conv_weight, norm_gain)

    in_specs = (P("tm", "space", None, None), P("space", None), P("space", None), P(), P())
    out_specs = P("tm", "space", None, None)
    return jax.shard_map(
        per_device, mesh=mesh, in_specs=in_specs, out_specs=out_specs, check_vma=False
    )
```

```python
import functools

import jax
import jax.numpy as jnp
from jax import lax
from jax.experimental import pallas as pl
from jax.experimental.pallas import tpu as pltpu
from jax.sharding import PartitionSpec as P

HEADS = 36
HEAD_DIM = 32
LANES = 128
MAIN = 64
REST = 16
STEPS = (1, 2, 3)
VMEM_LIMIT = 24 * 1024 * 1024
WHOLE_VMEM = 63 * 1024 * 1024


def entering(value, axis, combine, identity):
    devices, place = (lax.axis_size(axis), lax.axis_index(axis))
    everything = lax.all_gather(value.astype(jnp.bfloat16), axis)
    start = jnp.broadcast_to(jnp.asarray(identity, value.dtype), value.shape)

    def lap(k, before):
        reached = k < place
        new = combine(before, everything[k].astype(value.dtype))
        return jnp.where(reached, new, before)

    return lax.fori_loop(0, devices, lap, start)


def with_halo(block, sides, width):
    for axis, dim in sides:
        count = lax.axis_size(axis)
        forward = [(i, i + 1) for i in range(count - 1)]
        backward = [(target, source) for source, target in forward]
        low = lax.ppermute(
            lax.slice_in_dim(block, block.shape[dim] - width, None, axis=dim), axis, forward
        )
        high = lax.ppermute(lax.slice_in_dim(block, 0, width, axis=dim), axis, backward)
        block = jnp.concatenate([low, block, high], axis=dim)
    return block


def fold_product(left_side, block_rows):
    return jnp.dot(left_side, block_rows, preferred_element_type=jnp.float32)


def add_states(earlier, later):
    return earlier + later


def causal_states(key_feat, values):
    key_heads = key_feat.reshape(-1, HEADS, HEAD_DIM)
    value_heads = values.reshape(-1, HEADS, HEAD_DIM)
    frame_state = jnp.einsum(
        "thd,the->hde", key_heads, value_heads, preferred_element_type=jnp.float32
    )
    flat_state = frame_state.reshape(-1)
    frame_sum = lax.psum(flat_state.astype(jnp.bfloat16), "space").astype(jnp.float32)
    earlier = entering(frame_sum, "tm", add_states, jnp.zeros_like(frame_sum))
    whole_state = earlier + frame_sum
    return whole_state.reshape(HEADS, HEAD_DIM, HEAD_DIM)


def general_form(video_tokens, qkv_weight, out_weight, conv_weight, norm_gain):
    frame_now = video_tokens[0]
    row_count, col_count, feat_width = frame_now.shape
    tokens = frame_now.reshape(row_count * col_count, feat_width)
    projected = fold_product(tokens, lax.all_gather(qkv_weight, "space", axis=0, tiled=True))
    query_feat = jax.nn.relu(projected[:, :feat_width]).astype(jnp.bfloat16)
    key_feat = jax.nn.relu(projected[:, feat_width : 2 * feat_width]).astype(jnp.bfloat16)
    values = projected[:, 2 * feat_width :].astype(jnp.bfloat16)
    state_all = causal_states(key_feat, values)
    padded_rows = with_halo(values.reshape(row_count, col_count, feat_width), (("space", 0),), 1)
    padded = jnp.pad(padded_rows, ((0, 0), (1, 1), (0, 0))).astype(jnp.float32)
    local_term = jnp.zeros((row_count, col_count, feat_width), jnp.float32)
    for row_shift in range(3):
        for col_shift in range(3):
            local_term = (
                local_term
                + conv_weight[row_shift, col_shift]
                * padded[row_shift : row_shift + row_count, col_shift : col_shift + col_count]
            )
    state_low = state_all.astype(jnp.bfloat16)
    query_heads = query_feat.reshape(-1, HEADS, HEAD_DIM)
    readout = jnp.einsum("thd,hde->the", query_heads, state_low, preferred_element_type=jnp.float32)
    readout = readout.reshape(-1, feat_width)
    mean_square = jnp.mean(readout * readout, axis=-1, keepdims=True)
    normed = readout * lax.rsqrt(mean_square + 1e-06) * norm_gain
    mixture = (normed + local_term.reshape(-1, feat_width)).astype(jnp.bfloat16)
    result = fold_product(mixture, lax.all_gather(out_weight, "space", axis=0, tiled=True))
    return result.astype(jnp.bfloat16).reshape(1, row_count, col_count, feat_width)


def coordinates():
    place = lax.axis_index("tm")
    return lax.rem(place // 4, 2), lax.rem(place // 2, 2), lax.rem(place, 2)


def shifted(value, step):
    count = lax.axis_size("space")
    return lax.ppermute(value, "space", [(i, (i + step) % count) for i in range(count)])


def flipped(value, bit_on_core):
    return lax.ppermute(value, "tm", [(t, t ^ bit_on_core[t % 2]) for t in range(8)])


def after(value, *earlier):
    return lax.optimization_barrier((value,) + earlier)[0]


def chip_places(y, x):
    return (2 * y + x, 2 * y + (1 - x), 2 * (1 - y) + x, 2 * (1 - y) + (1 - x))


def source_plane(step):
    count = lax.axis_size("space")
    return lax.rem(lax.axis_index("space") - step + count, count)


def steps_through(within, size):
    run = sum(jnp.where(within >= size * k, 1, 0) for k in range(1, len(STEPS)))
    return run, within - size * run


def landed_order(at, width, rows):
    y, x, _ = coordinates()
    planes = [source_plane(step) for step in STEPS]
    row = at + lax.broadcasted_iota(jnp.int32, (1, width), 1)

    def pick(choices, index):
        chosen = choices[-1]
        for k in range(len(choices) - 2, -1, -1):
            chosen = jnp.where(index == k, choices[k], chosen)
        return chosen

    def landed(within, size, starts):
        count = len(STEPS) * size
        slot = sum(jnp.where(within >= count * k, 1, 0) for k in range(1, len(starts)))
        run, left = steps_through(within - count * slot, size)
        return pick(planes, run) * rows + pick(starts, slot) + left

    main = landed(row - rows, MAIN, [place * MAIN for place in chip_places(y, x)])
    rest_at = rows + 4 * len(STEPS) * MAIN
    rest = landed(row - rest_at, REST, [4 * MAIN + tile * REST for tile in (y, 1 - y)])
    own = lax.axis_index("space") * rows + row
    return jnp.where(row < rows, own, jnp.where(row < rest_at, main, rest))


def whole_vmem():
    return pl.BlockSpec(memory_space=pltpu.VMEM)


def anywhere():
    return pl.BlockSpec(memory_space=pltpu.HBM)


def kernel_call(
    body, outputs, inputs, in_specs, scratch=(), flops=0, bytes_accessed=0, limit=VMEM_LIMIT
):
    return pl.pallas_call(
        body,
        out_shape=outputs,
        in_specs=in_specs,
        out_specs=jax.tree.map(lambda _: whole_vmem(), outputs),
        scratch_shapes=list(scratch),
        compiler_params=pltpu.CompilerParams(vmem_limit_bytes=limit),
        cost_estimate=pl.CostEstimate(
            flops=flops, bytes_accessed=bytes_accessed, transcendentals=0
        ),
    )(*inputs)


def pieces_kernel(qkv_ref, out_ref, first_ref, second_ref, sems):
    y, x, core = coordinates()
    depth = out_ref.shape[1]
    main = pl.ds(pl.multiple_of((2 * y + x) * MAIN, REST), MAIN)
    rest = pl.ds(pl.multiple_of(4 * MAIN + y * REST, REST), REST)
    first_columns = pl.ds(pl.multiple_of(depth * (1 + core), LANES), depth)
    rest_columns = pl.ds(pl.multiple_of(jnp.where(x == 0, depth * (1 + core), 0), LANES), depth)

    def copy(source, target, k):
        return pltpu.make_async_copy(source, target, sems.at[k])

    first_main = copy(qkv_ref.at[main, first_columns], first_ref.at[pl.ds(0, MAIN), :], 0)
    first_main.start()
    rest_target = first_ref.at[pl.ds(MAIN, REST), :]
    from_out = (core == 1) & (x == 1)

    @pl.when(from_out)
    def _():
        copy(out_ref.at[rest, :], rest_target, 1).start()

    @pl.when(jnp.logical_not(from_out))
    def _():
        copy(qkv_ref.at[rest, rest_columns], rest_target, 1).start()

    places = chip_places(y, x)
    for k, place in enumerate((places[0], places[3])):
        rows = pl.ds(pl.multiple_of(place * MAIN, REST), MAIN)

        @pl.when(core == 0)
        def _():
            copy(qkv_ref.at[rows, pl.ds(0, depth)], second_ref.at[k], 2 + k).start()

        @pl.when(core == 1)
        def _():
            copy(out_ref.at[rows, :], second_ref.at[k], 2 + k).start()

    first_main.wait()
    copy(out_ref.at[rest, :], rest_target, 1).wait()
    for k in range(2):
        copy(out_ref.at[main, :], second_ref.at[k], 2 + k).wait()


def pieces_call(qkv_weight, out_weight):
    depth = out_weight.shape[1]
    outputs = [
        jax.ShapeDtypeStruct((MAIN + REST, depth), jnp.bfloat16),
        jax.ShapeDtypeStruct((2, MAIN, depth), jnp.bfloat16),
    ]
    return kernel_call(
        pieces_kernel,
        outputs,
        (qkv_weight, out_weight),
        [anywhere(), anywhere()],
        [pltpu.SemaphoreType.DMA((4,))],
        bytes_accessed=4 * (3 * MAIN + REST) * depth,
        limit=WHOLE_VMEM,
    )


def reorder_kernel(rows, tokens_ref, moved_ref):
    depth = tokens_ref.shape[1]
    width = 3 * LANES
    row = lax.broadcasted_iota(jnp.int32, (depth, width), 0)
    for at in range(0, depth, width):
        order = landed_order(at, width, rows)
        chosen = jnp.where(row == order, 1.0, 0.0).astype(jnp.bfloat16)
        moved = jnp.dot(tokens_ref[...], chosen, preferred_element_type=jnp.float32)
        moved_ref[:, at : at + width] = moved.astype(jnp.bfloat16)


def reorder_call(tokens, rows):
    depth = tokens.shape[1]
    return kernel_call(
        functools.partial(reorder_kernel, rows),
        jax.ShapeDtypeStruct(tokens.shape, jnp.bfloat16),
        (tokens,),
        [whole_vmem()],
        flops=2 * tokens.size * depth,
        bytes_accessed=2 * tokens.size,
    )


def first_kernel(*refs):
    tokens_ref, other_ref, qkv_ref, near_ref, away_ref, first_ref, far_ref, mine_ref = refs
    slots = (
        ((near_ref, 0), (first_ref, 0), (near_ref, 1)),
        ((near_ref, 2), (first_ref, 1), (near_ref, 3)),
        ((away_ref, 0), (far_ref, 0), (away_ref, 1)),
        ((away_ref, 2), (far_ref, 1), (away_ref, 3)),
    )
    _, x, core = coordinates()
    count, depth = tokens_ref.shape
    floor = jnp.where(core == 0, 0.0, -jnp.inf).astype(jnp.float32)
    width = 3 * LANES

    for at in range(0, depth, width):
        lanes = slice(at, at + width)

        def slot(k, low, high):
            return jnp.concatenate([ref[at, low:high, lanes] for ref, at in slots[k]], axis=0)

        def by_place(low, high):
            own, first, second, far = [slot(k, low, high) for k in range(4)]
            along_x = jnp.where(core == 0, first, second)
            along_y = jnp.where(core == 0, second, first)
            return own, along_x, along_y, far

        keys, values = [qkv_ref[:, depth * k + at : depth * k + at + width] for k in (1, 2)]
        own = jnp.where(core == 0, keys, values)
        rest = by_place(MAIN, MAIN + REST)
        even = jnp.concatenate([rest[0], rest[2]], axis=0)
        odd = jnp.concatenate([rest[1], rest[3]], axis=0)
        mine_ref[2 * count :, lanes] = jnp.where(x == 1, even, odd)
        columns = jnp.concatenate(
            (own,) + by_place(0, MAIN) + (jnp.where(x == 0, even, odd),), axis=0
        )
        for k, ref in enumerate((tokens_ref, other_ref)):
            product = jnp.dot(ref[...], columns, preferred_element_type=jnp.float32)
            product = jnp.maximum(product, floor).astype(jnp.bfloat16)
            mine_ref[k * count : (k + 1) * count, lanes] = product


def first_call(tokens, other, qkv_weight, *landed):
    count, depth = tokens.shape
    inputs = (tokens, other, qkv_weight) + landed
    return kernel_call(
        first_kernel,
        jax.ShapeDtypeStruct((2 * count + 2 * len(STEPS) * REST, depth), jnp.bfloat16),
        inputs,
        [whole_vmem()] * len(inputs),
        flops=4 * tokens.size * depth,
        bytes_accessed=2 * depth * depth,
    )


def diagonal_mask():
    rows = lax.broadcasted_iota(jnp.int32, (LANES, LANES), 0) // HEAD_DIM
    columns = lax.broadcasted_iota(jnp.int32, (LANES, LANES), 1) // HEAD_DIM
    return rows == columns


def state_kernel(mine_ref, other_ref, values_ref, top_ref, bottom_ref, upto_ref, total_ref):
    _, _, core = coordinates()
    mask = diagonal_mask()
    columns = top_ref.shape[1]
    count = values_ref.shape[0]
    later = jnp.where(core == 1, 1.0, 0.0).astype(jnp.float32)
    for group in range(mine_ref.shape[1] // LANES):
        at = slice(group * LANES, (group + 1) * LANES)

        def state(mine, other):
            keys = jnp.where(core == 0, mine, other)
            values = jnp.where(core == 0, other, mine)
            full = lax.dot_general(
                keys, values, (((0,), (0,)), ((), ())), preferred_element_type=jnp.float32
            )
            full = jnp.where(mask, full, 0.0)
            total = full[0:HEAD_DIM]
            for k in range(1, LANES // HEAD_DIM):
                total = total + full[k * HEAD_DIM : (k + 1) * HEAD_DIM]
            return total, values

        low, high = slice(0, count), slice(count, 2 * count)
        here, values = state(mine_ref[low, at], other_ref[high, at])
        there, _ = state(mine_ref[high, at], other_ref[low, at])
        values_ref[:, at] = values
        top_ref[0, :, at] = values[:columns]
        bottom_ref[0, :, at] = values[-columns:]
        upto_ref[group] = here + later * there
        total_ref[group] = (here + there).astype(jnp.bfloat16)


def state_call(mine, other, count, columns):
    depth = mine.shape[1]
    compact = (depth // LANES, HEAD_DIM, LANES)
    edge = jax.ShapeDtypeStruct((1, columns, depth), jnp.bfloat16)
    return kernel_call(
        state_kernel,
        [
            jax.ShapeDtypeStruct((count, depth), jnp.bfloat16),
            edge,
            edge,
            jax.ShapeDtypeStruct(compact, jnp.float32),
            jax.ShapeDtypeStruct(compact, jnp.bfloat16),
        ],
        (mine, other),
        [whole_vmem()] * 2,
        flops=4 * count * depth * LANES,
        bytes_accessed=8 * count * depth,
    )


def column_taps(sheet, taps):
    edge = jnp.zeros_like(sheet[:, :1])
    before = jnp.concatenate([edge, sheet[:, :-1]], axis=1)
    behind = jnp.concatenate([sheet[:, 1:], edge], axis=1)
    return taps[0] * before + taps[1] * sheet + taps[2] * behind


def local_kernel(values_ref, conv_ref, local_ref):
    rows, _, depth = values_ref.shape
    for at in range(0, depth, LANES):
        lanes = slice(at, at + LANES)
        taps = conv_ref[:, :, lanes]
        sheet = values_ref[:, :, lanes].astype(jnp.float32)
        local_ref[:, :, lanes] = column_taps(sheet, taps[1])
        local_ref[1:, :, lanes] = local_ref[1:, :, lanes] + column_taps(sheet[:-1], taps[0])
        local_ref[: rows - 1, :, lanes] = (
            local_ref[: rows - 1, :, lanes] + column_taps(sheet[1:], taps[2])
        )


def local_call(values, conv_weight):
    return kernel_call(
        local_kernel,
        jax.ShapeDtypeStruct(values.shape, jnp.float32),
        (values, conv_weight),
        [whole_vmem()] * 2,
        flops=18 * values.size,
        bytes_accessed=6 * values.size,
    )


def query_kernel(*refs):
    tokens_ref, qkv_ref, out_ref, *packs, ours_ref, other_ref, query_ref, weight_ref = refs
    y, x, core = coordinates()
    depth = tokens_ref.shape[1]
    rows = qkv_ref.shape[0]
    steps = len(STEPS)
    rest_at = ours_ref.shape[0] - 2 * steps * REST
    places = chip_places(y, x)
    width = 3 * LANES

    def block(of_core, index, lanes):
        pack, k = index
        mine_ref, theirs_ref = packs[2 * pack], packs[2 * pack + 1]
        return jnp.where(core == of_core, mine_ref[k, :, lanes], theirs_ref[k, :, lanes])


    def rest(of_core, lanes):
        return jnp.where(core == of_core, ours_ref[rest_at:, lanes], other_ref[rest_at:, lanes])

    def put(row, value, lanes):
        weight_ref[pl.ds(pl.multiple_of(row, REST), value.shape[0]), lanes] = value

    for at in range(0, depth, width):
        lanes = slice(at, at + width)
        order = [(0, 2 * k) for k in range(steps)] + [(1, k) for k in range(2 * steps)]
        order += [(0, 2 * k + 1) for k in range(steps)]
        columns = [qkv_ref[:, lanes]] + [block(0, k, lanes) for k in order] + [rest(0, lanes)]
        queries = jnp.dot(
            tokens_ref[...], jnp.concatenate(columns, axis=0), preferred_element_type=jnp.float32
        )
        query_ref[:, lanes] = jnp.maximum(queries, 0.0).astype(jnp.bfloat16)

        put(lax.axis_index("space") * rows, out_ref[:, lanes], lanes)
        tiles = rest(1, lanes)
        for k, step in enumerate(STEPS):
            base = source_plane(step) * rows
            held = ((0, 2 * k), (1, steps + k), (1, k), (0, 2 * k + 1))
            for place, index in zip(places, held):
                put(base + place * MAIN, block(1, index, lanes), lanes)
            for run, tile in enumerate((y, 1 - y)):
                start = (run * steps + k) * REST
                put(base + 4 * MAIN + tile * REST, tiles[start : start + REST], lanes)


def query_call(tokens, qkv_weight, out_weight, *landed):
    depth = tokens.shape[1]
    inputs = (tokens, qkv_weight, out_weight) + landed
    return kernel_call(
        query_kernel,
        [
            jax.ShapeDtypeStruct(tokens.shape, jnp.bfloat16),
            jax.ShapeDtypeStruct((depth, depth), jnp.bfloat16),
        ],
        inputs,
        [whole_vmem()] * len(inputs),
        flops=2 * tokens.size * depth,
        bytes_accessed=4 * depth * depth,
    )


def finish_kernel(*refs):
    queries_ref, weight_ref, state_ref, local_ref, above_ref, below_ref, *refs = refs
    conv_ref, gain_ref, result_ref, read_ref, mixture_ref = refs
    count, depth = queries_ref.shape
    columns = above_ref.shape[1]
    mask = diagonal_mask()
    square = jnp.zeros((count, LANES), jnp.float32)
    for group in range(depth // LANES):
        lanes = slice(group * LANES, (group + 1) * LANES)
        spread = jnp.concatenate([state_ref[group]] * (LANES // HEAD_DIM), axis=0)
        spread = jnp.where(mask, spread, 0.0).astype(jnp.bfloat16)
        read = jnp.dot(queries_ref[:, lanes], spread, preferred_element_type=jnp.float32)
        read_ref[:, lanes] = read
        square = square + read * read
    scale = lax.rsqrt(jnp.sum(square, axis=1, keepdims=True) / depth + 1e-06)
    for at in range(0, depth, LANES):
        lanes = slice(at, at + LANES)
        taps = conv_ref[:, :, lanes]
        mixture = read_ref[:, lanes] * scale * gain_ref[:, lanes] + local_ref[:, lanes]
        above = column_taps(above_ref[:, :, lanes].astype(jnp.float32), taps[0])[0]
        below = column_taps(below_ref[:, :, lanes].astype(jnp.float32), taps[2])[0]
        middle = mixture[columns : count - columns]
        mixture = jnp.concatenate(
            [mixture[:columns] + above, middle, mixture[count - columns :] + below], axis=0
        )
        mixture_ref[:, lanes] = mixture.astype(jnp.bfloat16)
    width = 3 * LANES
    for at in range(0, depth, width):
        lanes = slice(at, at + width)
        product = jnp.dot(
            mixture_ref[...], weight_ref[:, lanes], preferred_element_type=jnp.float32
        )
        result_ref[:, lanes] = product.astype(jnp.bfloat16)


def finish_call(queries, *inputs):
    return kernel_call(
        finish_kernel,
        jax.ShapeDtypeStruct(queries.shape, jnp.bfloat16),
        (queries,) + inputs,
        [whole_vmem()] * (1 + len(inputs)),
        [pltpu.VMEM(queries.shape, jnp.float32), pltpu.VMEM(queries.shape, jnp.bfloat16)],
        flops=2 * queries.size * queries.shape[1],
        bytes_accessed=2 * queries.shape[1] ** 2,
    )


def plane_form(video_tokens, qkv_weight, out_weight, conv_weight, norm_gain):
    frame_now = video_tokens[0]
    row_count, col_count, depth = frame_now.shape
    tokens = frame_now.reshape(row_count * col_count, depth)

    first_piece, second_piece = pieces_call(qkv_weight, out_weight)
    first_piece = first_piece[None]
    one = shifted(first_piece, 1)
    three = shifted(first_piece, -1)
    tokens = reorder_call(after(tokens, second_piece), qkv_weight.shape[0])
    other_tokens = flipped(tokens, (1, 1))
    one, three = after((one, three), tokens)

    pair = jnp.concatenate([one, three])
    two = shifted(one, 1)
    pair_first = flipped(pair, (2, 4))
    near = jnp.concatenate(after((pair, pair_first), other_tokens))
    away = flipped(near, (4, 2))
    two_near = jnp.concatenate([two, flipped(two, (2, 4))])
    two_away = flipped(two_near, (4, 2))

    second_ready = after(second_piece, one, three)
    second_one = shifted(second_ready, 1)
    second_three = shifted(second_ready, -1)
    second_two = shifted(after(second_one, two_near), 1)

    mine = first_call(after(tokens, second_one, second_three), other_tokens, qkv_weight, near, away, two_near, two_away)
    other = flipped(after(mine, second_two), (1, 1))
    straight = jnp.concatenate([second_one, second_two, second_three])
    swapped_straight = flipped(straight, (1, 1))
    values, top, bottom, upto, total = state_call(mine, other, tokens.shape[0], col_count)
    total = after(total, swapped_straight)

    second_own = jnp.stack([second_one[0], second_two[0], second_three[0]])
    second_first = flipped(second_own, (2, 4))
    second_second = flipped(second_own, (4, 2))

    for bit, guard in ((2, 2), (4, 4), (6, 4)):
        pairs = [(t, t ^ bit) for t in range(8) if not t & guard]
        upto = upto + lax.ppermute(total, "tm", pairs).astype(jnp.float32)
    count = lax.axis_size("space")
    forward = [(i, i + 1) for i in range(count - 1)]
    backward = [(target, source) for source, target in forward]
    state = after(upto, second_first, second_second)
    share = state.astype(jnp.bfloat16)
    grid = values.reshape(row_count, col_count, depth)
    local_term = local_call(grid, conv_weight).reshape(-1, depth)
    arrived = lax.ppermute(share, "space", [(i, i ^ 1) for i in range(count)])
    arrived = after(arrived, local_term)
    share = (share.astype(jnp.float32) + arrived.astype(jnp.float32)).astype(jnp.bfloat16)
    arrived = lax.ppermute(share, "space", [(i, i ^ 2) for i in range(count)])
    top, bottom = after((top, bottom), share)
    above = lax.ppermute(bottom, "space", forward)
    below = lax.ppermute(top, "space", backward)

    turned = jnp.concatenate([second_first, second_second])
    swapped_turned = flipped(after(turned, share), (1, 1))
    queries, weight = query_call(
        tokens,
        qkv_weight,
        out_weight,
        straight,
        swapped_straight,
        turned,
        swapped_turned,
        mine,
        other,
    )
    state = share.astype(jnp.float32) + arrived.astype(jnp.float32)
    above, below = after((above, below), queries, weight)
    result = finish_call(
        queries,
        weight,
        state,
        local_term,
        above,
        below,
        conv_weight,
        norm_gain[None],
    )
    return result.reshape(1, row_count, col_count, depth)


def solution(mesh):
    def per_device(video_tokens, qkv_weight, out_weight, conv_weight, norm_gain):
        fits = mesh.shape["tm"] == 8 and mesh.shape["space"] == 4
        fits = fits and qkv_weight.shape[0] == 4 * MAIN + 2 * REST
        form = plane_form if fits else general_form
        return form(video_tokens, qkv_weight, out_weight, conv_weight, norm_gain)

    in_specs = (P("tm", "space", None, None), P("space", None), P("space", None), P(), P())
    out_specs = P("tm", "space", None, None)
    return jax.shard_map(
        per_device, mesh=mesh, in_specs=in_specs, out_specs=out_specs, check_vma=False
    )
```

```python
import functools

import jax
import jax.numpy as jnp
from jax import lax
from jax.experimental import pallas as pl
from jax.experimental.pallas import tpu as pltpu
from jax.sharding import PartitionSpec as P

HEADS = 36
HEAD_DIM = 32
LANES = 128
MAIN = 64
REST = 16
STEPS = (1, 2, 3)
VMEM_LIMIT = 24 * 1024 * 1024
WHOLE_VMEM = 63 * 1024 * 1024


def entering(value, axis, combine, identity):
    devices, place = (lax.axis_size(axis), lax.axis_index(axis))
    everything = lax.all_gather(value.astype(jnp.bfloat16), axis)
    start = jnp.broadcast_to(jnp.asarray(identity, value.dtype), value.shape)

    def lap(k, before):
        reached = k < place
        new = combine(before, everything[k].astype(value.dtype))
        return jnp.where(reached, new, before)

    return lax.fori_loop(0, devices, lap, start)


def with_halo(block, sides, width):
    for axis, dim in sides:
        count = lax.axis_size(axis)
        forward = [(i, i + 1) for i in range(count - 1)]
        backward = [(target, source) for source, target in forward]
        low = lax.ppermute(
            lax.slice_in_dim(block, block.shape[dim] - width, None, axis=dim), axis, forward
        )
        high = lax.ppermute(lax.slice_in_dim(block, 0, width, axis=dim), axis, backward)
        block = jnp.concatenate([low, block, high], axis=dim)
    return block


def fold_product(left_side, block_rows):
    return jnp.dot(left_side, block_rows, preferred_element_type=jnp.float32)


def add_states(earlier, later):
    return earlier + later


def causal_states(key_feat, values):
    key_heads = key_feat.reshape(-1, HEADS, HEAD_DIM)
    value_heads = values.reshape(-1, HEADS, HEAD_DIM)
    frame_state = jnp.einsum(
        "thd,the->hde", key_heads, value_heads, preferred_element_type=jnp.float32
    )
    flat_state = frame_state.reshape(-1)
    frame_sum = lax.psum(flat_state.astype(jnp.bfloat16), "space").astype(jnp.float32)
    earlier = entering(frame_sum, "tm", add_states, jnp.zeros_like(frame_sum))
    whole_state = earlier + frame_sum
    return whole_state.reshape(HEADS, HEAD_DIM, HEAD_DIM)


def general_form(video_tokens, qkv_weight, out_weight, conv_weight, norm_gain):
    frame_now = video_tokens[0]
    row_count, col_count, feat_width = frame_now.shape
    tokens = frame_now.reshape(row_count * col_count, feat_width)
    projected = fold_product(tokens, lax.all_gather(qkv_weight, "space", axis=0, tiled=True))
    query_feat = jax.nn.relu(projected[:, :feat_width]).astype(jnp.bfloat16)
    key_feat = jax.nn.relu(projected[:, feat_width : 2 * feat_width]).astype(jnp.bfloat16)
    values = projected[:, 2 * feat_width :].astype(jnp.bfloat16)
    state_all = causal_states(key_feat, values)
    padded_rows = with_halo(values.reshape(row_count, col_count, feat_width), (("space", 0),), 1)
    padded = jnp.pad(padded_rows, ((0, 0), (1, 1), (0, 0))).astype(jnp.float32)
    local_term = jnp.zeros((row_count, col_count, feat_width), jnp.float32)
    for row_shift in range(3):
        for col_shift in range(3):
            local_term = (
                local_term
                + conv_weight[row_shift, col_shift]
                * padded[row_shift : row_shift + row_count, col_shift : col_shift + col_count]
            )
    state_low = state_all.astype(jnp.bfloat16)
    query_heads = query_feat.reshape(-1, HEADS, HEAD_DIM)
    readout = jnp.einsum("thd,hde->the", query_heads, state_low, preferred_element_type=jnp.float32)
    readout = readout.reshape(-1, feat_width)
    mean_square = jnp.mean(readout * readout, axis=-1, keepdims=True)
    normed = readout * lax.rsqrt(mean_square + 1e-06) * norm_gain
    mixture = (normed + local_term.reshape(-1, feat_width)).astype(jnp.bfloat16)
    result = fold_product(mixture, lax.all_gather(out_weight, "space", axis=0, tiled=True))
    return result.astype(jnp.bfloat16).reshape(1, row_count, col_count, feat_width)


def coordinates():
    place = lax.axis_index("tm")
    return lax.rem(place // 4, 2), lax.rem(place // 2, 2), lax.rem(place, 2)


def shifted(value, step):
    count = lax.axis_size("space")
    return lax.ppermute(value, "space", [(i, (i + step) % count) for i in range(count)])


def flipped(value, bit_on_core):
    return lax.ppermute(value, "tm", [(t, t ^ bit_on_core[t % 2]) for t in range(8)])


def after(value, *earlier):
    return lax.optimization_barrier((value,) + earlier)[0]


def chip_places(y, x):
    return (2 * y + x, 2 * y + (1 - x), 2 * (1 - y) + x, 2 * (1 - y) + (1 - x))


def source_plane(step):
    count = lax.axis_size("space")
    return lax.rem(lax.axis_index("space") - step + count, count)


def steps_through(within, size):
    run = sum(jnp.where(within >= size * k, 1, 0) for k in range(1, len(STEPS)))
    return run, within - size * run


def landed_order(at, width, rows):
    y, x, _ = coordinates()
    planes = [source_plane(step) for step in STEPS]
    row = at + lax.broadcasted_iota(jnp.int32, (1, width), 1)

    def pick(choices, index):
        chosen = choices[-1]
        for k in range(len(choices) - 2, -1, -1):
            chosen = jnp.where(index == k, choices[k], chosen)
        return chosen

    def landed(within, size, starts):
        count = len(STEPS) * size
        slot = sum(jnp.where(within >= count * k, 1, 0) for k in range(1, len(starts)))
        run, left = steps_through(within - count * slot, size)
        return pick(planes, run) * rows + pick(starts, slot) + left

    main = landed(row - rows, MAIN, [place * MAIN for place in chip_places(y, x)])
    rest_at = rows + 4 * len(STEPS) * MAIN
    rest = landed(row - rest_at, REST, [4 * MAIN + tile * REST for tile in (y, 1 - y)])
    own = lax.axis_index("space") * rows + row
    return jnp.where(row < rows, own, jnp.where(row < rest_at, main, rest))


def whole_vmem():
    return pl.BlockSpec(memory_space=pltpu.VMEM)


def anywhere():
    return pl.BlockSpec(memory_space=pltpu.HBM)


def kernel_call(
    body, outputs, inputs, in_specs, scratch=(), flops=0, bytes_accessed=0, limit=VMEM_LIMIT
):
    return pl.pallas_call(
        body,
        out_shape=outputs,
        in_specs=in_specs,
        out_specs=jax.tree.map(lambda _: whole_vmem(), outputs),
        scratch_shapes=list(scratch),
        compiler_params=pltpu.CompilerParams(vmem_limit_bytes=limit),
        cost_estimate=pl.CostEstimate(
            flops=flops, bytes_accessed=bytes_accessed, transcendentals=0
        ),
    )(*inputs)


def pieces_kernel(qkv_ref, out_ref, first_ref, second_ref, sems):
    y, x, core = coordinates()
    depth = out_ref.shape[1]
    main = pl.ds(pl.multiple_of((2 * y + x) * MAIN, REST), MAIN)
    rest = pl.ds(pl.multiple_of(4 * MAIN + y * REST, REST), REST)
    first_columns = pl.ds(pl.multiple_of(depth * (1 + core), LANES), depth)
    rest_columns = pl.ds(pl.multiple_of(jnp.where(x == 0, depth * (1 + core), 0), LANES), depth)

    def copy(source, target, k):
        return pltpu.make_async_copy(source, target, sems.at[k])

    first_main = copy(qkv_ref.at[main, first_columns], first_ref.at[pl.ds(0, MAIN), :], 0)
    first_main.start()
    rest_target = first_ref.at[pl.ds(MAIN, REST), :]
    from_out = (core == 1) & (x == 1)

    @pl.when(from_out)
    def _():
        copy(out_ref.at[rest, :], rest_target, 1).start()

    @pl.when(jnp.logical_not(from_out))
    def _():
        copy(qkv_ref.at[rest, rest_columns], rest_target, 1).start()

    places = chip_places(y, x)
    for k, place in enumerate((places[0], places[3])):
        rows = pl.ds(pl.multiple_of(place * MAIN, REST), MAIN)

        @pl.when(core == 0)
        def _():
            copy(qkv_ref.at[rows, pl.ds(0, depth)], second_ref.at[k], 2 + k).start()

        @pl.when(core == 1)
        def _():
            copy(out_ref.at[rows, :], second_ref.at[k], 2 + k).start()

    first_main.wait()
    copy(out_ref.at[rest, :], rest_target, 1).wait()
    for k in range(2):
        copy(out_ref.at[main, :], second_ref.at[k], 2 + k).wait()


def pieces_call(qkv_weight, out_weight):
    depth = out_weight.shape[1]
    outputs = [
        jax.ShapeDtypeStruct((MAIN + REST, depth), jnp.bfloat16),
        jax.ShapeDtypeStruct((2, MAIN, depth), jnp.bfloat16),
    ]
    return kernel_call(
        pieces_kernel,
        outputs,
        (qkv_weight, out_weight),
        [anywhere(), anywhere()],
        [pltpu.SemaphoreType.DMA((4,))],
        bytes_accessed=4 * (3 * MAIN + REST) * depth,
        limit=WHOLE_VMEM,
    )


def reorder_kernel(rows, tokens_ref, moved_ref):
    depth = tokens_ref.shape[1]
    width = 3 * LANES
    row = lax.broadcasted_iota(jnp.int32, (depth, width), 0)
    for at in range(0, depth, width):
        order = landed_order(at, width, rows)
        chosen = jnp.where(row == order, 1.0, 0.0).astype(jnp.bfloat16)
        moved = jnp.dot(tokens_ref[...], chosen, preferred_element_type=jnp.float32)
        moved_ref[:, at : at + width] = moved.astype(jnp.bfloat16)


def reorder_call(tokens, rows):
    depth = tokens.shape[1]
    return kernel_call(
        functools.partial(reorder_kernel, rows),
        jax.ShapeDtypeStruct(tokens.shape, jnp.bfloat16),
        (tokens,),
        [whole_vmem()],
        flops=2 * tokens.size * depth,
        bytes_accessed=2 * tokens.size,
    )


def first_kernel(*refs):
    tokens_ref, other_ref, qkv_ref, near_ref, away_ref, first_ref, far_ref, mine_ref = refs
    slots = (
        ((near_ref, 0), (first_ref, 0), (near_ref, 1)),
        ((near_ref, 2), (first_ref, 1), (near_ref, 3)),
        ((away_ref, 0), (far_ref, 0), (away_ref, 1)),
        ((away_ref, 2), (far_ref, 1), (away_ref, 3)),
    )
    _, x, core = coordinates()
    count, depth = tokens_ref.shape
    floor = jnp.where(core == 0, 0.0, -jnp.inf).astype(jnp.float32)
    width = 3 * LANES

    for at in range(0, depth, width):
        lanes = slice(at, at + width)

        def slot(k, low, high):
            return jnp.concatenate([ref[at, low:high, lanes] for ref, at in slots[k]], axis=0)

        def by_place(low, high):
            own, first, second, far = [slot(k, low, high) for k in range(4)]
            along_x = jnp.where(core == 0, first, second)
            along_y = jnp.where(core == 0, second, first)
            return own, along_x, along_y, far

        keys, values = [qkv_ref[:, depth * k + at : depth * k + at + width] for k in (1, 2)]
        own = jnp.where(core == 0, keys, values)
        rest = by_place(MAIN, MAIN + REST)
        even = jnp.concatenate([rest[0], rest[2]], axis=0)
        odd = jnp.concatenate([rest[1], rest[3]], axis=0)
        mine_ref[2 * count :, lanes] = jnp.where(x == 1, even, odd)
        columns = jnp.concatenate(
            (own,) + by_place(0, MAIN) + (jnp.where(x == 0, even, odd),), axis=0
        )
        for k, ref in enumerate((tokens_ref, other_ref)):
            product = jnp.dot(ref[...], columns, preferred_element_type=jnp.float32)
            product = jnp.maximum(product, floor).astype(jnp.bfloat16)
            mine_ref[k * count : (k + 1) * count, lanes] = product


def first_call(tokens, other, qkv_weight, *landed):
    count, depth = tokens.shape
    inputs = (tokens, other, qkv_weight) + landed
    return kernel_call(
        first_kernel,
        jax.ShapeDtypeStruct((2 * count + 2 * len(STEPS) * REST, depth), jnp.bfloat16),
        inputs,
        [whole_vmem()] * len(inputs),
        flops=4 * tokens.size * depth,
        bytes_accessed=2 * depth * depth,
    )


def diagonal_mask():
    rows = lax.broadcasted_iota(jnp.int32, (LANES, LANES), 0) // HEAD_DIM
    columns = lax.broadcasted_iota(jnp.int32, (LANES, LANES), 1) // HEAD_DIM
    return rows == columns


def state_kernel(mine_ref, other_ref, values_ref, top_ref, bottom_ref, upto_ref, total_ref):
    _, _, core = coordinates()
    mask = diagonal_mask()
    columns = top_ref.shape[1]
    count = values_ref.shape[0]
    later = jnp.where(core == 1, 1.0, 0.0).astype(jnp.float32)
    for group in range(mine_ref.shape[1] // LANES):
        at = slice(group * LANES, (group + 1) * LANES)

        def state(mine, other):
            keys = jnp.where(core == 0, mine, other)
            values = jnp.where(core == 0, other, mine)
            full = lax.dot_general(
                keys, values, (((0,), (0,)), ((), ())), preferred_element_type=jnp.float32
            )
            full = jnp.where(mask, full, 0.0)
            total = full[0:HEAD_DIM]
            for k in range(1, LANES // HEAD_DIM):
                total = total + full[k * HEAD_DIM : (k + 1) * HEAD_DIM]
            return total, values

        low, high = slice(0, count), slice(count, 2 * count)
        here, values = state(mine_ref[low, at], other_ref[high, at])
        there, _ = state(mine_ref[high, at], other_ref[low, at])
        values_ref[:, at] = values
        top_ref[0, :, at] = values[:columns]
        bottom_ref[0, :, at] = values[-columns:]
        upto_ref[group] = here + later * there
        total_ref[group] = (here + there).astype(jnp.bfloat16)


def state_call(mine, other, count, columns):
    depth = mine.shape[1]
    compact = (depth // LANES, HEAD_DIM, LANES)
    edge = jax.ShapeDtypeStruct((1, columns, depth), jnp.bfloat16)
    return kernel_call(
        state_kernel,
        [
            jax.ShapeDtypeStruct((count, depth), jnp.bfloat16),
            edge,
            edge,
            jax.ShapeDtypeStruct(compact, jnp.float32),
            jax.ShapeDtypeStruct(compact, jnp.bfloat16),
        ],
        (mine, other),
        [whole_vmem()] * 2,
        flops=4 * count * depth * LANES,
        bytes_accessed=8 * count * depth,
    )


def column_taps(sheet, taps):
    edge = jnp.zeros_like(sheet[:, :1])
    before = jnp.concatenate([edge, sheet[:, :-1]], axis=1)
    behind = jnp.concatenate([sheet[:, 1:], edge], axis=1)
    return taps[0] * before + taps[1] * sheet + taps[2] * behind


def local_kernel(values_ref, conv_ref, local_ref):
    rows, _, depth = values_ref.shape
    for at in range(0, depth, LANES):
        lanes = slice(at, at + LANES)
        taps = conv_ref[:, :, lanes]
        sheet = values_ref[:, :, lanes].astype(jnp.float32)
        local_ref[:, :, lanes] = column_taps(sheet, taps[1])
        local_ref[1:, :, lanes] = local_ref[1:, :, lanes] + column_taps(sheet[:-1], taps[0])
        local_ref[: rows - 1, :, lanes] = (
            local_ref[: rows - 1, :, lanes] + column_taps(sheet[1:], taps[2])
        )


def local_call(values, conv_weight):
    return kernel_call(
        local_kernel,
        jax.ShapeDtypeStruct(values.shape, jnp.float32),
        (values, conv_weight),
        [whole_vmem()] * 2,
        flops=18 * values.size,
        bytes_accessed=6 * values.size,
    )


def query_kernel(*refs):
    tokens_ref, qkv_ref, out_ref, *packs, ours_ref, other_ref, query_ref, weight_ref = refs
    y, x, core = coordinates()
    depth = tokens_ref.shape[1]
    rows = qkv_ref.shape[0]
    steps = len(STEPS)
    rest_at = ours_ref.shape[0] - 2 * steps * REST
    places = chip_places(y, x)
    width = 3 * LANES

    def block(of_core, index, lanes):
        pack, k = index
        mine_ref, theirs_ref = packs[2 * pack], packs[2 * pack + 1]
        return jnp.where(core == of_core, mine_ref[k, :, lanes], theirs_ref[k, :, lanes])


    def rest(of_core, lanes):
        return jnp.where(core == of_core, ours_ref[rest_at:, lanes], other_ref[rest_at:, lanes])

    def put(row, value, lanes):
        weight_ref[pl.ds(pl.multiple_of(row, REST), value.shape[0]), lanes] = value

    for at in range(0, depth, width):
        lanes = slice(at, at + width)
        order = [(0, 2 * k) for k in range(steps)] + [(1, k) for k in range(2 * steps)]
        order += [(0, 2 * k + 1) for k in range(steps)]
        columns = [qkv_ref[:, lanes]] + [block(0, k, lanes) for k in order] + [rest(0, lanes)]
        queries = jnp.dot(
            tokens_ref[...], jnp.concatenate(columns, axis=0), preferred_element_type=jnp.float32
        )
        query_ref[:, lanes] = jnp.maximum(queries, 0.0).astype(jnp.bfloat16)

        put(lax.axis_index("space") * rows, out_ref[:, lanes], lanes)
        tiles = rest(1, lanes)
        for k, step in enumerate(STEPS):
            base = source_plane(step) * rows
            held = ((0, 2 * k), (1, steps + k), (1, k), (0, 2 * k + 1))
            for place, index in zip(places, held):
                put(base + place * MAIN, block(1, index, lanes), lanes)
            for run, tile in enumerate((y, 1 - y)):
                start = (run * steps + k) * REST
                put(base + 4 * MAIN + tile * REST, tiles[start : start + REST], lanes)


def query_call(tokens, qkv_weight, out_weight, *landed):
    depth = tokens.shape[1]
    inputs = (tokens, qkv_weight, out_weight) + landed
    return kernel_call(
        query_kernel,
        [
            jax.ShapeDtypeStruct(tokens.shape, jnp.bfloat16),
            jax.ShapeDtypeStruct((depth, depth), jnp.bfloat16),
        ],
        inputs,
        [whole_vmem()] * len(inputs),
        flops=2 * tokens.size * depth,
        bytes_accessed=4 * depth * depth,
    )


def finish_kernel(*refs):
    queries_ref, weight_ref, state_ref, local_ref, above_ref, below_ref, *refs = refs
    conv_ref, gain_ref, result_ref, read_ref, mixture_ref = refs
    count, depth = queries_ref.shape
    columns = above_ref.shape[1]
    mask = diagonal_mask()
    square = jnp.zeros((count, LANES), jnp.float32)
    for group in range(depth // LANES):
        lanes = slice(group * LANES, (group + 1) * LANES)
        spread = jnp.concatenate([state_ref[group]] * (LANES // HEAD_DIM), axis=0)
        spread = jnp.where(mask, spread, 0.0).astype(jnp.bfloat16)
        read = jnp.dot(queries_ref[:, lanes], spread, preferred_element_type=jnp.float32)
        read_ref[:, lanes] = read
        square = square + read * read
    scale = lax.rsqrt(jnp.sum(square, axis=1, keepdims=True) / depth + 1e-06)
    for at in range(0, depth, LANES):
        lanes = slice(at, at + LANES)
        taps = conv_ref[:, :, lanes]
        mixture = read_ref[:, lanes] * scale * gain_ref[:, lanes] + local_ref[:, lanes]
        above = column_taps(above_ref[:, :, lanes].astype(jnp.float32), taps[0])[0]
        below = column_taps(below_ref[:, :, lanes].astype(jnp.float32), taps[2])[0]
        middle = mixture[columns : count - columns]
        mixture = jnp.concatenate(
            [mixture[:columns] + above, middle, mixture[count - columns :] + below], axis=0
        )
        mixture_ref[:, lanes] = mixture.astype(jnp.bfloat16)
    width = 3 * LANES
    for at in range(0, depth, width):
        lanes = slice(at, at + width)
        product = jnp.dot(
            mixture_ref[...], weight_ref[:, lanes], preferred_element_type=jnp.float32
        )
        result_ref[:, lanes] = product.astype(jnp.bfloat16)


def finish_call(queries, *inputs):
    return kernel_call(
        finish_kernel,
        jax.ShapeDtypeStruct(queries.shape, jnp.bfloat16),
        (queries,) + inputs,
        [whole_vmem()] * (1 + len(inputs)),
        [pltpu.VMEM(queries.shape, jnp.float32), pltpu.VMEM(queries.shape, jnp.bfloat16)],
        flops=2 * queries.size * queries.shape[1],
        bytes_accessed=2 * queries.shape[1] ** 2,
    )


def plane_form(video_tokens, qkv_weight, out_weight, conv_weight, norm_gain):
    frame_now = video_tokens[0]
    row_count, col_count, depth = frame_now.shape
    tokens = frame_now.reshape(row_count * col_count, depth)

    first_piece, second_piece = pieces_call(qkv_weight, out_weight)
    first_piece = first_piece[None]
    one = shifted(first_piece, 1)
    three = shifted(first_piece, -1)
    tokens = reorder_call(after(tokens, second_piece), qkv_weight.shape[0])
    other_tokens = flipped(tokens, (1, 1))
    one, three = after((one, three), tokens)

    pair = jnp.concatenate([one, three])
    two = shifted(one, 1)
    pair_first = flipped(pair, (2, 4))
    near = jnp.concatenate(after((pair, pair_first), other_tokens))
    away = flipped(near, (4, 2))
    two_near = jnp.concatenate([two, flipped(two, (2, 4))])
    two_away = flipped(two_near, (4, 2))

    second_ready = after(second_piece, one, three)
    second_one = shifted(second_ready, 1)
    second_three = shifted(second_ready, -1)
    second_two = shifted(after(second_one, two_near), 1)

    mine = first_call(after(tokens, second_one, second_three), other_tokens, qkv_weight, near, away, two_near, two_away)
    other = flipped(after(mine, second_two), (1, 1))
    straight = jnp.concatenate([second_one, second_two, second_three])
    swapped_straight = flipped(straight, (1, 1))
    values, top, bottom, upto, total = state_call(mine, other, tokens.shape[0], col_count)
    total = after(total, swapped_straight)

    second_own = jnp.stack([second_one[0], second_two[0], second_three[0]])
    second_first = flipped(second_own, (2, 4))
    second_second = flipped(second_own, (4, 2))

    for bit, guard in ((2, 2), (4, 4), (6, 4)):
        pairs = [(t, t ^ bit) for t in range(8) if not t & guard]
        upto = upto + lax.ppermute(total, "tm", pairs).astype(jnp.float32)
    count = lax.axis_size("space")
    forward = [(i, i + 1) for i in range(count - 1)]
    backward = [(target, source) for source, target in forward]
    state = after(upto, second_first, second_second)
    share = state.astype(jnp.bfloat16)
    grid = values.reshape(row_count, col_count, depth)
    local_term = local_call(grid, conv_weight).reshape(-1, depth)
    arrived = lax.ppermute(share, "space", [(i, i ^ 1) for i in range(count)])
    above = lax.ppermute(after(bottom, share), "space", forward)
    arrived = after(arrived, local_term, above)
    share = (share.astype(jnp.float32) + arrived.astype(jnp.float32)).astype(jnp.bfloat16)
    arrived = lax.ppermute(share, "space", [(i, i ^ 2) for i in range(count)])
    below = lax.ppermute(after(top, share), "space", backward)

    turned = jnp.concatenate([second_first, second_second])
    swapped_turned = flipped(after(turned, share), (1, 1))
    queries, weight = query_call(
        tokens,
        qkv_weight,
        out_weight,
        straight,
        swapped_straight,
        turned,
        swapped_turned,
        mine,
        other,
    )
    state = share.astype(jnp.float32) + arrived.astype(jnp.float32)
    above, below = after((above, below), queries, weight)
    result = finish_call(
        queries,
        weight,
        state,
        local_term,
        above,
        below,
        conv_weight,
        norm_gain[None],
    )
    return result.reshape(1, row_count, col_count, depth)


def solution(mesh):
    def per_device(video_tokens, qkv_weight, out_weight, conv_weight, norm_gain):
        fits = mesh.shape["tm"] == 8 and mesh.shape["space"] == 4
        fits = fits and qkv_weight.shape[0] == 4 * MAIN + 2 * REST
        form = plane_form if fits else general_form
        return form(video_tokens, qkv_weight, out_weight, conv_weight, norm_gain)

    in_specs = (P("tm", "space", None, None), P("space", None), P("space", None), P(), P())
    out_specs = P("tm", "space", None, None)
    return jax.shard_map(
        per_device, mesh=mesh, in_specs=in_specs, out_specs=out_specs, check_vma=False
    )
```

```python
import functools

import jax
import jax.numpy as jnp
from jax import lax
from jax.experimental import pallas as pl
from jax.experimental.pallas import tpu as pltpu
from jax.sharding import PartitionSpec as P

HEADS = 36
HEAD_DIM = 32
LANES = 128
MAIN = 64
REST = 16
STEPS = (1, 2, 3)
VMEM_LIMIT = 24 * 1024 * 1024
WHOLE_VMEM = 63 * 1024 * 1024


def entering(value, axis, combine, identity):
    devices, place = (lax.axis_size(axis), lax.axis_index(axis))
    everything = lax.all_gather(value.astype(jnp.bfloat16), axis)
    start = jnp.broadcast_to(jnp.asarray(identity, value.dtype), value.shape)

    def lap(k, before):
        reached = k < place
        new = combine(before, everything[k].astype(value.dtype))
        return jnp.where(reached, new, before)

    return lax.fori_loop(0, devices, lap, start)


def with_halo(block, sides, width):
    for axis, dim in sides:
        count = lax.axis_size(axis)
        forward = [(i, i + 1) for i in range(count - 1)]
        backward = [(target, source) for source, target in forward]
        low = lax.ppermute(
            lax.slice_in_dim(block, block.shape[dim] - width, None, axis=dim), axis, forward
        )
        high = lax.ppermute(lax.slice_in_dim(block, 0, width, axis=dim), axis, backward)
        block = jnp.concatenate([low, block, high], axis=dim)
    return block


def fold_product(left_side, block_rows):
    return jnp.dot(left_side, block_rows, preferred_element_type=jnp.float32)


def add_states(earlier, later):
    return earlier + later


def causal_states(key_feat, values):
    key_heads = key_feat.reshape(-1, HEADS, HEAD_DIM)
    value_heads = values.reshape(-1, HEADS, HEAD_DIM)
    frame_state = jnp.einsum(
        "thd,the->hde", key_heads, value_heads, preferred_element_type=jnp.float32
    )
    flat_state = frame_state.reshape(-1)
    frame_sum = lax.psum(flat_state.astype(jnp.bfloat16), "space").astype(jnp.float32)
    earlier = entering(frame_sum, "tm", add_states, jnp.zeros_like(frame_sum))
    whole_state = earlier + frame_sum
    return whole_state.reshape(HEADS, HEAD_DIM, HEAD_DIM)


def general_form(video_tokens, qkv_weight, out_weight, conv_weight, norm_gain):
    frame_now = video_tokens[0]
    row_count, col_count, feat_width = frame_now.shape
    tokens = frame_now.reshape(row_count * col_count, feat_width)
    projected = fold_product(tokens, lax.all_gather(qkv_weight, "space", axis=0, tiled=True))
    query_feat = jax.nn.relu(projected[:, :feat_width]).astype(jnp.bfloat16)
    key_feat = jax.nn.relu(projected[:, feat_width : 2 * feat_width]).astype(jnp.bfloat16)
    values = projected[:, 2 * feat_width :].astype(jnp.bfloat16)
    state_all = causal_states(key_feat, values)
    padded_rows = with_halo(values.reshape(row_count, col_count, feat_width), (("space", 0),), 1)
    padded = jnp.pad(padded_rows, ((0, 0), (1, 1), (0, 0))).astype(jnp.float32)
    local_term = jnp.zeros((row_count, col_count, feat_width), jnp.float32)
    for row_shift in range(3):
        for col_shift in range(3):
            local_term = (
                local_term
                + conv_weight[row_shift, col_shift]
                * padded[row_shift : row_shift + row_count, col_shift : col_shift + col_count]
            )
    state_low = state_all.astype(jnp.bfloat16)
    query_heads = query_feat.reshape(-1, HEADS, HEAD_DIM)
    readout = jnp.einsum("thd,hde->the", query_heads, state_low, preferred_element_type=jnp.float32)
    readout = readout.reshape(-1, feat_width)
    mean_square = jnp.mean(readout * readout, axis=-1, keepdims=True)
    normed = readout * lax.rsqrt(mean_square + 1e-06) * norm_gain
    mixture = (normed + local_term.reshape(-1, feat_width)).astype(jnp.bfloat16)
    result = fold_product(mixture, lax.all_gather(out_weight, "space", axis=0, tiled=True))
    return result.astype(jnp.bfloat16).reshape(1, row_count, col_count, feat_width)


def coordinates():
    place = lax.axis_index("tm")
    return lax.rem(place // 4, 2), lax.rem(place // 2, 2), lax.rem(place, 2)


def shifted(value, step):
    count = lax.axis_size("space")
    return lax.ppermute(value, "space", [(i, (i + step) % count) for i in range(count)])


def flipped(value, bit_on_core):
    return lax.ppermute(value, "tm", [(t, t ^ bit_on_core[t % 2]) for t in range(8)])


def after(value, *earlier):
    return lax.optimization_barrier((value,) + earlier)[0]


def chip_places(y, x):
    return (2 * y + x, 2 * y + (1 - x), 2 * (1 - y) + x, 2 * (1 - y) + (1 - x))


def source_plane(step):
    count = lax.axis_size("space")
    return lax.rem(lax.axis_index("space") - step + count, count)


def steps_through(within, size):
    run = sum(jnp.where(within >= size * k, 1, 0) for k in range(1, len(STEPS)))
    return run, within - size * run


def landed_order(at, width, rows):
    y, x, _ = coordinates()
    planes = [source_plane(step) for step in STEPS]
    row = at + lax.broadcasted_iota(jnp.int32, (1, width), 1)

    def pick(choices, index):
        chosen = choices[-1]
        for k in range(len(choices) - 2, -1, -1):
            chosen = jnp.where(index == k, choices[k], chosen)
        return chosen

    def landed(within, size, starts):
        count = len(STEPS) * size
        slot = sum(jnp.where(within >= count * k, 1, 0) for k in range(1, len(starts)))
        run, left = steps_through(within - count * slot, size)
        return pick(planes, run) * rows + pick(starts, slot) + left

    main = landed(row - rows, MAIN, [place * MAIN for place in chip_places(y, x)])
    rest_at = rows + 4 * len(STEPS) * MAIN
    rest = landed(row - rest_at, REST, [4 * MAIN + tile * REST for tile in (y, 1 - y)])
    own = lax.axis_index("space") * rows + row
    return jnp.where(row < rows, own, jnp.where(row < rest_at, main, rest))


def whole_vmem():
    return pl.BlockSpec(memory_space=pltpu.VMEM)


def anywhere():
    return pl.BlockSpec(memory_space=pltpu.HBM)


def kernel_call(
    body,
    outputs,
    inputs,
    in_specs,
    scratch=(),
    flops=0,
    bytes_accessed=0,
    limit=VMEM_LIMIT,
    out_spec=whole_vmem,
):
    return pl.pallas_call(
        body,
        out_shape=outputs,
        in_specs=in_specs,
        out_specs=jax.tree.map(lambda _: out_spec(), outputs),
        scratch_shapes=list(scratch),
        compiler_params=pltpu.CompilerParams(vmem_limit_bytes=limit),
        cost_estimate=pl.CostEstimate(
            flops=flops, bytes_accessed=bytes_accessed, transcendentals=0
        ),
    )(*inputs)


def pieces_kernel(qkv_ref, out_ref, first_ref, second_ref, sems):
    y, x, core = coordinates()
    depth = out_ref.shape[1]
    main = pl.ds(pl.multiple_of((2 * y + x) * MAIN, REST), MAIN)
    rest = pl.ds(pl.multiple_of(4 * MAIN + y * REST, REST), REST)
    first_columns = pl.ds(pl.multiple_of(depth * (1 + core), LANES), depth)
    rest_columns = pl.ds(pl.multiple_of(jnp.where(x == 0, depth * (1 + core), 0), LANES), depth)

    def copy(source, target, k):
        return pltpu.make_async_copy(source, target, sems.at[k])

    first_main = copy(qkv_ref.at[main, first_columns], first_ref.at[pl.ds(0, MAIN), :], 0)
    first_main.start()
    rest_target = first_ref.at[pl.ds(MAIN, REST), :]
    from_out = (core == 1) & (x == 1)

    @pl.when(from_out)
    def _():
        copy(out_ref.at[rest, :], rest_target, 1).start()

    @pl.when(jnp.logical_not(from_out))
    def _():
        copy(qkv_ref.at[rest, rest_columns], rest_target, 1).start()

    places = chip_places(y, x)
    for k, place in enumerate((places[0], places[3])):
        rows = pl.ds(pl.multiple_of(place * MAIN, REST), MAIN)

        @pl.when(core == 0)
        def _():
            copy(qkv_ref.at[rows, pl.ds(0, depth)], second_ref.at[k], 2 + k).start()

        @pl.when(core == 1)
        def _():
            copy(out_ref.at[rows, :], second_ref.at[k], 2 + k).start()

    first_main.wait()
    copy(out_ref.at[rest, :], rest_target, 1).wait()
    for k in range(2):
        copy(out_ref.at[main, :], second_ref.at[k], 2 + k).wait()


def pieces_call(qkv_weight, out_weight):
    depth = out_weight.shape[1]
    outputs = [
        jax.ShapeDtypeStruct((MAIN + REST, depth), jnp.bfloat16),
        jax.ShapeDtypeStruct((2, MAIN, depth), jnp.bfloat16),
    ]
    return kernel_call(
        pieces_kernel,
        outputs,
        (qkv_weight, out_weight),
        [anywhere(), anywhere()],
        [pltpu.SemaphoreType.DMA((4,))],
        bytes_accessed=4 * (3 * MAIN + REST) * depth,
        limit=WHOLE_VMEM,
        out_spec=anywhere,
    )


def reorder_kernel(rows, tokens_ref, moved_ref):
    depth = tokens_ref.shape[1]
    width = 3 * LANES
    row = lax.broadcasted_iota(jnp.int32, (depth, width), 0)
    for at in range(0, depth, width):
        order = landed_order(at, width, rows)
        chosen = jnp.where(row == order, 1.0, 0.0).astype(jnp.bfloat16)
        moved = jnp.dot(tokens_ref[...], chosen, preferred_element_type=jnp.float32)
        moved_ref[:, at : at + width] = moved.astype(jnp.bfloat16)


def reorder_call(tokens, rows):
    depth = tokens.shape[1]
    return kernel_call(
        functools.partial(reorder_kernel, rows),
        jax.ShapeDtypeStruct(tokens.shape, jnp.bfloat16),
        (tokens,),
        [whole_vmem()],
        flops=2 * tokens.size * depth,
        bytes_accessed=2 * tokens.size,
    )


def first_kernel(*refs):
    tokens_ref, other_ref, qkv_ref, near_ref, away_ref, first_ref, far_ref, mine_ref = refs
    slots = (
        ((near_ref, 0), (first_ref, 0), (near_ref, 1)),
        ((near_ref, 2), (first_ref, 1), (near_ref, 3)),
        ((away_ref, 0), (far_ref, 0), (away_ref, 1)),
        ((away_ref, 2), (far_ref, 1), (away_ref, 3)),
    )
    _, x, core = coordinates()
    count, depth = tokens_ref.shape
    floor = jnp.where(core == 0, 0.0, -jnp.inf).astype(jnp.float32)
    width = 3 * LANES

    for at in range(0, depth, width):
        lanes = slice(at, at + width)

        def slot(k, low, high):
            return jnp.concatenate([ref[at, low:high, lanes] for ref, at in slots[k]], axis=0)

        def by_place(low, high):
            own, first, second, far = [slot(k, low, high) for k in range(4)]
            along_x = jnp.where(core == 0, first, second)
            along_y = jnp.where(core == 0, second, first)
            return own, along_x, along_y, far

        keys, values = [qkv_ref[:, depth * k + at : depth * k + at + width] for k in (1, 2)]
        own = jnp.where(core == 0, keys, values)
        rest = by_place(MAIN, MAIN + REST)
        even = jnp.concatenate([rest[0], rest[2]], axis=0)
        odd = jnp.concatenate([rest[1], rest[3]], axis=0)
        mine_ref[2 * count :, lanes] = jnp.where(x == 1, even, odd)
        columns = jnp.concatenate(
            (own,) + by_place(0, MAIN) + (jnp.where(x == 0, even, odd),), axis=0
        )
        for k, ref in enumerate((tokens_ref, other_ref)):
            product = jnp.dot(ref[...], columns, preferred_element_type=jnp.float32)
            product = jnp.maximum(product, floor).astype(jnp.bfloat16)
            mine_ref[k * count : (k + 1) * count, lanes] = product


def first_call(tokens, other, qkv_weight, *landed):
    count, depth = tokens.shape
    inputs = (tokens, other, qkv_weight) + landed
    return kernel_call(
        first_kernel,
        jax.ShapeDtypeStruct((2 * count + 2 * len(STEPS) * REST, depth), jnp.bfloat16),
        inputs,
        [whole_vmem()] * len(inputs),
        flops=4 * tokens.size * depth,
        bytes_accessed=2 * depth * depth,
    )


def diagonal_mask():
    rows = lax.broadcasted_iota(jnp.int32, (LANES, LANES), 0) // HEAD_DIM
    columns = lax.broadcasted_iota(jnp.int32, (LANES, LANES), 1) // HEAD_DIM
    return rows == columns


def state_kernel(mine_ref, other_ref, values_ref, top_ref, bottom_ref, upto_ref, total_ref):
    _, _, core = coordinates()
    mask = diagonal_mask()
    columns = top_ref.shape[1]
    count = values_ref.shape[0]
    later = jnp.where(core == 1, 1.0, 0.0).astype(jnp.float32)
    for group in range(mine_ref.shape[1] // LANES):
        at = slice(group * LANES, (group + 1) * LANES)

        def state(mine, other):
            keys = jnp.where(core == 0, mine, other)
            values = jnp.where(core == 0, other, mine)
            full = lax.dot_general(
                keys, values, (((0,), (0,)), ((), ())), preferred_element_type=jnp.float32
            )
            full = jnp.where(mask, full, 0.0)
            total = full[0:HEAD_DIM]
            for k in range(1, LANES // HEAD_DIM):
                total = total + full[k * HEAD_DIM : (k + 1) * HEAD_DIM]
            return total, values

        low, high = slice(0, count), slice(count, 2 * count)
        here, values = state(mine_ref[low, at], other_ref[high, at])
        there, _ = state(mine_ref[high, at], other_ref[low, at])
        values_ref[:, at] = values
        top_ref[0, :, at] = values[:columns]
        bottom_ref[0, :, at] = values[-columns:]
        upto_ref[group] = here + later * there
        total_ref[group] = (here + there).astype(jnp.bfloat16)


def state_call(mine, other, count, columns):
    depth = mine.shape[1]
    compact = (depth // LANES, HEAD_DIM, LANES)
    edge = jax.ShapeDtypeStruct((1, columns, depth), jnp.bfloat16)
    return kernel_call(
        state_kernel,
        [
            jax.ShapeDtypeStruct((count, depth), jnp.bfloat16),
            edge,
            edge,
            jax.ShapeDtypeStruct(compact, jnp.float32),
            jax.ShapeDtypeStruct(compact, jnp.bfloat16),
        ],
        (mine, other),
        [whole_vmem()] * 2,
        flops=4 * count * depth * LANES,
        bytes_accessed=8 * count * depth,
    )


def column_taps(sheet, taps):
    edge = jnp.zeros_like(sheet[:, :1])
    before = jnp.concatenate([edge, sheet[:, :-1]], axis=1)
    behind = jnp.concatenate([sheet[:, 1:], edge], axis=1)
    return taps[0] * before + taps[1] * sheet + taps[2] * behind


def local_kernel(values_ref, conv_ref, local_ref):
    rows, _, depth = values_ref.shape
    for at in range(0, depth, LANES):
        lanes = slice(at, at + LANES)
        taps = conv_ref[:, :, lanes]
        sheet = values_ref[:, :, lanes].astype(jnp.float32)
        local_ref[:, :, lanes] = column_taps(sheet, taps[1])
        local_ref[1:, :, lanes] = local_ref[1:, :, lanes] + column_taps(sheet[:-1], taps[0])
        local_ref[: rows - 1, :, lanes] = (
            local_ref[: rows - 1, :, lanes] + column_taps(sheet[1:], taps[2])
        )


def local_call(values, conv_weight):
    return kernel_call(
        local_kernel,
        jax.ShapeDtypeStruct(values.shape, jnp.float32),
        (values, conv_weight),
        [whole_vmem()] * 2,
        flops=18 * values.size,
        bytes_accessed=6 * values.size,
    )


def query_kernel(*refs):
    tokens_ref, qkv_ref, out_ref, *packs, ours_ref, other_ref, query_ref, weight_ref = refs
    y, x, core = coordinates()
    depth = tokens_ref.shape[1]
    rows = qkv_ref.shape[0]
    steps = len(STEPS)
    rest_at = ours_ref.shape[0] - 2 * steps * REST
    places = chip_places(y, x)
    width = 3 * LANES

    def block(of_core, index, lanes):
        pack, k = index
        mine_ref, theirs_ref = packs[2 * pack], packs[2 * pack + 1]
        return jnp.where(core == of_core, mine_ref[k, :, lanes], theirs_ref[k, :, lanes])


    def rest(of_core, lanes):
        return jnp.where(core == of_core, ours_ref[rest_at:, lanes], other_ref[rest_at:, lanes])

    def put(row, value, lanes):
        weight_ref[pl.ds(pl.multiple_of(row, REST), value.shape[0]), lanes] = value

    for at in range(0, depth, width):
        lanes = slice(at, at + width)
        order = [(0, 2 * k) for k in range(steps)] + [(1, k) for k in range(2 * steps)]
        order += [(0, 2 * k + 1) for k in range(steps)]
        columns = [qkv_ref[:, lanes]] + [block(0, k, lanes) for k in order] + [rest(0, lanes)]
        queries = jnp.dot(
            tokens_ref[...], jnp.concatenate(columns, axis=0), preferred_element_type=jnp.float32
        )
        query_ref[:, lanes] = jnp.maximum(queries, 0.0).astype(jnp.bfloat16)

        put(lax.axis_index("space") * rows, out_ref[:, lanes], lanes)
        tiles = rest(1, lanes)
        for k, step in enumerate(STEPS):
            base = source_plane(step) * rows
            held = ((0, 2 * k), (1, steps + k), (1, k), (0, 2 * k + 1))
            for place, index in zip(places, held):
                put(base + place * MAIN, block(1, index, lanes), lanes)
            for run, tile in enumerate((y, 1 - y)):
                start = (run * steps + k) * REST
                put(base + 4 * MAIN + tile * REST, tiles[start : start + REST], lanes)


def query_call(tokens, qkv_weight, out_weight, *landed):
    depth = tokens.shape[1]
    inputs = (tokens, qkv_weight, out_weight) + landed
    return kernel_call(
        query_kernel,
        [
            jax.ShapeDtypeStruct(tokens.shape, jnp.bfloat16),
            jax.ShapeDtypeStruct((depth, depth), jnp.bfloat16),
        ],
        inputs,
        [whole_vmem()] * len(inputs),
        flops=2 * tokens.size * depth,
        bytes_accessed=4 * depth * depth,
    )


def finish_kernel(*refs):
    queries_ref, weight_ref, state_ref, local_ref, above_ref, below_ref, *refs = refs
    conv_ref, gain_ref, result_ref, read_ref, mixture_ref = refs
    count, depth = queries_ref.shape
    columns = above_ref.shape[1]
    mask = diagonal_mask()
    square = jnp.zeros((count, LANES), jnp.float32)
    for group in range(depth // LANES):
        lanes = slice(group * LANES, (group + 1) * LANES)
        spread = jnp.concatenate([state_ref[group]] * (LANES // HEAD_DIM), axis=0)
        spread = jnp.where(mask, spread, 0.0).astype(jnp.bfloat16)
        read = jnp.dot(queries_ref[:, lanes], spread, preferred_element_type=jnp.float32)
        read_ref[:, lanes] = read
        square = square + read * read
    scale = lax.rsqrt(jnp.sum(square, axis=1, keepdims=True) / depth + 1e-06)
    for at in range(0, depth, LANES):
        lanes = slice(at, at + LANES)
        taps = conv_ref[:, :, lanes]
        mixture = read_ref[:, lanes] * scale * gain_ref[:, lanes] + local_ref[:, lanes]
        above = column_taps(above_ref[:, :, lanes].astype(jnp.float32), taps[0])[0]
        below = column_taps(below_ref[:, :, lanes].astype(jnp.float32), taps[2])[0]
        middle = mixture[columns : count - columns]
        mixture = jnp.concatenate(
            [mixture[:columns] + above, middle, mixture[count - columns :] + below], axis=0
        )
        mixture_ref[:, lanes] = mixture.astype(jnp.bfloat16)
    width = 3 * LANES
    for at in range(0, depth, width):
        lanes = slice(at, at + width)
        product = jnp.dot(
            mixture_ref[...], weight_ref[:, lanes], preferred_element_type=jnp.float32
        )
        result_ref[:, lanes] = product.astype(jnp.bfloat16)


def finish_call(queries, *inputs):
    return kernel_call(
        finish_kernel,
        jax.ShapeDtypeStruct(queries.shape, jnp.bfloat16),
        (queries,) + inputs,
        [whole_vmem()] * (1 + len(inputs)),
        [pltpu.VMEM(queries.shape, jnp.float32), pltpu.VMEM(queries.shape, jnp.bfloat16)],
        flops=2 * queries.size * queries.shape[1],
        bytes_accessed=2 * queries.shape[1] ** 2,
    )


def plane_form(video_tokens, qkv_weight, out_weight, conv_weight, norm_gain):
    frame_now = video_tokens[0]
    row_count, col_count, depth = frame_now.shape
    tokens = frame_now.reshape(row_count * col_count, depth)

    first_piece, second_piece = pieces_call(qkv_weight, out_weight)
    first_piece = first_piece[None]
    one = shifted(first_piece, 1)
    three = shifted(first_piece, -1)
    tokens = reorder_call(after(tokens, second_piece), qkv_weight.shape[0])
    other_tokens = flipped(tokens, (1, 1))
    one, three = after((one, three), tokens)

    pair = jnp.concatenate([one, three])
    two = shifted(one, 1)
    pair_first = flipped(pair, (2, 4))
    near = jnp.concatenate(after((pair, pair_first), other_tokens))
    away = flipped(near, (4, 2))
    two_near = jnp.concatenate([two, flipped(two, (2, 4))])
    two_away = flipped(two_near, (4, 2))

    second_ready = after(second_piece, one, three)
    second_one = shifted(second_ready, 1)
    second_three = shifted(second_ready, -1)
    second_two = shifted(after(second_one, two_near), 1)

    mine = first_call(after(tokens, second_one, second_three), other_tokens, qkv_weight, near, away, two_near, two_away)
    other = flipped(after(mine, second_two), (1, 1))
    straight = jnp.concatenate([second_one, second_two, second_three])
    swapped_straight = flipped(straight, (1, 1))
    values, top, bottom, upto, total = state_call(mine, other, tokens.shape[0], col_count)
    total = after(total, swapped_straight)

    second_own = jnp.stack([second_one[0], second_two[0], second_three[0]])
    second_first = flipped(second_own, (2, 4))
    second_second = flipped(after(second_own, total), (4, 2))

    for bit, guard in ((2, 2), (4, 4), (6, 4)):
        pairs = [(t, t ^ bit) for t in range(8) if not t & guard]
        upto = upto + lax.ppermute(total, "tm", pairs).astype(jnp.float32)
    count = lax.axis_size("space")
    forward = [(i, i + 1) for i in range(count - 1)]
    backward = [(target, source) for source, target in forward]
    state = after(upto, second_first)
    share = state.astype(jnp.bfloat16)
    grid = values.reshape(row_count, col_count, depth)
    local_term = local_call(grid, conv_weight).reshape(-1, depth)
    arrived = lax.ppermute(share, "space", [(i, i ^ 1) for i in range(count)])
    arrived = after(arrived, local_term)
    share = (share.astype(jnp.float32) + arrived.astype(jnp.float32)).astype(jnp.bfloat16)
    arrived = lax.ppermute(share, "space", [(i, i ^ 2) for i in range(count)])
    top, bottom = after((top, bottom), share)
    above = lax.ppermute(bottom, "space", forward)
    below = lax.ppermute(top, "space", backward)

    turned = jnp.concatenate([second_first, second_second])
    swapped_turned = flipped(after(turned, share), (1, 1))
    queries, weight = query_call(
        tokens,
        qkv_weight,
        out_weight,
        straight,
        swapped_straight,
        turned,
        swapped_turned,
        mine,
        other,
    )
    state = share.astype(jnp.float32) + arrived.astype(jnp.float32)
    above, below = after((above, below), queries, weight)
    result = finish_call(
        queries,
        weight,
        state,
        local_term,
        above,
        below,
        conv_weight,
        norm_gain[None],
    )
    return result.reshape(1, row_count, col_count, depth)


def solution(mesh):
    def per_device(video_tokens, qkv_weight, out_weight, conv_weight, norm_gain):
        fits = mesh.shape["tm"] == 8 and mesh.shape["space"] == 4
        fits = fits and qkv_weight.shape[0] == 4 * MAIN + 2 * REST
        form = plane_form if fits else general_form
        return form(video_tokens, qkv_weight, out_weight, conv_weight, norm_gain)

    in_specs = (P("tm", "space", None, None), P("space", None), P("space", None), P(), P())
    out_specs = P("tm", "space", None, None)
    return jax.shard_map(
        per_device, mesh=mesh, in_specs=in_specs, out_specs=out_specs, check_vma=False
    )
```

```python
import functools

import jax
import jax.numpy as jnp
from jax import lax
from jax.experimental import pallas as pl
from jax.experimental.pallas import tpu as pltpu
from jax.sharding import PartitionSpec as P

HEADS = 36
HEAD_DIM = 32
LANES = 128
MAIN = 64
REST = 16
STEPS = (1, 2, 3)
VMEM_LIMIT = 24 * 1024 * 1024
WHOLE_VMEM = 63 * 1024 * 1024


def entering(value, axis, combine, identity):
    devices, place = (lax.axis_size(axis), lax.axis_index(axis))
    everything = lax.all_gather(value.astype(jnp.bfloat16), axis)
    start = jnp.broadcast_to(jnp.asarray(identity, value.dtype), value.shape)

    def lap(k, before):
        reached = k < place
        new = combine(before, everything[k].astype(value.dtype))
        return jnp.where(reached, new, before)

    return lax.fori_loop(0, devices, lap, start)


def with_halo(block, sides, width):
    for axis, dim in sides:
        count = lax.axis_size(axis)
        forward = [(i, i + 1) for i in range(count - 1)]
        backward = [(target, source) for source, target in forward]
        low = lax.ppermute(
            lax.slice_in_dim(block, block.shape[dim] - width, None, axis=dim), axis, forward
        )
        high = lax.ppermute(lax.slice_in_dim(block, 0, width, axis=dim), axis, backward)
        block = jnp.concatenate([low, block, high], axis=dim)
    return block


def fold_product(left_side, block_rows):
    return jnp.dot(left_side, block_rows, preferred_element_type=jnp.float32)


def add_states(earlier, later):
    return earlier + later


def causal_states(key_feat, values):
    key_heads = key_feat.reshape(-1, HEADS, HEAD_DIM)
    value_heads = values.reshape(-1, HEADS, HEAD_DIM)
    frame_state = jnp.einsum(
        "thd,the->hde", key_heads, value_heads, preferred_element_type=jnp.float32
    )
    flat_state = frame_state.reshape(-1)
    frame_sum = lax.psum(flat_state.astype(jnp.bfloat16), "space").astype(jnp.float32)
    earlier = entering(frame_sum, "tm", add_states, jnp.zeros_like(frame_sum))
    whole_state = earlier + frame_sum
    return whole_state.reshape(HEADS, HEAD_DIM, HEAD_DIM)


def general_form(video_tokens, qkv_weight, out_weight, conv_weight, norm_gain):
    frame_now = video_tokens[0]
    row_count, col_count, feat_width = frame_now.shape
    tokens = frame_now.reshape(row_count * col_count, feat_width)
    projected = fold_product(tokens, lax.all_gather(qkv_weight, "space", axis=0, tiled=True))
    query_feat = jax.nn.relu(projected[:, :feat_width]).astype(jnp.bfloat16)
    key_feat = jax.nn.relu(projected[:, feat_width : 2 * feat_width]).astype(jnp.bfloat16)
    values = projected[:, 2 * feat_width :].astype(jnp.bfloat16)
    state_all = causal_states(key_feat, values)
    padded_rows = with_halo(values.reshape(row_count, col_count, feat_width), (("space", 0),), 1)
    padded = jnp.pad(padded_rows, ((0, 0), (1, 1), (0, 0))).astype(jnp.float32)
    local_term = jnp.zeros((row_count, col_count, feat_width), jnp.float32)
    for row_shift in range(3):
        for col_shift in range(3):
            local_term = (
                local_term
                + conv_weight[row_shift, col_shift]
                * padded[row_shift : row_shift + row_count, col_shift : col_shift + col_count]
            )
    state_low = state_all.astype(jnp.bfloat16)
    query_heads = query_feat.reshape(-1, HEADS, HEAD_DIM)
    readout = jnp.einsum("thd,hde->the", query_heads, state_low, preferred_element_type=jnp.float32)
    readout = readout.reshape(-1, feat_width)
    mean_square = jnp.mean(readout * readout, axis=-1, keepdims=True)
    normed = readout * lax.rsqrt(mean_square + 1e-06) * norm_gain
    mixture = (normed + local_term.reshape(-1, feat_width)).astype(jnp.bfloat16)
    result = fold_product(mixture, lax.all_gather(out_weight, "space", axis=0, tiled=True))
    return result.astype(jnp.bfloat16).reshape(1, row_count, col_count, feat_width)


def coordinates():
    place = lax.axis_index("tm")
    return lax.rem(place // 4, 2), lax.rem(place // 2, 2), lax.rem(place, 2)


def shifted(value, step):
    count = lax.axis_size("space")
    return lax.ppermute(value, "space", [(i, (i + step) % count) for i in range(count)])


def flipped(value, bit_on_core):
    return lax.ppermute(value, "tm", [(t, t ^ bit_on_core[t % 2]) for t in range(8)])


def after(value, *earlier):
    return lax.optimization_barrier((value,) + earlier)[0]


def chip_places(y, x):
    return (2 * y + x, 2 * y + (1 - x), 2 * (1 - y) + x, 2 * (1 - y) + (1 - x))


def source_plane(step):
    count = lax.axis_size("space")
    return lax.rem(lax.axis_index("space") - step + count, count)


def steps_through(within, size):
    run = sum(jnp.where(within >= size * k, 1, 0) for k in range(1, len(STEPS)))
    return run, within - size * run


def landed_order(at, width, rows):
    y, x, _ = coordinates()
    planes = [source_plane(step) for step in STEPS]
    row = at + lax.broadcasted_iota(jnp.int32, (1, width), 1)

    def pick(choices, index):
        chosen = choices[-1]
        for k in range(len(choices) - 2, -1, -1):
            chosen = jnp.where(index == k, choices[k], chosen)
        return chosen

    def landed(within, size, starts):
        count = len(STEPS) * size
        slot = sum(jnp.where(within >= count * k, 1, 0) for k in range(1, len(starts)))
        run, left = steps_through(within - count * slot, size)
        return pick(planes, run) * rows + pick(starts, slot) + left

    main = landed(row - rows, MAIN, [place * MAIN for place in chip_places(y, x)])
    rest_at = rows + 4 * len(STEPS) * MAIN
    rest = landed(row - rest_at, REST, [4 * MAIN + tile * REST for tile in (y, 1 - y)])
    own = lax.axis_index("space") * rows + row
    return jnp.where(row < rows, own, jnp.where(row < rest_at, main, rest))


def whole_vmem():
    return pl.BlockSpec(memory_space=pltpu.VMEM)


def anywhere():
    return pl.BlockSpec(memory_space=pltpu.HBM)


def kernel_call(
    body, outputs, inputs, in_specs, scratch=(), flops=0, bytes_accessed=0, limit=VMEM_LIMIT
):
    return pl.pallas_call(
        body,
        out_shape=outputs,
        in_specs=in_specs,
        out_specs=jax.tree.map(lambda _: whole_vmem(), outputs),
        scratch_shapes=list(scratch),
        compiler_params=pltpu.CompilerParams(vmem_limit_bytes=limit),
        cost_estimate=pl.CostEstimate(
            flops=flops, bytes_accessed=bytes_accessed, transcendentals=0
        ),
    )(*inputs)


def pieces_kernel(qkv_ref, out_ref, first_ref, second_ref, sems):
    y, x, core = coordinates()
    depth = out_ref.shape[1]
    main = pl.ds(pl.multiple_of((2 * y + x) * MAIN, REST), MAIN)
    rest = pl.ds(pl.multiple_of(4 * MAIN + y * REST, REST), REST)
    first_columns = pl.ds(pl.multiple_of(depth * (1 + core), LANES), depth)
    rest_columns = pl.ds(pl.multiple_of(jnp.where(x == 0, depth * (1 + core), 0), LANES), depth)

    def copy(source, target, k):
        return pltpu.make_async_copy(source, target, sems.at[k])

    first_main = copy(qkv_ref.at[main, first_columns], first_ref.at[pl.ds(0, MAIN), :], 0)
    first_main.start()
    rest_target = first_ref.at[pl.ds(MAIN, REST), :]
    from_out = (core == 1) & (x == 1)

    @pl.when(from_out)
    def _():
        copy(out_ref.at[rest, :], rest_target, 1).start()

    @pl.when(jnp.logical_not(from_out))
    def _():
        copy(qkv_ref.at[rest, rest_columns], rest_target, 1).start()

    places = chip_places(y, x)
    for k, place in enumerate((places[0], places[3])):
        rows = pl.ds(pl.multiple_of(place * MAIN, REST), MAIN)

        @pl.when(core == 0)
        def _():
            copy(qkv_ref.at[rows, pl.ds(0, depth)], second_ref.at[k], 2 + k).start()

        @pl.when(core == 1)
        def _():
            copy(out_ref.at[rows, :], second_ref.at[k], 2 + k).start()

    first_main.wait()
    copy(out_ref.at[rest, :], rest_target, 1).wait()
    for k in range(2):
        copy(out_ref.at[main, :], second_ref.at[k], 2 + k).wait()


def pieces_call(qkv_weight, out_weight):
    depth = out_weight.shape[1]
    outputs = [
        jax.ShapeDtypeStruct((MAIN + REST, depth), jnp.bfloat16),
        jax.ShapeDtypeStruct((2, MAIN, depth), jnp.bfloat16),
    ]
    return kernel_call(
        pieces_kernel,
        outputs,
        (qkv_weight, out_weight),
        [anywhere(), anywhere()],
        [pltpu.SemaphoreType.DMA((4,))],
        bytes_accessed=4 * (3 * MAIN + REST) * depth,
        limit=WHOLE_VMEM,
    )


def reorder_kernel(rows, tokens_ref, moved_ref):
    depth = tokens_ref.shape[1]
    width = 3 * LANES
    row = lax.broadcasted_iota(jnp.int32, (depth, width), 0)
    for at in range(0, depth, width):
        order = landed_order(at, width, rows)
        chosen = jnp.where(row == order, 1.0, 0.0).astype(jnp.bfloat16)
        moved = jnp.dot(tokens_ref[...], chosen, preferred_element_type=jnp.float32)
        moved_ref[:, at : at + width] = moved.astype(jnp.bfloat16)


def reorder_call(tokens, rows):
    depth = tokens.shape[1]
    return kernel_call(
        functools.partial(reorder_kernel, rows),
        jax.ShapeDtypeStruct(tokens.shape, jnp.bfloat16),
        (tokens,),
        [whole_vmem()],
        flops=2 * tokens.size * depth,
        bytes_accessed=2 * tokens.size,
    )


def first_kernel(*refs):
    tokens_ref, other_ref, qkv_ref, near_ref, away_ref, first_ref, far_ref, mine_ref = refs
    slots = (
        ((near_ref, 0), (first_ref, 0), (near_ref, 1)),
        ((near_ref, 2), (first_ref, 1), (near_ref, 3)),
        ((away_ref, 0), (far_ref, 0), (away_ref, 1)),
        ((away_ref, 2), (far_ref, 1), (away_ref, 3)),
    )
    _, x, core = coordinates()
    count, depth = tokens_ref.shape
    floor = jnp.where(core == 0, 0.0, -jnp.inf).astype(jnp.float32)
    width = 3 * LANES

    for at in range(0, depth, width):
        lanes = slice(at, at + width)

        def slot(k, low, high):
            return jnp.concatenate([ref[at, low:high, lanes] for ref, at in slots[k]], axis=0)

        def by_place(low, high):
            own, first, second, far = [slot(k, low, high) for k in range(4)]
            along_x = jnp.where(core == 0, first, second)
            along_y = jnp.where(core == 0, second, first)
            return own, along_x, along_y, far

        keys, values = [qkv_ref[:, depth * k + at : depth * k + at + width] for k in (1, 2)]
        own = jnp.where(core == 0, keys, values)
        rest = by_place(MAIN, MAIN + REST)
        even = jnp.concatenate([rest[0], rest[2]], axis=0)
        odd = jnp.concatenate([rest[1], rest[3]], axis=0)
        mine_ref[2 * count :, lanes] = jnp.where(x == 1, even, odd)
        columns = jnp.concatenate(
            (own,) + by_place(0, MAIN) + (jnp.where(x == 0, even, odd),), axis=0
        )
        for k, ref in enumerate((tokens_ref, other_ref)):
            product = jnp.dot(ref[...], columns, preferred_element_type=jnp.float32)
            product = jnp.maximum(product, floor).astype(jnp.bfloat16)
            mine_ref[k * count : (k + 1) * count, lanes] = product


def first_call(tokens, other, qkv_weight, *landed):
    count, depth = tokens.shape
    inputs = (tokens, other, qkv_weight) + landed
    return kernel_call(
        first_kernel,
        jax.ShapeDtypeStruct((2 * count + 2 * len(STEPS) * REST, depth), jnp.bfloat16),
        inputs,
        [whole_vmem()] * len(inputs),
        flops=4 * tokens.size * depth,
        bytes_accessed=2 * depth * depth,
    )


def diagonal_mask():
    rows = lax.broadcasted_iota(jnp.int32, (LANES, LANES), 0) // HEAD_DIM
    columns = lax.broadcasted_iota(jnp.int32, (LANES, LANES), 1) // HEAD_DIM
    return rows == columns


def state_kernel(mine_ref, other_ref, values_ref, top_ref, bottom_ref, upto_ref, total_ref):
    _, _, core = coordinates()
    mask = diagonal_mask()
    columns = top_ref.shape[1]
    count = values_ref.shape[0]
    later = jnp.where(core == 1, 1.0, 0.0).astype(jnp.float32)
    for group in range(mine_ref.shape[1] // LANES):
        at = slice(group * LANES, (group + 1) * LANES)

        def state(mine, other):
            keys = jnp.where(core == 0, mine, other)
            values = jnp.where(core == 0, other, mine)
            full = lax.dot_general(
                keys, values, (((0,), (0,)), ((), ())), preferred_element_type=jnp.float32
            )
            full = jnp.where(mask, full, 0.0)
            total = full[0:HEAD_DIM]
            for k in range(1, LANES // HEAD_DIM):
                total = total + full[k * HEAD_DIM : (k + 1) * HEAD_DIM]
            return total, values

        low, high = slice(0, count), slice(count, 2 * count)
        here, values = state(mine_ref[low, at], other_ref[high, at])
        there, _ = state(mine_ref[high, at], other_ref[low, at])
        values_ref[:, at] = values
        top_ref[0, :, at] = values[:columns]
        bottom_ref[0, :, at] = values[-columns:]
        upto_ref[group] = here + later * there
        total_ref[group] = (here + there).astype(jnp.bfloat16)


def state_call(mine, other, count, columns):
    depth = mine.shape[1]
    compact = (depth // LANES, HEAD_DIM, LANES)
    edge = jax.ShapeDtypeStruct((1, columns, depth), jnp.bfloat16)
    return kernel_call(
        state_kernel,
        [
            jax.ShapeDtypeStruct((count, depth), jnp.bfloat16),
            edge,
            edge,
            jax.ShapeDtypeStruct(compact, jnp.float32),
            jax.ShapeDtypeStruct(compact, jnp.bfloat16),
        ],
        (mine, other),
        [whole_vmem()] * 2,
        flops=4 * count * depth * LANES,
        bytes_accessed=8 * count * depth,
    )


def column_taps(sheet, taps):
    edge = jnp.zeros_like(sheet[:, :1])
    before = jnp.concatenate([edge, sheet[:, :-1]], axis=1)
    behind = jnp.concatenate([sheet[:, 1:], edge], axis=1)
    return taps[0] * before + taps[1] * sheet + taps[2] * behind


def local_kernel(values_ref, conv_ref, local_ref):
    rows, _, depth = values_ref.shape
    for at in range(0, depth, LANES):
        lanes = slice(at, at + LANES)
        taps = conv_ref[:, :, lanes]
        sheet = values_ref[:, :, lanes].astype(jnp.float32)
        local_ref[:, :, lanes] = column_taps(sheet, taps[1])
        local_ref[1:, :, lanes] = local_ref[1:, :, lanes] + column_taps(sheet[:-1], taps[0])
        local_ref[: rows - 1, :, lanes] = (
            local_ref[: rows - 1, :, lanes] + column_taps(sheet[1:], taps[2])
        )


def local_call(values, conv_weight):
    return kernel_call(
        local_kernel,
        jax.ShapeDtypeStruct(values.shape, jnp.float32),
        (values, conv_weight),
        [whole_vmem()] * 2,
        flops=18 * values.size,
        bytes_accessed=6 * values.size,
    )


def query_kernel(*refs):
    tokens_ref, qkv_ref, out_ref, *packs, ours_ref, other_ref, query_ref, weight_ref = refs
    y, x, core = coordinates()
    depth = tokens_ref.shape[1]
    rows = qkv_ref.shape[0]
    steps = len(STEPS)
    rest_at = ours_ref.shape[0] - 2 * steps * REST
    places = chip_places(y, x)
    width = 3 * LANES

    def block(of_core, index, lanes):
        pack, k = index
        mine_ref, theirs_ref = packs[2 * pack], packs[2 * pack + 1]
        return jnp.where(core == of_core, mine_ref[k, :, lanes], theirs_ref[k, :, lanes])


    def rest(of_core, lanes):
        return jnp.where(core == of_core, ours_ref[rest_at:, lanes], other_ref[rest_at:, lanes])

    def put(row, value, lanes):
        weight_ref[pl.ds(pl.multiple_of(row, REST), value.shape[0]), lanes] = value

    for at in range(0, depth, width):
        lanes = slice(at, at + width)
        order = [(0, 2 * k) for k in range(steps)] + [(1, k) for k in range(2 * steps)]
        order += [(0, 2 * k + 1) for k in range(steps)]
        columns = [qkv_ref[:, lanes]] + [block(0, k, lanes) for k in order] + [rest(0, lanes)]
        queries = jnp.dot(
            tokens_ref[...], jnp.concatenate(columns, axis=0), preferred_element_type=jnp.float32
        )
        query_ref[:, lanes] = jnp.maximum(queries, 0.0).astype(jnp.bfloat16)

        put(lax.axis_index("space") * rows, out_ref[:, lanes], lanes)
        tiles = rest(1, lanes)
        for k, step in enumerate(STEPS):
            base = source_plane(step) * rows
            held = ((0, 2 * k), (1, steps + k), (1, k), (0, 2 * k + 1))
            for place, index in zip(places, held):
                put(base + place * MAIN, block(1, index, lanes), lanes)
            for run, tile in enumerate((y, 1 - y)):
                start = (run * steps + k) * REST
                put(base + 4 * MAIN + tile * REST, tiles[start : start + REST], lanes)


def query_call(tokens, qkv_weight, out_weight, *landed):
    depth = tokens.shape[1]
    inputs = (tokens, qkv_weight, out_weight) + landed
    return kernel_call(
        query_kernel,
        [
            jax.ShapeDtypeStruct(tokens.shape, jnp.bfloat16),
            jax.ShapeDtypeStruct((depth, depth), jnp.bfloat16),
        ],
        inputs,
        [whole_vmem()] * len(inputs),
        flops=2 * tokens.size * depth,
        bytes_accessed=4 * depth * depth,
    )


def finish_kernel(*refs):
    queries_ref, weight_ref, state_ref, local_ref, above_ref, below_ref, *refs = refs
    conv_ref, gain_ref, result_ref, read_ref, mixture_ref = refs
    count, depth = queries_ref.shape
    columns = above_ref.shape[1]
    mask = diagonal_mask()
    square = jnp.zeros((count, LANES), jnp.float32)
    for group in range(depth // LANES):
        lanes = slice(group * LANES, (group + 1) * LANES)
        spread = jnp.concatenate([state_ref[group]] * (LANES // HEAD_DIM), axis=0)
        spread = jnp.where(mask, spread, 0.0).astype(jnp.bfloat16)
        read = jnp.dot(queries_ref[:, lanes], spread, preferred_element_type=jnp.float32)
        read_ref[:, lanes] = read
        square = square + read * read
    scale = lax.rsqrt(jnp.sum(square, axis=1, keepdims=True) / depth + 1e-06)
    for at in range(0, depth, LANES):
        lanes = slice(at, at + LANES)
        taps = conv_ref[:, :, lanes]
        mixture = read_ref[:, lanes] * scale * gain_ref[:, lanes] + local_ref[:, lanes]
        above = column_taps(above_ref[:, :, lanes].astype(jnp.float32), taps[0])[0]
        below = column_taps(below_ref[:, :, lanes].astype(jnp.float32), taps[2])[0]
        middle = mixture[columns : count - columns]
        mixture = jnp.concatenate(
            [mixture[:columns] + above, middle, mixture[count - columns :] + below], axis=0
        )
        mixture_ref[:, lanes] = mixture.astype(jnp.bfloat16)
    width = 3 * LANES
    for at in range(0, depth, width):
        lanes = slice(at, at + width)
        product = jnp.dot(
            mixture_ref[...], weight_ref[:, lanes], preferred_element_type=jnp.float32
        )
        result_ref[:, lanes] = product.astype(jnp.bfloat16)


def finish_call(queries, *inputs):
    return kernel_call(
        finish_kernel,
        jax.ShapeDtypeStruct(queries.shape, jnp.bfloat16),
        (queries,) + inputs,
        [whole_vmem()] * (1 + len(inputs)),
        [pltpu.VMEM(queries.shape, jnp.float32), pltpu.VMEM(queries.shape, jnp.bfloat16)],
        flops=2 * queries.size * queries.shape[1],
        bytes_accessed=2 * queries.shape[1] ** 2,
    )


def plane_form(video_tokens, qkv_weight, out_weight, conv_weight, norm_gain):
    frame_now = video_tokens[0]
    row_count, col_count, depth = frame_now.shape
    tokens = frame_now.reshape(row_count * col_count, depth)

    first_piece, second_piece = pieces_call(qkv_weight, out_weight)
    first_piece = first_piece[None]
    one = shifted(first_piece, 1)
    three = shifted(first_piece, -1)
    tokens = reorder_call(after(tokens, second_piece), qkv_weight.shape[0])
    other_tokens = flipped(tokens, (1, 1))
    one, three = after((one, three), tokens)

    pair = jnp.concatenate([one, three])
    two = shifted(one, 1)
    pair_first = flipped(pair, (2, 4))
    near = jnp.concatenate(after((pair, pair_first), other_tokens))
    away = flipped(near, (4, 2))
    two_near = jnp.concatenate([two, flipped(two, (2, 4))])
    two_away = flipped(two_near, (4, 2))

    second_ready = after(second_piece, one, three)
    second_one = shifted(second_ready, 1)
    second_three = shifted(second_ready, -1)
    second_two = shifted(after(second_one, two_near), 1)

    mine = first_call(after(tokens, second_one, second_three), other_tokens, qkv_weight, near, away, two_near, two_away)
    other = flipped(after(mine, second_two), (1, 1))
    straight = jnp.concatenate([second_one, second_two, second_three])
    swapped_straight = flipped(straight, (1, 1))
    values, top, bottom, upto, total = state_call(mine, other, tokens.shape[0], col_count)
    total = after(total, swapped_straight)

    second_own = jnp.stack([second_one[0], second_two[0], second_three[0]])
    second_first = flipped(second_own, (2, 4))
    second_second = flipped(second_own, (4, 2))

    for bit, guard in ((2, 2), (4, 4), (6, 4)):
        pairs = [(t, t ^ bit) for t in range(8) if not t & guard]
        upto = upto + lax.ppermute(total, "tm", pairs).astype(jnp.float32)
    count = lax.axis_size("space")
    forward = [(i, i + 1) for i in range(count - 1)]
    backward = [(target, source) for source, target in forward]
    state = after(upto, second_first, second_second)
    share = state.astype(jnp.bfloat16)
    grid = values.reshape(row_count, col_count, depth)
    local_term = local_call(grid, conv_weight).reshape(-1, depth)
    arrived = lax.ppermute(share, "space", [(i, i ^ 1) for i in range(count)])
    arrived = after(arrived, local_term)
    share = (share.astype(jnp.float32) + arrived.astype(jnp.float32)).astype(jnp.bfloat16)
    arrived = lax.ppermute(share, "space", [(i, i ^ 2) for i in range(count)])
    top, bottom = after((top, bottom), share)
    above = lax.ppermute(bottom, "space", forward)
    below = lax.ppermute(top, "space", backward)

    turned = jnp.concatenate(after((second_first, second_second), total))
    swapped_turned = flipped(after(turned, upto), (1, 1))
    queries, weight = query_call(
        tokens,
        qkv_weight,
        out_weight,
        straight,
        swapped_straight,
        turned,
        swapped_turned,
        mine,
        other,
    )
    state = share.astype(jnp.float32) + arrived.astype(jnp.float32)
    above, below = after((above, below), queries, weight)
    result = finish_call(
        queries,
        weight,
        state,
        local_term,
        above,
        below,
        conv_weight,
        norm_gain[None],
    )
    return result.reshape(1, row_count, col_count, depth)


def solution(mesh):
    def per_device(video_tokens, qkv_weight, out_weight, conv_weight, norm_gain):
        fits = mesh.shape["tm"] == 8 and mesh.shape["space"] == 4
        fits = fits and qkv_weight.shape[0] == 4 * MAIN + 2 * REST
        form = plane_form if fits else general_form
        return form(video_tokens, qkv_weight, out_weight, conv_weight, norm_gain)

    in_specs = (P("tm", "space", None, None), P("space", None), P("space", None), P(), P())
    out_specs = P("tm", "space", None, None)
    return jax.shard_map(
        per_device, mesh=mesh, in_specs=in_specs, out_specs=out_specs, check_vma=False
    )
```

```python
import functools

import jax
import jax.numpy as jnp
from jax import lax
from jax.experimental import pallas as pl
from jax.experimental.pallas import tpu as pltpu
from jax.sharding import PartitionSpec as P

HEADS = 36
HEAD_DIM = 32
LANES = 128
MAIN = 64
REST = 16
STEPS = (1, 2, 3)
VMEM_LIMIT = 24 * 1024 * 1024
WHOLE_VMEM = 63 * 1024 * 1024


def entering(value, axis, combine, identity):
    devices, place = (lax.axis_size(axis), lax.axis_index(axis))
    everything = lax.all_gather(value.astype(jnp.bfloat16), axis)
    start = jnp.broadcast_to(jnp.asarray(identity, value.dtype), value.shape)

    def lap(k, before):
        reached = k < place
        new = combine(before, everything[k].astype(value.dtype))
        return jnp.where(reached, new, before)

    return lax.fori_loop(0, devices, lap, start)


def with_halo(block, sides, width):
    for axis, dim in sides:
        count = lax.axis_size(axis)
        forward = [(i, i + 1) for i in range(count - 1)]
        backward = [(target, source) for source, target in forward]
        low = lax.ppermute(
            lax.slice_in_dim(block, block.shape[dim] - width, None, axis=dim), axis, forward
        )
        high = lax.ppermute(lax.slice_in_dim(block, 0, width, axis=dim), axis, backward)
        block = jnp.concatenate([low, block, high], axis=dim)
    return block


def fold_product(left_side, block_rows):
    return jnp.dot(left_side, block_rows, preferred_element_type=jnp.float32)


def add_states(earlier, later):
    return earlier + later


def causal_states(key_feat, values):
    key_heads = key_feat.reshape(-1, HEADS, HEAD_DIM)
    value_heads = values.reshape(-1, HEADS, HEAD_DIM)
    frame_state = jnp.einsum(
        "thd,the->hde", key_heads, value_heads, preferred_element_type=jnp.float32
    )
    flat_state = frame_state.reshape(-1)
    frame_sum = lax.psum(flat_state.astype(jnp.bfloat16), "space").astype(jnp.float32)
    earlier = entering(frame_sum, "tm", add_states, jnp.zeros_like(frame_sum))
    whole_state = earlier + frame_sum
    return whole_state.reshape(HEADS, HEAD_DIM, HEAD_DIM)


def general_form(video_tokens, qkv_weight, out_weight, conv_weight, norm_gain):
    frame_now = video_tokens[0]
    row_count, col_count, feat_width = frame_now.shape
    tokens = frame_now.reshape(row_count * col_count, feat_width)
    projected = fold_product(tokens, lax.all_gather(qkv_weight, "space", axis=0, tiled=True))
    query_feat = jax.nn.relu(projected[:, :feat_width]).astype(jnp.bfloat16)
    key_feat = jax.nn.relu(projected[:, feat_width : 2 * feat_width]).astype(jnp.bfloat16)
    values = projected[:, 2 * feat_width :].astype(jnp.bfloat16)
    state_all = causal_states(key_feat, values)
    padded_rows = with_halo(values.reshape(row_count, col_count, feat_width), (("space", 0),), 1)
    padded = jnp.pad(padded_rows, ((0, 0), (1, 1), (0, 0))).astype(jnp.float32)
    local_term = jnp.zeros((row_count, col_count, feat_width), jnp.float32)
    for row_shift in range(3):
        for col_shift in range(3):
            local_term = (
                local_term
                + conv_weight[row_shift, col_shift]
                * padded[row_shift : row_shift + row_count, col_shift : col_shift + col_count]
            )
    state_low = state_all.astype(jnp.bfloat16)
    query_heads = query_feat.reshape(-1, HEADS, HEAD_DIM)
    readout = jnp.einsum("thd,hde->the", query_heads, state_low, preferred_element_type=jnp.float32)
    readout = readout.reshape(-1, feat_width)
    mean_square = jnp.mean(readout * readout, axis=-1, keepdims=True)
    normed = readout * lax.rsqrt(mean_square + 1e-06) * norm_gain
    mixture = (normed + local_term.reshape(-1, feat_width)).astype(jnp.bfloat16)
    result = fold_product(mixture, lax.all_gather(out_weight, "space", axis=0, tiled=True))
    return result.astype(jnp.bfloat16).reshape(1, row_count, col_count, feat_width)


def coordinates():
    place = lax.axis_index("tm")
    return lax.rem(place // 4, 2), lax.rem(place // 2, 2), lax.rem(place, 2)


def shifted(value, step):
    count = lax.axis_size("space")
    return lax.ppermute(value, "space", [(i, (i + step) % count) for i in range(count)])


def flipped(value, bit_on_core):
    return lax.ppermute(value, "tm", [(t, t ^ bit_on_core[t % 2]) for t in range(8)])


def after(value, *earlier):
    return lax.optimization_barrier((value,) + earlier)[0]


def chip_places(y, x):
    return (2 * y + x, 2 * y + (1 - x), 2 * (1 - y) + x, 2 * (1 - y) + (1 - x))


def source_plane(step):
    count = lax.axis_size("space")
    return lax.rem(lax.axis_index("space") - step + count, count)


def steps_through(within, size):
    run = sum(jnp.where(within >= size * k, 1, 0) for k in range(1, len(STEPS)))
    return run, within - size * run


def landed_order(at, width, rows):
    y, x, _ = coordinates()
    planes = [source_plane(step) for step in STEPS]
    row = at + lax.broadcasted_iota(jnp.int32, (1, width), 1)

    def pick(choices, index):
        chosen = choices[-1]
        for k in range(len(choices) - 2, -1, -1):
            chosen = jnp.where(index == k, choices[k], chosen)
        return chosen

    def landed(within, size, starts):
        count = len(STEPS) * size
        slot = sum(jnp.where(within >= count * k, 1, 0) for k in range(1, len(starts)))
        run, left = steps_through(within - count * slot, size)
        return pick(planes, run) * rows + pick(starts, slot) + left

    main = landed(row - rows, MAIN, [place * MAIN for place in chip_places(y, x)])
    rest_at = rows + 4 * len(STEPS) * MAIN
    rest = landed(row - rest_at, REST, [4 * MAIN + tile * REST for tile in (y, 1 - y)])
    own = lax.axis_index("space") * rows + row
    return jnp.where(row < rows, own, jnp.where(row < rest_at, main, rest))


def whole_vmem():
    return pl.BlockSpec(memory_space=pltpu.VMEM)


def anywhere():
    return pl.BlockSpec(memory_space=pltpu.HBM)


def kernel_call(
    body, outputs, inputs, in_specs, scratch=(), flops=0, bytes_accessed=0, limit=VMEM_LIMIT
):
    return pl.pallas_call(
        body,
        out_shape=outputs,
        in_specs=in_specs,
        out_specs=jax.tree.map(lambda _: whole_vmem(), outputs),
        scratch_shapes=list(scratch),
        compiler_params=pltpu.CompilerParams(vmem_limit_bytes=limit),
        cost_estimate=pl.CostEstimate(
            flops=flops, bytes_accessed=bytes_accessed, transcendentals=0
        ),
    )(*inputs)


def pieces_kernel(qkv_ref, out_ref, first_ref, second_ref, sems):
    y, x, core = coordinates()
    depth = out_ref.shape[1]
    main = pl.ds(pl.multiple_of((2 * y + x) * MAIN, REST), MAIN)
    rest = pl.ds(pl.multiple_of(4 * MAIN + y * REST, REST), REST)
    first_columns = pl.ds(pl.multiple_of(depth * (1 + core), LANES), depth)
    rest_columns = pl.ds(pl.multiple_of(jnp.where(x == 0, depth * (1 + core), 0), LANES), depth)

    def copy(source, target, k):
        return pltpu.make_async_copy(source, target, sems.at[k])

    first_main = copy(qkv_ref.at[main, first_columns], first_ref.at[pl.ds(0, MAIN), :], 0)
    first_main.start()
    rest_target = first_ref.at[pl.ds(MAIN, REST), :]
    from_out = (core == 1) & (x == 1)

    @pl.when(from_out)
    def _():
        copy(out_ref.at[rest, :], rest_target, 1).start()

    @pl.when(jnp.logical_not(from_out))
    def _():
        copy(qkv_ref.at[rest, rest_columns], rest_target, 1).start()

    places = chip_places(y, x)
    for k, place in enumerate((places[0], places[3])):
        rows = pl.ds(pl.multiple_of(place * MAIN, REST), MAIN)

        @pl.when(core == 0)
        def _():
            copy(qkv_ref.at[rows, pl.ds(0, depth)], second_ref.at[k], 2 + k).start()

        @pl.when(core == 1)
        def _():
            copy(out_ref.at[rows, :], second_ref.at[k], 2 + k).start()

    first_main.wait()
    copy(out_ref.at[rest, :], rest_target, 1).wait()
    for k in range(2):
        copy(out_ref.at[main, :], second_ref.at[k], 2 + k).wait()


def pieces_call(qkv_weight, out_weight):
    depth = out_weight.shape[1]
    outputs = [
        jax.ShapeDtypeStruct((MAIN + REST, depth), jnp.bfloat16),
        jax.ShapeDtypeStruct((2, MAIN, depth), jnp.bfloat16),
    ]
    return kernel_call(
        pieces_kernel,
        outputs,
        (qkv_weight, out_weight),
        [anywhere(), anywhere()],
        [pltpu.SemaphoreType.DMA((4,))],
        bytes_accessed=4 * (3 * MAIN + REST) * depth,
        limit=WHOLE_VMEM,
    )


def reorder_kernel(rows, tokens_ref, moved_ref):
    depth = tokens_ref.shape[1]
    width = 3 * LANES
    row = lax.broadcasted_iota(jnp.int32, (depth, width), 0)
    for at in range(0, depth, width):
        order = landed_order(at, width, rows)
        chosen = jnp.where(row == order, 1.0, 0.0).astype(jnp.bfloat16)
        moved = jnp.dot(tokens_ref[...], chosen, preferred_element_type=jnp.float32)
        moved_ref[:, at : at + width] = moved.astype(jnp.bfloat16)


def reorder_call(tokens, rows):
    depth = tokens.shape[1]
    return kernel_call(
        functools.partial(reorder_kernel, rows),
        jax.ShapeDtypeStruct(tokens.shape, jnp.bfloat16),
        (tokens,),
        [whole_vmem()],
        flops=2 * tokens.size * depth,
        bytes_accessed=2 * tokens.size,
    )


def first_kernel(*refs):
    tokens_ref, other_ref, qkv_ref, near_ref, away_ref, first_ref, far_ref, mine_ref = refs
    slots = (
        ((near_ref, 0), (first_ref, 0), (near_ref, 1)),
        ((near_ref, 2), (first_ref, 1), (near_ref, 3)),
        ((away_ref, 0), (far_ref, 0), (away_ref, 1)),
        ((away_ref, 2), (far_ref, 1), (away_ref, 3)),
    )
    _, x, core = coordinates()
    count, depth = tokens_ref.shape
    floor = jnp.where(core == 0, 0.0, -jnp.inf).astype(jnp.float32)
    width = 3 * LANES

    for at in range(0, depth, width):
        lanes = slice(at, at + width)

        def slot(k, low, high):
            return jnp.concatenate([ref[at, low:high, lanes] for ref, at in slots[k]], axis=0)

        def by_place(low, high):
            own, first, second, far = [slot(k, low, high) for k in range(4)]
            along_x = jnp.where(core == 0, first, second)
            along_y = jnp.where(core == 0, second, first)
            return own, along_x, along_y, far

        keys, values = [qkv_ref[:, depth * k + at : depth * k + at + width] for k in (1, 2)]
        own = jnp.where(core == 0, keys, values)
        rest = by_place(MAIN, MAIN + REST)
        even = jnp.concatenate([rest[0], rest[2]], axis=0)
        odd = jnp.concatenate([rest[1], rest[3]], axis=0)
        mine_ref[2 * count :, lanes] = jnp.where(x == 1, even, odd)
        columns = jnp.concatenate(
            (own,) + by_place(0, MAIN) + (jnp.where(x == 0, even, odd),), axis=0
        )
        for k, ref in enumerate((tokens_ref, other_ref)):
            product = jnp.dot(ref[...], columns, preferred_element_type=jnp.float32)
            product = jnp.maximum(product, floor).astype(jnp.bfloat16)
            mine_ref[k * count : (k + 1) * count, lanes] = product


def first_call(tokens, other, qkv_weight, *landed):
    count, depth = tokens.shape
    inputs = (tokens, other, qkv_weight) + landed
    return kernel_call(
        first_kernel,
        jax.ShapeDtypeStruct((2 * count + 2 * len(STEPS) * REST, depth), jnp.bfloat16),
        inputs,
        [whole_vmem()] * len(inputs),
        flops=4 * tokens.size * depth,
        bytes_accessed=2 * depth * depth,
    )


def diagonal_mask():
    rows = lax.broadcasted_iota(jnp.int32, (LANES, LANES), 0) // HEAD_DIM
    columns = lax.broadcasted_iota(jnp.int32, (LANES, LANES), 1) // HEAD_DIM
    return rows == columns


def state_kernel(mine_ref, other_ref, values_ref, near_ref, next_ref, upto_ref, total_ref):
    even = lax.rem(lax.axis_index("space"), 2) == 0
    _, _, core = coordinates()
    mask = diagonal_mask()
    columns = near_ref.shape[1]
    count = values_ref.shape[0]
    later = jnp.where(core == 1, 1.0, 0.0).astype(jnp.float32)
    for group in range(mine_ref.shape[1] // LANES):
        at = slice(group * LANES, (group + 1) * LANES)

        def state(mine, other):
            keys = jnp.where(core == 0, mine, other)
            values = jnp.where(core == 0, other, mine)
            full = lax.dot_general(
                keys, values, (((0,), (0,)), ((), ())), preferred_element_type=jnp.float32
            )
            full = jnp.where(mask, full, 0.0)
            total = full[0:HEAD_DIM]
            for k in range(1, LANES // HEAD_DIM):
                total = total + full[k * HEAD_DIM : (k + 1) * HEAD_DIM]
            return total, values

        low, high = slice(0, count), slice(count, 2 * count)
        here, values = state(mine_ref[low, at], other_ref[high, at])
        there, _ = state(mine_ref[high, at], other_ref[low, at])
        values_ref[:, at] = values
        top, bottom = values[:columns], values[-columns:]
        near_ref[0, :, at] = jnp.where(even, bottom, top)
        next_ref[0, :, at] = jnp.where(even, top, bottom)
        upto_ref[group] = here + later * there
        total_ref[group] = (here + there).astype(jnp.bfloat16)


def state_call(mine, other, count, columns):
    depth = mine.shape[1]
    compact = (depth // LANES, HEAD_DIM, LANES)
    edge = jax.ShapeDtypeStruct((1, columns, depth), jnp.bfloat16)
    return kernel_call(
        state_kernel,
        [
            jax.ShapeDtypeStruct((count, depth), jnp.bfloat16),
            edge,
            edge,
            jax.ShapeDtypeStruct(compact, jnp.float32),
            jax.ShapeDtypeStruct(compact, jnp.bfloat16),
        ],
        (mine, other),
        [whole_vmem()] * 2,
        flops=4 * count * depth * LANES,
        bytes_accessed=8 * count * depth,
    )


def column_taps(sheet, taps):
    edge = jnp.zeros_like(sheet[:, :1])
    before = jnp.concatenate([edge, sheet[:, :-1]], axis=1)
    behind = jnp.concatenate([sheet[:, 1:], edge], axis=1)
    return taps[0] * before + taps[1] * sheet + taps[2] * behind


def local_kernel(values_ref, conv_ref, local_ref):
    rows, _, depth = values_ref.shape
    for at in range(0, depth, LANES):
        lanes = slice(at, at + LANES)
        taps = conv_ref[:, :, lanes]
        sheet = values_ref[:, :, lanes].astype(jnp.float32)
        local_ref[:, :, lanes] = column_taps(sheet, taps[1])
        local_ref[1:, :, lanes] = local_ref[1:, :, lanes] + column_taps(sheet[:-1], taps[0])
        local_ref[: rows - 1, :, lanes] = (
            local_ref[: rows - 1, :, lanes] + column_taps(sheet[1:], taps[2])
        )


def local_call(values, conv_weight):
    return kernel_call(
        local_kernel,
        jax.ShapeDtypeStruct(values.shape, jnp.float32),
        (values, conv_weight),
        [whole_vmem()] * 2,
        flops=18 * values.size,
        bytes_accessed=6 * values.size,
    )


def query_kernel(*refs):
    tokens_ref, qkv_ref, out_ref, *packs, ours_ref, other_ref, query_ref, weight_ref = refs
    y, x, core = coordinates()
    depth = tokens_ref.shape[1]
    rows = qkv_ref.shape[0]
    steps = len(STEPS)
    rest_at = ours_ref.shape[0] - 2 * steps * REST
    places = chip_places(y, x)
    width = 3 * LANES

    def block(of_core, index, lanes):
        pack, k = index
        mine_ref, theirs_ref = packs[2 * pack], packs[2 * pack + 1]
        return jnp.where(core == of_core, mine_ref[k, :, lanes], theirs_ref[k, :, lanes])


    def rest(of_core, lanes):
        return jnp.where(core == of_core, ours_ref[rest_at:, lanes], other_ref[rest_at:, lanes])

    def put(row, value, lanes):
        weight_ref[pl.ds(pl.multiple_of(row, REST), value.shape[0]), lanes] = value

    for at in range(0, depth, width):
        lanes = slice(at, at + width)
        order = [(0, 2 * k) for k in range(steps)] + [(1, k) for k in range(2 * steps)]
        order += [(0, 2 * k + 1) for k in range(steps)]
        columns = [qkv_ref[:, lanes]] + [block(0, k, lanes) for k in order] + [rest(0, lanes)]
        queries = jnp.dot(
            tokens_ref[...], jnp.concatenate(columns, axis=0), preferred_element_type=jnp.float32
        )
        query_ref[:, lanes] = jnp.maximum(queries, 0.0).astype(jnp.bfloat16)

        put(lax.axis_index("space") * rows, out_ref[:, lanes], lanes)
        tiles = rest(1, lanes)
        for k, step in enumerate(STEPS):
            base = source_plane(step) * rows
            held = ((0, 2 * k), (1, steps + k), (1, k), (0, 2 * k + 1))
            for place, index in zip(places, held):
                put(base + place * MAIN, block(1, index, lanes), lanes)
            for run, tile in enumerate((y, 1 - y)):
                start = (run * steps + k) * REST
                put(base + 4 * MAIN + tile * REST, tiles[start : start + REST], lanes)


def query_call(tokens, qkv_weight, out_weight, *landed):
    depth = tokens.shape[1]
    inputs = (tokens, qkv_weight, out_weight) + landed
    return kernel_call(
        query_kernel,
        [
            jax.ShapeDtypeStruct(tokens.shape, jnp.bfloat16),
            jax.ShapeDtypeStruct((depth, depth), jnp.bfloat16),
        ],
        inputs,
        [whole_vmem()] * len(inputs),
        flops=2 * tokens.size * depth,
        bytes_accessed=4 * depth * depth,
    )


def finish_kernel(*refs):
    queries_ref, weight_ref, state_ref, local_ref, near_ref, next_ref, *refs = refs
    conv_ref, gain_ref, result_ref, read_ref, mixture_ref = refs
    count, depth = queries_ref.shape
    columns = near_ref.shape[1]
    even = lax.rem(lax.axis_index("space"), 2) == 0
    mask = diagonal_mask()
    square = jnp.zeros((count, LANES), jnp.float32)
    for group in range(depth // LANES):
        lanes = slice(group * LANES, (group + 1) * LANES)
        spread = jnp.concatenate([state_ref[group]] * (LANES // HEAD_DIM), axis=0)
        spread = jnp.where(mask, spread, 0.0).astype(jnp.bfloat16)
        read = jnp.dot(queries_ref[:, lanes], spread, preferred_element_type=jnp.float32)
        read_ref[:, lanes] = read
        square = square + read * read
    scale = lax.rsqrt(jnp.sum(square, axis=1, keepdims=True) / depth + 1e-06)
    for at in range(0, depth, LANES):
        lanes = slice(at, at + LANES)
        taps = conv_ref[:, :, lanes]
        mixture = read_ref[:, lanes] * scale * gain_ref[:, lanes] + local_ref[:, lanes]
        near = near_ref[:, :, lanes].astype(jnp.float32)
        beyond = next_ref[:, :, lanes].astype(jnp.float32)
        above = column_taps(jnp.where(even, beyond, near), taps[0])[0]
        below = column_taps(jnp.where(even, near, beyond), taps[2])[0]
        middle = mixture[columns : count - columns]
        mixture = jnp.concatenate(
            [mixture[:columns] + above, middle, mixture[count - columns :] + below], axis=0
        )
        mixture_ref[:, lanes] = mixture.astype(jnp.bfloat16)
    width = 3 * LANES
    for at in range(0, depth, width):
        lanes = slice(at, at + width)
        product = jnp.dot(
            mixture_ref[...], weight_ref[:, lanes], preferred_element_type=jnp.float32
        )
        result_ref[:, lanes] = product.astype(jnp.bfloat16)


def finish_call(queries, *inputs):
    return kernel_call(
        finish_kernel,
        jax.ShapeDtypeStruct(queries.shape, jnp.bfloat16),
        (queries,) + inputs,
        [whole_vmem()] * (1 + len(inputs)),
        [pltpu.VMEM(queries.shape, jnp.float32), pltpu.VMEM(queries.shape, jnp.bfloat16)],
        flops=2 * queries.size * queries.shape[1],
        bytes_accessed=2 * queries.shape[1] ** 2,
    )


def plane_form(video_tokens, qkv_weight, out_weight, conv_weight, norm_gain):
    frame_now = video_tokens[0]
    row_count, col_count, depth = frame_now.shape
    tokens = frame_now.reshape(row_count * col_count, depth)

    first_piece, second_piece = pieces_call(qkv_weight, out_weight)
    first_piece = first_piece[None]
    one = shifted(first_piece, 1)
    three = shifted(first_piece, -1)
    tokens = reorder_call(after(tokens, second_piece), qkv_weight.shape[0])
    other_tokens = flipped(tokens, (1, 1))
    one, three = after((one, three), tokens)

    pair = jnp.concatenate([one, three])
    two = shifted(one, 1)
    pair_first = flipped(pair, (2, 4))
    near = jnp.concatenate(after((pair, pair_first), other_tokens))
    away = flipped(near, (4, 2))
    two_near = jnp.concatenate([two, flipped(two, (2, 4))])
    two_away = flipped(two_near, (4, 2))

    second_ready = after(second_piece, one, three)
    second_one = shifted(second_ready, 1)
    second_three = shifted(second_ready, -1)
    second_two = shifted(after(second_one, two_near), 1)

    mine = first_call(after(tokens, second_one, second_three), other_tokens, qkv_weight, near, away, two_near, two_away)
    other = flipped(after(mine, second_two), (1, 1))
    straight = jnp.concatenate([second_one, second_two, second_three])
    swapped_straight = flipped(straight, (1, 1))
    values, edge_near, edge_next, upto, total = state_call(mine, other, tokens.shape[0], col_count)
    total = after(total, swapped_straight)

    second_own = jnp.stack([second_one[0], second_two[0], second_three[0]])
    second_first = flipped(second_own, (2, 4))
    second_second = flipped(second_own, (4, 2))

    for bit, guard in ((2, 2), (4, 4), (6, 4)):
        pairs = [(t, t ^ bit) for t in range(8) if not t & guard]
        upto = upto + lax.ppermute(total, "tm", pairs).astype(jnp.float32)
    count = lax.axis_size("space")
    state = after(upto, second_first, second_second)
    share = state.astype(jnp.bfloat16)
    grid = values.reshape(row_count, col_count, depth)
    local_term = local_call(grid, conv_weight).reshape(-1, depth)
    arrived = lax.ppermute(share, "space", [(i, i ^ 1) for i in range(count)])
    arrived = after(arrived, local_term)
    share = (share.astype(jnp.float32) + arrived.astype(jnp.float32)).astype(jnp.bfloat16)
    arrived = lax.ppermute(share, "space", [(i, count - 1 - i) for i in range(count)])
    edge_near, edge_next = after((edge_near, edge_next), share)
    edge_near = lax.ppermute(edge_near, "space", [(i, i ^ 1) for i in range(count)])
    between = [(i, i + 1) for i in range(1, count - 1, 2)]
    between += [(target, source) for source, target in between]
    edge_next = lax.ppermute(edge_next, "space", between)

    turned = jnp.concatenate(after((second_first, second_second), total))
    swapped_turned = flipped(after(turned, upto), (1, 1))
    queries, weight = query_call(
        tokens,
        qkv_weight,
        out_weight,
        straight,
        swapped_straight,
        turned,
        swapped_turned,
        mine,
        other,
    )
    state = share.astype(jnp.float32) + arrived.astype(jnp.float32)
    edge_near, edge_next = after((edge_near, edge_next), queries, weight)
    result = finish_call(
        queries,
        weight,
        state,
        local_term,
        edge_near,
        edge_next,
        conv_weight,
        norm_gain[None],
    )
    return result.reshape(1, row_count, col_count, depth)


def solution(mesh):
    def per_device(video_tokens, qkv_weight, out_weight, conv_weight, norm_gain):
        fits = mesh.shape["tm"] == 8 and mesh.shape["space"] == 4
        fits = fits and qkv_weight.shape[0] == 4 * MAIN + 2 * REST
        form = plane_form if fits else general_form
        return form(video_tokens, qkv_weight, out_weight, conv_weight, norm_gain)

    in_specs = (P("tm", "space", None, None), P("space", None), P("space", None), P(), P())
    out_specs = P("tm", "space", None, None)
    return jax.shard_map(
        per_device, mesh=mesh, in_specs=in_specs, out_specs=out_specs, check_vma=False
    )
```

```python
import functools

import jax
import jax.numpy as jnp
from jax import lax
from jax.experimental import pallas as pl
from jax.experimental.pallas import tpu as pltpu
from jax.sharding import PartitionSpec as P

HEADS = 36
HEAD_DIM = 32
LANES = 128
MAIN = 64
REST = 16
STEPS = (1, 2, 3)
VMEM_LIMIT = 24 * 1024 * 1024
WHOLE_VMEM = 63 * 1024 * 1024


def entering(value, axis, combine, identity):
    devices, place = (lax.axis_size(axis), lax.axis_index(axis))
    everything = lax.all_gather(value.astype(jnp.bfloat16), axis)
    start = jnp.broadcast_to(jnp.asarray(identity, value.dtype), value.shape)

    def lap(k, before):
        reached = k < place
        new = combine(before, everything[k].astype(value.dtype))
        return jnp.where(reached, new, before)

    return lax.fori_loop(0, devices, lap, start)


def with_halo(block, sides, width):
    for axis, dim in sides:
        count = lax.axis_size(axis)
        forward = [(i, i + 1) for i in range(count - 1)]
        backward = [(target, source) for source, target in forward]
        low = lax.ppermute(
            lax.slice_in_dim(block, block.shape[dim] - width, None, axis=dim), axis, forward
        )
        high = lax.ppermute(lax.slice_in_dim(block, 0, width, axis=dim), axis, backward)
        block = jnp.concatenate([low, block, high], axis=dim)
    return block


def fold_product(left_side, block_rows):
    return jnp.dot(left_side, block_rows, preferred_element_type=jnp.float32)


def add_states(earlier, later):
    return earlier + later


def causal_states(key_feat, values):
    key_heads = key_feat.reshape(-1, HEADS, HEAD_DIM)
    value_heads = values.reshape(-1, HEADS, HEAD_DIM)
    frame_state = jnp.einsum(
        "thd,the->hde", key_heads, value_heads, preferred_element_type=jnp.float32
    )
    flat_state = frame_state.reshape(-1)
    frame_sum = lax.psum(flat_state.astype(jnp.bfloat16), "space").astype(jnp.float32)
    earlier = entering(frame_sum, "tm", add_states, jnp.zeros_like(frame_sum))
    whole_state = earlier + frame_sum
    return whole_state.reshape(HEADS, HEAD_DIM, HEAD_DIM)


def general_form(video_tokens, qkv_weight, out_weight, conv_weight, norm_gain):
    frame_now = video_tokens[0]
    row_count, col_count, feat_width = frame_now.shape
    tokens = frame_now.reshape(row_count * col_count, feat_width)
    projected = fold_product(tokens, lax.all_gather(qkv_weight, "space", axis=0, tiled=True))
    query_feat = jax.nn.relu(projected[:, :feat_width]).astype(jnp.bfloat16)
    key_feat = jax.nn.relu(projected[:, feat_width : 2 * feat_width]).astype(jnp.bfloat16)
    values = projected[:, 2 * feat_width :].astype(jnp.bfloat16)
    state_all = causal_states(key_feat, values)
    padded_rows = with_halo(values.reshape(row_count, col_count, feat_width), (("space", 0),), 1)
    padded = jnp.pad(padded_rows, ((0, 0), (1, 1), (0, 0))).astype(jnp.float32)
    local_term = jnp.zeros((row_count, col_count, feat_width), jnp.float32)
    for row_shift in range(3):
        for col_shift in range(3):
            local_term = (
                local_term
                + conv_weight[row_shift, col_shift]
                * padded[row_shift : row_shift + row_count, col_shift : col_shift + col_count]
            )
    state_low = state_all.astype(jnp.bfloat16)
    query_heads = query_feat.reshape(-1, HEADS, HEAD_DIM)
    readout = jnp.einsum("thd,hde->the", query_heads, state_low, preferred_element_type=jnp.float32)
    readout = readout.reshape(-1, feat_width)
    mean_square = jnp.mean(readout * readout, axis=-1, keepdims=True)
    normed = readout * lax.rsqrt(mean_square + 1e-06) * norm_gain
    mixture = (normed + local_term.reshape(-1, feat_width)).astype(jnp.bfloat16)
    result = fold_product(mixture, lax.all_gather(out_weight, "space", axis=0, tiled=True))
    return result.astype(jnp.bfloat16).reshape(1, row_count, col_count, feat_width)


def coordinates():
    place = lax.axis_index("tm")
    return lax.rem(place // 4, 2), lax.rem(place // 2, 2), lax.rem(place, 2)


def shifted(value, step):
    count = lax.axis_size("space")
    return lax.ppermute(value, "space", [(i, (i + step) % count) for i in range(count)])


def flipped(value, bit_on_core):
    return lax.ppermute(value, "tm", [(t, t ^ bit_on_core[t % 2]) for t in range(8)])


def after(value, *earlier):
    return lax.optimization_barrier((value,) + earlier)[0]


def chip_places(y, x):
    return (2 * y + x, 2 * y + (1 - x), 2 * (1 - y) + x, 2 * (1 - y) + (1 - x))


def source_plane(step):
    count = lax.axis_size("space")
    return lax.rem(lax.axis_index("space") - step + count, count)


def steps_through(within, size):
    run = sum(jnp.where(within >= size * k, 1, 0) for k in range(1, len(STEPS)))
    return run, within - size * run


def landed_order(at, width, rows):
    y, x, _ = coordinates()
    planes = [source_plane(step) for step in STEPS]
    row = at + lax.broadcasted_iota(jnp.int32, (1, width), 1)

    def pick(choices, index):
        chosen = choices[-1]
        for k in range(len(choices) - 2, -1, -1):
            chosen = jnp.where(index == k, choices[k], chosen)
        return chosen

    def landed(within, size, starts):
        count = len(STEPS) * size
        slot = sum(jnp.where(within >= count * k, 1, 0) for k in range(1, len(starts)))
        run, left = steps_through(within - count * slot, size)
        return pick(planes, run) * rows + pick(starts, slot) + left

    main = landed(row - rows, MAIN, [place * MAIN for place in chip_places(y, x)])
    rest_at = rows + 4 * len(STEPS) * MAIN
    rest = landed(row - rest_at, REST, [4 * MAIN + tile * REST for tile in (y, 1 - y)])
    own = lax.axis_index("space") * rows + row
    return jnp.where(row < rows, own, jnp.where(row < rest_at, main, rest))


def whole_vmem():
    return pl.BlockSpec(memory_space=pltpu.VMEM)


def anywhere():
    return pl.BlockSpec(memory_space=pltpu.HBM)


def kernel_call(
    body, outputs, inputs, in_specs, scratch=(), flops=0, bytes_accessed=0, limit=VMEM_LIMIT
):
    return pl.pallas_call(
        body,
        out_shape=outputs,
        in_specs=in_specs,
        out_specs=jax.tree.map(lambda _: whole_vmem(), outputs),
        scratch_shapes=list(scratch),
        compiler_params=pltpu.CompilerParams(vmem_limit_bytes=limit),
        cost_estimate=pl.CostEstimate(
            flops=flops, bytes_accessed=bytes_accessed, transcendentals=0
        ),
    )(*inputs)


def pieces_kernel(qkv_ref, out_ref, first_ref, second_ref, sems):
    y, x, core = coordinates()
    depth = out_ref.shape[1]
    main = pl.ds(pl.multiple_of((2 * y + x) * MAIN, REST), MAIN)
    rest = pl.ds(pl.multiple_of(4 * MAIN + y * REST, REST), REST)
    first_columns = pl.ds(pl.multiple_of(depth * (1 + core), LANES), depth)
    rest_columns = pl.ds(pl.multiple_of(jnp.where(x == 0, depth * (1 + core), 0), LANES), depth)

    def copy(source, target, k):
        return pltpu.make_async_copy(source, target, sems.at[k])

    first_main = copy(qkv_ref.at[main, first_columns], first_ref.at[pl.ds(0, MAIN), :], 0)
    first_main.start()
    rest_target = first_ref.at[pl.ds(MAIN, REST), :]
    from_out = (core == 1) & (x == 1)

    @pl.when(from_out)
    def _():
        copy(out_ref.at[rest, :], rest_target, 1).start()

    @pl.when(jnp.logical_not(from_out))
    def _():
        copy(qkv_ref.at[rest, rest_columns], rest_target, 1).start()

    places = chip_places(y, x)
    for k, place in enumerate((places[0], places[3])):
        rows = pl.ds(pl.multiple_of(place * MAIN, REST), MAIN)

        @pl.when(core == 0)
        def _():
            copy(qkv_ref.at[rows, pl.ds(0, depth)], second_ref.at[k], 2 + k).start()

        @pl.when(core == 1)
        def _():
            copy(out_ref.at[rows, :], second_ref.at[k], 2 + k).start()

    first_main.wait()
    copy(out_ref.at[rest, :], rest_target, 1).wait()
    for k in range(2):
        copy(out_ref.at[main, :], second_ref.at[k], 2 + k).wait()


def pieces_call(qkv_weight, out_weight):
    depth = out_weight.shape[1]
    outputs = [
        jax.ShapeDtypeStruct((MAIN + REST, depth), jnp.bfloat16),
        jax.ShapeDtypeStruct((2, MAIN, depth), jnp.bfloat16),
    ]
    return kernel_call(
        pieces_kernel,
        outputs,
        (qkv_weight, out_weight),
        [anywhere(), anywhere()],
        [pltpu.SemaphoreType.DMA((4,))],
        bytes_accessed=4 * (3 * MAIN + REST) * depth,
        limit=WHOLE_VMEM,
    )


def reorder_kernel(rows, tokens_ref, moved_ref):
    depth = tokens_ref.shape[1]
    width = 3 * LANES
    row = lax.broadcasted_iota(jnp.int32, (depth, width), 0)
    for at in range(0, depth, width):
        order = landed_order(at, width, rows)
        chosen = jnp.where(row == order, 1.0, 0.0).astype(jnp.bfloat16)
        moved = jnp.dot(tokens_ref[...], chosen, preferred_element_type=jnp.float32)
        moved_ref[:, at : at + width] = moved.astype(jnp.bfloat16)


def reorder_call(tokens, rows):
    depth = tokens.shape[1]
    return kernel_call(
        functools.partial(reorder_kernel, rows),
        jax.ShapeDtypeStruct(tokens.shape, jnp.bfloat16),
        (tokens,),
        [whole_vmem()],
        flops=2 * tokens.size * depth,
        bytes_accessed=2 * tokens.size,
    )


def first_kernel(*refs):
    tokens_ref, other_ref, qkv_ref, near_ref, away_ref, first_ref, far_ref, mine_ref = refs
    slots = (
        ((near_ref, 0), (first_ref, 0), (near_ref, 1)),
        ((near_ref, 2), (first_ref, 1), (near_ref, 3)),
        ((away_ref, 0), (far_ref, 0), (away_ref, 1)),
        ((away_ref, 2), (far_ref, 1), (away_ref, 3)),
    )
    _, x, core = coordinates()
    count, depth = tokens_ref.shape
    floor = jnp.where(core == 0, 0.0, -jnp.inf).astype(jnp.float32)
    width = 3 * LANES

    for at in range(0, depth, width):
        lanes = slice(at, at + width)

        def slot(k, low, high):
            return jnp.concatenate([ref[at, low:high, lanes] for ref, at in slots[k]], axis=0)

        def by_place(low, high):
            own, first, second, far = [slot(k, low, high) for k in range(4)]
            along_x = jnp.where(core == 0, first, second)
            along_y = jnp.where(core == 0, second, first)
            return own, along_x, along_y, far

        keys, values = [qkv_ref[:, depth * k + at : depth * k + at + width] for k in (1, 2)]
        own = jnp.where(core == 0, keys, values)
        rest = by_place(MAIN, MAIN + REST)
        even = jnp.concatenate([rest[0], rest[2]], axis=0)
        odd = jnp.concatenate([rest[1], rest[3]], axis=0)
        mine_ref[2 * count :, lanes] = jnp.where(x == 1, even, odd)
        columns = jnp.concatenate(
            (own,) + by_place(0, MAIN) + (jnp.where(x == 0, even, odd),), axis=0
        )
        for k, ref in enumerate((tokens_ref, other_ref)):
            product = jnp.dot(ref[...], columns, preferred_element_type=jnp.float32)
            product = jnp.maximum(product, floor).astype(jnp.bfloat16)
            mine_ref[k * count : (k + 1) * count, lanes] = product


def first_call(tokens, other, qkv_weight, *landed):
    count, depth = tokens.shape
    inputs = (tokens, other, qkv_weight) + landed
    return kernel_call(
        first_kernel,
        jax.ShapeDtypeStruct((2 * count + 2 * len(STEPS) * REST, depth), jnp.bfloat16),
        inputs,
        [whole_vmem()] * len(inputs),
        flops=4 * tokens.size * depth,
        bytes_accessed=2 * depth * depth,
    )


def diagonal_mask():
    rows = lax.broadcasted_iota(jnp.int32, (LANES, LANES), 0) // HEAD_DIM
    columns = lax.broadcasted_iota(jnp.int32, (LANES, LANES), 1) // HEAD_DIM
    return rows == columns


def state_kernel(mine_ref, other_ref, values_ref, near_ref, next_ref, upto_ref, total_ref):
    even = lax.rem(lax.axis_index("space"), 2) == 0
    _, _, core = coordinates()
    mask = diagonal_mask()
    columns = near_ref.shape[1]
    count = values_ref.shape[0]
    later = jnp.where(core == 1, 1.0, 0.0).astype(jnp.float32)
    for group in range(mine_ref.shape[1] // LANES):
        at = slice(group * LANES, (group + 1) * LANES)

        def state(mine, other):
            keys = jnp.where(core == 0, mine, other)
            values = jnp.where(core == 0, other, mine)
            full = lax.dot_general(
                keys, values, (((0,), (0,)), ((), ())), preferred_element_type=jnp.float32
            )
            full = jnp.where(mask, full, 0.0)
            total = full[0:HEAD_DIM]
            for k in range(1, LANES // HEAD_DIM):
                total = total + full[k * HEAD_DIM : (k + 1) * HEAD_DIM]
            return total, values

        low, high = slice(0, count), slice(count, 2 * count)
        here, values = state(mine_ref[low, at], other_ref[high, at])
        there, _ = state(mine_ref[high, at], other_ref[low, at])
        values_ref[:, at] = values
        top, bottom = values[:columns], values[-columns:]
        near_ref[0, :, at] = jnp.where(even, bottom, top)
        next_ref[0, :, at] = jnp.where(even, top, bottom)
        upto_ref[group] = here + later * there
        total_ref[group] = (here + there).astype(jnp.bfloat16)


def state_call(mine, other, count, columns):
    depth = mine.shape[1]
    compact = (depth // LANES, HEAD_DIM, LANES)
    edge = jax.ShapeDtypeStruct((1, columns, depth), jnp.bfloat16)
    return kernel_call(
        state_kernel,
        [
            jax.ShapeDtypeStruct((count, depth), jnp.bfloat16),
            edge,
            edge,
            jax.ShapeDtypeStruct(compact, jnp.float32),
            jax.ShapeDtypeStruct(compact, jnp.bfloat16),
        ],
        (mine, other),
        [whole_vmem()] * 2,
        flops=4 * count * depth * LANES,
        bytes_accessed=8 * count * depth,
    )


def column_taps(sheet, taps):
    edge = jnp.zeros_like(sheet[:, :1])
    before = jnp.concatenate([edge, sheet[:, :-1]], axis=1)
    behind = jnp.concatenate([sheet[:, 1:], edge], axis=1)
    return taps[0] * before + taps[1] * sheet + taps[2] * behind


def local_kernel(values_ref, conv_ref, local_ref):
    rows, _, depth = values_ref.shape
    for at in range(0, depth, LANES):
        lanes = slice(at, at + LANES)
        taps = conv_ref[:, :, lanes]
        sheet = values_ref[:, :, lanes].astype(jnp.float32)
        local_ref[:, :, lanes] = column_taps(sheet, taps[1])
        local_ref[1:, :, lanes] = local_ref[1:, :, lanes] + column_taps(sheet[:-1], taps[0])
        local_ref[: rows - 1, :, lanes] = (
            local_ref[: rows - 1, :, lanes] + column_taps(sheet[1:], taps[2])
        )


def local_call(values, conv_weight):
    return kernel_call(
        local_kernel,
        jax.ShapeDtypeStruct(values.shape, jnp.float32),
        (values, conv_weight),
        [whole_vmem()] * 2,
        flops=18 * values.size,
        bytes_accessed=6 * values.size,
    )


def query_kernel(*refs):
    tokens_ref, qkv_ref, out_ref, *packs, ours_ref, other_ref, query_ref, weight_ref = refs
    y, x, core = coordinates()
    depth = tokens_ref.shape[1]
    rows = qkv_ref.shape[0]
    steps = len(STEPS)
    rest_at = ours_ref.shape[0] - 2 * steps * REST
    places = chip_places(y, x)
    width = 3 * LANES

    def block(of_core, index, lanes):
        pack, k = index
        mine_ref, theirs_ref = packs[2 * pack], packs[2 * pack + 1]
        return jnp.where(core == of_core, mine_ref[k, :, lanes], theirs_ref[k, :, lanes])


    def rest(of_core, lanes):
        return jnp.where(core == of_core, ours_ref[rest_at:, lanes], other_ref[rest_at:, lanes])

    def put(row, value, lanes):
        weight_ref[pl.ds(pl.multiple_of(row, REST), value.shape[0]), lanes] = value

    for at in range(0, depth, width):
        lanes = slice(at, at + width)
        order = [(0, 2 * k) for k in range(steps)] + [(1, k) for k in range(2 * steps)]
        order += [(0, 2 * k + 1) for k in range(steps)]
        columns = [qkv_ref[:, lanes]] + [block(0, k, lanes) for k in order] + [rest(0, lanes)]
        queries = jnp.dot(
            tokens_ref[...], jnp.concatenate(columns, axis=0), preferred_element_type=jnp.float32
        )
        query_ref[:, lanes] = jnp.maximum(queries, 0.0).astype(jnp.bfloat16)

        put(lax.axis_index("space") * rows, out_ref[:, lanes], lanes)
        tiles = rest(1, lanes)
        for k, step in enumerate(STEPS):
            base = source_plane(step) * rows
            held = ((0, 2 * k), (1, steps + k), (1, k), (0, 2 * k + 1))
            for place, index in zip(places, held):
                put(base + place * MAIN, block(1, index, lanes), lanes)
            for run, tile in enumerate((y, 1 - y)):
                start = (run * steps + k) * REST
                put(base + 4 * MAIN + tile * REST, tiles[start : start + REST], lanes)


def query_call(tokens, qkv_weight, out_weight, *landed):
    depth = tokens.shape[1]
    inputs = (tokens, qkv_weight, out_weight) + landed
    return kernel_call(
        query_kernel,
        [
            jax.ShapeDtypeStruct(tokens.shape, jnp.bfloat16),
            jax.ShapeDtypeStruct((depth, depth), jnp.bfloat16),
        ],
        inputs,
        [whole_vmem()] * len(inputs),
        flops=2 * tokens.size * depth,
        bytes_accessed=4 * depth * depth,
    )


def finish_kernel(*refs):
    queries_ref, weight_ref, state_ref, local_ref, near_ref, next_ref, *refs = refs
    conv_ref, gain_ref, result_ref, read_ref, mixture_ref = refs
    count, depth = queries_ref.shape
    columns = near_ref.shape[1]
    even = lax.rem(lax.axis_index("space"), 2) == 0
    mask = diagonal_mask()
    square = jnp.zeros((count, LANES), jnp.float32)
    for group in range(depth // LANES):
        lanes = slice(group * LANES, (group + 1) * LANES)
        spread = jnp.concatenate([state_ref[group]] * (LANES // HEAD_DIM), axis=0)
        spread = jnp.where(mask, spread, 0.0).astype(jnp.bfloat16)
        read = jnp.dot(queries_ref[:, lanes], spread, preferred_element_type=jnp.float32)
        read_ref[:, lanes] = read
        square = square + read * read
    scale = lax.rsqrt(jnp.sum(square, axis=1, keepdims=True) / depth + 1e-06)
    for at in range(0, depth, LANES):
        lanes = slice(at, at + LANES)
        taps = conv_ref[:, :, lanes]
        mixture = read_ref[:, lanes] * scale * gain_ref[:, lanes] + local_ref[:, lanes]
        near = near_ref[:, :, lanes].astype(jnp.float32)
        beyond = next_ref[:, :, lanes].astype(jnp.float32)
        above = column_taps(jnp.where(even, beyond, near), taps[0])[0]
        below = column_taps(jnp.where(even, near, beyond), taps[2])[0]
        middle = mixture[columns : count - columns]
        mixture = jnp.concatenate(
            [mixture[:columns] + above, middle, mixture[count - columns :] + below], axis=0
        )
        mixture_ref[:, lanes] = mixture.astype(jnp.bfloat16)
    width = 3 * LANES
    for at in range(0, depth, width):
        lanes = slice(at, at + width)
        product = jnp.dot(
            mixture_ref[...], weight_ref[:, lanes], preferred_element_type=jnp.float32
        )
        result_ref[:, lanes] = product.astype(jnp.bfloat16)


def finish_call(queries, *inputs):
    return kernel_call(
        finish_kernel,
        jax.ShapeDtypeStruct(queries.shape, jnp.bfloat16),
        (queries,) + inputs,
        [whole_vmem()] * (1 + len(inputs)),
        [pltpu.VMEM(queries.shape, jnp.float32), pltpu.VMEM(queries.shape, jnp.bfloat16)],
        flops=2 * queries.size * queries.shape[1],
        bytes_accessed=2 * queries.shape[1] ** 2,
    )


def plane_form(video_tokens, qkv_weight, out_weight, conv_weight, norm_gain):
    frame_now = video_tokens[0]
    row_count, col_count, depth = frame_now.shape
    tokens = frame_now.reshape(row_count * col_count, depth)

    first_piece, second_piece = pieces_call(qkv_weight, out_weight)
    first_piece = first_piece[None]
    one = shifted(first_piece, 1)
    three = shifted(first_piece, -1)
    tokens = reorder_call(after(tokens, second_piece), qkv_weight.shape[0])
    other_tokens = flipped(tokens, (1, 1))
    one, three = after((one, three), tokens)

    pair = jnp.concatenate([one, three])
    two = shifted(one, 1)
    pair_first = flipped(pair, (2, 4))
    near = jnp.concatenate(after((pair, pair_first), other_tokens))
    away = flipped(near, (4, 2))
    two_near = jnp.concatenate([two, flipped(two, (2, 4))])
    two_away = flipped(two_near, (4, 2))

    second_ready = after(second_piece, one, three)
    second_one = shifted(second_ready, 1)
    second_three = shifted(second_ready, -1)
    second_two = shifted(after(second_one, two_near), 1)

    mine = first_call(after(tokens, second_one, second_three), other_tokens, qkv_weight, near, away, two_near, two_away)
    other = flipped(after(mine, second_two), (1, 1))
    straight = jnp.concatenate([second_one, second_two, second_three])
    swapped_straight = flipped(straight, (1, 1))
    values, edge_near, edge_next, upto, total = state_call(mine, other, tokens.shape[0], col_count)
    total = after(total, swapped_straight)

    second_own = jnp.stack([second_one[0], second_two[0], second_three[0]])
    second_first = flipped(second_own, (2, 4))
    second_second = flipped(second_own, (4, 2))

    for bit, guard in ((2, 2), (4, 4), (6, 4)):
        pairs = [(t, t ^ bit) for t in range(8) if not t & guard]
        upto = upto + lax.ppermute(total, "tm", pairs).astype(jnp.float32)
    count = lax.axis_size("space")
    state = after(upto, second_first, second_second)
    turned = jnp.concatenate(after((second_first, second_second), total))
    swapped_turned = flipped(after(turned, upto), (1, 1))
    queries, weight = query_call(
        tokens,
        qkv_weight,
        out_weight,
        straight,
        swapped_straight,
        turned,
        swapped_turned,
        mine,
        other,
    )
    share = state.astype(jnp.bfloat16)
    grid = values.reshape(row_count, col_count, depth)
    local_term = local_call(grid, conv_weight).reshape(-1, depth)
    arrived = lax.ppermute(share, "space", [(i, i ^ 1) for i in range(count)])
    arrived = after(arrived, local_term, queries, weight)
    share = (share.astype(jnp.float32) + arrived.astype(jnp.float32)).astype(jnp.bfloat16)
    arrived = lax.ppermute(share, "space", [(i, count - 1 - i) for i in range(count)])
    edge_near, edge_next = after((edge_near, edge_next), share)
    edge_near = lax.ppermute(edge_near, "space", [(i, i ^ 1) for i in range(count)])
    between = [(i, i + 1) for i in range(1, count - 1, 2)]
    between += [(target, source) for source, target in between]
    edge_next = lax.ppermute(edge_next, "space", between)


    state = share.astype(jnp.float32) + arrived.astype(jnp.float32)
    result = finish_call(
        queries,
        weight,
        state,
        local_term,
        edge_near,
        edge_next,
        conv_weight,
        norm_gain[None],
    )
    return result.reshape(1, row_count, col_count, depth)


def solution(mesh):
    def per_device(video_tokens, qkv_weight, out_weight, conv_weight, norm_gain):
        fits = mesh.shape["tm"] == 8 and mesh.shape["space"] == 4
        fits = fits and qkv_weight.shape[0] == 4 * MAIN + 2 * REST
        form = plane_form if fits else general_form
        return form(video_tokens, qkv_weight, out_weight, conv_weight, norm_gain)

    in_specs = (P("tm", "space", None, None), P("space", None), P("space", None), P(), P())
    out_specs = P("tm", "space", None, None)
    return jax.shard_map(
        per_device, mesh=mesh, in_specs=in_specs, out_specs=out_specs, check_vma=False
    )
```

```python
import functools

import jax
import jax.numpy as jnp
from jax import lax
from jax.experimental import pallas as pl
from jax.experimental.pallas import tpu as pltpu
from jax.sharding import PartitionSpec as P

HEADS = 36
HEAD_DIM = 32
LANES = 128
MAIN = 64
REST = 16
STEPS = (1, 2, 3)
VMEM_LIMIT = 24 * 1024 * 1024
WHOLE_VMEM = 63 * 1024 * 1024


def entering(value, axis, combine, identity):
    devices, place = (lax.axis_size(axis), lax.axis_index(axis))
    everything = lax.all_gather(value.astype(jnp.bfloat16), axis)
    start = jnp.broadcast_to(jnp.asarray(identity, value.dtype), value.shape)

    def lap(k, before):
        reached = k < place
        new = combine(before, everything[k].astype(value.dtype))
        return jnp.where(reached, new, before)

    return lax.fori_loop(0, devices, lap, start)


def with_halo(block, sides, width):
    for axis, dim in sides:
        count = lax.axis_size(axis)
        forward = [(i, i + 1) for i in range(count - 1)]
        backward = [(target, source) for source, target in forward]
        low = lax.ppermute(
            lax.slice_in_dim(block, block.shape[dim] - width, None, axis=dim), axis, forward
        )
        high = lax.ppermute(lax.slice_in_dim(block, 0, width, axis=dim), axis, backward)
        block = jnp.concatenate([low, block, high], axis=dim)
    return block


def fold_product(left_side, block_rows):
    return jnp.dot(left_side, block_rows, preferred_element_type=jnp.float32)


def add_states(earlier, later):
    return earlier + later


def causal_states(key_feat, values):
    key_heads = key_feat.reshape(-1, HEADS, HEAD_DIM)
    value_heads = values.reshape(-1, HEADS, HEAD_DIM)
    frame_state = jnp.einsum(
        "thd,the->hde", key_heads, value_heads, preferred_element_type=jnp.float32
    )
    flat_state = frame_state.reshape(-1)
    frame_sum = lax.psum(flat_state.astype(jnp.bfloat16), "space").astype(jnp.float32)
    earlier = entering(frame_sum, "tm", add_states, jnp.zeros_like(frame_sum))
    whole_state = earlier + frame_sum
    return whole_state.reshape(HEADS, HEAD_DIM, HEAD_DIM)


def general_form(video_tokens, qkv_weight, out_weight, conv_weight, norm_gain):
    frame_now = video_tokens[0]
    row_count, col_count, feat_width = frame_now.shape
    tokens = frame_now.reshape(row_count * col_count, feat_width)
    projected = fold_product(tokens, lax.all_gather(qkv_weight, "space", axis=0, tiled=True))
    query_feat = jax.nn.relu(projected[:, :feat_width]).astype(jnp.bfloat16)
    key_feat = jax.nn.relu(projected[:, feat_width : 2 * feat_width]).astype(jnp.bfloat16)
    values = projected[:, 2 * feat_width :].astype(jnp.bfloat16)
    state_all = causal_states(key_feat, values)
    padded_rows = with_halo(values.reshape(row_count, col_count, feat_width), (("space", 0),), 1)
    padded = jnp.pad(padded_rows, ((0, 0), (1, 1), (0, 0))).astype(jnp.float32)
    local_term = jnp.zeros((row_count, col_count, feat_width), jnp.float32)
    for row_shift in range(3):
        for col_shift in range(3):
            local_term = (
                local_term
                + conv_weight[row_shift, col_shift]
                * padded[row_shift : row_shift + row_count, col_shift : col_shift + col_count]
            )
    state_low = state_all.astype(jnp.bfloat16)
    query_heads = query_feat.reshape(-1, HEADS, HEAD_DIM)
    readout = jnp.einsum("thd,hde->the", query_heads, state_low, preferred_element_type=jnp.float32)
    readout = readout.reshape(-1, feat_width)
    mean_square = jnp.mean(readout * readout, axis=-1, keepdims=True)
    normed = readout * lax.rsqrt(mean_square + 1e-06) * norm_gain
    mixture = (normed + local_term.reshape(-1, feat_width)).astype(jnp.bfloat16)
    result = fold_product(mixture, lax.all_gather(out_weight, "space", axis=0, tiled=True))
    return result.astype(jnp.bfloat16).reshape(1, row_count, col_count, feat_width)


def coordinates():
    place = lax.axis_index("tm")
    return lax.rem(place // 4, 2), lax.rem(place // 2, 2), lax.rem(place, 2)


def shifted(value, step):
    count = lax.axis_size("space")
    return lax.ppermute(value, "space", [(i, (i + step) % count) for i in range(count)])


def flipped(value, bit_on_core):
    return lax.ppermute(value, "tm", [(t, t ^ bit_on_core[t % 2]) for t in range(8)])


def after(value, *earlier):
    return lax.optimization_barrier((value,) + earlier)[0]


def chip_places(y, x):
    return (2 * y + x, 2 * y + (1 - x), 2 * (1 - y) + x, 2 * (1 - y) + (1 - x))


def source_plane(step):
    count = lax.axis_size("space")
    return lax.rem(lax.axis_index("space") - step + count, count)


def steps_through(within, size):
    run = sum(jnp.where(within >= size * k, 1, 0) for k in range(1, len(STEPS)))
    return run, within - size * run


def landed_order(at, width, rows):
    y, x, _ = coordinates()
    planes = [source_plane(step) for step in STEPS]
    row = at + lax.broadcasted_iota(jnp.int32, (1, width), 1)

    def pick(choices, index):
        chosen = choices[-1]
        for k in range(len(choices) - 2, -1, -1):
            chosen = jnp.where(index == k, choices[k], chosen)
        return chosen

    def landed(within, size, starts):
        count = len(STEPS) * size
        slot = sum(jnp.where(within >= count * k, 1, 0) for k in range(1, len(starts)))
        run, left = steps_through(within - count * slot, size)
        return pick(planes, run) * rows + pick(starts, slot) + left

    main = landed(row - rows, MAIN, [place * MAIN for place in chip_places(y, x)])
    rest_at = rows + 4 * len(STEPS) * MAIN
    rest = landed(row - rest_at, REST, [4 * MAIN + tile * REST for tile in (y, 1 - y)])
    own = lax.axis_index("space") * rows + row
    return jnp.where(row < rows, own, jnp.where(row < rest_at, main, rest))


def whole_vmem():
    return pl.BlockSpec(memory_space=pltpu.VMEM)


def anywhere():
    return pl.BlockSpec(memory_space=pltpu.HBM)


def kernel_call(
    body, outputs, inputs, in_specs, scratch=(), flops=0, bytes_accessed=0, limit=VMEM_LIMIT
):
    return pl.pallas_call(
        body,
        out_shape=outputs,
        in_specs=in_specs,
        out_specs=jax.tree.map(lambda _: whole_vmem(), outputs),
        scratch_shapes=list(scratch),
        compiler_params=pltpu.CompilerParams(vmem_limit_bytes=limit),
        cost_estimate=pl.CostEstimate(
            flops=flops, bytes_accessed=bytes_accessed, transcendentals=0
        ),
    )(*inputs)


def pieces_kernel(qkv_ref, out_ref, first_ref, second_ref, sems):
    y, x, core = coordinates()
    depth = out_ref.shape[1]
    main = pl.ds(pl.multiple_of((2 * y + x) * MAIN, REST), MAIN)
    rest = pl.ds(pl.multiple_of(4 * MAIN + y * REST, REST), REST)
    first_columns = pl.ds(pl.multiple_of(depth * (1 + core), LANES), depth)
    rest_columns = pl.ds(pl.multiple_of(jnp.where(x == 0, depth * (1 + core), 0), LANES), depth)

    def copy(source, target, k):
        return pltpu.make_async_copy(source, target, sems.at[k])

    first_main = copy(qkv_ref.at[main, first_columns], first_ref.at[pl.ds(0, MAIN), :], 0)
    first_main.start()
    rest_target = first_ref.at[pl.ds(MAIN, REST), :]
    from_out = (core == 1) & (x == 1)

    @pl.when(from_out)
    def _():
        copy(out_ref.at[rest, :], rest_target, 1).start()

    @pl.when(jnp.logical_not(from_out))
    def _():
        copy(qkv_ref.at[rest, rest_columns], rest_target, 1).start()

    places = chip_places(y, x)
    for k, place in enumerate((places[0], places[3])):
        rows = pl.ds(pl.multiple_of(place * MAIN, REST), MAIN)

        @pl.when(core == 0)
        def _():
            copy(qkv_ref.at[rows, pl.ds(0, depth)], second_ref.at[k], 2 + k).start()

        @pl.when(core == 1)
        def _():
            copy(out_ref.at[rows, :], second_ref.at[k], 2 + k).start()

    first_main.wait()
    copy(out_ref.at[rest, :], rest_target, 1).wait()
    for k in range(2):
        copy(out_ref.at[main, :], second_ref.at[k], 2 + k).wait()


def pieces_call(qkv_weight, out_weight):
    depth = out_weight.shape[1]
    outputs = [
        jax.ShapeDtypeStruct((MAIN + REST, depth), jnp.bfloat16),
        jax.ShapeDtypeStruct((2, MAIN, depth), jnp.bfloat16),
    ]
    return kernel_call(
        pieces_kernel,
        outputs,
        (qkv_weight, out_weight),
        [anywhere(), anywhere()],
        [pltpu.SemaphoreType.DMA((4,))],
        bytes_accessed=4 * (3 * MAIN + REST) * depth,
        limit=WHOLE_VMEM,
    )


def reorder_kernel(rows, tokens_ref, moved_ref):
    depth = tokens_ref.shape[1]
    width = 3 * LANES
    row = lax.broadcasted_iota(jnp.int32, (depth, width), 0)
    for at in range(0, depth, width):
        order = landed_order(at, width, rows)
        chosen = jnp.where(row == order, 1.0, 0.0).astype(jnp.bfloat16)
        moved = jnp.dot(tokens_ref[...], chosen, preferred_element_type=jnp.float32)
        moved_ref[:, at : at + width] = moved.astype(jnp.bfloat16)


def reorder_call(tokens, rows):
    depth = tokens.shape[1]
    return kernel_call(
        functools.partial(reorder_kernel, rows),
        jax.ShapeDtypeStruct(tokens.shape, jnp.bfloat16),
        (tokens,),
        [whole_vmem()],
        flops=2 * tokens.size * depth,
        bytes_accessed=2 * tokens.size,
    )


def first_kernel(*refs):
    tokens_ref, other_ref, qkv_ref, near_ref, away_ref, first_ref, far_ref, mine_ref = refs
    slots = (
        ((near_ref, 0), (first_ref, 0), (near_ref, 1)),
        ((near_ref, 2), (first_ref, 1), (near_ref, 3)),
        ((away_ref, 0), (far_ref, 0), (away_ref, 1)),
        ((away_ref, 2), (far_ref, 1), (away_ref, 3)),
    )
    _, x, core = coordinates()
    count, depth = tokens_ref.shape
    floor = jnp.where(core == 0, 0.0, -jnp.inf).astype(jnp.float32)
    width = 3 * LANES

    for at in range(0, depth, width):
        lanes = slice(at, at + width)

        def slot(k, low, high):
            return jnp.concatenate([ref[at, low:high, lanes] for ref, at in slots[k]], axis=0)

        def by_place(low, high):
            own, first, second, far = [slot(k, low, high) for k in range(4)]
            along_x = jnp.where(core == 0, first, second)
            along_y = jnp.where(core == 0, second, first)
            return own, along_x, along_y, far

        keys, values = [qkv_ref[:, depth * k + at : depth * k + at + width] for k in (1, 2)]
        own = jnp.where(core == 0, keys, values)
        rest = by_place(MAIN, MAIN + REST)
        even = jnp.concatenate([rest[0], rest[2]], axis=0)
        odd = jnp.concatenate([rest[1], rest[3]], axis=0)
        mine_ref[2 * count :, lanes] = jnp.where(x == 1, even, odd)
        columns = jnp.concatenate(
            (own,) + by_place(0, MAIN) + (jnp.where(x == 0, even, odd),), axis=0
        )
        for k, ref in enumerate((tokens_ref, other_ref)):
            product = jnp.dot(ref[...], columns, preferred_element_type=jnp.float32)
            product = jnp.maximum(product, floor).astype(jnp.bfloat16)
            mine_ref[k * count : (k + 1) * count, lanes] = product


def first_call(tokens, other, qkv_weight, *landed):
    count, depth = tokens.shape
    inputs = (tokens, other, qkv_weight) + landed
    return kernel_call(
        first_kernel,
        jax.ShapeDtypeStruct((2 * count + 2 * len(STEPS) * REST, depth), jnp.bfloat16),
        inputs,
        [whole_vmem()] * len(inputs),
        flops=4 * tokens.size * depth,
        bytes_accessed=2 * depth * depth,
    )


def diagonal_mask():
    rows = lax.broadcasted_iota(jnp.int32, (LANES, LANES), 0) // HEAD_DIM
    columns = lax.broadcasted_iota(jnp.int32, (LANES, LANES), 1) // HEAD_DIM
    return rows == columns


def state_kernel(mine_ref, other_ref, values_ref, near_ref, next_ref, upto_ref, total_ref):
    even = lax.rem(lax.axis_index("space"), 2) == 0
    _, _, core = coordinates()
    mask = diagonal_mask()
    columns = near_ref.shape[1]
    count = values_ref.shape[0]
    later = jnp.where(core == 1, 1.0, 0.0).astype(jnp.float32)
    for group in range(mine_ref.shape[1] // LANES):
        at = slice(group * LANES, (group + 1) * LANES)

        def state(mine, other):
            keys = jnp.where(core == 0, mine, other)
            values = jnp.where(core == 0, other, mine)
            full = lax.dot_general(
                keys, values, (((0,), (0,)), ((), ())), preferred_element_type=jnp.float32
            )
            full = jnp.where(mask, full, 0.0)
            total = full[0:HEAD_DIM]
            for k in range(1, LANES // HEAD_DIM):
                total = total + full[k * HEAD_DIM : (k + 1) * HEAD_DIM]
            return total, values

        low, high = slice(0, count), slice(count, 2 * count)
        here, values = state(mine_ref[low, at], other_ref[high, at])
        there, _ = state(mine_ref[high, at], other_ref[low, at])
        values_ref[:, at] = values
        top, bottom = values[:columns], values[-columns:]
        near_ref[0, :, at] = jnp.where(even, bottom, top)
        next_ref[0, :, at] = jnp.where(even, top, bottom)
        upto_ref[group] = here + later * there
        total_ref[group] = (here + there).astype(jnp.bfloat16)


def state_call(mine, other, count, columns):
    depth = mine.shape[1]
    compact = (depth // LANES, HEAD_DIM, LANES)
    edge = jax.ShapeDtypeStruct((1, columns, depth), jnp.bfloat16)
    return kernel_call(
        state_kernel,
        [
            jax.ShapeDtypeStruct((count, depth), jnp.bfloat16),
            edge,
            edge,
            jax.ShapeDtypeStruct(compact, jnp.float32),
            jax.ShapeDtypeStruct(compact, jnp.bfloat16),
        ],
        (mine, other),
        [whole_vmem()] * 2,
        flops=4 * count * depth * LANES,
        bytes_accessed=8 * count * depth,
    )


def column_taps(sheet, taps):
    edge = jnp.zeros_like(sheet[:, :1])
    before = jnp.concatenate([edge, sheet[:, :-1]], axis=1)
    behind = jnp.concatenate([sheet[:, 1:], edge], axis=1)
    return taps[0] * before + taps[1] * sheet + taps[2] * behind


def local_kernel(values_ref, conv_ref, local_ref):
    rows, _, depth = values_ref.shape
    for at in range(0, depth, LANES):
        lanes = slice(at, at + LANES)
        taps = conv_ref[:, :, lanes]
        sheet = values_ref[:, :, lanes].astype(jnp.float32)
        local_ref[:, :, lanes] = column_taps(sheet, taps[1])
        local_ref[1:, :, lanes] = local_ref[1:, :, lanes] + column_taps(sheet[:-1], taps[0])
        local_ref[: rows - 1, :, lanes] = (
            local_ref[: rows - 1, :, lanes] + column_taps(sheet[1:], taps[2])
        )


def local_call(values, conv_weight):
    return kernel_call(
        local_kernel,
        jax.ShapeDtypeStruct(values.shape, jnp.float32),
        (values, conv_weight),
        [whole_vmem()] * 2,
        flops=18 * values.size,
        bytes_accessed=6 * values.size,
    )


def query_kernel(*refs):
    tokens_ref, qkv_ref, out_ref, *packs, ours_ref, other_ref, query_ref, weight_ref = refs
    y, x, core = coordinates()
    depth = tokens_ref.shape[1]
    rows = qkv_ref.shape[0]
    steps = len(STEPS)
    rest_at = ours_ref.shape[0] - 2 * steps * REST
    places = chip_places(y, x)
    width = 3 * LANES

    def block(of_core, index, lanes):
        pack, k = index
        mine_ref, theirs_ref = packs[2 * pack], packs[2 * pack + 1]
        return jnp.where(core == of_core, mine_ref[k, :, lanes], theirs_ref[k, :, lanes])


    def rest(of_core, lanes):
        return jnp.where(core == of_core, ours_ref[rest_at:, lanes], other_ref[rest_at:, lanes])

    def put(row, value, lanes):
        weight_ref[pl.ds(pl.multiple_of(row, REST), value.shape[0]), lanes] = value

    for at in range(0, depth, width):
        lanes = slice(at, at + width)
        order = [(0, 2 * k) for k in range(steps)] + [(1, k) for k in range(2 * steps)]
        order += [(0, 2 * k + 1) for k in range(steps)]
        columns = [qkv_ref[:, lanes]] + [block(0, k, lanes) for k in order] + [rest(0, lanes)]
        queries = jnp.dot(
            tokens_ref[...], jnp.concatenate(columns, axis=0), preferred_element_type=jnp.float32
        )
        query_ref[:, lanes] = jnp.maximum(queries, 0.0).astype(jnp.bfloat16)

        put(lax.axis_index("space") * rows, out_ref[:, lanes], lanes)
        tiles = rest(1, lanes)
        for k, step in enumerate(STEPS):
            base = source_plane(step) * rows
            held = ((0, 2 * k), (1, steps + k), (1, k), (0, 2 * k + 1))
            for place, index in zip(places, held):
                put(base + place * MAIN, block(1, index, lanes), lanes)
            for run, tile in enumerate((y, 1 - y)):
                start = (run * steps + k) * REST
                put(base + 4 * MAIN + tile * REST, tiles[start : start + REST], lanes)


def query_call(tokens, qkv_weight, out_weight, *landed):
    depth = tokens.shape[1]
    inputs = (tokens, qkv_weight, out_weight) + landed
    return kernel_call(
        query_kernel,
        [
            jax.ShapeDtypeStruct(tokens.shape, jnp.bfloat16),
            jax.ShapeDtypeStruct((depth, depth), jnp.bfloat16),
        ],
        inputs,
        [whole_vmem()] * len(inputs),
        flops=2 * tokens.size * depth,
        bytes_accessed=4 * depth * depth,
    )


def finish_kernel(*refs):
    queries_ref, weight_ref, share_ref, arrived_ref, local_ref, near_ref, next_ref, *refs = refs
    conv_ref, gain_ref, result_ref, read_ref, mixture_ref = refs
    count, depth = queries_ref.shape
    columns = near_ref.shape[1]
    even = lax.rem(lax.axis_index("space"), 2) == 0
    mask = diagonal_mask()
    square = jnp.zeros((count, LANES), jnp.float32)
    for group in range(depth // LANES):
        lanes = slice(group * LANES, (group + 1) * LANES)
        compact = share_ref[group].astype(jnp.float32) + arrived_ref[group].astype(jnp.float32)
        spread = jnp.concatenate([compact] * (LANES // HEAD_DIM), axis=0)
        spread = jnp.where(mask, spread, 0.0).astype(jnp.bfloat16)
        read = jnp.dot(queries_ref[:, lanes], spread, preferred_element_type=jnp.float32)
        read_ref[:, lanes] = read
        square = square + read * read
    scale = lax.rsqrt(jnp.sum(square, axis=1, keepdims=True) / depth + 1e-06)
    for at in range(0, depth, LANES):
        lanes = slice(at, at + LANES)
        taps = conv_ref[:, :, lanes]
        mixture = read_ref[:, lanes] * scale * gain_ref[:, lanes] + local_ref[:, lanes]
        near = near_ref[:, :, lanes].astype(jnp.float32)
        beyond = next_ref[:, :, lanes].astype(jnp.float32)
        above = column_taps(jnp.where(even, beyond, near), taps[0])[0]
        below = column_taps(jnp.where(even, near, beyond), taps[2])[0]
        middle = mixture[columns : count - columns]
        mixture = jnp.concatenate(
            [mixture[:columns] + above, middle, mixture[count - columns :] + below], axis=0
        )
        mixture_ref[:, lanes] = mixture.astype(jnp.bfloat16)
    width = 3 * LANES
    for at in range(0, depth, width):
        lanes = slice(at, at + width)
        product = jnp.dot(
            mixture_ref[...], weight_ref[:, lanes], preferred_element_type=jnp.float32
        )
        result_ref[:, lanes] = product.astype(jnp.bfloat16)


def finish_call(queries, *inputs):
    return kernel_call(
        finish_kernel,
        jax.ShapeDtypeStruct(queries.shape, jnp.bfloat16),
        (queries,) + inputs,
        [whole_vmem()] * (1 + len(inputs)),
        [pltpu.VMEM(queries.shape, jnp.float32), pltpu.VMEM(queries.shape, jnp.bfloat16)],
        flops=2 * queries.size * queries.shape[1],
        bytes_accessed=2 * queries.shape[1] ** 2,
    )


def plane_form(video_tokens, qkv_weight, out_weight, conv_weight, norm_gain):
    frame_now = video_tokens[0]
    row_count, col_count, depth = frame_now.shape
    tokens = frame_now.reshape(row_count * col_count, depth)

    first_piece, second_piece = pieces_call(qkv_weight, out_weight)
    first_piece = first_piece[None]
    one = shifted(first_piece, 1)
    three = shifted(first_piece, -1)
    tokens = reorder_call(after(tokens, second_piece), qkv_weight.shape[0])
    other_tokens = flipped(tokens, (1, 1))
    one, three = after((one, three), tokens)

    pair = jnp.concatenate([one, three])
    two = shifted(one, 1)
    pair_first = flipped(pair, (2, 4))
    near = jnp.concatenate(after((pair, pair_first), other_tokens))
    away = flipped(near, (4, 2))
    two_near = jnp.concatenate([two, flipped(two, (2, 4))])
    two_away = flipped(two_near, (4, 2))

    second_ready = after(second_piece, one, three)
    second_one = shifted(second_ready, 1)
    second_three = shifted(second_ready, -1)
    second_two = shifted(after(second_one, two_near), 1)

    mine = first_call(after(tokens, second_one, second_three), other_tokens, qkv_weight, near, away, two_near, two_away)
    other = flipped(after(mine, second_two), (1, 1))
    straight = jnp.concatenate([second_one, second_two, second_three])
    swapped_straight = flipped(straight, (1, 1))
    values, edge_near, edge_next, upto, total = state_call(mine, other, tokens.shape[0], col_count)
    total = after(total, swapped_straight)

    second_own = jnp.stack([second_one[0], second_two[0], second_three[0]])
    second_first = flipped(second_own, (2, 4))
    second_second = flipped(second_own, (4, 2))

    for bit, guard in ((2, 2), (4, 4), (6, 4)):
        pairs = [(t, t ^ bit) for t in range(8) if not t & guard]
        upto = upto + lax.ppermute(total, "tm", pairs).astype(jnp.float32)
    count = lax.axis_size("space")
    state = after(upto, second_first, second_second)
    turned = jnp.concatenate(after((second_first, second_second), total))
    swapped_turned = flipped(after(turned, upto), (1, 1))
    queries, weight = query_call(
        tokens,
        qkv_weight,
        out_weight,
        straight,
        swapped_straight,
        turned,
        swapped_turned,
        mine,
        other,
    )
    share = state.astype(jnp.bfloat16)
    grid = values.reshape(row_count, col_count, depth)
    local_term = local_call(grid, conv_weight).reshape(-1, depth)
    arrived = lax.ppermute(share, "space", [(i, count - 1 - i) for i in range(count)])
    arrived = after(arrived, local_term, queries, weight)
    share = (share.astype(jnp.float32) + arrived.astype(jnp.float32)).astype(jnp.bfloat16)
    arrived = lax.ppermute(share, "space", [(i, i ^ 1) for i in range(count)])
    edge_near, edge_next = after((edge_near, edge_next), share)
    edge_near = lax.ppermute(edge_near, "space", [(i, i ^ 1) for i in range(count)])
    between = [(i, i + 1) for i in range(1, count - 1, 2)]
    between += [(target, source) for source, target in between]
    edge_next = lax.ppermute(edge_next, "space", between)


    result = finish_call(
        queries,
        weight,
        share,
        arrived,
        local_term,
        edge_near,
        edge_next,
        conv_weight,
        norm_gain[None],
    )
    return result.reshape(1, row_count, col_count, depth)


def solution(mesh):
    def per_device(video_tokens, qkv_weight, out_weight, conv_weight, norm_gain):
        fits = mesh.shape["tm"] == 8 and mesh.shape["space"] == 4
        fits = fits and qkv_weight.shape[0] == 4 * MAIN + 2 * REST
        form = plane_form if fits else general_form
        return form(video_tokens, qkv_weight, out_weight, conv_weight, norm_gain)

    in_specs = (P("tm", "space", None, None), P("space", None), P("space", None), P(), P())
    out_specs = P("tm", "space", None, None)
    return jax.shard_map(
        per_device, mesh=mesh, in_specs=in_specs, out_specs=out_specs, check_vma=False
    )
```

```python
import functools

import jax
import jax.numpy as jnp
from jax import lax
from jax.experimental import pallas as pl
from jax.experimental.pallas import tpu as pltpu
from jax.sharding import PartitionSpec as P

HEADS = 36
HEAD_DIM = 32
LANES = 128
MAIN = 64
REST = 16
STEPS = (1, 2, 3)
VMEM_LIMIT = 24 * 1024 * 1024
WHOLE_VMEM = 63 * 1024 * 1024


def entering(value, axis, combine, identity):
    devices, place = (lax.axis_size(axis), lax.axis_index(axis))
    everything = lax.all_gather(value.astype(jnp.bfloat16), axis)
    start = jnp.broadcast_to(jnp.asarray(identity, value.dtype), value.shape)

    def lap(k, before):
        reached = k < place
        new = combine(before, everything[k].astype(value.dtype))
        return jnp.where(reached, new, before)

    return lax.fori_loop(0, devices, lap, start)


def with_halo(block, sides, width):
    for axis, dim in sides:
        count = lax.axis_size(axis)
        forward = [(i, i + 1) for i in range(count - 1)]
        backward = [(target, source) for source, target in forward]
        low = lax.ppermute(
            lax.slice_in_dim(block, block.shape[dim] - width, None, axis=dim), axis, forward
        )
        high = lax.ppermute(lax.slice_in_dim(block, 0, width, axis=dim), axis, backward)
        block = jnp.concatenate([low, block, high], axis=dim)
    return block


def fold_product(left_side, block_rows):
    return jnp.dot(left_side, block_rows, preferred_element_type=jnp.float32)


def add_states(earlier, later):
    return earlier + later


def causal_states(key_feat, values):
    key_heads = key_feat.reshape(-1, HEADS, HEAD_DIM)
    value_heads = values.reshape(-1, HEADS, HEAD_DIM)
    frame_state = jnp.einsum(
        "thd,the->hde", key_heads, value_heads, preferred_element_type=jnp.float32
    )
    flat_state = frame_state.reshape(-1)
    frame_sum = lax.psum(flat_state.astype(jnp.bfloat16), "space").astype(jnp.float32)
    earlier = entering(frame_sum, "tm", add_states, jnp.zeros_like(frame_sum))
    whole_state = earlier + frame_sum
    return whole_state.reshape(HEADS, HEAD_DIM, HEAD_DIM)


def general_form(video_tokens, qkv_weight, out_weight, conv_weight, norm_gain):
    frame_now = video_tokens[0]
    row_count, col_count, feat_width = frame_now.shape
    tokens = frame_now.reshape(row_count * col_count, feat_width)
    projected = fold_product(tokens, lax.all_gather(qkv_weight, "space", axis=0, tiled=True))
    query_feat = jax.nn.relu(projected[:, :feat_width]).astype(jnp.bfloat16)
    key_feat = jax.nn.relu(projected[:, feat_width : 2 * feat_width]).astype(jnp.bfloat16)
    values = projected[:, 2 * feat_width :].astype(jnp.bfloat16)
    state_all = causal_states(key_feat, values)
    padded_rows = with_halo(values.reshape(row_count, col_count, feat_width), (("space", 0),), 1)
    padded = jnp.pad(padded_rows, ((0, 0), (1, 1), (0, 0))).astype(jnp.float32)
    local_term = jnp.zeros((row_count, col_count, feat_width), jnp.float32)
    for row_shift in range(3):
        for col_shift in range(3):
            local_term = (
                local_term
                + conv_weight[row_shift, col_shift]
                * padded[row_shift : row_shift + row_count, col_shift : col_shift + col_count]
            )
    state_low = state_all.astype(jnp.bfloat16)
    query_heads = query_feat.reshape(-1, HEADS, HEAD_DIM)
    readout = jnp.einsum("thd,hde->the", query_heads, state_low, preferred_element_type=jnp.float32)
    readout = readout.reshape(-1, feat_width)
    mean_square = jnp.mean(readout * readout, axis=-1, keepdims=True)
    normed = readout * lax.rsqrt(mean_square + 1e-06) * norm_gain
    mixture = (normed + local_term.reshape(-1, feat_width)).astype(jnp.bfloat16)
    result = fold_product(mixture, lax.all_gather(out_weight, "space", axis=0, tiled=True))
    return result.astype(jnp.bfloat16).reshape(1, row_count, col_count, feat_width)


def coordinates():
    place = lax.axis_index("tm")
    return lax.rem(place // 4, 2), lax.rem(place // 2, 2), lax.rem(place, 2)


def shifted(value, step):
    count = lax.axis_size("space")
    return lax.ppermute(value, "space", [(i, (i + step) % count) for i in range(count)])


def flipped(value, bit_on_core):
    return lax.ppermute(value, "tm", [(t, t ^ bit_on_core[t % 2]) for t in range(8)])


def after(value, *earlier):
    return lax.optimization_barrier((value,) + earlier)[0]


def chip_places(y, x):
    return (2 * y + x, 2 * y + (1 - x), 2 * (1 - y) + x, 2 * (1 - y) + (1 - x))


def source_plane(step):
    count = lax.axis_size("space")
    return lax.rem(lax.axis_index("space") - step + count, count)


def steps_through(within, size):
    run = sum(jnp.where(within >= size * k, 1, 0) for k in range(1, len(STEPS)))
    return run, within - size * run


def landed_order(at, width, rows):
    y, x, _ = coordinates()
    planes = [source_plane(step) for step in STEPS]
    row = at + lax.broadcasted_iota(jnp.int32, (1, width), 1)

    def pick(choices, index):
        chosen = choices[-1]
        for k in range(len(choices) - 2, -1, -1):
            chosen = jnp.where(index == k, choices[k], chosen)
        return chosen

    def landed(within, size, starts):
        count = len(STEPS) * size
        slot = sum(jnp.where(within >= count * k, 1, 0) for k in range(1, len(starts)))
        run, left = steps_through(within - count * slot, size)
        return pick(planes, run) * rows + pick(starts, slot) + left

    main = landed(row - rows, MAIN, [place * MAIN for place in chip_places(y, x)])
    rest_at = rows + 4 * len(STEPS) * MAIN
    rest = landed(row - rest_at, REST, [4 * MAIN + tile * REST for tile in (y, 1 - y)])
    own = lax.axis_index("space") * rows + row
    return jnp.where(row < rows, own, jnp.where(row < rest_at, main, rest))


def whole_vmem():
    return pl.BlockSpec(memory_space=pltpu.VMEM)


def anywhere():
    return pl.BlockSpec(memory_space=pltpu.HBM)


def kernel_call(
    body, outputs, inputs, in_specs, scratch=(), flops=0, bytes_accessed=0, limit=VMEM_LIMIT
):
    return pl.pallas_call(
        body,
        out_shape=outputs,
        in_specs=in_specs,
        out_specs=jax.tree.map(lambda _: whole_vmem(), outputs),
        scratch_shapes=list(scratch),
        compiler_params=pltpu.CompilerParams(vmem_limit_bytes=limit),
        cost_estimate=pl.CostEstimate(
            flops=flops, bytes_accessed=bytes_accessed, transcendentals=0
        ),
    )(*inputs)


def pieces_kernel(qkv_ref, out_ref, first_ref, second_ref, sems):
    y, x, core = coordinates()
    depth = out_ref.shape[1]
    main = pl.ds(pl.multiple_of((2 * y + x) * MAIN, REST), MAIN)
    rest = pl.ds(pl.multiple_of(4 * MAIN + y * REST, REST), REST)
    first_columns = pl.ds(pl.multiple_of(depth * (1 + core), LANES), depth)
    rest_columns = pl.ds(pl.multiple_of(jnp.where(x == 0, depth * (1 + core), 0), LANES), depth)

    def copy(source, target, k):
        return pltpu.make_async_copy(source, target, sems.at[k])

    first_main = copy(qkv_ref.at[main, first_columns], first_ref.at[pl.ds(0, MAIN), :], 0)
    first_main.start()
    rest_target = first_ref.at[pl.ds(MAIN, REST), :]
    from_out = (core == 1) & (x == 1)

    @pl.when(from_out)
    def _():
        copy(out_ref.at[rest, :], rest_target, 1).start()

    @pl.when(jnp.logical_not(from_out))
    def _():
        copy(qkv_ref.at[rest, rest_columns], rest_target, 1).start()

    places = chip_places(y, x)
    for k, place in enumerate((places[0], places[3])):
        rows = pl.ds(pl.multiple_of(place * MAIN, REST), MAIN)

        @pl.when(core == 0)
        def _():
            copy(qkv_ref.at[rows, pl.ds(0, depth)], second_ref.at[k], 2 + k).start()

        @pl.when(core == 1)
        def _():
            copy(out_ref.at[rows, :], second_ref.at[k], 2 + k).start()

    first_main.wait()
    copy(out_ref.at[rest, :], rest_target, 1).wait()
    for k in range(2):
        copy(out_ref.at[main, :], second_ref.at[k], 2 + k).wait()


def pieces_call(qkv_weight, out_weight):
    depth = out_weight.shape[1]
    outputs = [
        jax.ShapeDtypeStruct((MAIN + REST, depth), jnp.bfloat16),
        jax.ShapeDtypeStruct((2, MAIN, depth), jnp.bfloat16),
    ]
    return kernel_call(
        pieces_kernel,
        outputs,
        (qkv_weight, out_weight),
        [anywhere(), anywhere()],
        [pltpu.SemaphoreType.DMA((4,))],
        bytes_accessed=4 * (3 * MAIN + REST) * depth,
        limit=WHOLE_VMEM,
    )


def reorder_kernel(rows, tokens_ref, moved_ref):
    depth = tokens_ref.shape[1]
    width = 3 * LANES
    row = lax.broadcasted_iota(jnp.int32, (depth, width), 0)
    for at in range(0, depth, width):
        order = landed_order(at, width, rows)
        chosen = jnp.where(row == order, 1.0, 0.0).astype(jnp.bfloat16)
        moved = jnp.dot(tokens_ref[...], chosen, preferred_element_type=jnp.float32)
        moved_ref[:, at : at + width] = moved.astype(jnp.bfloat16)


def reorder_call(tokens, rows):
    depth = tokens.shape[1]
    return kernel_call(
        functools.partial(reorder_kernel, rows),
        jax.ShapeDtypeStruct(tokens.shape, jnp.bfloat16),
        (tokens,),
        [whole_vmem()],
        flops=2 * tokens.size * depth,
        bytes_accessed=2 * tokens.size,
    )


def first_kernel(*refs):
    tokens_ref, other_ref, qkv_ref, near_ref, away_ref, first_ref, far_ref, mine_ref = refs
    slots = (
        ((near_ref, 0), (first_ref, 0), (near_ref, 1)),
        ((near_ref, 2), (first_ref, 1), (near_ref, 3)),
        ((away_ref, 0), (far_ref, 0), (away_ref, 1)),
        ((away_ref, 2), (far_ref, 1), (away_ref, 3)),
    )
    _, x, core = coordinates()
    count, depth = tokens_ref.shape
    floor = jnp.where(core == 0, 0.0, -jnp.inf).astype(jnp.float32)
    width = 3 * LANES

    for at in range(0, depth, width):
        lanes = slice(at, at + width)

        def slot(k, low, high):
            return jnp.concatenate([ref[at, low:high, lanes] for ref, at in slots[k]], axis=0)

        def by_place(low, high):
            own, first, second, far = [slot(k, low, high) for k in range(4)]
            along_x = jnp.where(core == 0, first, second)
            along_y = jnp.where(core == 0, second, first)
            return own, along_x, along_y, far

        keys, values = [qkv_ref[:, depth * k + at : depth * k + at + width] for k in (1, 2)]
        own = jnp.where(core == 0, keys, values)
        rest = by_place(MAIN, MAIN + REST)
        even = jnp.concatenate([rest[0], rest[2]], axis=0)
        odd = jnp.concatenate([rest[1], rest[3]], axis=0)
        mine_ref[2 * count :, lanes] = jnp.where(x == 1, even, odd)
        columns = jnp.concatenate(
            (own,) + by_place(0, MAIN) + (jnp.where(x == 0, even, odd),), axis=0
        )
        for k, ref in enumerate((tokens_ref, other_ref)):
            product = jnp.dot(ref[...], columns, preferred_element_type=jnp.float32)
            product = jnp.maximum(product, floor).astype(jnp.bfloat16)
            mine_ref[k * count : (k + 1) * count, lanes] = product


def first_call(tokens, other, qkv_weight, *landed):
    count, depth = tokens.shape
    inputs = (tokens, other, qkv_weight) + landed
    return kernel_call(
        first_kernel,
        jax.ShapeDtypeStruct((2 * count + 2 * len(STEPS) * REST, depth), jnp.bfloat16),
        inputs,
        [whole_vmem()] * len(inputs),
        flops=4 * tokens.size * depth,
        bytes_accessed=2 * depth * depth,
    )


def diagonal_mask():
    rows = lax.broadcasted_iota(jnp.int32, (LANES, LANES), 0) // HEAD_DIM
    columns = lax.broadcasted_iota(jnp.int32, (LANES, LANES), 1) // HEAD_DIM
    return rows == columns


def state_kernel(mine_ref, other_ref, values_ref, near_ref, next_ref, upto_ref, total_ref):
    even = lax.rem(lax.axis_index("space"), 2) == 0
    _, _, core = coordinates()
    mask = diagonal_mask()
    columns = near_ref.shape[1]
    count = values_ref.shape[0]
    later = jnp.where(core == 1, 1.0, 0.0).astype(jnp.float32)
    for group in range(mine_ref.shape[1] // LANES):
        at = slice(group * LANES, (group + 1) * LANES)

        def state(mine, other):
            keys = jnp.where(core == 0, mine, other)
            values = jnp.where(core == 0, other, mine)
            full = lax.dot_general(
                keys, values, (((0,), (0,)), ((), ())), preferred_element_type=jnp.float32
            )
            full = jnp.where(mask, full, 0.0)
            total = full[0:HEAD_DIM]
            for k in range(1, LANES // HEAD_DIM):
                total = total + full[k * HEAD_DIM : (k + 1) * HEAD_DIM]
            return total, values

        low, high = slice(0, count), slice(count, 2 * count)
        here, values = state(mine_ref[low, at], other_ref[high, at])
        there, _ = state(mine_ref[high, at], other_ref[low, at])
        values_ref[:, at] = values
        top, bottom = values[:columns], values[-columns:]
        near_ref[0, :, at] = jnp.where(even, bottom, top)
        next_ref[0, :, at] = jnp.where(even, top, bottom)
        upto_ref[group] = here + later * there
        total_ref[group] = (here + there).astype(jnp.bfloat16)


def state_call(mine, other, count, columns):
    depth = mine.shape[1]
    compact = (depth // LANES, HEAD_DIM, LANES)
    edge = jax.ShapeDtypeStruct((1, columns, depth), jnp.bfloat16)
    return kernel_call(
        state_kernel,
        [
            jax.ShapeDtypeStruct((count, depth), jnp.bfloat16),
            edge,
            edge,
            jax.ShapeDtypeStruct(compact, jnp.float32),
            jax.ShapeDtypeStruct(compact, jnp.bfloat16),
        ],
        (mine, other),
        [whole_vmem()] * 2,
        flops=4 * count * depth * LANES,
        bytes_accessed=8 * count * depth,
    )


def column_taps(sheet, taps):
    edge = jnp.zeros_like(sheet[:, :1])
    before = jnp.concatenate([edge, sheet[:, :-1]], axis=1)
    behind = jnp.concatenate([sheet[:, 1:], edge], axis=1)
    return taps[0] * before + taps[1] * sheet + taps[2] * behind


def local_kernel(values_ref, conv_ref, local_ref):
    rows, _, depth = values_ref.shape
    for at in range(0, depth, LANES):
        lanes = slice(at, at + LANES)
        taps = conv_ref[:, :, lanes]
        sheet = values_ref[:, :, lanes].astype(jnp.float32)
        local_ref[:, :, lanes] = column_taps(sheet, taps[1])
        local_ref[1:, :, lanes] = local_ref[1:, :, lanes] + column_taps(sheet[:-1], taps[0])
        local_ref[: rows - 1, :, lanes] = (
            local_ref[: rows - 1, :, lanes] + column_taps(sheet[1:], taps[2])
        )


def local_call(values, conv_weight):
    return kernel_call(
        local_kernel,
        jax.ShapeDtypeStruct(values.shape, jnp.float32),
        (values, conv_weight),
        [whole_vmem()] * 2,
        flops=18 * values.size,
        bytes_accessed=6 * values.size,
    )


def query_kernel(*refs):
    tokens_ref, qkv_ref, out_ref, *packs, ours_ref, other_ref, query_ref, weight_ref = refs
    y, x, core = coordinates()
    depth = tokens_ref.shape[1]
    rows = qkv_ref.shape[0]
    steps = len(STEPS)
    rest_at = ours_ref.shape[0] - 2 * steps * REST
    places = chip_places(y, x)
    width = 3 * LANES

    def block(of_core, index, lanes):
        pack, k = index
        mine_ref, theirs_ref = packs[2 * pack], packs[2 * pack + 1]
        return jnp.where(core == of_core, mine_ref[k, :, lanes], theirs_ref[k, :, lanes])


    def rest(of_core, lanes):
        return jnp.where(core == of_core, ours_ref[rest_at:, lanes], other_ref[rest_at:, lanes])

    def put(row, value, lanes):
        weight_ref[pl.ds(pl.multiple_of(row, REST), value.shape[0]), lanes] = value

    for at in range(0, depth, width):
        lanes = slice(at, at + width)
        order = [(0, 2 * k) for k in range(steps)] + [(1, k) for k in range(2 * steps)]
        order += [(0, 2 * k + 1) for k in range(steps)]
        columns = [qkv_ref[:, lanes]] + [block(0, k, lanes) for k in order] + [rest(0, lanes)]
        queries = jnp.dot(
            tokens_ref[...], jnp.concatenate(columns, axis=0), preferred_element_type=jnp.float32
        )
        query_ref[:, lanes] = jnp.maximum(queries, 0.0).astype(jnp.bfloat16)

        put(lax.axis_index("space") * rows, out_ref[:, lanes], lanes)
        tiles = rest(1, lanes)
        for k, step in enumerate(STEPS):
            base = source_plane(step) * rows
            held = ((0, 2 * k), (1, steps + k), (1, k), (0, 2 * k + 1))
            for place, index in zip(places, held):
                put(base + place * MAIN, block(1, index, lanes), lanes)
            for run, tile in enumerate((y, 1 - y)):
                start = (run * steps + k) * REST
                put(base + 4 * MAIN + tile * REST, tiles[start : start + REST], lanes)


def query_call(tokens, qkv_weight, out_weight, *landed):
    depth = tokens.shape[1]
    inputs = (tokens, qkv_weight, out_weight) + landed
    return kernel_call(
        query_kernel,
        [
            jax.ShapeDtypeStruct(tokens.shape, jnp.bfloat16),
            jax.ShapeDtypeStruct((depth, depth), jnp.bfloat16),
        ],
        inputs,
        [whole_vmem()] * len(inputs),
        flops=2 * tokens.size * depth,
        bytes_accessed=4 * depth * depth,
    )


def finish_kernel(*refs):
    queries_ref, weight_ref, state_ref, local_ref, near_ref, next_ref, *refs = refs
    conv_ref, gain_ref, result_ref, read_ref, mixture_ref = refs
    count, depth = queries_ref.shape
    columns = near_ref.shape[1]
    even = lax.rem(lax.axis_index("space"), 2) == 0
    mask = diagonal_mask()
    square = jnp.zeros((count, LANES), jnp.float32)
    for group in range(depth // LANES):
        lanes = slice(group * LANES, (group + 1) * LANES)
        spread = jnp.concatenate([state_ref[group]] * (LANES // HEAD_DIM), axis=0)
        spread = jnp.where(mask, spread, 0.0).astype(jnp.bfloat16)
        read = jnp.dot(queries_ref[:, lanes], spread, preferred_element_type=jnp.float32)
        read_ref[:, lanes] = read
        square = square + read * read
    scale = lax.rsqrt(jnp.sum(square, axis=1, keepdims=True) / depth + 1e-06)
    for at in range(0, depth, LANES):
        lanes = slice(at, at + LANES)
        taps = conv_ref[:, :, lanes]
        mixture = read_ref[:, lanes] * scale * gain_ref[:, lanes] + local_ref[:, lanes]
        near = near_ref[:, :, lanes].astype(jnp.float32)
        beyond = next_ref[:, :, lanes].astype(jnp.float32)
        above = column_taps(jnp.where(even, beyond, near), taps[0])[0]
        below = column_taps(jnp.where(even, near, beyond), taps[2])[0]
        middle = mixture[columns : count - columns]
        mixture = jnp.concatenate(
            [mixture[:columns] + above, middle, mixture[count - columns :] + below], axis=0
        )
        mixture_ref[:, lanes] = mixture.astype(jnp.bfloat16)
    width = 3 * LANES
    for at in range(0, depth, width):
        lanes = slice(at, at + width)
        product = jnp.dot(
            mixture_ref[...], weight_ref[:, lanes], preferred_element_type=jnp.float32
        )
        result_ref[:, lanes] = product.astype(jnp.bfloat16)


def finish_call(queries, *inputs):
    return kernel_call(
        finish_kernel,
        jax.ShapeDtypeStruct(queries.shape, jnp.bfloat16),
        (queries,) + inputs,
        [whole_vmem()] * (1 + len(inputs)),
        [pltpu.VMEM(queries.shape, jnp.float32), pltpu.VMEM(queries.shape, jnp.bfloat16)],
        flops=2 * queries.size * queries.shape[1],
        bytes_accessed=2 * queries.shape[1] ** 2,
    )


def plane_form(video_tokens, qkv_weight, out_weight, conv_weight, norm_gain):
    frame_now = video_tokens[0]
    row_count, col_count, depth = frame_now.shape
    tokens = frame_now.reshape(row_count * col_count, depth)

    first_piece, second_piece = pieces_call(qkv_weight, out_weight)
    first_piece = first_piece[None]
    one = shifted(first_piece, 1)
    three = shifted(first_piece, -1)
    tokens = reorder_call(after(tokens, second_piece), qkv_weight.shape[0])
    other_tokens = flipped(tokens, (1, 1))
    one, three = after((one, three), tokens)

    pair = jnp.concatenate([one, three])
    two = shifted(one, 1)
    pair_first = flipped(pair, (2, 4))
    near = jnp.concatenate(after((pair, pair_first), other_tokens))
    away = flipped(near, (4, 2))
    two_near = jnp.concatenate([two, flipped(two, (2, 4))])
    two_away = flipped(two_near, (4, 2))

    second_ready = after(second_piece, one, three)
    second_one = shifted(second_ready, 1)
    second_three = shifted(second_ready, -1)
    second_two = shifted(after(second_one, two_near), 1)

    mine = first_call(after(tokens, second_one, second_three), other_tokens, qkv_weight, near, away, two_near, two_away)
    other = flipped(after(mine, second_two), (1, 1))
    straight = jnp.concatenate([second_one, second_two, second_three])
    swapped_straight = flipped(straight, (1, 1))
    values, edge_near, edge_next, upto, total = state_call(mine, other, tokens.shape[0], col_count)
    total = after(total, swapped_straight)

    second_own = jnp.stack([second_one[0], second_two[0], second_three[0]])
    second_first = flipped(second_own, (2, 4))
    second_second = flipped(second_own, (4, 2))

    for bit, guard in ((2, 2), (4, 4), (6, 4)):
        pairs = [(t, t ^ bit) for t in range(8) if not t & guard]
        upto = upto + lax.ppermute(total, "tm", pairs).astype(jnp.float32)
    count = lax.axis_size("space")
    state = after(upto, second_first, second_second)
    turned = jnp.concatenate(after((second_first, second_second), total))
    swapped_turned = flipped(after(turned, upto), (1, 1))
    queries, weight = query_call(
        tokens,
        qkv_weight,
        out_weight,
        straight,
        swapped_straight,
        turned,
        swapped_turned,
        mine,
        other,
    )
    share = state.astype(jnp.bfloat16)
    grid = values.reshape(row_count, col_count, depth)
    local_term = local_call(grid, conv_weight).reshape(-1, depth)
    arrived = lax.ppermute(share, "space", [(i, count - 1 - i) for i in range(count)])
    arrived = after(arrived, local_term, queries, weight)
    share = (share.astype(jnp.float32) + arrived.astype(jnp.float32)).astype(jnp.bfloat16)
    arrived = lax.ppermute(share, "space", [(i, i ^ 1) for i in range(count)])
    edge_near, edge_next = after((edge_near, edge_next), share)
    edge_near = lax.ppermute(edge_near, "space", [(i, i ^ 1) for i in range(count)])
    between = [(i, i + 1) for i in range(1, count - 1, 2)]
    between += [(target, source) for source, target in between]
    edge_next = lax.ppermute(edge_next, "space", between)


    state = share.astype(jnp.float32) + arrived.astype(jnp.float32)
    result = finish_call(
        queries,
        weight,
        state,
        local_term,
        edge_near,
        edge_next,
        conv_weight,
        norm_gain[None],
    )
    return result.reshape(1, row_count, col_count, depth)


def solution(mesh):
    def per_device(video_tokens, qkv_weight, out_weight, conv_weight, norm_gain):
        fits = mesh.shape["tm"] == 8 and mesh.shape["space"] == 4
        fits = fits and qkv_weight.shape[0] == 4 * MAIN + 2 * REST
        form = plane_form if fits else general_form
        return form(video_tokens, qkv_weight, out_weight, conv_weight, norm_gain)

    in_specs = (P("tm", "space", None, None), P("space", None), P("space", None), P(), P())
    out_specs = P("tm", "space", None, None)
    return jax.shard_map(
        per_device, mesh=mesh, in_specs=in_specs, out_specs=out_specs, check_vma=False
    )
```

```python
import functools

import jax
import jax.numpy as jnp
from jax import lax
from jax.experimental import pallas as pl
from jax.experimental.pallas import tpu as pltpu
from jax.sharding import PartitionSpec as P

HEADS = 36
HEAD_DIM = 32
LANES = 128
MAIN = 64
REST = 16
STEPS = (1, 2, 3)
VMEM_LIMIT = 24 * 1024 * 1024
WHOLE_VMEM = 63 * 1024 * 1024


def entering(value, axis, combine, identity):
    devices, place = (lax.axis_size(axis), lax.axis_index(axis))
    everything = lax.all_gather(value.astype(jnp.bfloat16), axis)
    start = jnp.broadcast_to(jnp.asarray(identity, value.dtype), value.shape)

    def lap(k, before):
        reached = k < place
        new = combine(before, everything[k].astype(value.dtype))
        return jnp.where(reached, new, before)

    return lax.fori_loop(0, devices, lap, start)


def with_halo(block, sides, width):
    for axis, dim in sides:
        count = lax.axis_size(axis)
        forward = [(i, i + 1) for i in range(count - 1)]
        backward = [(target, source) for source, target in forward]
        low = lax.ppermute(
            lax.slice_in_dim(block, block.shape[dim] - width, None, axis=dim), axis, forward
        )
        high = lax.ppermute(lax.slice_in_dim(block, 0, width, axis=dim), axis, backward)
        block = jnp.concatenate([low, block, high], axis=dim)
    return block


def fold_product(left_side, block_rows):
    return jnp.dot(left_side, block_rows, preferred_element_type=jnp.float32)


def add_states(earlier, later):
    return earlier + later


def causal_states(key_feat, values):
    key_heads = key_feat.reshape(-1, HEADS, HEAD_DIM)
    value_heads = values.reshape(-1, HEADS, HEAD_DIM)
    frame_state = jnp.einsum(
        "thd,the->hde", key_heads, value_heads, preferred_element_type=jnp.float32
    )
    flat_state = frame_state.reshape(-1)
    frame_sum = lax.psum(flat_state.astype(jnp.bfloat16), "space").astype(jnp.float32)
    earlier = entering(frame_sum, "tm", add_states, jnp.zeros_like(frame_sum))
    whole_state = earlier + frame_sum
    return whole_state.reshape(HEADS, HEAD_DIM, HEAD_DIM)


def general_form(video_tokens, qkv_weight, out_weight, conv_weight, norm_gain):
    frame_now = video_tokens[0]
    row_count, col_count, feat_width = frame_now.shape
    tokens = frame_now.reshape(row_count * col_count, feat_width)
    projected = fold_product(tokens, lax.all_gather(qkv_weight, "space", axis=0, tiled=True))
    query_feat = jax.nn.relu(projected[:, :feat_width]).astype(jnp.bfloat16)
    key_feat = jax.nn.relu(projected[:, feat_width : 2 * feat_width]).astype(jnp.bfloat16)
    values = projected[:, 2 * feat_width :].astype(jnp.bfloat16)
    state_all = causal_states(key_feat, values)
    padded_rows = with_halo(values.reshape(row_count, col_count, feat_width), (("space", 0),), 1)
    padded = jnp.pad(padded_rows, ((0, 0), (1, 1), (0, 0))).astype(jnp.float32)
    local_term = jnp.zeros((row_count, col_count, feat_width), jnp.float32)
    for row_shift in range(3):
        for col_shift in range(3):
            local_term = (
                local_term
                + conv_weight[row_shift, col_shift]
                * padded[row_shift : row_shift + row_count, col_shift : col_shift + col_count]
            )
    state_low = state_all.astype(jnp.bfloat16)
    query_heads = query_feat.reshape(-1, HEADS, HEAD_DIM)
    readout = jnp.einsum("thd,hde->the", query_heads, state_low, preferred_element_type=jnp.float32)
    readout = readout.reshape(-1, feat_width)
    mean_square = jnp.mean(readout * readout, axis=-1, keepdims=True)
    normed = readout * lax.rsqrt(mean_square + 1e-06) * norm_gain
    mixture = (normed + local_term.reshape(-1, feat_width)).astype(jnp.bfloat16)
    result = fold_product(mixture, lax.all_gather(out_weight, "space", axis=0, tiled=True))
    return result.astype(jnp.bfloat16).reshape(1, row_count, col_count, feat_width)


def coordinates():
    place = lax.axis_index("tm")
    return lax.rem(place // 4, 2), lax.rem(place // 2, 2), lax.rem(place, 2)


def shifted(value, step):
    count = lax.axis_size("space")
    return lax.ppermute(value, "space", [(i, (i + step) % count) for i in range(count)])


def flipped(value, bit_on_core):
    return lax.ppermute(value, "tm", [(t, t ^ bit_on_core[t % 2]) for t in range(8)])


def after(value, *earlier):
    return lax.optimization_barrier((value,) + earlier)[0]


def chip_places(y, x):
    return (2 * y + x, 2 * y + (1 - x), 2 * (1 - y) + x, 2 * (1 - y) + (1 - x))


def source_plane(step):
    count = lax.axis_size("space")
    return lax.rem(lax.axis_index("space") - step + count, count)


def steps_through(within, size):
    run = sum(jnp.where(within >= size * k, 1, 0) for k in range(1, len(STEPS)))
    return run, within - size * run


def landed_order(at, width, rows):
    y, x, _ = coordinates()
    planes = [source_plane(step) for step in STEPS]
    row = at + lax.broadcasted_iota(jnp.int32, (1, width), 1)

    def pick(choices, index):
        chosen = choices[-1]
        for k in range(len(choices) - 2, -1, -1):
            chosen = jnp.where(index == k, choices[k], chosen)
        return chosen

    def landed(within, size, starts):
        count = len(STEPS) * size
        slot = sum(jnp.where(within >= count * k, 1, 0) for k in range(1, len(starts)))
        run, left = steps_through(within - count * slot, size)
        return pick(planes, run) * rows + pick(starts, slot) + left

    main = landed(row - rows, MAIN, [place * MAIN for place in chip_places(y, x)])
    rest_at = rows + 4 * len(STEPS) * MAIN
    rest = landed(row - rest_at, REST, [4 * MAIN + tile * REST for tile in (y, 1 - y)])
    own = lax.axis_index("space") * rows + row
    return jnp.where(row < rows, own, jnp.where(row < rest_at, main, rest))


def whole_vmem():
    return pl.BlockSpec(memory_space=pltpu.VMEM)


def anywhere():
    return pl.BlockSpec(memory_space=pltpu.HBM)


def kernel_call(
    body, outputs, inputs, in_specs, scratch=(), flops=0, bytes_accessed=0, limit=VMEM_LIMIT
):
    return pl.pallas_call(
        body,
        out_shape=outputs,
        in_specs=in_specs,
        out_specs=jax.tree.map(lambda _: whole_vmem(), outputs),
        scratch_shapes=list(scratch),
        compiler_params=pltpu.CompilerParams(vmem_limit_bytes=limit),
        cost_estimate=pl.CostEstimate(
            flops=flops, bytes_accessed=bytes_accessed, transcendentals=0
        ),
    )(*inputs)


def pieces_kernel(qkv_ref, out_ref, first_ref, second_ref, sems):
    y, x, core = coordinates()
    depth = out_ref.shape[1]
    main = pl.ds(pl.multiple_of((2 * y + x) * MAIN, REST), MAIN)
    rest = pl.ds(pl.multiple_of(4 * MAIN + y * REST, REST), REST)
    first_columns = pl.ds(pl.multiple_of(depth * (1 + core), LANES), depth)
    rest_columns = pl.ds(pl.multiple_of(jnp.where(x == 0, depth * (1 + core), 0), LANES), depth)

    def copy(source, target, k):
        return pltpu.make_async_copy(source, target, sems.at[k])

    first_main = copy(qkv_ref.at[main, first_columns], first_ref.at[pl.ds(0, MAIN), :], 0)
    first_main.start()
    rest_target = first_ref.at[pl.ds(MAIN, REST), :]
    from_out = (core == 1) & (x == 1)

    @pl.when(from_out)
    def _():
        copy(out_ref.at[rest, :], rest_target, 1).start()

    @pl.when(jnp.logical_not(from_out))
    def _():
        copy(qkv_ref.at[rest, rest_columns], rest_target, 1).start()

    places = chip_places(y, x)
    for k, place in enumerate((places[0], places[3])):
        rows = pl.ds(pl.multiple_of(place * MAIN, REST), MAIN)

        @pl.when(core == 0)
        def _():
            copy(qkv_ref.at[rows, pl.ds(0, depth)], second_ref.at[k], 2 + k).start()

        @pl.when(core == 1)
        def _():
            copy(out_ref.at[rows, :], second_ref.at[k], 2 + k).start()

    first_main.wait()
    copy(out_ref.at[rest, :], rest_target, 1).wait()
    for k in range(2):
        copy(out_ref.at[main, :], second_ref.at[k], 2 + k).wait()


def pieces_call(qkv_weight, out_weight):
    depth = out_weight.shape[1]
    outputs = [
        jax.ShapeDtypeStruct((MAIN + REST, depth), jnp.bfloat16),
        jax.ShapeDtypeStruct((2, MAIN, depth), jnp.bfloat16),
    ]
    return kernel_call(
        pieces_kernel,
        outputs,
        (qkv_weight, out_weight),
        [anywhere(), anywhere()],
        [pltpu.SemaphoreType.DMA((4,))],
        bytes_accessed=4 * (3 * MAIN + REST) * depth,
        limit=WHOLE_VMEM,
    )


def reorder_kernel(rows, tokens_ref, moved_ref):
    depth = tokens_ref.shape[1]
    width = 3 * LANES
    row = lax.broadcasted_iota(jnp.int32, (depth, width), 0)
    for at in range(0, depth, width):
        order = landed_order(at, width, rows)
        chosen = jnp.where(row == order, 1.0, 0.0).astype(jnp.bfloat16)
        moved = jnp.dot(tokens_ref[...], chosen, preferred_element_type=jnp.float32)
        moved_ref[:, at : at + width] = moved.astype(jnp.bfloat16)


def reorder_call(tokens, rows):
    depth = tokens.shape[1]
    return kernel_call(
        functools.partial(reorder_kernel, rows),
        jax.ShapeDtypeStruct(tokens.shape, jnp.bfloat16),
        (tokens,),
        [whole_vmem()],
        flops=2 * tokens.size * depth,
        bytes_accessed=2 * tokens.size,
    )


def first_kernel(*refs):
    tokens_ref, other_ref, qkv_ref, near_ref, away_ref, first_ref, far_ref, mine_ref = refs
    slots = (
        ((near_ref, 0), (first_ref, 0), (near_ref, 1)),
        ((near_ref, 2), (first_ref, 1), (near_ref, 3)),
        ((away_ref, 0), (far_ref, 0), (away_ref, 1)),
        ((away_ref, 2), (far_ref, 1), (away_ref, 3)),
    )
    _, x, core = coordinates()
    count, depth = tokens_ref.shape
    floor = jnp.where(core == 0, 0.0, -jnp.inf).astype(jnp.float32)
    width = 3 * LANES

    for at in range(0, depth, width):
        lanes = slice(at, at + width)

        def slot(k, low, high):
            return jnp.concatenate([ref[at, low:high, lanes] for ref, at in slots[k]], axis=0)

        def by_place(low, high):
            own, first, second, far = [slot(k, low, high) for k in range(4)]
            along_x = jnp.where(core == 0, first, second)
            along_y = jnp.where(core == 0, second, first)
            return own, along_x, along_y, far

        keys, values = [qkv_ref[:, depth * k + at : depth * k + at + width] for k in (1, 2)]
        own = jnp.where(core == 0, keys, values)
        rest = by_place(MAIN, MAIN + REST)
        even = jnp.concatenate([rest[0], rest[2]], axis=0)
        odd = jnp.concatenate([rest[1], rest[3]], axis=0)
        mine_ref[2 * count :, lanes] = jnp.where(x == 1, even, odd)
        columns = jnp.concatenate(
            (own,) + by_place(0, MAIN) + (jnp.where(x == 0, even, odd),), axis=0
        )
        for k, ref in enumerate((tokens_ref, other_ref)):
            product = jnp.dot(ref[...], columns, preferred_element_type=jnp.float32)
            product = jnp.maximum(product, floor).astype(jnp.bfloat16)
            mine_ref[k * count : (k + 1) * count, lanes] = product


def first_call(tokens, other, qkv_weight, *landed):
    count, depth = tokens.shape
    inputs = (tokens, other, qkv_weight) + landed
    return kernel_call(
        first_kernel,
        jax.ShapeDtypeStruct((2 * count + 2 * len(STEPS) * REST, depth), jnp.bfloat16),
        inputs,
        [whole_vmem()] * len(inputs),
        flops=4 * tokens.size * depth,
        bytes_accessed=2 * depth * depth,
    )


def diagonal_mask():
    rows = lax.broadcasted_iota(jnp.int32, (LANES, LANES), 0) // HEAD_DIM
    columns = lax.broadcasted_iota(jnp.int32, (LANES, LANES), 1) // HEAD_DIM
    return rows == columns


def state_kernel(mine_ref, other_ref, values_ref, near_ref, next_ref, upto_ref, total_ref):
    even = lax.rem(lax.axis_index("space"), 2) == 0
    _, _, core = coordinates()
    mask = diagonal_mask()
    columns = near_ref.shape[1]
    count = values_ref.shape[0]
    later = jnp.where(core == 1, 1.0, 0.0).astype(jnp.float32)
    for group in range(mine_ref.shape[1] // LANES):
        at = slice(group * LANES, (group + 1) * LANES)

        def state(mine, other):
            keys = jnp.where(core == 0, mine, other)
            values = jnp.where(core == 0, other, mine)
            full = lax.dot_general(
                keys, values, (((0,), (0,)), ((), ())), preferred_element_type=jnp.float32
            )
            full = jnp.where(mask, full, 0.0)
            total = full[0:HEAD_DIM]
            for k in range(1, LANES // HEAD_DIM):
                total = total + full[k * HEAD_DIM : (k + 1) * HEAD_DIM]
            return total, values

        low, high = slice(0, count), slice(count, 2 * count)
        here, values = state(mine_ref[low, at], other_ref[high, at])
        there, _ = state(mine_ref[high, at], other_ref[low, at])
        values_ref[:, at] = values
        top, bottom = values[:columns], values[-columns:]
        near_ref[0, :, at] = jnp.where(even, bottom, top)
        next_ref[0, :, at] = jnp.where(even, top, bottom)
        upto_ref[group] = here + later * there
        total_ref[group] = (here + there).astype(jnp.bfloat16)


def state_call(mine, other, count, columns):
    depth = mine.shape[1]
    compact = (depth // LANES, HEAD_DIM, LANES)
    edge = jax.ShapeDtypeStruct((1, columns, depth), jnp.bfloat16)
    return kernel_call(
        state_kernel,
        [
            jax.ShapeDtypeStruct((count, depth), jnp.bfloat16),
            edge,
            edge,
            jax.ShapeDtypeStruct(compact, jnp.float32),
            jax.ShapeDtypeStruct(compact, jnp.bfloat16),
        ],
        (mine, other),
        [whole_vmem()] * 2,
        flops=4 * count * depth * LANES,
        bytes_accessed=8 * count * depth,
    )


def row_kernel(upto_ref, total_ref, beside_ref, prefix_ref, row_ref):
    _, x, _ = coordinates()
    beside = beside_ref[...].astype(jnp.float32)
    prefix_ref[...] = upto_ref[...] + jnp.where(x == 1, beside, 0.0)
    row_ref[...] = (total_ref[...].astype(jnp.float32) + beside).astype(jnp.bfloat16)


def row_call(upto, total, beside):
    return kernel_call(
        row_kernel,
        [
            jax.ShapeDtypeStruct(upto.shape, jnp.float32),
            jax.ShapeDtypeStruct(upto.shape, jnp.bfloat16),
        ],
        (upto, total, beside),
        [whole_vmem()] * 3,
        flops=2 * upto.size,
        bytes_accessed=12 * upto.size,
    )


def column_taps(sheet, taps):
    edge = jnp.zeros_like(sheet[:, :1])
    before = jnp.concatenate([edge, sheet[:, :-1]], axis=1)
    behind = jnp.concatenate([sheet[:, 1:], edge], axis=1)
    return taps[0] * before + taps[1] * sheet + taps[2] * behind


def local_kernel(values_ref, conv_ref, local_ref):
    rows, _, depth = values_ref.shape
    for at in range(0, depth, LANES):
        lanes = slice(at, at + LANES)
        taps = conv_ref[:, :, lanes]
        sheet = values_ref[:, :, lanes].astype(jnp.float32)
        local_ref[:, :, lanes] = column_taps(sheet, taps[1])
        local_ref[1:, :, lanes] = local_ref[1:, :, lanes] + column_taps(sheet[:-1], taps[0])
        local_ref[: rows - 1, :, lanes] = (
            local_ref[: rows - 1, :, lanes] + column_taps(sheet[1:], taps[2])
        )


def local_call(values, conv_weight):
    return kernel_call(
        local_kernel,
        jax.ShapeDtypeStruct(values.shape, jnp.float32),
        (values, conv_weight),
        [whole_vmem()] * 2,
        flops=18 * values.size,
        bytes_accessed=6 * values.size,
    )


def query_kernel(*refs):
    tokens_ref, qkv_ref, out_ref, *packs, ours_ref, other_ref, query_ref, weight_ref = refs
    y, x, core = coordinates()
    depth = tokens_ref.shape[1]
    rows = qkv_ref.shape[0]
    steps = len(STEPS)
    rest_at = ours_ref.shape[0] - 2 * steps * REST
    places = chip_places(y, x)
    width = 3 * LANES

    def block(of_core, index, lanes):
        pack, k = index
        mine_ref, theirs_ref = packs[2 * pack], packs[2 * pack + 1]
        return jnp.where(core == of_core, mine_ref[k, :, lanes], theirs_ref[k, :, lanes])


    def rest(of_core, lanes):
        return jnp.where(core == of_core, ours_ref[rest_at:, lanes], other_ref[rest_at:, lanes])

    def put(row, value, lanes):
        weight_ref[pl.ds(pl.multiple_of(row, REST), value.shape[0]), lanes] = value

    for at in range(0, depth, width):
        lanes = slice(at, at + width)
        order = [(0, 2 * k) for k in range(steps)] + [(1, k) for k in range(2 * steps)]
        order += [(0, 2 * k + 1) for k in range(steps)]
        columns = [qkv_ref[:, lanes]] + [block(0, k, lanes) for k in order] + [rest(0, lanes)]
        queries = jnp.dot(
            tokens_ref[...], jnp.concatenate(columns, axis=0), preferred_element_type=jnp.float32
        )
        query_ref[:, lanes] = jnp.maximum(queries, 0.0).astype(jnp.bfloat16)

        put(lax.axis_index("space") * rows, out_ref[:, lanes], lanes)
        tiles = rest(1, lanes)
        for k, step in enumerate(STEPS):
            base = source_plane(step) * rows
            held = ((0, 2 * k), (1, steps + k), (1, k), (0, 2 * k + 1))
            for place, index in zip(places, held):
                put(base + place * MAIN, block(1, index, lanes), lanes)
            for run, tile in enumerate((y, 1 - y)):
                start = (run * steps + k) * REST
                put(base + 4 * MAIN + tile * REST, tiles[start : start + REST], lanes)


def query_call(tokens, qkv_weight, out_weight, *landed):
    depth = tokens.shape[1]
    inputs = (tokens, qkv_weight, out_weight) + landed
    return kernel_call(
        query_kernel,
        [
            jax.ShapeDtypeStruct(tokens.shape, jnp.bfloat16),
            jax.ShapeDtypeStruct((depth, depth), jnp.bfloat16),
        ],
        inputs,
        [whole_vmem()] * len(inputs),
        flops=2 * tokens.size * depth,
        bytes_accessed=4 * depth * depth,
    )


def finish_kernel(*refs):
    queries_ref, weight_ref, state_ref, local_ref, near_ref, next_ref, *refs = refs
    conv_ref, gain_ref, result_ref, read_ref, mixture_ref = refs
    count, depth = queries_ref.shape
    columns = near_ref.shape[1]
    even = lax.rem(lax.axis_index("space"), 2) == 0
    mask = diagonal_mask()
    square = jnp.zeros((count, LANES), jnp.float32)
    for group in range(depth // LANES):
        lanes = slice(group * LANES, (group + 1) * LANES)
        spread = jnp.concatenate([state_ref[group]] * (LANES // HEAD_DIM), axis=0)
        spread = jnp.where(mask, spread, 0.0).astype(jnp.bfloat16)
        read = jnp.dot(queries_ref[:, lanes], spread, preferred_element_type=jnp.float32)
        read_ref[:, lanes] = read
        square = square + read * read
    scale = lax.rsqrt(jnp.sum(square, axis=1, keepdims=True) / depth + 1e-06)
    for at in range(0, depth, LANES):
        lanes = slice(at, at + LANES)
        taps = conv_ref[:, :, lanes]
        mixture = read_ref[:, lanes] * scale * gain_ref[:, lanes] + local_ref[:, lanes]
        near = near_ref[:, :, lanes].astype(jnp.float32)
        beyond = next_ref[:, :, lanes].astype(jnp.float32)
        above = column_taps(jnp.where(even, beyond, near), taps[0])[0]
        below = column_taps(jnp.where(even, near, beyond), taps[2])[0]
        middle = mixture[columns : count - columns]
        mixture = jnp.concatenate(
            [mixture[:columns] + above, middle, mixture[count - columns :] + below], axis=0
        )
        mixture_ref[:, lanes] = mixture.astype(jnp.bfloat16)
    width = 3 * LANES
    for at in range(0, depth, width):
        lanes = slice(at, at + width)
        product = jnp.dot(
            mixture_ref[...], weight_ref[:, lanes], preferred_element_type=jnp.float32
        )
        result_ref[:, lanes] = product.astype(jnp.bfloat16)


def finish_call(queries, *inputs):
    return kernel_call(
        finish_kernel,
        jax.ShapeDtypeStruct(queries.shape, jnp.bfloat16),
        (queries,) + inputs,
        [whole_vmem()] * (1 + len(inputs)),
        [pltpu.VMEM(queries.shape, jnp.float32), pltpu.VMEM(queries.shape, jnp.bfloat16)],
        flops=2 * queries.size * queries.shape[1],
        bytes_accessed=2 * queries.shape[1] ** 2,
    )


def plane_form(video_tokens, qkv_weight, out_weight, conv_weight, norm_gain):
    frame_now = video_tokens[0]
    row_count, col_count, depth = frame_now.shape
    tokens = frame_now.reshape(row_count * col_count, depth)

    first_piece, second_piece = pieces_call(qkv_weight, out_weight)
    first_piece = first_piece[None]
    one = shifted(first_piece, 1)
    three = shifted(first_piece, -1)
    tokens = reorder_call(after(tokens, second_piece), qkv_weight.shape[0])
    other_tokens = flipped(tokens, (1, 1))
    one, three = after((one, three), tokens)

    pair = jnp.concatenate([one, three])
    two = shifted(one, 1)
    pair_first = flipped(pair, (2, 4))
    near = jnp.concatenate(after((pair, pair_first), other_tokens))
    away = flipped(near, (4, 2))
    two_near = jnp.concatenate([two, flipped(two, (2, 4))])
    two_away = flipped(two_near, (4, 2))

    second_ready = after(second_piece, one, three)
    second_one = shifted(second_ready, 1)
    second_three = shifted(second_ready, -1)
    second_two = shifted(after(second_one, two_near), 1)

    mine = first_call(after(tokens, second_one, second_three), other_tokens, qkv_weight, near, away, two_near, two_away)
    other = flipped(after(mine, second_two), (1, 1))
    straight = jnp.concatenate([second_one, second_two, second_three])
    swapped_straight = flipped(straight, (1, 1))
    values, edge_near, edge_next, upto, total = state_call(mine, other, tokens.shape[0], col_count)
    total = after(total, swapped_straight)

    second_own = jnp.stack([second_one[0], second_two[0], second_three[0]])
    second_first = flipped(second_own, (2, 4))
    second_second = flipped(second_own, (4, 2))

    upto, row_total = row_call(upto, total, flipped(total, (2, 2)))
    upto = upto + lax.ppermute(row_total, "tm", [(t, t ^ 4) for t in range(4)]).astype(jnp.float32)
    count = lax.axis_size("space")
    state = after(upto, second_first, second_second)
    turned = jnp.concatenate(after((second_first, second_second), upto))
    swapped_turned = flipped(after(turned, upto), (1, 1))
    queries, weight = query_call(
        tokens,
        qkv_weight,
        out_weight,
        straight,
        swapped_straight,
        turned,
        swapped_turned,
        mine,
        other,
    )
    share = state.astype(jnp.bfloat16)
    grid = values.reshape(row_count, col_count, depth)
    local_term = local_call(grid, conv_weight).reshape(-1, depth)
    arrived = lax.ppermute(share, "space", [(i, i ^ 1) for i in range(count)])
    arrived = after(arrived, local_term, queries, weight)
    share = (share.astype(jnp.float32) + arrived.astype(jnp.float32)).astype(jnp.bfloat16)
    arrived = lax.ppermute(share, "space", [(i, count - 1 - i) for i in range(count)])
    edge_near, edge_next = after((edge_near, edge_next), share)
    edge_near = lax.ppermute(edge_near, "space", [(i, i ^ 1) for i in range(count)])
    between = [(i, i + 1) for i in range(1, count - 1, 2)]
    between += [(target, source) for source, target in between]
    edge_next = lax.ppermute(edge_next, "space", between)


    state = share.astype(jnp.float32) + arrived.astype(jnp.float32)
    result = finish_call(
        queries,
        weight,
        state,
        local_term,
        edge_near,
        edge_next,
        conv_weight,
        norm_gain[None],
    )
    return result.reshape(1, row_count, col_count, depth)


def solution(mesh):
    def per_device(video_tokens, qkv_weight, out_weight, conv_weight, norm_gain):
        fits = mesh.shape["tm"] == 8 and mesh.shape["space"] == 4
        fits = fits and qkv_weight.shape[0] == 4 * MAIN + 2 * REST
        form = plane_form if fits else general_form
        return form(video_tokens, qkv_weight, out_weight, conv_weight, norm_gain)

    in_specs = (P("tm", "space", None, None), P("space", None), P("space", None), P(), P())
    out_specs = P("tm", "space", None, None)
    return jax.shard_map(
        per_device, mesh=mesh, in_specs=in_specs, out_specs=out_specs, check_vma=False
    )
```

```python
import functools

import jax
import jax.numpy as jnp
from jax import lax
from jax.experimental import pallas as pl
from jax.experimental.pallas import tpu as pltpu
from jax.sharding import PartitionSpec as P

HEADS = 36
HEAD_DIM = 32
LANES = 128
WIDE = 2 * LANES
MAIN = 64
REST = 16
STEPS = (1, 2, 3)
VMEM_LIMIT = 24 * 1024 * 1024
WHOLE_VMEM = 63 * 1024 * 1024


def entering(value, axis, combine, identity):
    devices, place = (lax.axis_size(axis), lax.axis_index(axis))
    everything = lax.all_gather(value.astype(jnp.bfloat16), axis)
    start = jnp.broadcast_to(jnp.asarray(identity, value.dtype), value.shape)

    def lap(k, before):
        reached = k < place
        new = combine(before, everything[k].astype(value.dtype))
        return jnp.where(reached, new, before)

    return lax.fori_loop(0, devices, lap, start)


def with_halo(block, sides, width):
    for axis, dim in sides:
        count = lax.axis_size(axis)
        forward = [(i, i + 1) for i in range(count - 1)]
        backward = [(target, source) for source, target in forward]
        low = lax.ppermute(
            lax.slice_in_dim(block, block.shape[dim] - width, None, axis=dim), axis, forward
        )
        high = lax.ppermute(lax.slice_in_dim(block, 0, width, axis=dim), axis, backward)
        block = jnp.concatenate([low, block, high], axis=dim)
    return block


def fold_product(left_side, block_rows):
    return jnp.dot(left_side, block_rows, preferred_element_type=jnp.float32)


def add_states(earlier, later):
    return earlier + later


def causal_states(key_feat, values):
    key_heads = key_feat.reshape(-1, HEADS, HEAD_DIM)
    value_heads = values.reshape(-1, HEADS, HEAD_DIM)
    frame_state = jnp.einsum(
        "thd,the->hde", key_heads, value_heads, preferred_element_type=jnp.float32
    )
    flat_state = frame_state.reshape(-1)
    frame_sum = lax.psum(flat_state.astype(jnp.bfloat16), "space").astype(jnp.float32)
    earlier = entering(frame_sum, "tm", add_states, jnp.zeros_like(frame_sum))
    whole_state = earlier + frame_sum
    return whole_state.reshape(HEADS, HEAD_DIM, HEAD_DIM)


def general_form(video_tokens, qkv_weight, out_weight, conv_weight, norm_gain):
    frame_now = video_tokens[0]
    row_count, col_count, feat_width = frame_now.shape
    tokens = frame_now.reshape(row_count * col_count, feat_width)
    projected = fold_product(tokens, lax.all_gather(qkv_weight, "space", axis=0, tiled=True))
    query_feat = jax.nn.relu(projected[:, :feat_width]).astype(jnp.bfloat16)
    key_feat = jax.nn.relu(projected[:, feat_width : 2 * feat_width]).astype(jnp.bfloat16)
    values = projected[:, 2 * feat_width :].astype(jnp.bfloat16)
    state_all = causal_states(key_feat, values)
    padded_rows = with_halo(values.reshape(row_count, col_count, feat_width), (("space", 0),), 1)
    padded = jnp.pad(padded_rows, ((0, 0), (1, 1), (0, 0))).astype(jnp.float32)
    local_term = jnp.zeros((row_count, col_count, feat_width), jnp.float32)
    for row_shift in range(3):
        for col_shift in range(3):
            local_term = (
                local_term
                + conv_weight[row_shift, col_shift]
                * padded[row_shift : row_shift + row_count, col_shift : col_shift + col_count]
            )
    state_low = state_all.astype(jnp.bfloat16)
    query_heads = query_feat.reshape(-1, HEADS, HEAD_DIM)
    readout = jnp.einsum("thd,hde->the", query_heads, state_low, preferred_element_type=jnp.float32)
    readout = readout.reshape(-1, feat_width)
    mean_square = jnp.mean(readout * readout, axis=-1, keepdims=True)
    normed = readout * lax.rsqrt(mean_square + 1e-06) * norm_gain
    mixture = (normed + local_term.reshape(-1, feat_width)).astype(jnp.bfloat16)
    result = fold_product(mixture, lax.all_gather(out_weight, "space", axis=0, tiled=True))
    return result.astype(jnp.bfloat16).reshape(1, row_count, col_count, feat_width)


def coordinates():
    place = lax.axis_index("tm")
    return lax.rem(place // 4, 2), lax.rem(place // 2, 2), lax.rem(place, 2)


def shifted(value, step):
    count = lax.axis_size("space")
    return lax.ppermute(value, "space", [(i, (i + step) % count) for i in range(count)])


def flipped(value, bit_on_core):
    return lax.ppermute(value, "tm", [(t, t ^ bit_on_core[t % 2]) for t in range(8)])


def after(value, *earlier):
    return lax.optimization_barrier((value,) + earlier)[0]


def chip_places(y, x):
    return (2 * y + x, 2 * y + (1 - x), 2 * (1 - y) + x, 2 * (1 - y) + (1 - x))


def source_plane(step):
    count = lax.axis_size("space")
    return lax.rem(lax.axis_index("space") - step + count, count)


def steps_through(within, size):
    run = sum(jnp.where(within >= size * k, 1, 0) for k in range(1, len(STEPS)))
    return run, within - size * run


def landed_order(at, width, rows):
    y, x, _ = coordinates()
    planes = [source_plane(step) for step in STEPS]
    row = at + lax.broadcasted_iota(jnp.int32, (1, width), 1)

    def pick(choices, index):
        chosen = choices[-1]
        for k in range(len(choices) - 2, -1, -1):
            chosen = jnp.where(index == k, choices[k], chosen)
        return chosen

    def landed(within, size, starts):
        count = len(STEPS) * size
        slot = sum(jnp.where(within >= count * k, 1, 0) for k in range(1, len(starts)))
        run, left = steps_through(within - count * slot, size)
        return pick(planes, run) * rows + pick(starts, slot) + left

    main = landed(row - rows, MAIN, [place * MAIN for place in chip_places(y, x)])
    rest_at = rows + 4 * len(STEPS) * MAIN
    rest = landed(row - rest_at, REST, [4 * MAIN + tile * REST for tile in (y, 1 - y)])
    own = lax.axis_index("space") * rows + row
    return jnp.where(row < rows, own, jnp.where(row < rest_at, main, rest))


def whole_vmem():
    return pl.BlockSpec(memory_space=pltpu.VMEM)


def anywhere():
    return pl.BlockSpec(memory_space=pltpu.HBM)


def kernel_call(
    body, outputs, inputs, in_specs, scratch=(), flops=0, bytes_accessed=0, limit=VMEM_LIMIT
):
    return pl.pallas_call(
        body,
        out_shape=outputs,
        in_specs=in_specs,
        out_specs=jax.tree.map(lambda _: whole_vmem(), outputs),
        scratch_shapes=list(scratch),
        compiler_params=pltpu.CompilerParams(vmem_limit_bytes=limit),
        cost_estimate=pl.CostEstimate(
            flops=flops, bytes_accessed=bytes_accessed, transcendentals=0
        ),
    )(*inputs)


def pieces_kernel(qkv_ref, out_ref, first_ref, second_ref, sems):
    y, x, core = coordinates()
    depth = out_ref.shape[1]
    main = pl.ds(pl.multiple_of((2 * y + x) * MAIN, REST), MAIN)
    rest = pl.ds(pl.multiple_of(4 * MAIN + y * REST, REST), REST)
    first_columns = pl.ds(pl.multiple_of(depth * (1 + core), LANES), depth)
    rest_columns = pl.ds(pl.multiple_of(jnp.where(x == 0, depth * (1 + core), 0), LANES), depth)

    def copy(source, target, k):
        return pltpu.make_async_copy(source, target, sems.at[k])

    first_main = copy(qkv_ref.at[main, first_columns], first_ref.at[pl.ds(0, MAIN), :], 0)
    first_main.start()
    rest_target = first_ref.at[pl.ds(MAIN, REST), :]
    from_out = (core == 1) & (x == 1)

    @pl.when(from_out)
    def _():
        copy(out_ref.at[rest, :], rest_target, 1).start()

    @pl.when(jnp.logical_not(from_out))
    def _():
        copy(qkv_ref.at[rest, rest_columns], rest_target, 1).start()

    places = chip_places(y, x)
    for k, place in enumerate((places[0], places[3])):
        rows = pl.ds(pl.multiple_of(place * MAIN, REST), MAIN)

        @pl.when(core == 0)
        def _():
            copy(qkv_ref.at[rows, pl.ds(0, depth)], second_ref.at[k], 2 + k).start()

        @pl.when(core == 1)
        def _():
            copy(out_ref.at[rows, :], second_ref.at[k], 2 + k).start()

    first_main.wait()
    copy(out_ref.at[rest, :], rest_target, 1).wait()
    for k in range(2):
        copy(out_ref.at[main, :], second_ref.at[k], 2 + k).wait()


def pieces_call(qkv_weight, out_weight):
    depth = out_weight.shape[1]
    outputs = [
        jax.ShapeDtypeStruct((MAIN + REST, depth), jnp.bfloat16),
        jax.ShapeDtypeStruct((2, MAIN, depth), jnp.bfloat16),
    ]
    return kernel_call(
        pieces_kernel,
        outputs,
        (qkv_weight, out_weight),
        [anywhere(), anywhere()],
        [pltpu.SemaphoreType.DMA((4,))],
        bytes_accessed=4 * (3 * MAIN + REST) * depth,
        limit=WHOLE_VMEM,
    )


def reorder_kernel(rows, tokens_ref, moved_ref):
    depth = tokens_ref.shape[1]
    width = 3 * LANES
    row = lax.broadcasted_iota(jnp.int32, (depth, width), 0)
    for at in range(0, depth, width):
        order = landed_order(at, width, rows)
        chosen = jnp.where(row == order, 1.0, 0.0).astype(jnp.bfloat16)
        moved = jnp.dot(tokens_ref[...], chosen, preferred_element_type=jnp.float32)
        moved_ref[:, at : at + width] = moved.astype(jnp.bfloat16)


def reorder_call(tokens, rows):
    depth = tokens.shape[1]
    return kernel_call(
        functools.partial(reorder_kernel, rows),
        jax.ShapeDtypeStruct(tokens.shape, jnp.bfloat16),
        (tokens,),
        [whole_vmem()],
        flops=2 * tokens.size * depth,
        bytes_accessed=2 * tokens.size,
    )


def first_kernel(*refs):
    tokens_ref, other_ref, qkv_ref, near_ref, away_ref, first_ref, far_ref, mine_ref = refs
    slots = (
        ((near_ref, 0), (first_ref, 0), (near_ref, 1)),
        ((near_ref, 2), (first_ref, 1), (near_ref, 3)),
        ((away_ref, 0), (far_ref, 0), (away_ref, 1)),
        ((away_ref, 2), (far_ref, 1), (away_ref, 3)),
    )
    _, x, core = coordinates()
    count, depth = tokens_ref.shape
    floor = jnp.where(core == 0, 0.0, -jnp.inf).astype(jnp.float32)
    for at in range(0, depth, WIDE):
        width = min(WIDE, depth - at)
        lanes = slice(at, at + width)

        def slot(k, low, high):
            return jnp.concatenate([ref[at, low:high, lanes] for ref, at in slots[k]], axis=0)

        def by_place(low, high):
            own, first, second, far = [slot(k, low, high) for k in range(4)]
            along_x = jnp.where(core == 0, first, second)
            along_y = jnp.where(core == 0, second, first)
            return own, along_x, along_y, far

        keys, values = [qkv_ref[:, depth * k + at : depth * k + at + width] for k in (1, 2)]
        own = jnp.where(core == 0, keys, values)
        rest = by_place(MAIN, MAIN + REST)
        even = jnp.concatenate([rest[0], rest[2]], axis=0)
        odd = jnp.concatenate([rest[1], rest[3]], axis=0)
        mine_ref[2 * count :, lanes] = jnp.where(x == 1, even, odd)
        columns = jnp.concatenate(
            (own,) + by_place(0, MAIN) + (jnp.where(x == 0, even, odd),), axis=0
        )
        for k, ref in enumerate((tokens_ref, other_ref)):
            product = jnp.dot(ref[...], columns, preferred_element_type=jnp.float32)
            product = jnp.maximum(product, floor).astype(jnp.bfloat16)
            mine_ref[k * count : (k + 1) * count, lanes] = product


def first_call(tokens, other, qkv_weight, *landed):
    count, depth = tokens.shape
    inputs = (tokens, other, qkv_weight) + landed
    return kernel_call(
        first_kernel,
        jax.ShapeDtypeStruct((2 * count + 2 * len(STEPS) * REST, depth), jnp.bfloat16),
        inputs,
        [whole_vmem()] * len(inputs),
        flops=4 * tokens.size * depth,
        bytes_accessed=2 * depth * depth,
    )


def diagonal_mask():
    rows = lax.broadcasted_iota(jnp.int32, (LANES, LANES), 0) // HEAD_DIM
    columns = lax.broadcasted_iota(jnp.int32, (LANES, LANES), 1) // HEAD_DIM
    return rows == columns


def state_kernel(mine_ref, other_ref, values_ref, near_ref, next_ref, upto_ref, total_ref):
    even = lax.rem(lax.axis_index("space"), 2) == 0
    _, _, core = coordinates()
    mask = diagonal_mask()
    columns = near_ref.shape[1]
    count = values_ref.shape[0]
    later = jnp.where(core == 1, 1.0, 0.0).astype(jnp.float32)
    for group in range(mine_ref.shape[1] // LANES):
        at = slice(group * LANES, (group + 1) * LANES)

        def state(mine, other):
            keys = jnp.where(core == 0, mine, other)
            values = jnp.where(core == 0, other, mine)
            full = lax.dot_general(
                keys, values, (((0,), (0,)), ((), ())), preferred_element_type=jnp.float32
            )
            full = jnp.where(mask, full, 0.0)
            total = full[0:HEAD_DIM]
            for k in range(1, LANES // HEAD_DIM):
                total = total + full[k * HEAD_DIM : (k + 1) * HEAD_DIM]
            return total, values

        low, high = slice(0, count), slice(count, 2 * count)
        here, values = state(mine_ref[low, at], other_ref[high, at])
        there, _ = state(mine_ref[high, at], other_ref[low, at])
        values_ref[:, at] = values
        top, bottom = values[:columns], values[-columns:]
        near_ref[0, :, at] = jnp.where(even, bottom, top)
        next_ref[0, :, at] = jnp.where(even, top, bottom)
        upto_ref[group] = here + later * there
        total_ref[group] = (here + there).astype(jnp.bfloat16)


def state_call(mine, other, count, columns):
    depth = mine.shape[1]
    compact = (depth // LANES, HEAD_DIM, LANES)
    edge = jax.ShapeDtypeStruct((1, columns, depth), jnp.bfloat16)
    return kernel_call(
        state_kernel,
        [
            jax.ShapeDtypeStruct((count, depth), jnp.bfloat16),
            edge,
            edge,
            jax.ShapeDtypeStruct(compact, jnp.float32),
            jax.ShapeDtypeStruct(compact, jnp.bfloat16),
        ],
        (mine, other),
        [whole_vmem()] * 2,
        flops=4 * count * depth * LANES,
        bytes_accessed=8 * count * depth,
    )


def column_taps(sheet, taps):
    edge = jnp.zeros_like(sheet[:, :1])
    before = jnp.concatenate([edge, sheet[:, :-1]], axis=1)
    behind = jnp.concatenate([sheet[:, 1:], edge], axis=1)
    return taps[0] * before + taps[1] * sheet + taps[2] * behind


def local_kernel(values_ref, conv_ref, local_ref):
    rows, _, depth = values_ref.shape
    for at in range(0, depth, LANES):
        lanes = slice(at, at + LANES)
        taps = conv_ref[:, :, lanes]
        sheet = values_ref[:, :, lanes].astype(jnp.float32)
        local_ref[:, :, lanes] = column_taps(sheet, taps[1])
        local_ref[1:, :, lanes] = local_ref[1:, :, lanes] + column_taps(sheet[:-1], taps[0])
        local_ref[: rows - 1, :, lanes] = (
            local_ref[: rows - 1, :, lanes] + column_taps(sheet[1:], taps[2])
        )


def local_call(values, conv_weight):
    return kernel_call(
        local_kernel,
        jax.ShapeDtypeStruct(values.shape, jnp.float32),
        (values, conv_weight),
        [whole_vmem()] * 2,
        flops=18 * values.size,
        bytes_accessed=6 * values.size,
    )


def query_kernel(*refs):
    tokens_ref, qkv_ref, out_ref, *packs, ours_ref, other_ref, query_ref, weight_ref = refs
    y, x, core = coordinates()
    depth = tokens_ref.shape[1]
    rows = qkv_ref.shape[0]
    steps = len(STEPS)
    rest_at = ours_ref.shape[0] - 2 * steps * REST
    places = chip_places(y, x)

    def block(of_core, index, lanes):
        pack, k = index
        mine_ref, theirs_ref = packs[2 * pack], packs[2 * pack + 1]
        return jnp.where(core == of_core, mine_ref[k, :, lanes], theirs_ref[k, :, lanes])


    def rest(of_core, lanes):
        return jnp.where(core == of_core, ours_ref[rest_at:, lanes], other_ref[rest_at:, lanes])

    def put(row, value, lanes):
        weight_ref[pl.ds(pl.multiple_of(row, REST), value.shape[0]), lanes] = value

    for at in range(0, depth, WIDE):
        lanes = slice(at, min(at + WIDE, depth))
        order = [(0, 2 * k) for k in range(steps)] + [(1, k) for k in range(2 * steps)]
        order += [(0, 2 * k + 1) for k in range(steps)]
        columns = [qkv_ref[:, lanes]] + [block(0, k, lanes) for k in order] + [rest(0, lanes)]
        queries = jnp.dot(
            tokens_ref[...], jnp.concatenate(columns, axis=0), preferred_element_type=jnp.float32
        )
        query_ref[:, lanes] = jnp.maximum(queries, 0.0).astype(jnp.bfloat16)

        put(lax.axis_index("space") * rows, out_ref[:, lanes], lanes)
        tiles = rest(1, lanes)
        for k, step in enumerate(STEPS):
            base = source_plane(step) * rows
            held = ((0, 2 * k), (1, steps + k), (1, k), (0, 2 * k + 1))
            for place, index in zip(places, held):
                put(base + place * MAIN, block(1, index, lanes), lanes)
            for run, tile in enumerate((y, 1 - y)):
                start = (run * steps + k) * REST
                put(base + 4 * MAIN + tile * REST, tiles[start : start + REST], lanes)


def query_call(tokens, qkv_weight, out_weight, *landed):
    depth = tokens.shape[1]
    inputs = (tokens, qkv_weight, out_weight) + landed
    return kernel_call(
        query_kernel,
        [
            jax.ShapeDtypeStruct(tokens.shape, jnp.bfloat16),
            jax.ShapeDtypeStruct((depth, depth), jnp.bfloat16),
        ],
        inputs,
        [whole_vmem()] * len(inputs),
        flops=2 * tokens.size * depth,
        bytes_accessed=4 * depth * depth,
    )


def finish_kernel(*refs):
    queries_ref, weight_ref, state_ref, local_ref, near_ref, next_ref, *refs = refs
    conv_ref, gain_ref, result_ref, read_ref, mixture_ref = refs
    count, depth = queries_ref.shape
    columns = near_ref.shape[1]
    even = lax.rem(lax.axis_index("space"), 2) == 0
    mask = diagonal_mask()
    square = jnp.zeros((count, LANES), jnp.float32)
    for group in range(depth // LANES):
        lanes = slice(group * LANES, (group + 1) * LANES)
        spread = jnp.concatenate([state_ref[group]] * (LANES // HEAD_DIM), axis=0)
        spread = jnp.where(mask, spread, 0.0).astype(jnp.bfloat16)
        read = jnp.dot(queries_ref[:, lanes], spread, preferred_element_type=jnp.float32)
        read_ref[:, lanes] = read
        square = square + read * read
    scale = lax.rsqrt(jnp.sum(square, axis=1, keepdims=True) / depth + 1e-06)
    for at in range(0, depth, LANES):
        lanes = slice(at, at + LANES)
        taps = conv_ref[:, :, lanes]
        mixture = read_ref[:, lanes] * scale * gain_ref[:, lanes] + local_ref[:, lanes]
        near = near_ref[:, :, lanes].astype(jnp.float32)
        beyond = next_ref[:, :, lanes].astype(jnp.float32)
        above = column_taps(jnp.where(even, beyond, near), taps[0])[0]
        below = column_taps(jnp.where(even, near, beyond), taps[2])[0]
        middle = mixture[columns : count - columns]
        mixture = jnp.concatenate(
            [mixture[:columns] + above, middle, mixture[count - columns :] + below], axis=0
        )
        mixture_ref[:, lanes] = mixture.astype(jnp.bfloat16)
    for at in range(0, depth, WIDE):
        lanes = slice(at, min(at + WIDE, depth))
        product = jnp.dot(
            mixture_ref[...], weight_ref[:, lanes], preferred_element_type=jnp.float32
        )
        result_ref[:, lanes] = product.astype(jnp.bfloat16)


def finish_call(queries, *inputs):
    return kernel_call(
        finish_kernel,
        jax.ShapeDtypeStruct(queries.shape, jnp.bfloat16),
        (queries,) + inputs,
        [whole_vmem()] * (1 + len(inputs)),
        [pltpu.VMEM(queries.shape, jnp.float32), pltpu.VMEM(queries.shape, jnp.bfloat16)],
        flops=2 * queries.size * queries.shape[1],
        bytes_accessed=2 * queries.shape[1] ** 2,
    )


def plane_form(video_tokens, qkv_weight, out_weight, conv_weight, norm_gain):
    frame_now = video_tokens[0]
    row_count, col_count, depth = frame_now.shape
    tokens = frame_now.reshape(row_count * col_count, depth)

    first_piece, second_piece = pieces_call(qkv_weight, out_weight)
    first_piece = first_piece[None]
    one = shifted(first_piece, 1)
    three = shifted(first_piece, -1)
    tokens = reorder_call(after(tokens, second_piece), qkv_weight.shape[0])
    other_tokens = flipped(tokens, (1, 1))
    one, three = after((one, three), tokens)

    pair = jnp.concatenate([one, three])
    two = shifted(one, 1)
    pair_first = flipped(pair, (2, 4))
    near = jnp.concatenate(after((pair, pair_first), other_tokens))
    away = flipped(near, (4, 2))
    two_near = jnp.concatenate([two, flipped(two, (2, 4))])
    two_away = flipped(two_near, (4, 2))

    second_ready = after(second_piece, one, three)
    second_one = shifted(second_ready, 1)
    second_three = shifted(second_ready, -1)
    second_two = shifted(after(second_one, two_near), 1)

    mine = first_call(after(tokens, second_one, second_three), other_tokens, qkv_weight, near, away, two_near, two_away)
    other = flipped(after(mine, second_two), (1, 1))
    straight = jnp.concatenate([second_one, second_two, second_three])
    swapped_straight = flipped(straight, (1, 1))
    values, edge_near, edge_next, upto, total = state_call(mine, other, tokens.shape[0], col_count)
    total = after(total, swapped_straight)

    second_own = jnp.stack([second_one[0], second_two[0], second_three[0]])
    second_first = flipped(second_own, (2, 4))
    second_second = flipped(second_own, (4, 2))

    for bit, guard in ((2, 2), (4, 4), (6, 4)):
        pairs = [(t, t ^ bit) for t in range(8) if not t & guard]
        upto = upto + lax.ppermute(total, "tm", pairs).astype(jnp.float32)
    count = lax.axis_size("space")
    state = after(upto, second_first, second_second)
    turned = jnp.concatenate(after((second_first, second_second), total))
    swapped_turned = flipped(after(turned, upto), (1, 1))
    queries, weight = query_call(
        tokens,
        qkv_weight,
        out_weight,
        straight,
        swapped_straight,
        turned,
        swapped_turned,
        mine,
        other,
    )
    share = state.astype(jnp.bfloat16)
    grid = values.reshape(row_count, col_count, depth)
    local_term = local_call(grid, conv_weight).reshape(-1, depth)
    arrived = lax.ppermute(share, "space", [(i, i ^ 1) for i in range(count)])
    arrived = after(arrived, local_term, queries, weight)
    share = (share.astype(jnp.float32) + arrived.astype(jnp.float32)).astype(jnp.bfloat16)
    arrived = lax.ppermute(share, "space", [(i, count - 1 - i) for i in range(count)])
    edge_near, edge_next = after((edge_near, edge_next), share)
    edge_near = lax.ppermute(edge_near, "space", [(i, i ^ 1) for i in range(count)])
    between = [(i, i + 1) for i in range(1, count - 1, 2)]
    between += [(target, source) for source, target in between]
    edge_next = lax.ppermute(edge_next, "space", between)


    state = share.astype(jnp.float32) + arrived.astype(jnp.float32)
    result = finish_call(
        queries,
        weight,
        state,
        local_term,
        edge_near,
        edge_next,
        conv_weight,
        norm_gain[None],
    )
    return result.reshape(1, row_count, col_count, depth)


def solution(mesh):
    def per_device(video_tokens, qkv_weight, out_weight, conv_weight, norm_gain):
        fits = mesh.shape["tm"] == 8 and mesh.shape["space"] == 4
        fits = fits and qkv_weight.shape[0] == 4 * MAIN + 2 * REST
        form = plane_form if fits else general_form
        return form(video_tokens, qkv_weight, out_weight, conv_weight, norm_gain)

    in_specs = (P("tm", "space", None, None), P("space", None), P("space", None), P(), P())
    out_specs = P("tm", "space", None, None)
    return jax.shard_map(
        per_device, mesh=mesh, in_specs=in_specs, out_specs=out_specs, check_vma=False
    )
```

```python
import functools

import jax
import jax.numpy as jnp
from jax import lax
from jax.experimental import pallas as pl
from jax.experimental.pallas import tpu as pltpu
from jax.sharding import PartitionSpec as P

HEADS = 36
HEAD_DIM = 32
LANES = 128
WIDE = 2 * LANES
MAIN = 64
REST = 16
STEPS = (1, 2, 3)
VMEM_LIMIT = 24 * 1024 * 1024
WHOLE_VMEM = 63 * 1024 * 1024


def entering(value, axis, combine, identity):
    devices, place = (lax.axis_size(axis), lax.axis_index(axis))
    everything = lax.all_gather(value.astype(jnp.bfloat16), axis)
    start = jnp.broadcast_to(jnp.asarray(identity, value.dtype), value.shape)

    def lap(k, before):
        reached = k < place
        new = combine(before, everything[k].astype(value.dtype))
        return jnp.where(reached, new, before)

    return lax.fori_loop(0, devices, lap, start)


def with_halo(block, sides, width):
    for axis, dim in sides:
        count = lax.axis_size(axis)
        forward = [(i, i + 1) for i in range(count - 1)]
        backward = [(target, source) for source, target in forward]
        low = lax.ppermute(
            lax.slice_in_dim(block, block.shape[dim] - width, None, axis=dim), axis, forward
        )
        high = lax.ppermute(lax.slice_in_dim(block, 0, width, axis=dim), axis, backward)
        block = jnp.concatenate([low, block, high], axis=dim)
    return block


def fold_product(left_side, block_rows):
    return jnp.dot(left_side, block_rows, preferred_element_type=jnp.float32)


def add_states(earlier, later):
    return earlier + later


def causal_states(key_feat, values):
    key_heads = key_feat.reshape(-1, HEADS, HEAD_DIM)
    value_heads = values.reshape(-1, HEADS, HEAD_DIM)
    frame_state = jnp.einsum(
        "thd,the->hde", key_heads, value_heads, preferred_element_type=jnp.float32
    )
    flat_state = frame_state.reshape(-1)
    frame_sum = lax.psum(flat_state.astype(jnp.bfloat16), "space").astype(jnp.float32)
    earlier = entering(frame_sum, "tm", add_states, jnp.zeros_like(frame_sum))
    whole_state = earlier + frame_sum
    return whole_state.reshape(HEADS, HEAD_DIM, HEAD_DIM)


def general_form(video_tokens, qkv_weight, out_weight, conv_weight, norm_gain):
    frame_now = video_tokens[0]
    row_count, col_count, feat_width = frame_now.shape
    tokens = frame_now.reshape(row_count * col_count, feat_width)
    projected = fold_product(tokens, lax.all_gather(qkv_weight, "space", axis=0, tiled=True))
    query_feat = jax.nn.relu(projected[:, :feat_width]).astype(jnp.bfloat16)
    key_feat = jax.nn.relu(projected[:, feat_width : 2 * feat_width]).astype(jnp.bfloat16)
    values = projected[:, 2 * feat_width :].astype(jnp.bfloat16)
    state_all = causal_states(key_feat, values)
    padded_rows = with_halo(values.reshape(row_count, col_count, feat_width), (("space", 0),), 1)
    padded = jnp.pad(padded_rows, ((0, 0), (1, 1), (0, 0))).astype(jnp.float32)
    local_term = jnp.zeros((row_count, col_count, feat_width), jnp.float32)
    for row_shift in range(3):
        for col_shift in range(3):
            local_term = (
                local_term
                + conv_weight[row_shift, col_shift]
                * padded[row_shift : row_shift + row_count, col_shift : col_shift + col_count]
            )
    state_low = state_all.astype(jnp.bfloat16)
    query_heads = query_feat.reshape(-1, HEADS, HEAD_DIM)
    readout = jnp.einsum("thd,hde->the", query_heads, state_low, preferred_element_type=jnp.float32)
    readout = readout.reshape(-1, feat_width)
    mean_square = jnp.mean(readout * readout, axis=-1, keepdims=True)
    normed = readout * lax.rsqrt(mean_square + 1e-06) * norm_gain
    mixture = (normed + local_term.reshape(-1, feat_width)).astype(jnp.bfloat16)
    result = fold_product(mixture, lax.all_gather(out_weight, "space", axis=0, tiled=True))
    return result.astype(jnp.bfloat16).reshape(1, row_count, col_count, feat_width)


def coordinates():
    place = lax.axis_index("tm")
    return lax.rem(place // 4, 2), lax.rem(place // 2, 2), lax.rem(place, 2)


def shifted(value, step):
    count = lax.axis_size("space")
    return lax.ppermute(value, "space", [(i, (i + step) % count) for i in range(count)])


def flipped(value, bit_on_core):
    return lax.ppermute(value, "tm", [(t, t ^ bit_on_core[t % 2]) for t in range(8)])


def after(value, *earlier):
    return lax.optimization_barrier((value,) + earlier)[0]


def chip_places(y, x):
    return (2 * y + x, 2 * y + (1 - x), 2 * (1 - y) + x, 2 * (1 - y) + (1 - x))


def source_plane(step):
    count = lax.axis_size("space")
    return lax.rem(lax.axis_index("space") - step + count, count)


def steps_through(within, size):
    run = sum(jnp.where(within >= size * k, 1, 0) for k in range(1, len(STEPS)))
    return run, within - size * run


def landed_order(at, width, rows):
    y, x, _ = coordinates()
    planes = [source_plane(step) for step in STEPS]
    row = at + lax.broadcasted_iota(jnp.int32, (1, width), 1)

    def pick(choices, index):
        chosen = choices[-1]
        for k in range(len(choices) - 2, -1, -1):
            chosen = jnp.where(index == k, choices[k], chosen)
        return chosen

    def landed(within, size, starts):
        count = len(STEPS) * size
        slot = sum(jnp.where(within >= count * k, 1, 0) for k in range(1, len(starts)))
        run, left = steps_through(within - count * slot, size)
        return pick(planes, run) * rows + pick(starts, slot) + left

    main = landed(row - rows, MAIN, [place * MAIN for place in chip_places(y, x)])
    rest_at = rows + 4 * len(STEPS) * MAIN
    rest = landed(row - rest_at, REST, [4 * MAIN + tile * REST for tile in (y, 1 - y)])
    own = lax.axis_index("space") * rows + row
    return jnp.where(row < rows, own, jnp.where(row < rest_at, main, rest))


def whole_vmem():
    return pl.BlockSpec(memory_space=pltpu.VMEM)


def anywhere():
    return pl.BlockSpec(memory_space=pltpu.HBM)


def kernel_call(
    body, outputs, inputs, in_specs, scratch=(), flops=0, bytes_accessed=0, limit=VMEM_LIMIT
):
    return pl.pallas_call(
        body,
        out_shape=outputs,
        in_specs=in_specs,
        out_specs=jax.tree.map(lambda _: whole_vmem(), outputs),
        scratch_shapes=list(scratch),
        compiler_params=pltpu.CompilerParams(vmem_limit_bytes=limit),
        cost_estimate=pl.CostEstimate(
            flops=flops, bytes_accessed=bytes_accessed, transcendentals=0
        ),
    )(*inputs)


def pieces_kernel(qkv_ref, out_ref, first_ref, second_ref, sems):
    y, x, core = coordinates()
    depth = out_ref.shape[1]
    main = pl.ds(pl.multiple_of((2 * y + x) * MAIN, REST), MAIN)
    rest = pl.ds(pl.multiple_of(4 * MAIN + y * REST, REST), REST)
    first_columns = pl.ds(pl.multiple_of(depth * (1 + core), LANES), depth)
    rest_columns = pl.ds(pl.multiple_of(jnp.where(x == 0, depth * (1 + core), 0), LANES), depth)

    def copy(source, target, k):
        return pltpu.make_async_copy(source, target, sems.at[k])

    first_main = copy(qkv_ref.at[main, first_columns], first_ref.at[pl.ds(0, MAIN), :], 0)
    first_main.start()
    rest_target = first_ref.at[pl.ds(MAIN, REST), :]
    from_out = (core == 1) & (x == 1)

    @pl.when(from_out)
    def _():
        copy(out_ref.at[rest, :], rest_target, 1).start()

    @pl.when(jnp.logical_not(from_out))
    def _():
        copy(qkv_ref.at[rest, rest_columns], rest_target, 1).start()

    places = chip_places(y, x)
    for k, place in enumerate((places[0], places[3])):
        rows = pl.ds(pl.multiple_of(place * MAIN, REST), MAIN)

        @pl.when(core == 0)
        def _():
            copy(qkv_ref.at[rows, pl.ds(0, depth)], second_ref.at[k], 2 + k).start()

        @pl.when(core == 1)
        def _():
            copy(out_ref.at[rows, :], second_ref.at[k], 2 + k).start()

    first_main.wait()
    copy(out_ref.at[rest, :], rest_target, 1).wait()
    for k in range(2):
        copy(out_ref.at[main, :], second_ref.at[k], 2 + k).wait()


def pieces_call(qkv_weight, out_weight):
    depth = out_weight.shape[1]
    outputs = [
        jax.ShapeDtypeStruct((MAIN + REST, depth), jnp.bfloat16),
        jax.ShapeDtypeStruct((2, MAIN, depth), jnp.bfloat16),
    ]
    return kernel_call(
        pieces_kernel,
        outputs,
        (qkv_weight, out_weight),
        [anywhere(), anywhere()],
        [pltpu.SemaphoreType.DMA((4,))],
        bytes_accessed=4 * (3 * MAIN + REST) * depth,
        limit=WHOLE_VMEM,
    )


def reorder_kernel(rows, tokens_ref, moved_ref):
    depth = tokens_ref.shape[1]
    width = 3 * LANES
    row = lax.broadcasted_iota(jnp.int32, (depth, width), 0)
    for at in range(0, depth, width):
        order = landed_order(at, width, rows)
        chosen = jnp.where(row == order, 1.0, 0.0).astype(jnp.bfloat16)
        moved = jnp.dot(tokens_ref[...], chosen, preferred_element_type=jnp.float32)
        moved_ref[:, at : at + width] = moved.astype(jnp.bfloat16)


def reorder_call(tokens, rows):
    depth = tokens.shape[1]
    return kernel_call(
        functools.partial(reorder_kernel, rows),
        jax.ShapeDtypeStruct(tokens.shape, jnp.bfloat16),
        (tokens,),
        [whole_vmem()],
        flops=2 * tokens.size * depth,
        bytes_accessed=2 * tokens.size,
    )


def first_kernel(*refs):
    tokens_ref, other_ref, qkv_ref, near_ref, away_ref, first_ref, far_ref, mine_ref = refs
    slots = (
        ((near_ref, 0), (first_ref, 0), (near_ref, 1)),
        ((near_ref, 2), (first_ref, 1), (near_ref, 3)),
        ((away_ref, 0), (far_ref, 0), (away_ref, 1)),
        ((away_ref, 2), (far_ref, 1), (away_ref, 3)),
    )
    _, x, core = coordinates()
    count, depth = tokens_ref.shape
    floor = jnp.where(core == 0, 0.0, -jnp.inf).astype(jnp.float32)
    for at in range(0, depth, WIDE):
        width = min(WIDE, depth - at)
        lanes = slice(at, at + width)

        def slot(k, low, high):
            return jnp.concatenate([ref[at, low:high, lanes] for ref, at in slots[k]], axis=0)

        def by_place(low, high):
            own, first, second, far = [slot(k, low, high) for k in range(4)]
            along_x = jnp.where(core == 0, first, second)
            along_y = jnp.where(core == 0, second, first)
            return own, along_x, along_y, far

        keys, values = [qkv_ref[:, depth * k + at : depth * k + at + width] for k in (1, 2)]
        own = jnp.where(core == 0, keys, values)
        rest = by_place(MAIN, MAIN + REST)
        even = jnp.concatenate([rest[0], rest[2]], axis=0)
        odd = jnp.concatenate([rest[1], rest[3]], axis=0)
        mine_ref[2 * count :, lanes] = jnp.where(x == 1, even, odd)
        columns = jnp.concatenate(
            (own,) + by_place(0, MAIN) + (jnp.where(x == 0, even, odd),), axis=0
        )
        for k, ref in enumerate((tokens_ref, other_ref)):
            product = jnp.dot(ref[...], columns, preferred_element_type=jnp.float32)
            product = jnp.maximum(product, floor).astype(jnp.bfloat16)
            mine_ref[k * count : (k + 1) * count, lanes] = product


def first_call(tokens, other, qkv_weight, *landed):
    count, depth = tokens.shape
    inputs = (tokens, other, qkv_weight) + landed
    return kernel_call(
        first_kernel,
        jax.ShapeDtypeStruct((2 * count + 2 * len(STEPS) * REST, depth), jnp.bfloat16),
        inputs,
        [whole_vmem()] * len(inputs),
        flops=4 * tokens.size * depth,
        bytes_accessed=2 * depth * depth,
    )


def diagonal_mask():
    rows = lax.broadcasted_iota(jnp.int32, (LANES, LANES), 0) // HEAD_DIM
    columns = lax.broadcasted_iota(jnp.int32, (LANES, LANES), 1) // HEAD_DIM
    return rows == columns


def state_kernel(mine_ref, other_ref, values_ref, near_ref, next_ref, upto_ref, total_ref):
    even = lax.rem(lax.axis_index("space"), 2) == 0
    _, _, core = coordinates()
    mask = diagonal_mask()
    columns = near_ref.shape[1]
    count = values_ref.shape[0]
    later = jnp.where(core == 1, 1.0, 0.0).astype(jnp.float32)
    for group in range(mine_ref.shape[1] // LANES):
        at = slice(group * LANES, (group + 1) * LANES)

        def state(mine, other):
            keys = jnp.where(core == 0, mine, other)
            values = jnp.where(core == 0, other, mine)
            full = lax.dot_general(
                keys, values, (((0,), (0,)), ((), ())), preferred_element_type=jnp.float32
            )
            full = jnp.where(mask, full, 0.0)
            total = full[0:HEAD_DIM]
            for k in range(1, LANES // HEAD_DIM):
                total = total + full[k * HEAD_DIM : (k + 1) * HEAD_DIM]
            return total, values

        low, high = slice(0, count), slice(count, 2 * count)
        here, values = state(mine_ref[low, at], other_ref[high, at])
        there, _ = state(mine_ref[high, at], other_ref[low, at])
        values_ref[:, at] = values
        top, bottom = values[:columns], values[-columns:]
        near_ref[0, :, at] = jnp.where(even, bottom, top)
        next_ref[0, :, at] = jnp.where(even, top, bottom)
        upto_ref[group] = here + later * there
        total_ref[group] = (here + there).astype(jnp.bfloat16)


def state_call(mine, other, count, columns):
    depth = mine.shape[1]
    compact = (depth // LANES, HEAD_DIM, LANES)
    edge = jax.ShapeDtypeStruct((1, columns, depth), jnp.bfloat16)
    return kernel_call(
        state_kernel,
        [
            jax.ShapeDtypeStruct((count, depth), jnp.bfloat16),
            edge,
            edge,
            jax.ShapeDtypeStruct(compact, jnp.float32),
            jax.ShapeDtypeStruct(compact, jnp.bfloat16),
        ],
        (mine, other),
        [whole_vmem()] * 2,
        flops=4 * count * depth * LANES,
        bytes_accessed=8 * count * depth,
    )


def column_taps(sheet, taps):
    edge = jnp.zeros_like(sheet[:, :1])
    before = jnp.concatenate([edge, sheet[:, :-1]], axis=1)
    behind = jnp.concatenate([sheet[:, 1:], edge], axis=1)
    return taps[0] * before + taps[1] * sheet + taps[2] * behind


def local_kernel(values_ref, conv_ref, local_ref):
    rows, _, depth = values_ref.shape
    for at in range(0, depth, LANES):
        lanes = slice(at, at + LANES)
        taps = conv_ref[:, :, lanes]
        sheet = values_ref[:, :, lanes].astype(jnp.float32)
        local_ref[:, :, lanes] = column_taps(sheet, taps[1])
        local_ref[1:, :, lanes] = local_ref[1:, :, lanes] + column_taps(sheet[:-1], taps[0])
        local_ref[: rows - 1, :, lanes] = (
            local_ref[: rows - 1, :, lanes] + column_taps(sheet[1:], taps[2])
        )


def local_call(values, conv_weight):
    return kernel_call(
        local_kernel,
        jax.ShapeDtypeStruct(values.shape, jnp.float32),
        (values, conv_weight),
        [whole_vmem()] * 2,
        flops=18 * values.size,
        bytes_accessed=6 * values.size,
    )


def query_kernel(*refs):
    tokens_ref, qkv_ref, out_ref, *packs, ours_ref, other_ref, query_ref, weight_ref = refs
    y, x, core = coordinates()
    depth = tokens_ref.shape[1]
    rows = qkv_ref.shape[0]
    steps = len(STEPS)
    rest_at = ours_ref.shape[0] - 2 * steps * REST
    places = chip_places(y, x)

    def block(of_core, index, lanes):
        pack, k = index
        mine_ref, theirs_ref = packs[2 * pack], packs[2 * pack + 1]
        return jnp.where(core == of_core, mine_ref[k, :, lanes], theirs_ref[k, :, lanes])


    def rest(of_core, lanes):
        return jnp.where(core == of_core, ours_ref[rest_at:, lanes], other_ref[rest_at:, lanes])

    def put(row, value, lanes):
        weight_ref[pl.ds(pl.multiple_of(row, REST), value.shape[0]), lanes] = value

    for at in range(0, depth, WIDE):
        lanes = slice(at, min(at + WIDE, depth))
        order = [(0, 2 * k) for k in range(steps)] + [(1, k) for k in range(2 * steps)]
        order += [(0, 2 * k + 1) for k in range(steps)]
        columns = [qkv_ref[:, lanes]] + [block(0, k, lanes) for k in order] + [rest(0, lanes)]
        queries = jnp.dot(
            tokens_ref[...], jnp.concatenate(columns, axis=0), preferred_element_type=jnp.float32
        )
        query_ref[:, lanes] = jnp.maximum(queries, 0.0).astype(jnp.bfloat16)

        put(lax.axis_index("space") * rows, out_ref[:, lanes], lanes)
        tiles = rest(1, lanes)
        for k, step in enumerate(STEPS):
            base = source_plane(step) * rows
            held = ((0, 2 * k), (1, steps + k), (1, k), (0, 2 * k + 1))
            for place, index in zip(places, held):
                put(base + place * MAIN, block(1, index, lanes), lanes)
            for run, tile in enumerate((y, 1 - y)):
                start = (run * steps + k) * REST
                put(base + 4 * MAIN + tile * REST, tiles[start : start + REST], lanes)


def query_call(tokens, qkv_weight, out_weight, *landed):
    depth = tokens.shape[1]
    inputs = (tokens, qkv_weight, out_weight) + landed
    return kernel_call(
        query_kernel,
        [
            jax.ShapeDtypeStruct(tokens.shape, jnp.bfloat16),
            jax.ShapeDtypeStruct((depth, depth), jnp.bfloat16),
        ],
        inputs,
        [whole_vmem()] * len(inputs),
        flops=2 * tokens.size * depth,
        bytes_accessed=4 * depth * depth,
    )


def finish_kernel(*refs):
    queries_ref, weight_ref, state_ref, local_ref, near_ref, next_ref, *refs = refs
    conv_ref, gain_ref, result_ref, read_ref, mixture_ref = refs
    count, depth = queries_ref.shape
    columns = near_ref.shape[1]
    even = lax.rem(lax.axis_index("space"), 2) == 0
    mask = diagonal_mask()
    square = jnp.zeros((count, LANES), jnp.float32)
    empty = jnp.zeros((LANES, LANES), jnp.bfloat16)

    def spread(group):
        tall = jnp.concatenate([state_ref[group]] * (LANES // HEAD_DIM), axis=0)
        return jnp.where(mask, tall, 0.0).astype(jnp.bfloat16)

    for at in range(0, depth, WIDE):
        lanes = slice(at, min(at + WIDE, depth))
        block = spread(at // LANES)
        if at + WIDE <= depth:
            right = jnp.concatenate([empty, spread(at // LANES + 1)], axis=0)
            block = jnp.concatenate([jnp.concatenate([block, empty], axis=0), right], axis=1)
        read = jnp.dot(queries_ref[:, lanes], block, preferred_element_type=jnp.float32)
        read_ref[:, lanes] = read
        for k in range(read.shape[1] // LANES):
            part = read[:, k * LANES : (k + 1) * LANES]
            square = square + part * part
    scale = lax.rsqrt(jnp.sum(square, axis=1, keepdims=True) / depth + 1e-06)
    for at in range(0, depth, LANES):
        lanes = slice(at, at + LANES)
        taps = conv_ref[:, :, lanes]
        mixture = read_ref[:, lanes] * scale * gain_ref[:, lanes] + local_ref[:, lanes]
        near = near_ref[:, :, lanes].astype(jnp.float32)
        beyond = next_ref[:, :, lanes].astype(jnp.float32)
        above = column_taps(jnp.where(even, beyond, near), taps[0])[0]
        below = column_taps(jnp.where(even, near, beyond), taps[2])[0]
        middle = mixture[columns : count - columns]
        mixture = jnp.concatenate(
            [mixture[:columns] + above, middle, mixture[count - columns :] + below], axis=0
        )
        mixture_ref[:, lanes] = mixture.astype(jnp.bfloat16)
    for at in range(0, depth, WIDE):
        lanes = slice(at, min(at + WIDE, depth))
        product = jnp.dot(
            mixture_ref[...], weight_ref[:, lanes], preferred_element_type=jnp.float32
        )
        result_ref[:, lanes] = product.astype(jnp.bfloat16)


def finish_call(queries, *inputs):
    return kernel_call(
        finish_kernel,
        jax.ShapeDtypeStruct(queries.shape, jnp.bfloat16),
        (queries,) + inputs,
        [whole_vmem()] * (1 + len(inputs)),
        [pltpu.VMEM(queries.shape, jnp.float32), pltpu.VMEM(queries.shape, jnp.bfloat16)],
        flops=2 * queries.size * queries.shape[1],
        bytes_accessed=2 * queries.shape[1] ** 2,
    )


def plane_form(video_tokens, qkv_weight, out_weight, conv_weight, norm_gain):
    frame_now = video_tokens[0]
    row_count, col_count, depth = frame_now.shape
    tokens = frame_now.reshape(row_count * col_count, depth)

    first_piece, second_piece = pieces_call(qkv_weight, out_weight)
    first_piece = first_piece[None]
    one = shifted(first_piece, 1)
    three = shifted(first_piece, -1)
    tokens = reorder_call(after(tokens, second_piece), qkv_weight.shape[0])
    other_tokens = flipped(tokens, (1, 1))
    one, three = after((one, three), tokens)

    pair = jnp.concatenate([one, three])
    two = shifted(one, 1)
    pair_first = flipped(pair, (2, 4))
    near = jnp.concatenate(after((pair, pair_first), other_tokens))
    away = flipped(near, (4, 2))
    two_near = jnp.concatenate([two, flipped(two, (2, 4))])
    two_away = flipped(two_near, (4, 2))

    second_ready = after(second_piece, one, three)
    second_one = shifted(second_ready, 1)
    second_three = shifted(second_ready, -1)
    second_two = shifted(after(second_one, two_near), 1)

    mine = first_call(after(tokens, second_one, second_three), other_tokens, qkv_weight, near, away, two_near, two_away)
    other = flipped(after(mine, second_two), (1, 1))
    straight = jnp.concatenate([second_one, second_two, second_three])
    swapped_straight = flipped(straight, (1, 1))
    values, edge_near, edge_next, upto, total = state_call(mine, other, tokens.shape[0], col_count)
    total = after(total, swapped_straight)

    second_own = jnp.stack([second_one[0], second_two[0], second_three[0]])
    second_first = flipped(second_own, (2, 4))
    second_second = flipped(second_own, (4, 2))

    for bit, guard in ((2, 2), (4, 4), (6, 4)):
        pairs = [(t, t ^ bit) for t in range(8) if not t & guard]
        upto = upto + lax.ppermute(total, "tm", pairs).astype(jnp.float32)
    count = lax.axis_size("space")
    state = after(upto, second_first, second_second)
    turned = jnp.concatenate(after((second_first, second_second), total))
    swapped_turned = flipped(after(turned, upto), (1, 1))
    queries, weight = query_call(
        tokens,
        qkv_weight,
        out_weight,
        straight,
        swapped_straight,
        turned,
        swapped_turned,
        mine,
        other,
    )
    share = state.astype(jnp.bfloat16)
    grid = values.reshape(row_count, col_count, depth)
    local_term = local_call(grid, conv_weight).reshape(-1, depth)
    arrived = lax.ppermute(share, "space", [(i, i ^ 1) for i in range(count)])
    arrived = after(arrived, local_term, queries, weight)
    share = (share.astype(jnp.float32) + arrived.astype(jnp.float32)).astype(jnp.bfloat16)
    arrived = lax.ppermute(share, "space", [(i, count - 1 - i) for i in range(count)])
    edge_near, edge_next = after((edge_near, edge_next), share)
    edge_near = lax.ppermute(edge_near, "space", [(i, i ^ 1) for i in range(count)])
    between = [(i, i + 1) for i in range(1, count - 1, 2)]
    between += [(target, source) for source, target in between]
    edge_next = lax.ppermute(edge_next, "space", between)


    state = share.astype(jnp.float32) + arrived.astype(jnp.float32)
    result = finish_call(
        queries,
        weight,
        state,
        local_term,
        edge_near,
        edge_next,
        conv_weight,
        norm_gain[None],
    )
    return result.reshape(1, row_count, col_count, depth)


def solution(mesh):
    def per_device(video_tokens, qkv_weight, out_weight, conv_weight, norm_gain):
        fits = mesh.shape["tm"] == 8 and mesh.shape["space"] == 4
        fits = fits and qkv_weight.shape[0] == 4 * MAIN + 2 * REST
        form = plane_form if fits else general_form
        return form(video_tokens, qkv_weight, out_weight, conv_weight, norm_gain)

    in_specs = (P("tm", "space", None, None), P("space", None), P("space", None), P(), P())
    out_specs = P("tm", "space", None, None)
    return jax.shard_map(
        per_device, mesh=mesh, in_specs=in_specs, out_specs=out_specs, check_vma=False
    )
```
